32 devices in a mesh: dp: 8 (over z, y), seq: 4 (over x, core).
Axes of the slice: x: 2, y: 2, z: 4, core: 2. Of those that a mesh axis runs over, the one named last changes fastest.
Arguments:
- tokens: bfloat16 [24, 1024, 384], P('dp', 'seq'), may hold values from -6 to 6
- timestep: bfloat16 [24, 384], P('dp'), may hold values from -6 to 6
- counts: int32 [8], P('dp'), may hold values from 1 to 3, as said below
- token_mask: int32 [24, 1024], P('dp', 'seq'), may hold values 0 or 1
- ada_weight: bfloat16 [384, 1152], replicated, may hold values from -0.3125 to 0.3125
- ada_bias: float32 [1152], replicated, may hold values from -1.5 to 1.5
- input_weight: bfloat16 [384, 1536], replicated, may hold values from -0.3125 to 0.3125
- conv_weight: float32 [2, 4, 768], replicated, may hold values from -2.5 to 2.5
- conv_bias: float32 [2, 768], replicated, may hold values from -1.5 to 1.5
- x_weight: bfloat16 [2, 768, 56], replicated, may hold values from -0.109375 to 0.109375
- dt_weight: bfloat16 [2, 24, 768], replicated, may hold values from -6 to 6
- dt_bias: float32 [2, 768], replicated, may hold values from -2 to 0.5
- decay_rate: float32 [2, 16, 768], replicated, may hold values from 0.0001 to 0.05
- skip_gain: float32 [2, 768], replicated, may hold values from 0.5 to 1.5
- output_weight: bfloat16 [768, 384], replicated, may hold values from -0.21875 to 0.21875
- cotangent: bfloat16 [24, 1024, 384], P('dp', 'seq'), may hold values from -6 to 6
Outputs:
- mixed: bfloat16 [24, 1024, 384], P('dp', 'seq')
- grad_tokens: float32 [24, 1024, 384], P('dp', 'seq')
- grad_time: float32 [24, 384], P('dp')
- grad_ada: float32 [384, 1152], replicated
- grad_ada_bias: float32 [1152], replicated
- input_weight_gradient: float32 [384, 1536], replicated
- grad_conv: float32 [2, 4, 768], replicated
- grad_conv_bias: float32 [2, 768], replicated
- grad_xproj: float32 [2, 768, 56], replicated
- grad_dtproj: float32 [2, 24, 768], replicated
- grad_dt_bias: float32 [2, 768], replicated
- grad_rate: float32 [2, 16, 768], replicated
- grad_skip: float32 [2, 768], replicated
- output_weight_gradient: float32 [768, 384], replicated
The draws below stay inside these ranges and needn't reach their ends.
Inputs may be any that keep to these rules, and one draw needn't show every extreme that they name: `counts`: number of live item slots of each dp index; padding slots are the highest ones; every draw has an index with 3 and one with 1. `token_mask`: 1 for a valid token, 0 for a dropped one.
All inputs are finite; a program needn't handle non-finite values. No bound on the sum of `token_mask` on one device may be relied on, other than what follows from the above.
Results may differ from the reference program's by a relative error of at most 0.008.
The reference program's roundings to bfloat16 on the way count: a program that leaves them out, or rounds other values in their place, can miss the bound.
Values may be sent and summed in bfloat16 or wider, within the bound.
A program may use at most 192 MiB of HBM per device.

```python
import math
import jax
import jax.numpy as jnp
from jax import lax

D = 384
E = 768
N = 16
R = 24
K = 4
ITEM_LEN = 1024
SLOTS = 3
BLOCK = 16
ITEMS = 24
PROJ = 56
N_DP = 8


def draw_counts(key, part):
    key = jax.random.fold_in(key, 11)
    key_one, key_two, key_three = jax.random.split(key, 3)
    values = jax.random.randint(key_one, (N_DP,), 1, SLOTS + 1)
    top_at = jax.random.randint(key_two, (), 0, N_DP)
    low_at = (top_at + jax.random.randint(key_three, (), 1, N_DP)) % N_DP
    values = values.at[top_at].set(SLOTS)
    values = values.at[low_at].set(1)
    return values.astype(jnp.int32)


def touch_ends(values, rng, least, top_value):
    place = [jax.random.randint(jax.random.fold_in(rng, axis), (), 0, length) for axis, length in enumerate(values.shape)]
    longest = values.shape.index(max(values.shape))
    neighbour = place[:longest] + [(place[longest] + 1) % values.shape[longest]] + place[longest + 1:]
    return values.at[tuple(place)].set(least).at[tuple(neighbour)].set(top_value)


def steps_of(key, extent, shards, smallest, largest):
    factor_of, own = 1.0, jax.random.fold_in(key, 6)
    for axis_at, parts in shards:
        draws = jnp.exp(jax.random.uniform(jax.random.fold_in(own, axis_at), (parts,), jnp.float32, smallest / len(shards), largest / len(shards)))
        factor_of = factor_of * jnp.repeat(draws, extent[axis_at] // parts).reshape([-1 if axis == axis_at else 1 for axis in range(len(extent))])
    return factor_of


def bell_draw(key, extent, spread, bound, shards=(), kind=jnp.bfloat16):
    factor_of = steps_of(key, extent, shards, -0.22, 0.18) if shards else 1.0
    entries = jax.random.normal(key, extent, jnp.float32) * spread * factor_of
    return jnp.minimum(jnp.maximum(entries, -bound), bound).astype(kind)


def setup_inputs(seed: int = 0) -> dict:
    key_list = jax.random.split(jax.random.key(seed), 17)
    tokens = bell_draw(key_list[0], (ITEMS, ITEM_LEN, D), 1.0, 6.0, ((0, 8), (1, 4)))
    timestep = bell_draw(key_list[1], (ITEMS, D), 1.0, 6.0, ((0, 8),))
    counts = draw_counts(jax.random.fold_in(key_list[16], 71), 0)
    token_mask = touch_ends((jax.random.randint(key_list[3], (ITEMS, ITEM_LEN), 0, 16) < 15).astype(jnp.int32), jax.random.fold_in(key_list[3], 1), 0, 1)
    ada_weight = bell_draw(key_list[4], (D, 3 * D), D ** -0.5, 0.3125)
    ada_bias = bell_draw(key_list[5], (3 * D,), 0.3, 1.5, (), jnp.float32)
    input_weight = bell_draw(key_list[6], (D, 2 * E), D ** -0.5, 0.3125)
    conv_weight = bell_draw(key_list[7], (2, K, E), 0.5, 2.5, (), jnp.float32)
    conv_bias = bell_draw(key_list[8], (2, E), 0.3, 1.5, (), jnp.float32)
    x_weight = bell_draw(key_list[9], (2, E, PROJ), (4 * E) ** -0.5, 0.109375)
    dt_weight = bell_draw(key_list[10], (2, R, E), (max(R // 16, 1)) ** -0.5, 6.0)
    dt_bias = jnp.clip(jax.random.uniform(key_list[11], (2, E), jnp.float32, -2.0, 0.5), -2.0, 0.5)
    decay_rate = jnp.clip(jnp.exp(jax.random.uniform(key_list[12], (2, N, E), jnp.float32, math.log(0.0001), math.log(0.05))), 0.0001, 0.05)
    skip_gain = jnp.clip(jax.random.uniform(key_list[13], (2, E), jnp.float32, 0.5, 1.5), 0.5, 1.5)
    output_weight = bell_draw(key_list[14], (E, D), E ** -0.5, 0.21875)
    cotangent = bell_draw(key_list[15], (ITEMS, ITEM_LEN, D), 1.0, 6.0, ((0, 8), (1, 4)))
    return {"tokens": tokens, "timestep": timestep, "counts": counts, "token_mask": token_mask, "ada_weight": ada_weight, "ada_bias": ada_bias, "input_weight": input_weight, "conv_weight": conv_weight, "conv_bias": conv_bias, "x_weight": x_weight, "dt_weight": dt_weight, "dt_bias": dt_bias, "decay_rate": decay_rate, "skip_gain": skip_gain, "output_weight": output_weight, "cotangent": cotangent}


@jax.custom_vjp
def low(v):
    return lax.optimization_barrier(v.astype(jnp.bfloat16)).astype(jnp.float32)

@jax.custom_vjp
def low_back(v):
    return v

def low_keep(v):
    return (low(v), None)

def low_pass(kept, grad):
    return (grad,)

def back_keep(v):
    return (v, None)

def back_low(kept, grad):
    return (low(grad),)
low.defvjp(low_keep, low_pass)
low_back.defvjp(back_keep, back_low)
EPSILON = 1e-06

def product(left, right, form):
    return jnp.einsum(form, left, right, precision=lax.Precision.HIGHEST)

def convolve(padded, weight, tok_len, backward_dir):
    tap_count = weight.shape[0]
    result = jnp.zeros(padded.shape[:1] + (tok_len,) + padded.shape[2:], jnp.float32)
    for tap_index in range(tap_count):
        offset = 2 * (tap_count - 1) - tap_index if backward_dir else tap_index
        result = result + weight[tap_index] * padded[:, offset:offset + tok_len]
    return result

def to_blocks(member):
    lead_dim, tok_len = (member.shape[0], member.shape[1])
    shaped = member.reshape((lead_dim, tok_len // BLOCK, BLOCK) + member.shape[2:])
    return jnp.moveaxis(shaped, 0, 2)

def from_blocks(member, lead_dim):
    shaped = jnp.moveaxis(member, 2, 0)
    return shaped.reshape((lead_dim, -1) + shaped.shape[3:])

def advance(carried, pieces, decay_rate):

    def advance_one(carried, moment):
        delta_t, act_t, b_t, c_t = moment
        multiplier = jnp.exp(-decay_rate * delta_t[:, None, :])
        carried = multiplier * carried + (delta_t * act_t)[:, None, :] * b_t[:, :, None]
        return (carried, lax.optimization_barrier(jnp.sum(c_t[:, :, None] * carried, axis=1)))
    return lax.scan(advance_one, carried, pieces)

def recurrence(delta, act_in, b_proj, c_proj, decay_rate):
    batch_count = delta.shape[0]
    checked = jax.checkpoint(advance)

    def run_block(carried, pieces):
        return checked(carried, pieces, decay_rate)
    initial = jnp.zeros((batch_count,) + decay_rate.shape, jnp.float32)
    pieces = tuple((to_blocks(member) for member in (delta, act_in, b_proj, c_proj)))
    y_blocks = lax.scan(run_block, initial, pieces)[1]
    return from_blocks(y_blocks, batch_count)

def mamba_layer(tokens_f, time_f, valid, ada_weight, ada_bias, input_weight, conv_weight, conv_bias, x_weight, dt_weight, dt_bias, decay_rate, skip_gain, output_weight):
    modulate = low_back(product(low(jax.nn.silu(time_f)), ada_weight, 'bd,df->bf') + ada_bias)
    shift_mod = modulate[:, None, :D]
    scale_mod = modulate[:, None, D:2 * D]
    gate_mod = modulate[:, None, 2 * D:]
    centered = tokens_f - lax.optimization_barrier(jnp.mean(tokens_f, axis=-1, keepdims=True))
    variance = lax.optimization_barrier(jnp.mean(centered * centered, axis=-1, keepdims=True))
    normed = centered * lax.rsqrt(variance + EPSILON)
    hidden_state = low(normed * (1.0 + scale_mod) + shift_mod)
    x_and_z = low_back(product(hidden_state, input_weight, 'bld,df->blf')) * valid[:, :, None]
    x_low = low(x_and_z[:, :, :E])
    z_gate = x_and_z[:, :, E:]
    padded = jnp.pad(x_low, ((0, 0), (K - 1, K - 1), (0, 0)))
    summed = jnp.zeros_like(z_gate)
    for branch in range(2):
        conv_out = convolve(padded, conv_weight[branch], ITEM_LEN, branch == 1) + conv_bias[branch]
        act_in = low(jax.nn.silu(conv_out))
        projected = low_back(product(act_in, x_weight[branch], 'ble,ep->blp'))
        dt_low = low(projected[:, :, :R])
        b_proj = projected[:, :, R:R + N]
        c_proj = projected[:, :, R + N:]
        delta = jax.nn.softplus(low_back(product(dt_low, dt_weight[branch], 'blr,re->ble')) + dt_bias[branch])
        ordered = [delta, act_in, b_proj, c_proj]
        if branch == 1:
            ordered = [jnp.flip(member, 1) for member in ordered]
        y_scan = recurrence(ordered[0], ordered[1], ordered[2], ordered[3], decay_rate[branch])
        if branch == 1:
            y_scan = jnp.flip(y_scan, 1)
        summed = summed + y_scan + skip_gain[branch] * act_in
    gated_output = low(summed * jax.nn.silu(z_gate))
    branch_result = low_back(product(gated_output, output_weight, 'ble,ed->bld'))
    return tokens_f + gate_mod * branch_result

def reference(tokens, timestep, counts, token_mask, ada_weight, ada_bias, input_weight, conv_weight, conv_bias, x_weight, dt_weight, dt_bias, decay_rate, skip_gain, output_weight, cotangent):
    item_ids = jnp.arange(ITEMS)
    live = (item_ids % SLOTS < counts[item_ids // SLOTS]).astype(jnp.float32)
    valid = token_mask.astype(jnp.float32) * live[:, None]
    grouped = math.gcd(4, ITEMS)
    group_count = ITEMS // grouped
    weights = tuple((member.astype(jnp.float32) for member in (ada_weight, ada_bias, input_weight, conv_weight, conv_bias, x_weight, dt_weight, dt_bias, decay_rate, skip_gain, output_weight)))
    layer_checked = jax.checkpoint(mamba_layer)

    def whole(tokens_f, time_f, *params):

        def one_group(carry, pieces):
            return (carry, layer_checked(pieces[0], pieces[1], pieces[2], *params))
        pieces = (tokens_f.reshape(group_count, grouped, ITEM_LEN, D), time_f.reshape(group_count, grouped, D), valid.reshape(group_count, grouped, ITEM_LEN))
        results = lax.scan(one_group, jnp.zeros((), jnp.float32), pieces)[1]
        return results.reshape(ITEMS, ITEM_LEN, D)
    result, pullback = jax.vjp(whole, tokens.astype(jnp.float32), timestep.astype(jnp.float32), *weights)
    grads = pullback(cotangent.astype(jnp.float32))
    return (result.astype(jnp.bfloat16), grads[0], grads[1], grads[2], grads[3], grads[4], grads[5], grads[6], grads[7], grads[8], grads[9], grads[10], grads[11], grads[12])
```

```python
import functools
import math

import jax
import jax.numpy as jnp
from jax import lax
from jax.experimental import pallas as pl
from jax.experimental.pallas import tpu as pltpu
from jax.sharding import PartitionSpec as P

EPSILON = 1e-06
BLK = 16
HALO = 16
LOG2E = math.log2(math.e)
F32, BF16 = jnp.float32, jnp.bfloat16
NT = (((1,), (1,)), ((), ()))
TN = (((0,), (0,)), ((), ()))
VMEM_LIMIT = 60 << 20


def dot(a, b):
    return jnp.dot(a, b, preferred_element_type=F32)


def dot_nt(a, b):
    return lax.dot_general(a, b, NT, preferred_element_type=F32)


def dot_tn(a, b):
    return lax.dot_general(a, b, TN, preferred_element_type=F32)


def reversal(size):
    rows = lax.broadcasted_iota(jnp.int32, (size, size), 0)
    cols = lax.broadcasted_iota(jnp.int32, (size, size), 1)
    return (rows + cols == size - 1).astype(BF16)


def flip_low(value):
    return dot(reversal(value.shape[0]), value).astype(BF16)


def flip_full(value):
    order = reversal(value.shape[0])
    high = value.astype(BF16)
    return dot(order, high) + dot(order, (value - high.astype(F32)).astype(BF16))


def normalise(tokens_f):
    centered = tokens_f - jnp.mean(tokens_f, axis=-1, keepdims=True)
    inv_std = lax.rsqrt(jnp.mean(centered * centered, axis=-1, keepdims=True) + EPSILON)
    return centered * inv_std, inv_std


def enter_kernel(tok, prev, nxt, cot, mod, valid, win, wout, xe, dy, z_out, hid_out):
    dim = tok.shape[-1]
    inner = wout.shape[0]
    shift, scale, gate = mod[:, :dim], mod[:, dim : 2 * dim], mod[:, 2 * dim :]

    def hidden_of(part):
        normed, _ = normalise(part.astype(F32))
        return (normed * (1.0 + scale) + shift).astype(BF16)

    hid = hidden_of(tok[...])
    hid_out[...] = hid
    xz = dot(hid, win[...]) * valid[...]
    x_low = xz[:, :inner].astype(BF16)
    z = xz[:, inner:]
    z_out[...] = z
    rims = jnp.concatenate([prev[...], nxt[...]], axis=0)
    rim_x = dot(hidden_of(rims[:, :dim]), win[:, :inner]) * rims[:, dim : dim + 1].astype(F32)
    rim_x = rim_x.astype(BF16)
    xe[0, :HALO, :] = rim_x[:HALO]
    xe[0, HALO:, :] = x_low
    xe[1, :HALO, :] = flip_low(rim_x[HALO:])
    xe[1, HALO:, :] = flip_low(x_low)
    d_branch = (cot[...].astype(F32) * gate).astype(BF16)
    d_summed = dot_nt(d_branch, wout[...]) * z * jax.nn.sigmoid(z)
    dy[0] = d_summed
    dy[1] = flip_full(d_summed)


def twice(row8):
    return jnp.concatenate([row8, row8], axis=0)


def spread(ref, index):
    return twice(ref[pl.ds(index, 8, stride=0), :])


def columns(ref, block, first, count):
    lane = pl.multiple_of((block // 8) * 128, 128)
    return pltpu.roll(ref[first : first + count, pl.ds(lane, 128)], (128 - (block % 8) * BLK) % 128, 1)


def first_kernel(
    xe, dy, taps, tap_bias, xwt, dtw, dt_bias, rate2,
    act_out, dsilu_out, delta_out, sig_out, proj_out, end_out, back_out, total_out, starts_out, sums_out,
    xf, dl, dx, drow, xrow, yrow, decay, through,
):
    toks, inner = dy.shape
    states = rate2.shape[0]
    blocks = toks // BLK
    rank = dtw.shape[0]
    tap_count = taps.shape[0]
    xf[...] = xe[...].astype(F32)
    conv = tap_bias[...] + jnp.zeros((toks, inner), F32)
    for k in range(tap_count):
        conv = conv + taps[k : k + 1, :] * xf[HALO - tap_count + 1 + k : HALO - tap_count + 1 + k + toks, :]
    sig = jax.nn.sigmoid(conv)
    act = (conv * sig).astype(BF16)
    dsilu_out[...] = sig * (1.0 + conv * (1.0 - sig))
    act_out[...] = act
    proj = dot_nt(xwt[...], act)
    proj_out[...] = proj
    pre = dot_tn(proj[:rank, :].astype(BF16), dtw[...]) + dt_bias[...]
    delta = jnp.maximum(pre, 0.0) + jnp.log1p(jnp.exp(-jnp.abs(pre)))
    delta_out[...] = delta
    sig_out[...] = jax.nn.sigmoid(pre)
    dl[...] = delta
    dx[...] = delta * act.astype(F32)
    end_out[...] = jnp.zeros((states, inner), F32)
    back_out[...] = jnp.zeros((states, inner), F32)
    through[...] = jnp.zeros((8, inner), F32)

    def block_step(j, _):
        t0 = pl.multiple_of(j * BLK, BLK)
        drow[...] = dl[pl.ds(t0, BLK), :]
        xrow[...] = dx[pl.ds(t0, BLK), :]
        yrow[...] = dy[pl.ds(t0, BLK), :]
        bt = columns(proj_out, j, rank, states)
        ct = columns(proj_out, j, rank + states, states)
        rate = rate2[...]
        s = end_out[...]
        starts_out[j] = s
        before = through[...]
        sums_out[j] = before[:1, :]
        for i in range(BLK):
            a = jnp.exp2(spread(drow, i) * rate)
            decay[i] = a
            s = a * s + spread(xrow, i) * jnp.broadcast_to(bt[:, i : i + 1], (states, inner))
        end_out[...] = s
        m = jnp.zeros((states, inner), F32)
        for i in reversed(range(BLK)):
            m = decay[i] * (m + spread(yrow, i) * jnp.broadcast_to(ct[:, i : i + 1], (states, inner)))
        back_out[...] = back_out[...] + m * jnp.exp2(twice(before) * rate)
        through[...] = before + jnp.sum(drow[...], axis=0, keepdims=True)
        return 0

    lax.fori_loop(0, blocks, block_step, 0)
    total_out[...] = through[:1, :]


def second_kernel(
    place, ends, backs, totals, starts, sums, rate2, rate, xe, act, dsilu, delta, sig, dy, proj, xwt, bwide, cwide, dtw, taps, skip,
    y_out, dxe_out, rate_grad, skip_grad, dtb_grad, dtp_grad, xp_grad, tap_grad, tapb_grad,
    enter, carry, dxs, bdiag, cdiag, drow, xrow, yrow, decay, states_low, lam_low, rq_low, racc, gsum, hsum, db, dc, pads, xf,
):
    toks, inner = dy.shape
    states = rate2.shape[0]
    blocks = toks // BLK
    rank = dtw.shape[0]
    tap_count = taps.shape[0]
    branch = pl.program_id(0)
    item = pl.program_id(1)
    runs = ends.shape[0]
    me = place[0]
    r2 = rate2[...]
    mine = jnp.where(branch == 0, me, runs - 1 - me)
    s_in = jnp.zeros((states, inner), F32)
    lam_in = jnp.zeros((states, inner), F32)
    for position in range(runs):
        run = jnp.where(branch == 0, position, runs - 1 - position)
        passing = jnp.exp2(twice(jnp.broadcast_to(totals[run], (8, inner))) * r2)
        s_in = jnp.where(position < mine, passing * s_in + ends[run], s_in)
    for position in reversed(range(runs)):
        run = jnp.where(branch == 0, position, runs - 1 - position)
        passing = jnp.exp2(twice(jnp.broadcast_to(totals[run], (8, inner))) * r2)
        lam_in = jnp.where(position > mine, passing * lam_in + backs[run], lam_in)
    enter[...] = s_in
    carry[...] = lam_in
    act_low = act[...]
    act_f = act_low.astype(F32)
    dxs[...] = delta[...] * act_f
    width = bwide.shape[1]
    own = lax.broadcasted_iota(jnp.int32, (toks, width), 0) % BLK == lax.broadcasted_iota(jnp.int32, (toks, width), 1) // states
    bdiag[...] = jnp.where(own, dot(act_low, bwide[...]), 0.0).astype(BF16)
    cdiag[...] = jnp.where(own, dot(act_low, cwide[...]), 0.0).astype(BF16)
    racc[...] = jnp.zeros((states, inner), F32)

    def block_step(step, _):
        j = blocks - 1 - step
        t0 = pl.multiple_of(j * BLK, BLK)
        drow[...] = delta[pl.ds(t0, BLK), :]
        xrow[...] = dxs[pl.ds(t0, BLK), :]
        yrow[...] = dy[pl.ds(t0, BLK), :]
        bt = columns(proj, j, rank, states)
        ct = columns(proj, j, rank + states, states)
        r2 = rate2[...]
        rr = rate[...]
        s = starts[j] + enter[...] * jnp.exp2(twice(jnp.broadcast_to(sums[j], (8, inner))) * r2)
        states_low[:states, :] = s.astype(BF16)
        for i in range(BLK):
            a = jnp.exp2(spread(drow, i) * r2)
            decay[i] = a
            s = a * s + spread(xrow, i) * jnp.broadcast_to(bt[:, i : i + 1], (states, inner))
            states_low[(i + 1) * states : (i + 2) * states, :] = s.astype(BF16)
        cr = carry[...]
        ra = racc[...]
        for i in reversed(range(BLK)):
            lam = cr + spread(yrow, i) * jnp.broadcast_to(ct[:, i : i + 1], (states, inner))
            lam_low[i * states : (i + 1) * states, :] = lam.astype(BF16)
            cr = decay[i] * lam
            q = cr * states_low[i * states : (i + 1) * states, :].astype(F32)
            rq_low[i * states : (i + 1) * states, :] = (q * rr).astype(BF16)
            ra = ra + q * spread(drow, i)
        carry[...] = cr
        racc[...] = ra
        after = states_low[states:, :]
        lam_all = lam_low[...]
        y_out[pl.ds(t0, BLK), :] = dot(cdiag[pl.ds(t0, BLK), :], after)
        gsum[pl.ds(t0, BLK), :] = dot(bdiag[pl.ds(t0, BLK), :], lam_all)
        ones = (
            lax.broadcasted_iota(jnp.int32, (BLK, BLK * states), 1) // states
            == lax.broadcasted_iota(jnp.int32, (BLK, BLK * states), 0)
        )
        hsum[pl.ds(t0, BLK), :] = dot(ones.astype(BF16), rq_low[...])
        dc[pl.ds(t0, BLK), :] = jnp.where(ones, dot_nt(yrow[...].astype(BF16), after), 0.0).astype(BF16)
        db[pl.ds(t0, BLK), :] = jnp.where(ones, dot_nt(xrow[...].astype(BF16), lam_all), 0.0).astype(BF16)
        return 0

    lax.fori_loop(0, blocks, block_step, 0)

    @pl.when(item == 0)
    def _():
        for ref in (rate_grad, skip_grad, dtb_grad, dtp_grad, xp_grad, tap_grad, tapb_grad):
            ref[...] = jnp.zeros(ref.shape, ref.dtype)

    rate_grad[...] += -racc[...]
    d_summed = dy[...]
    g = gsum[...]
    skip_grad[...] += jnp.sum(d_summed * act_f, axis=0, keepdims=True)
    y_out[...] += skip[...] * act_f
    d_pre = (act_f * g - hsum[...]) * sig[...]
    dtb_grad[...] += jnp.sum(d_pre, axis=0, keepdims=True)
    d_pre_low = d_pre.astype(BF16)
    dtp_grad[...] += dot(proj[:rank, :].astype(BF16), d_pre_low)
    fold = (
        lax.broadcasted_iota(jnp.int32, (states, width), 1) % states == lax.broadcasted_iota(jnp.int32, (states, width), 0)
    ).astype(BF16)
    d_proj = jnp.concatenate(
        [dot_nt(dtw[...], d_pre_low), dot_nt(fold, db[...]), dot_nt(fold, dc[...])], axis=0
    ).astype(BF16)
    xp_grad[...] += dot(d_proj, act_low)
    d_act = delta[...] * g + skip[...] * d_summed + dot_tn(d_proj, xwt[...])
    d_conv = d_act * dsilu[...]
    tapb_grad[...] += jnp.sum(d_conv, axis=0, keepdims=True)
    xf[...] = xe[...].astype(F32)
    pads[:HALO, :] = jnp.zeros((HALO, inner), F32)
    pads[HALO : HALO + toks, :] = d_conv
    pads[HALO + toks :, :] = jnp.zeros((HALO, inner), F32)
    d_window = jnp.zeros((HALO + toks, inner), F32)
    first = HALO - tap_count + 1
    for k in range(tap_count):
        tap_grad[k : k + 1, :] += jnp.sum(d_conv * xf[first + k : first + k + toks, :], axis=0, keepdims=True)
        d_window = d_window + taps[k : k + 1, :] * pads[tap_count - 1 - k : tap_count - 1 - k + HALO + toks, :]
    dxe_out[...] = d_window


def third_kernel(
    tok, cot, mod, valid, hid, z_in, y, dxe, late, win, wout,
    mixed, d_tokens, d_mod, out_grad, in_grad,
):
    dim = tok.shape[-1]
    toks, inner = z_in.shape
    shift, scale, gate = mod[:, :dim], mod[:, dim : 2 * dim], mod[:, 2 * dim :]
    tok_f = tok[...].astype(F32)
    normed, inv_std = normalise(tok_f)
    cot_f = cot[...].astype(F32)
    z = z_in[...]
    z_sig = jax.nn.sigmoid(z)
    summed = y[0] + flip_full(y[1])
    gated = (summed * z * z_sig).astype(BF16)
    branch_out = dot(gated, wout[...])
    mixed[...] = (tok_f + gate * branch_out).astype(BF16)
    d_branch = (cot_f * gate).astype(BF16)
    d_gated = dot_nt(d_branch, wout[...])
    d_zgate = d_gated * summed * z_sig * (1.0 + z * (1.0 - z_sig))
    edge = late.shape[1]

    def with_late(part, extra):
        return jnp.concatenate([part[: toks - edge], part[toks - edge :] + extra], axis=0)

    d_x = with_late(dxe[0, HALO:, :], late[0]) + flip_full(with_late(dxe[1, HALO:, :], late[1]))
    d_xz = (jnp.concatenate([d_x, d_zgate], axis=1) * valid[...]).astype(BF16)
    d_hidden = dot_nt(d_xz, win[...])

    @pl.when(pl.program_id(0) == 0)
    def _():
        out_grad[...] = jnp.zeros(out_grad.shape, F32)
        in_grad[...] = jnp.zeros(in_grad.shape, F32)

    out_grad[...] += dot_tn(gated, d_branch)
    in_grad[...] += dot_tn(hid[...], d_xz)
    d_mod[:, :dim] = jnp.sum(d_hidden, axis=0, keepdims=True)
    d_mod[:, dim : 2 * dim] = jnp.sum(d_hidden * normed, axis=0, keepdims=True)
    d_mod[:, 2 * dim :] = jnp.sum(cot_f * branch_out, axis=0, keepdims=True)
    d_normed = d_hidden * (1.0 + scale)
    d_tokens[...] = cot_f + inv_std * (
        d_normed
        - jnp.mean(d_normed, axis=-1, keepdims=True)
        - normed * jnp.mean(d_normed * normed, axis=-1, keepdims=True)
    )


def params(**more):
    return pltpu.CompilerParams(vmem_limit_bytes=VMEM_LIMIT, **more)


def spec(block, index):
    return pl.BlockSpec(block, index)


def per_device(
    tokens, timestep, counts, token_mask, ada_weight, ada_bias, input_weight, conv_weight, conv_bias, x_weight, dt_weight,
    dt_bias, decay_rate, skip_gain, output_weight, cotangent,
):
    slots, toks, dim = tokens.shape
    inner = output_weight.shape[0]
    rank = dt_weight.shape[1]
    states = decay_rate.shape[1]
    tap_count = conv_weight.shape[1]
    wide_rank = 32
    proj_rows = wide_rank + 2 * states
    blocks = toks // BLK
    runs = lax.axis_size("seq")
    place = lax.axis_index("seq")
    live = (jnp.arange(slots) < counts[0]).astype(F32)
    valid = (token_mask.astype(F32) * live[:, None])[:, :, None]
    time_f = timestep.astype(F32)
    time_sig = jax.nn.sigmoid(time_f)
    time_low = (time_f * time_sig).astype(BF16)
    modulate = (dot(time_low, ada_weight) + ada_bias)[:, None, :]

    rim = jnp.concatenate([tokens, jnp.broadcast_to(valid, (slots, toks, 128)).astype(BF16)], axis=2)
    up = [(i, i + 1) for i in range(runs - 1)]
    down = [(i + 1, i) for i in range(runs - 1)]
    from_prev = lax.ppermute(rim[:, toks - HALO :], "seq", up)
    from_next = lax.ppermute(rim[:, :HALO], "seq", down)

    xwt = jnp.swapaxes(x_weight, 1, 2)
    xwt = jnp.concatenate(
        [xwt[:, :rank], jnp.zeros((2, wide_rank - rank, inner), BF16), xwt[:, rank:]], axis=1
    )
    dtw = jnp.concatenate([dt_weight, jnp.zeros((2, wide_rank - rank, inner), BF16)], axis=1)
    bwide = jnp.tile(x_weight[:, :, rank : rank + states], (1, 1, BLK))
    cwide = jnp.tile(x_weight[:, :, rank + states :], (1, 1, BLK))
    rate2 = -LOG2E * decay_rate
    vec = lambda a: a[:, None, :]

    def item(*block):
        return spec((None,) + block, lambda i: (i,) + (0,) * len(block))

    def whole(*block):
        return spec(block, lambda *_: (0,) * len(block))

    xe, dy, z_gate, hid = pl.pallas_call(
        enter_kernel,
        grid=(slots,),
        in_specs=[
            item(toks, dim), item(HALO, dim + 128), item(HALO, dim + 128), item(toks, dim), item(1, 3 * dim), item(toks, 1),
            whole(dim, 2 * inner), whole(inner, dim),
        ],
        out_specs=[item(2, HALO + toks, inner), item(2, toks, inner), item(toks, inner), item(toks, dim)],
        out_shape=[
            jax.ShapeDtypeStruct((slots, 2, HALO + toks, inner), BF16),
            jax.ShapeDtypeStruct((slots, 2, toks, inner), F32),
            jax.ShapeDtypeStruct((slots, toks, inner), F32),
            jax.ShapeDtypeStruct((slots, toks, dim), BF16),
        ],
        compiler_params=params(),
        name="enter",
    )(tokens, from_prev, from_next, cotangent, modulate, valid, input_weight, output_weight)

    def unit(*block):
        return spec((None, None) + block, lambda b, i: (i, b) + (0,) * len(block))

    def branch(*block):
        return spec((None,) + block, lambda b, i: (b,) + (0,) * len(block))

    def unit_shape(*block, kind=F32):
        return jax.ShapeDtypeStruct((slots, 2) + block, kind)

    act, dsilu, delta, sig, proj, end, back, total, starts, sums = pl.pallas_call(
        first_kernel,
        grid=(2, slots),
        in_specs=[
            unit(HALO + toks, inner), unit(toks, inner), branch(tap_count, inner), branch(1, inner), branch(proj_rows, inner),
            branch(wide_rank, inner), branch(1, inner), branch(states, inner),
        ],
        out_specs=[
            unit(toks, inner), unit(toks, inner), unit(toks, inner), unit(toks, inner), unit(proj_rows, toks),
            unit(states, inner), unit(states, inner), unit(1, inner), unit(blocks, states, inner), unit(blocks, 1, inner),
        ],
        out_shape=[
            unit_shape(toks, inner, kind=BF16), unit_shape(toks, inner), unit_shape(toks, inner), unit_shape(toks, inner),
            unit_shape(proj_rows, toks), unit_shape(states, inner), unit_shape(states, inner), unit_shape(1, inner),
            unit_shape(blocks, states, inner), unit_shape(blocks, 1, inner),
        ],
        scratch_shapes=[
            pltpu.VMEM((HALO + toks, inner), F32), pltpu.VMEM((toks, inner), F32), pltpu.VMEM((toks, inner), F32),
            pltpu.VMEM((BLK, inner), F32), pltpu.VMEM((BLK, inner), F32), pltpu.VMEM((BLK, inner), F32),
            pltpu.VMEM((BLK, states, inner), F32), pltpu.VMEM((8, inner), F32),
        ],
        compiler_params=params(),
        name="first",
    )(xe, dy, conv_weight, vec(conv_bias), xwt, dtw, vec(dt_bias), rate2)

    ends, backs, totals = (lax.all_gather(a, "seq") for a in (end, back, total))

    def gathered(*block):
        return spec((runs, None, None) + block, lambda b, i: (0, i, b) + (0,) * len(block))

    y, dxe, rate_grad, skip_grad, dtb_grad, dtp_grad, xp_grad, tap_grad, tapb_grad = pl.pallas_call(
        second_kernel,
        grid=(2, slots),
        in_specs=[
            pl.BlockSpec(memory_space=pltpu.SMEM),
            gathered(states, inner), gathered(states, inner), gathered(1, inner), unit(blocks, states, inner),
            unit(blocks, 1, inner), branch(states, inner), branch(states, inner), unit(HALO + toks, inner), unit(toks, inner),
            unit(toks, inner), unit(toks, inner), unit(toks, inner), unit(toks, inner), unit(proj_rows, toks),
            branch(proj_rows, inner), branch(inner, BLK * states), branch(inner, BLK * states), branch(wide_rank, inner),
            branch(tap_count, inner), branch(1, inner),
        ],
        out_specs=[
            unit(toks, inner), unit(HALO + toks, inner), branch(states, inner), branch(1, inner), branch(1, inner),
            branch(wide_rank, inner), branch(proj_rows, inner), branch(tap_count, inner), branch(1, inner),
        ],
        out_shape=[
            unit_shape(toks, inner), unit_shape(HALO + toks, inner),
        ] + [
            jax.ShapeDtypeStruct((2, rows, inner), F32) for rows in (states, 1, 1, wide_rank, proj_rows, tap_count, 1)
        ],
        scratch_shapes=[
            pltpu.VMEM((states, inner), F32), pltpu.VMEM((states, inner), F32), pltpu.VMEM((toks, inner), F32),
            pltpu.VMEM((toks, BLK * states), BF16), pltpu.VMEM((toks, BLK * states), BF16),
            pltpu.VMEM((BLK, inner), F32), pltpu.VMEM((BLK, inner), F32), pltpu.VMEM((BLK, inner), F32),
            pltpu.VMEM((BLK, states, inner), F32), pltpu.VMEM(((BLK + 1) * states, inner), BF16),
            pltpu.VMEM((BLK * states, inner), BF16), pltpu.VMEM((BLK * states, inner), BF16),
            pltpu.VMEM((states, inner), F32), pltpu.VMEM((toks, inner), F32), pltpu.VMEM((toks, inner), F32),
            pltpu.VMEM((toks, BLK * states), BF16), pltpu.VMEM((toks, BLK * states), BF16),
            pltpu.VMEM((toks + 2 * HALO, inner), F32), pltpu.VMEM((toks + HALO, inner), F32),
        ],
        compiler_params=params(),
        name="second",
    )(
        jnp.reshape(place, (1,)).astype(jnp.int32), ends, backs, totals, starts, sums, rate2, decay_rate, xe, act, dsilu, delta,
        sig, dy, proj, xwt, bwide, cwide, dtw, conv_weight, vec(skip_gain),
    )

    late = jnp.stack(
        [
            lax.ppermute(dxe[:, 0, HALO - 8 : HALO], "seq", down),
            lax.ppermute(dxe[:, 1, HALO - 8 : HALO], "seq", up),
        ],
        axis=1,
    )

    mixed, d_tokens, d_mod, out_grad, in_grad = pl.pallas_call(
        third_kernel,
        grid=(slots,),
        in_specs=[
            item(toks, dim), item(toks, dim), item(1, 3 * dim), item(toks, 1), item(toks, dim), item(toks, inner),
            item(2, toks, inner), item(2, HALO + toks, inner), item(2, 8, inner), whole(dim, 2 * inner), whole(inner, dim),
        ],
        out_specs=[item(toks, dim), item(toks, dim), item(1, 3 * dim), whole(inner, dim), whole(dim, 2 * inner)],
        out_shape=[
            jax.ShapeDtypeStruct((slots, toks, dim), BF16), jax.ShapeDtypeStruct((slots, toks, dim), F32),
            jax.ShapeDtypeStruct((slots, 1, 3 * dim), F32), jax.ShapeDtypeStruct((inner, dim), F32),
            jax.ShapeDtypeStruct((dim, 2 * inner), F32),
        ],
        compiler_params=params(),
        name="third",
    )(tokens, cotangent, modulate, valid, hid, z_gate, y, dxe, late, input_weight, output_weight)

    d_mod_low = lax.psum(d_mod[:, 0], "seq").astype(BF16)
    d_time = dot_nt(d_mod_low, ada_weight) * time_sig * (1.0 + time_f * (1.0 - time_sig))
    factors = lax.all_gather(jnp.concatenate([time_low, d_mod_low], axis=1), "dp", tiled=True)
    all_time, all_mod = factors[:, :dim], factors[:, dim:]
    grad_ada = dot_tn(all_time, all_mod)
    grad_ada_bias = jnp.sum(all_mod.astype(F32), axis=0)
    summed = lax.psum(
        (in_grad, out_grad, rate_grad, skip_grad, dtb_grad, dtp_grad, xp_grad, tap_grad, tapb_grad), ("dp", "seq")
    )
    in_grad, out_grad, rate_grad, skip_grad, dtb_grad, dtp_grad, xp_grad, tap_grad, tapb_grad = summed
    xp_grad = jnp.swapaxes(jnp.concatenate([xp_grad[:, :rank], xp_grad[:, wide_rank:]], axis=1), 1, 2)
    return (
        mixed, d_tokens, d_time, grad_ada, grad_ada_bias, in_grad, tap_grad, tapb_grad[:, 0], xp_grad, dtp_grad[:, :rank],
        dtb_grad[:, 0], rate_grad, skip_grad[:, 0], out_grad,
    )


def solution(mesh):
    runs = P("dp", "seq", None)
    return jax.shard_map(
        per_device,
        mesh=mesh,
        in_specs=(runs, P("dp", None), P("dp"), P("dp", "seq")) + (P(),) * 11 + (runs,),
        out_specs=(runs, runs, P("dp", None)) + (P(),) * 11,
        check_vma=False,
    )
```

```python
import functools
import math

import jax
import jax.numpy as jnp
from jax import lax
from jax.experimental import pallas as pl
from jax.experimental.pallas import tpu as pltpu
from jax.sharding import PartitionSpec as P

EPSILON = 1e-06
BLK = 16
HALO = 16
LOG2E = math.log2(math.e)
F32, BF16 = jnp.float32, jnp.bfloat16
NT = (((1,), (1,)), ((), ()))
TN = (((0,), (0,)), ((), ()))
VMEM_LIMIT = 60 << 20
MESH = pl.DeviceIdType.MESH


def dot(a, b):
    return jnp.dot(a, b, preferred_element_type=F32)


def dot_nt(a, b):
    return lax.dot_general(a, b, NT, preferred_element_type=F32)


def dot_tn(a, b):
    return lax.dot_general(a, b, TN, preferred_element_type=F32)


def reversal(size):
    rows = lax.broadcasted_iota(jnp.int32, (size, size), 0)
    cols = lax.broadcasted_iota(jnp.int32, (size, size), 1)
    return (rows + cols == size - 1).astype(BF16)


def flip_low(value):
    return dot(reversal(value.shape[0]), value).astype(BF16)


def flip_full(value):
    order = reversal(value.shape[0])
    high = value.astype(BF16)
    return dot(order, high) + dot(order, (value - high.astype(F32)).astype(BF16))


def normalise(tokens_f):
    centered = tokens_f - jnp.mean(tokens_f, axis=-1, keepdims=True)
    inv_std = lax.rsqrt(jnp.mean(centered * centered, axis=-1, keepdims=True) + EPSILON)
    return centered * inv_std, inv_std


def eye(size):
    rows = lax.broadcasted_iota(jnp.int32, (size, size), 0)
    cols = lax.broadcasted_iota(jnp.int32, (size, size), 1)
    return (rows == cols).astype(BF16)


def as_column(row):
    return dot_nt(eye(row.shape[1]), jnp.broadcast_to(row.astype(F32).astype(BF16), (8, row.shape[1])))[:, :1]


def remote(src, dst, send_sem, recv_sem, target):
    return pltpu.make_async_remote_copy(
        src_ref=src, dst_ref=dst, send_sem=send_sem, recv_sem=recv_sem, device_id=target, device_id_type=MESH
    )


def greet(targets):
    barrier = pltpu.get_barrier_semaphore()
    for target in targets:
        pl.semaphore_signal(barrier, inc=1, device_id=target, device_id_type=MESH)
    pl.semaphore_wait(barrier, len(targets))


def greet_line(me, runs):
    barrier = pltpu.get_barrier_semaphore()

    @pl.when(me > 0)
    def _():
        pl.semaphore_signal(barrier, inc=1, device_id={"seq": me - 1}, device_id_type=MESH)

    @pl.when(me < runs - 1)
    def _():
        pl.semaphore_signal(barrier, inc=1, device_id={"seq": me + 1}, device_id_type=MESH)

    neighbours = (me + runs - 1) // runs + (2 * runs - 2 - me) // runs
    pl.semaphore_wait(barrier, neighbours)


def swap_along_line(me, runs, ups, downs, start):
    up = [remote(src, dst, ss, rs, {"seq": me + 1}) for src, dst, ss, rs in ups]
    down = [remote(src, dst, ss, rs, {"seq": me - 1}) for src, dst, ss, rs in downs]

    @pl.when(me < runs - 1)
    def _():
        for copy in up:
            if start:
                copy.start()
            else:
                copy.wait_send()
        if not start:
            for copy in down:
                copy.wait_recv()

    @pl.when(me > 0)
    def _():
        for copy in down:
            if start:
                copy.start()
            else:
                copy.wait_send()
        if not start:
            for copy in up:
                copy.wait_recv()


def enter_kernel(
    runs, tok, cot, mask, counts, step, ada, ada_bias, win, wout,
    xe, dy, z_out, hid_out, mod_out,
    prev_tok, next_tok, prev_mask, next_mask, send_sem, recv_sem,
):
    slots, toks, dim = tok.shape
    inner = wout.shape[0]
    me = lax.axis_index("seq")
    i = pl.program_id(0)
    ups = [
        (tok.at[:, pl.ds(toks - HALO, HALO), :], prev_tok, send_sem.at[0], recv_sem.at[0]),
        (mask, prev_mask, send_sem.at[1], recv_sem.at[1]),
    ]
    downs = [
        (tok.at[:, pl.ds(0, HALO), :], next_tok, send_sem.at[2], recv_sem.at[2]),
        (mask, next_mask, send_sem.at[3], recv_sem.at[3]),
    ]

    @pl.when(i == 0)
    def _():
        greet_line(me, runs)
        swap_along_line(me, runs, ups, downs, True)

        @pl.when(me == 0)
        def _():
            prev_tok[...] = jnp.zeros(prev_tok.shape, BF16)
            prev_mask[...] = jnp.zeros(prev_mask.shape, jnp.int32)

        @pl.when(me == runs - 1)
        def _():
            next_tok[...] = jnp.zeros(next_tok.shape, BF16)
            next_mask[...] = jnp.zeros(next_mask.shape, jnp.int32)

    live = (counts[...] > i).astype(F32)
    time_f = step[...].astype(F32)
    time_low = (time_f * jax.nn.sigmoid(time_f)).astype(BF16)
    mod = dot(time_low, ada[...]) + ada_bias[...]
    mod_out[...] = mod
    shift, scale, gate = mod[:, :dim], mod[:, dim : 2 * dim], mod[:, 2 * dim :]

    def hidden_of(part):
        normed, _ = normalise(part.astype(F32))
        return (normed * (1.0 + scale) + shift).astype(BF16)

    hid = hidden_of(tok[i])
    hid_out[...] = hid
    xz = dot(hid, win[...]) * (as_column(mask[pl.ds(i, 1), :]) * live)
    x_low = xz[:, :inner].astype(BF16)
    z = xz[:, inner:]
    z_out[...] = z
    d_branch = (cot[...].astype(F32) * gate).astype(BF16)
    d_summed = dot_nt(d_branch, wout[...]) * z * jax.nn.sigmoid(z)
    dy[0] = d_summed
    dy[1] = flip_full(d_summed)
    xe[0, HALO:, :] = x_low
    xe[1, HALO:, :] = flip_low(x_low)

    @pl.when(i == 0)
    def _():
        swap_along_line(me, runs, ups, downs, False)

    rims = jnp.concatenate([prev_tok[i], next_tok[i]], axis=0)
    prev_col = as_column(prev_mask[pl.ds(i, 1), :])[toks - HALO :]
    next_col = as_column(next_mask[pl.ds(i, 1), :])[:HALO]
    rim_x = dot(hidden_of(rims), win[:, :inner]) * (jnp.concatenate([prev_col, next_col], axis=0) * live)
    rim_x = rim_x.astype(BF16)
    xe[0, :HALO, :] = rim_x[:HALO]
    xe[1, :HALO, :] = flip_low(rim_x[HALO:])


def twice(row8):
    return jnp.concatenate([row8, row8], axis=0)


def spread(ref, index):
    return twice(ref[pl.ds(index, 8, stride=0), :])


def columns(ref, block, first, count):
    lane = pl.multiple_of((block // 8) * 128, 128)
    return pltpu.roll(ref[first : first + count, pl.ds(lane, 128)], (128 - (block % 8) * BLK) % 128, 1)


def first_kernel(
    xe, dy, taps, tap_bias, xwt, dtw, dt_bias, rate2,
    act_out, dsilu_out, delta_out, sig_out, proj_out, end_out, back_out, total_out, starts_out, sums_out,
    xf, dl, dx, drow, xrow, yrow, decay, through,
):
    toks, inner = dy.shape
    states = rate2.shape[0]
    blocks = toks // BLK
    rank = dtw.shape[0]
    tap_count = taps.shape[0]
    xf[...] = xe[...].astype(F32)
    conv = tap_bias[...] + jnp.zeros((toks, inner), F32)
    for k in range(tap_count):
        conv = conv + taps[k : k + 1, :] * xf[HALO - tap_count + 1 + k : HALO - tap_count + 1 + k + toks, :]
    sig = jax.nn.sigmoid(conv)
    act = (conv * sig).astype(BF16)
    dsilu_out[...] = sig * (1.0 + conv * (1.0 - sig))
    act_out[...] = act
    proj = dot_nt(xwt[...], act)
    proj_out[...] = proj
    pre = dot_tn(proj[:rank, :].astype(BF16), dtw[...]) + dt_bias[...]
    delta = jnp.maximum(pre, 0.0) + jnp.log1p(jnp.exp(-jnp.abs(pre)))
    delta_out[...] = delta
    sig_out[...] = jax.nn.sigmoid(pre)
    dl[...] = delta
    dx[...] = delta * act.astype(F32)
    end_out[...] = jnp.zeros((states, inner), F32)
    back_out[...] = jnp.zeros((states, inner), F32)
    through[...] = jnp.zeros((8, inner), F32)

    def block_step(j, _):
        t0 = pl.multiple_of(j * BLK, BLK)
        drow[...] = dl[pl.ds(t0, BLK), :]
        xrow[...] = dx[pl.ds(t0, BLK), :]
        yrow[...] = dy[pl.ds(t0, BLK), :]
        bt = columns(proj_out, j, rank, states)
        ct = columns(proj_out, j, rank + states, states)
        rate = rate2[...]
        s = end_out[...]
        starts_out[j] = s
        before = through[...]
        sums_out[j] = before[:1, :]
        for i in range(BLK):
            a = jnp.exp2(spread(drow, i) * rate)
            decay[i] = a
            s = a * s + spread(xrow, i) * jnp.broadcast_to(bt[:, i : i + 1], (states, inner))
        end_out[...] = s
        m = jnp.zeros((states, inner), F32)
        for i in reversed(range(BLK)):
            m = decay[i] * (m + spread(yrow, i) * jnp.broadcast_to(ct[:, i : i + 1], (states, inner)))
        back_out[...] = back_out[...] + m * jnp.exp2(twice(before) * rate)
        through[...] = before + jnp.sum(drow[...], axis=0, keepdims=True)
        return 0

    lax.fori_loop(0, blocks, block_step, 0)
    total_out[...] = through[:1, :]


def second_kernel(
    s_in, lam_in, starts, sums, rate2, rate, xe, act, dsilu, delta, sig, dy, proj, xwt, bwide, cwide, dtw, taps, skip,
    y_out, dx_out, rim_out, rate_grad, skip_grad, dtb_grad, dtp_grad, xp_grad, tap_grad, tapb_grad,
    carry, dxs, bdiag, cdiag, drow, xrow, yrow, decay, states_low, lam_low, rq_low, racc, gsum, hsum, db, dc, pads, xf,
):
    toks, inner = dy.shape
    states = rate2.shape[0]
    blocks = toks // BLK
    rank = dtw.shape[0]
    tap_count = taps.shape[0]
    item = pl.program_id(1)
    carry[...] = lam_in[...]
    act_low = act[...]
    act_f = act_low.astype(F32)
    dxs[...] = delta[...] * act_f
    width = bwide.shape[1]
    own = lax.broadcasted_iota(jnp.int32, (toks, width), 0) % BLK == lax.broadcasted_iota(jnp.int32, (toks, width), 1) // states
    bdiag[...] = jnp.where(own, dot(act_low, bwide[...]), 0.0).astype(BF16)
    cdiag[...] = jnp.where(own, dot(act_low, cwide[...]), 0.0).astype(BF16)
    racc[...] = jnp.zeros((states, inner), F32)

    def block_step(step, _):
        j = blocks - 1 - step
        t0 = pl.multiple_of(j * BLK, BLK)
        drow[...] = delta[pl.ds(t0, BLK), :]
        xrow[...] = dxs[pl.ds(t0, BLK), :]
        yrow[...] = dy[pl.ds(t0, BLK), :]
        bt = columns(proj, j, rank, states)
        ct = columns(proj, j, rank + states, states)
        r2 = rate2[...]
        rr = rate[...]
        s = starts[j] + s_in[...] * jnp.exp2(twice(jnp.broadcast_to(sums[j], (8, inner))) * r2)
        states_low[:states, :] = s.astype(BF16)
        for i in range(BLK):
            a = jnp.exp2(spread(drow, i) * r2)
            decay[i] = a
            s = a * s + spread(xrow, i) * jnp.broadcast_to(bt[:, i : i + 1], (states, inner))
            states_low[(i + 1) * states : (i + 2) * states, :] = s.astype(BF16)
        cr = carry[...]
        ra = racc[...]
        for i in reversed(range(BLK)):
            lam = cr + spread(yrow, i) * jnp.broadcast_to(ct[:, i : i + 1], (states, inner))
            lam_low[i * states : (i + 1) * states, :] = lam.astype(BF16)
            cr = decay[i] * lam
            q = cr * states_low[i * states : (i + 1) * states, :].astype(F32)
            rq_low[i * states : (i + 1) * states, :] = (q * rr).astype(BF16)
            ra = ra + q * spread(drow, i)
        carry[...] = cr
        racc[...] = ra
        after = states_low[states:, :]
        lam_all = lam_low[...]
        y_out[pl.ds(t0, BLK), :] = dot(cdiag[pl.ds(t0, BLK), :], after)
        gsum[pl.ds(t0, BLK), :] = dot(bdiag[pl.ds(t0, BLK), :], lam_all)
        ones = (
            lax.broadcasted_iota(jnp.int32, (BLK, BLK * states), 1) // states
            == lax.broadcasted_iota(jnp.int32, (BLK, BLK * states), 0)
        )
        hsum[pl.ds(t0, BLK), :] = dot(ones.astype(BF16), rq_low[...])
        dc[pl.ds(t0, BLK), :] = jnp.where(ones, dot_nt(yrow[...].astype(BF16), after), 0.0).astype(BF16)
        db[pl.ds(t0, BLK), :] = jnp.where(ones, dot_nt(xrow[...].astype(BF16), lam_all), 0.0).astype(BF16)
        return 0

    lax.fori_loop(0, blocks, block_step, 0)

    @pl.when(item == 0)
    def _():
        for ref in (rate_grad, skip_grad, dtb_grad, dtp_grad, xp_grad, tap_grad, tapb_grad):
            ref[...] = jnp.zeros(ref.shape, ref.dtype)

    rate_grad[...] += -racc[...]
    d_summed = dy[...]
    g = gsum[...]
    skip_grad[...] += jnp.sum(d_summed * act_f, axis=0, keepdims=True)
    y_out[...] += skip[...] * act_f
    d_pre = (act_f * g - hsum[...]) * sig[...]
    dtb_grad[...] += jnp.sum(d_pre, axis=0, keepdims=True)
    d_pre_low = d_pre.astype(BF16)
    dtp_grad[...] += dot(proj[:rank, :].astype(BF16), d_pre_low)
    fold = (
        lax.broadcasted_iota(jnp.int32, (states, width), 1) % states == lax.broadcasted_iota(jnp.int32, (states, width), 0)
    ).astype(BF16)
    d_proj = jnp.concatenate(
        [dot_nt(dtw[...], d_pre_low), dot_nt(fold, db[...]), dot_nt(fold, dc[...])], axis=0
    ).astype(BF16)
    xp_grad[...] += dot(d_proj, act_low)
    d_act = delta[...] * g + skip[...] * d_summed + dot_tn(d_proj, xwt[...])
    d_conv = d_act * dsilu[...]
    tapb_grad[...] += jnp.sum(d_conv, axis=0, keepdims=True)
    xf[...] = xe[...].astype(F32)
    pads[:HALO, :] = jnp.zeros((HALO, inner), F32)
    pads[HALO : HALO + toks, :] = d_conv
    pads[HALO + toks :, :] = jnp.zeros((HALO, inner), F32)
    d_window = jnp.zeros((HALO + toks, inner), F32)
    first = HALO - tap_count + 1
    for k in range(tap_count):
        tap_grad[k : k + 1, :] += jnp.sum(d_conv * xf[first + k : first + k + toks, :], axis=0, keepdims=True)
        d_window = d_window + taps[k : k + 1, :] * pads[tap_count - 1 - k : tap_count - 1 - k + HALO + toks, :]
    rim_out[...] = d_window[HALO - 8 : HALO]
    dx_out[...] = d_window[HALO:]


def third_kernel(
    runs, tok, cot, mod, mask, counts, hid, z_in, y, dx, rims, win, wout,
    mixed, d_tokens, d_mod, out_grad, in_grad,
    late_up, late_down, send_sem, recv_sem,
):
    dim = tok.shape[-1]
    toks, inner = z_in.shape
    me = lax.axis_index("seq")
    i = pl.program_id(0)
    ups = [(rims.at[1], late_up, send_sem.at[0], recv_sem.at[0])]
    downs = [(rims.at[0], late_down, send_sem.at[1], recv_sem.at[1])]

    @pl.when(i == 0)
    def _():
        greet_line(me, runs)
        swap_along_line(me, runs, ups, downs, True)

        @pl.when(me == 0)
        def _():
            late_up[...] = jnp.zeros(late_up.shape, F32)

        @pl.when(me == runs - 1)
        def _():
            late_down[...] = jnp.zeros(late_down.shape, F32)

        out_grad[...] = jnp.zeros(out_grad.shape, F32)
        in_grad[...] = jnp.zeros(in_grad.shape, F32)

    shift, scale, gate = mod[:, :dim], mod[:, dim : 2 * dim], mod[:, 2 * dim :]
    valid = as_column(mask[pl.ds(i, 1), :]) * (counts[...] > i).astype(F32)
    tok_f = tok[...].astype(F32)
    normed, inv_std = normalise(tok_f)
    cot_f = cot[...].astype(F32)
    z = z_in[...]
    z_sig = jax.nn.sigmoid(z)
    summed = y[0] + flip_full(y[1])
    gated = (summed * z * z_sig).astype(BF16)
    branch_out = dot(gated, wout[...])
    mixed[...] = (tok_f + gate * branch_out).astype(BF16)
    d_branch = (cot_f * gate).astype(BF16)
    d_gated = dot_nt(d_branch, wout[...])
    d_zgate = d_gated * summed * z_sig * (1.0 + z * (1.0 - z_sig))
    out_grad[...] += dot_tn(gated, d_branch)

    @pl.when(i == 0)
    def _():
        swap_along_line(me, runs, ups, downs, False)

    edge = late_up.shape[1]

    def with_late(part, extra):
        return jnp.concatenate([part[: toks - edge], part[toks - edge :] + extra], axis=0)

    d_x = with_late(dx[0], late_down[i]) + flip_full(with_late(dx[1], late_up[i]))
    d_xz = (jnp.concatenate([d_x, d_zgate], axis=1) * valid).astype(BF16)
    d_hidden = dot_nt(d_xz, win[...])
    in_grad[...] += dot_tn(hid[...], d_xz)
    d_mod[0:1, :] = jnp.sum(d_hidden, axis=0, keepdims=True)
    d_mod[1:2, :] = jnp.sum(d_hidden * normed, axis=0, keepdims=True)
    d_mod[2:3, :] = jnp.sum(cot_f * branch_out, axis=0, keepdims=True)
    d_normed = d_hidden * (1.0 + scale)
    d_tokens[...] = cot_f + inv_std * (
        d_normed
        - jnp.mean(d_normed, axis=-1, keepdims=True)
        - normed * jnp.mean(d_normed * normed, axis=-1, keepdims=True)
    )


def bit_of(index, bit):
    return (index // (1 << bit)) % 2


def across(axis, bit):
    me = lax.axis_index(axis)
    mine = bit_of(me, bit)
    return mine, {axis: me + (1 - 2 * mine) * (1 << bit)}


def exchange_kernel(runs, end, back, total, rate2, s_in, lam_in, group, span, pre, pre_span, sends, arrivals, send_sem, recv_sem):
    slots, _, states, inner = end.shape
    bits = int(math.log2(runs))
    links = [across("seq", bit) for bit in range(bits)]
    greet([target for _, target in links])
    flows = (((end, 0), (back, 1)), ((end, 1), (back, 0)))
    units = 2 * slots
    rows = units * states
    pre[...] = jnp.zeros(pre.shape, F32)
    pre_span[...] = jnp.zeros(pre_span.shape, F32)
    for flow in range(2):
        for kind, (array, branch) in enumerate(flows[flow]):
            for i in range(slots):
                group[flow, kind * slots + i] = array[i, branch]
                span[flow, kind * slots + i] = jnp.broadcast_to(total[i, branch], (8, inner))

    def load(flow, slot):
        for unit in range(units):
            sends[slot, unit * states : (unit + 1) * states, :] = group[flow, unit].astype(BF16)
            high = span[flow, unit].astype(BF16)
            low = (span[flow, unit] - high.astype(F32)).astype(BF16)
            at = rows + unit * 16
            sends[slot, at : at + 16, :] = jnp.concatenate([high.astype(F32), low.astype(F32)], axis=0).astype(BF16)

    def join(flow, slot, earlier, last):
        for unit in range(units):
            rate = rate2[flows[flow][unit // slots][1]]
            state = arrivals[slot, unit * states : (unit + 1) * states, :].astype(F32)
            at = rows + unit * 16
            both = arrivals[slot, at : at + 16, :].astype(F32)
            length = both[:8] + both[8:]
            mine, mine_span = pre[flow, unit], pre_span[flow, unit]
            joined = state * jnp.exp2(rate * twice(mine_span)) + mine
            pre[flow, unit] = jnp.where(earlier, joined, mine)
            pre_span[flow, unit] = jnp.where(earlier, length + mine_span, mine_span)
            if not last:
                own, own_span = group[flow, unit], span[flow, unit]
                first = jnp.where(earlier, state, own)
                second = jnp.where(earlier, own, state)
                second_span = jnp.where(earlier, own_span, length)
                group[flow, unit] = first * jnp.exp2(rate * twice(second_span)) + second
                span[flow, unit] = own_span + length

    for stage, (mine, target) in enumerate(links):
        last = stage == bits - 1
        if last:
            slot = 2 * stage

            @pl.when(mine == 0)
            def _():
                load(0, slot)

            @pl.when(mine == 1)
            def _():
                load(1, slot)

            copies = [remote(sends.at[slot], arrivals.at[slot], send_sem.at[slot], recv_sem.at[slot], target)]
        else:
            copies = []
            for flow in range(2):
                slot = 2 * stage + flow
                load(flow, slot)
                copies.append(
                    remote(sends.at[slot], arrivals.at[slot], send_sem.at[slot], recv_sem.at[slot], target)
                )
        for copy in copies:
            copy.start()
        for copy in copies:
            copy.wait()
        if last:

            @pl.when(mine == 1)
            def _():
                join(0, 2 * stage, True, True)

            @pl.when(mine == 0)
            def _():
                join(1, 2 * stage, True, True)
        else:
            join(0, 2 * stage, mine == 1, False)
            join(1, 2 * stage + 1, mine == 0, False)
    for flow in range(2):
        for kind, (_, branch) in enumerate(flows[flow]):
            result = (s_in, lam_in)[kind]
            for i in range(slots):
                result[i, branch] = pre[flow, kind * slots + i]


PARTS = 3
LAST_ROWS = 16


def reduce_rows(dim, inner, small):
    rows = 3 * dim + small
    unit = PARTS * LAST_ROWS * 32
    return -(-rows // unit) * unit


def reduce_kernel(
    plan, in_grad, out_grad, xp_grad, dtp_grad, rate_grad, tap_grad, tapb_grad, skip_grad, dtb_grad, d_mod, step,
    result, factors,
    acc, sends, arrivals, gathered, mod_sum, mod_in, table, send_sem, recv_sem, small_send, small_recv,
):
    runs, groups, total_rows = plan
    dim = in_grad.shape[0]
    inner = out_grad.shape[0]
    slots = step.shape[0]
    seq_bits = [("seq", bit) for bit in range(int(math.log2(runs)))]
    dp_bits = [("dp", bit) for bit in range(int(math.log2(groups)))]
    all_bits = seq_bits + dp_bits
    links = {key: across(*key) for key in all_bits}
    greet([links[key][1] for key in all_bits])
    middle = all_bits[1:-1]
    orders = [
        all_bits[:1] + middle[part % max(len(middle), 1) :] + middle[: part % max(len(middle), 1)] + all_bits[1:][-1:]
        for part in range(PARTS)
    ]
    part_rows = total_rows // PARTS

    mod_sum[...] = jnp.zeros(mod_sum.shape, F32)
    for i in range(slots):
        mod_sum[3 * i : 3 * i + 3, :] = d_mod[i]

    def small_copy(stage):
        axis, bit = all_bits[stage]
        target = links[(axis, bit)][1]
        if axis == "seq":
            return remote(mod_sum, mod_in.at[stage], small_send.at[stage], small_recv.at[stage], target)
        size = 16 << bit
        at = pl.multiple_of(lax.axis_index("dp") // (1 << bit) * size, 16)
        here = table.at[pl.ds(at, size), :]
        return remote(here, here, small_send.at[stage], small_recv.at[stage], target)

    def fill_table():
        time_f = step[...].astype(F32)
        time_low = time_f * jax.nn.sigmoid(time_f)
        at = pl.multiple_of(lax.axis_index("dp") * 16, 16)
        own = jnp.concatenate([mod_sum[: 3 * slots, :], time_low, mod_sum[4 * slots :, :]], axis=0)
        table[pl.ds(at, 16), :] = own.astype(BF16)

    half = dim
    acc[0:dim, :] = in_grad[:, :inner]
    acc[dim : 2 * dim, :] = in_grad[:, inner:]
    acc[2 * dim : 3 * dim, :] = jnp.concatenate([out_grad[:half, :], out_grad[half:, :]], axis=1)
    at = 3 * dim
    for ref in (xp_grad, dtp_grad, rate_grad, tap_grad):
        for branch in range(2):
            size = ref.shape[1]
            acc[at : at + size, :] = ref[branch]
            at += size
    tail = [ref[branch] for ref in (tapb_grad, skip_grad, dtb_grad) for branch in range(2)]
    acc[at : at + 8, :] = jnp.concatenate(tail + [jnp.zeros((2, inner), F32)], axis=0)
    at += 8
    acc[at:, :] = jnp.zeros((total_rows - at, inner), F32)

    starts = [part * part_rows for part in range(PARTS)]
    sizes = [part_rows] * PARTS
    history = [[] for _ in range(PARTS)]
    offsets = [part * part_rows for part in range(PARTS)]
    count = len(all_bits)
    for stage in range(count):
        copies = []
        for part in range(PARTS):
            mine, target = links[orders[part][stage]]
            start, size = starts[part], sizes[part]
            split = size >= 2 * LAST_ROWS
            moved = size // 2 if split else size
            if split:
                away = pl.multiple_of(start + (1 - mine) * moved, LAST_ROWS)
                keep = pl.multiple_of(start + mine * moved, LAST_ROWS)
            else:
                away = keep = start
            history[part].append((start, size, split))
            at = offsets[part]
            offsets[part] += moved
            here = sends.at[pl.ds(at, moved), :]
            sends[at : at + moved, :] = acc[pl.ds(away, moved), :].astype(BF16)
            copy = remote(
                here, arrivals.at[pl.ds(at, moved), :], send_sem.at[part, stage], recv_sem.at[part, stage], target
            )
            copy.start()
            copies.append((copy, part, keep, moved, at, split))
            starts[part], sizes[part] = keep, moved
        if stage == len(seq_bits):
            fill_table()
        small = small_copy(stage)
        small.start()
        for copy, part, keep, moved, at, split in copies:
            copy.wait()
            held = acc[pl.ds(keep, moved), :]
            if not split:
                held = held.astype(BF16).astype(F32)
            acc[pl.ds(keep, moved), :] = held + arrivals[at : at + moved, :].astype(F32)
        small.wait()
        if all_bits[stage][0] == "seq":
            mod_sum[...] += mod_in[stage]
    if not dp_bits:
        fill_table()
    factors[...] = table[...]
    for part in range(PARTS):
        where = pl.ds(starts[part], sizes[part])
        gathered[where, :] = acc[where, :].astype(BF16)
    for stage in reversed(range(count)):
        copies = []
        for part in range(PARTS):
            start, size, split = history[part][stage]
            if not split:
                continue
            target = links[orders[part][stage]][1]
            here = gathered.at[pl.ds(starts[part], sizes[part]), :]
            copy = remote(
                here, here, send_sem.at[part, count + stage], recv_sem.at[part, count + stage], target
            )
            copy.start()
            copies.append(copy)
            starts[part], sizes[part] = start, size
        for copy in copies:
            copy.wait()
    result[...] = gathered[...]


def finish_kernel(
    ranks, result, factors, own, step, ada,
    grad_time, grad_ada, grad_ada_bias, in_grad, tap_grad, tapb_grad, xp_grad, dtp_grad, dtb_grad, rate_grad, skip_grad, out_grad,
):
    rank, wide_rank = ranks
    dim = in_grad.shape[0]
    inner = out_grad.shape[0]
    slots = step.shape[0]
    states = rate_grad.shape[1]
    taps = tap_grad.shape[1]

    def rows(at, size):
        return result[at : at + size, :].astype(F32)

    in_grad[:, :inner] = rows(0, dim)
    in_grad[:, inner:] = rows(dim, dim)
    both = rows(2 * dim, dim)
    out_grad[:dim, :] = both[:, :dim]
    out_grad[dim:, :] = both[:, dim:]
    at = 3 * dim
    wide = wide_rank + 2 * states
    for branch in range(2):
        part = rows(at, wide)
        part = jnp.concatenate([part[:rank], part[wide_rank:], part[rank:wide_rank]], axis=0)
        part = jnp.concatenate([part, jnp.zeros((128 - wide, inner), F32)], axis=0)
        xp_grad[branch] = part.T[:, : rank + 2 * states]
        at += wide
    for branch in range(2):
        dtp_grad[branch] = rows(at, wide_rank)[:rank]
        at += wide_rank
    for branch in range(2):
        rate_grad[branch] = rows(at, states)
        at += states
    tail = rows(at, 16)
    for branch in range(2):
        tap_grad[branch] = tail[branch * taps : (branch + 1) * taps]
    tapb_grad[...] = tail[2 * taps : 2 * taps + 2]
    skip_grad[...] = tail[2 * taps + 2 : 2 * taps + 4]
    dtb_grad[...] = tail[2 * taps + 4 : 2 * taps + 6]

    table = factors[...]
    length = table.shape[0]
    groups = length // 16
    items = groups * 8

    def pick(place):
        row = lax.broadcasted_iota(jnp.int32, (items, length), 0)
        col = lax.broadcasted_iota(jnp.int32, (items, length), 1)
        slot = row % 8
        wanted = row // 8 * 16 + place(slot)
        return dot(((col == wanted) & (slot < slots)).astype(BF16), table)

    times = pick(lambda slot: 3 * slots + slot).astype(BF16)
    time_f = step[...].astype(F32)
    time_sig = jax.nn.sigmoid(time_f)
    d_time = jnp.zeros((slots, dim), F32)
    mine = own[...].astype(F32)
    for part in range(3):
        mods = pick(lambda slot: 3 * slot + part)
        lanes = slice(part * dim, (part + 1) * dim)
        grad_ada[:, lanes] = dot_tn(times, mods.astype(BF16))
        grad_ada_bias[:, lanes] = jnp.sum(mods, axis=0, keepdims=True)
        picked = jnp.concatenate([mine[3 * i + part : 3 * i + part + 1] for i in range(slots)], axis=0)
        d_time = d_time + dot_nt(picked.astype(BF16), ada[:, lanes])
    grad_time[...] = d_time * time_sig * (1.0 + time_f * (1.0 - time_sig))


def params(**more):
    return pltpu.CompilerParams(vmem_limit_bytes=VMEM_LIMIT, **more)


def spec(block, index):
    return pl.BlockSpec(block, index)


def per_device(
    tokens, timestep, counts, token_mask, ada_weight, ada_bias, input_weight, conv_weight, conv_bias, x_weight, dt_weight,
    dt_bias, decay_rate, skip_gain, output_weight, cotangent,
):
    slots, toks, dim = tokens.shape
    inner = output_weight.shape[0]
    rank = dt_weight.shape[1]
    states = decay_rate.shape[1]
    tap_count = conv_weight.shape[1]
    wide_rank = 32
    proj_rows = wide_rank + 2 * states
    blocks = toks // BLK
    runs = lax.axis_size("seq")
    groups = lax.axis_size("dp")
    counts2 = counts[:, None]
    step3 = timestep[:, None, :]
    xwt = jnp.swapaxes(x_weight, 1, 2)
    xwt = jnp.concatenate(
        [xwt[:, :rank], jnp.zeros((2, wide_rank - rank, inner), BF16), xwt[:, rank:]], axis=1
    )
    dtw = jnp.concatenate([dt_weight, jnp.zeros((2, wide_rank - rank, inner), BF16)], axis=1)
    bwide = jnp.tile(x_weight[:, :, rank : rank + states], (1, 1, BLK))
    cwide = jnp.tile(x_weight[:, :, rank + states :], (1, 1, BLK))
    rate2 = -LOG2E * decay_rate
    vec = lambda a: a[:, None, :]

    def item(*block):
        return spec((None,) + block, lambda i: (i,) + (0,) * len(block))

    def whole(*block):
        return spec(block, lambda *_: (0,) * len(block))

    xe, dy, z_gate, hid, modulate = pl.pallas_call(
        functools.partial(enter_kernel, runs),
        grid=(slots,),
        in_specs=[
            whole(slots, toks, dim), item(toks, dim), whole(slots, toks), whole(1, 1), item(1, dim), whole(dim, 3 * dim),
            whole(1, 3 * dim), whole(dim, 2 * inner), whole(inner, dim),
        ],
        out_specs=[
            item(2, HALO + toks, inner), item(2, toks, inner), item(toks, inner), item(toks, dim), item(1, 3 * dim),
        ],
        out_shape=[
            jax.ShapeDtypeStruct((slots, 2, HALO + toks, inner), BF16),
            jax.ShapeDtypeStruct((slots, 2, toks, inner), F32),
            jax.ShapeDtypeStruct((slots, toks, inner), F32),
            jax.ShapeDtypeStruct((slots, toks, dim), BF16),
            jax.ShapeDtypeStruct((slots, 1, 3 * dim), F32),
        ],
        scratch_shapes=[
            pltpu.VMEM((slots, HALO, dim), BF16), pltpu.VMEM((slots, HALO, dim), BF16), pltpu.VMEM((slots, toks), jnp.int32),
            pltpu.VMEM((slots, toks), jnp.int32), pltpu.SemaphoreType.DMA((4,)), pltpu.SemaphoreType.DMA((4,)),
        ],
        compiler_params=params(collective_id=1, has_side_effects=True),
        name="enter",
    )(
        tokens, cotangent, token_mask, counts2, step3, ada_weight, ada_bias[None, :], input_weight, output_weight,
    )

    def unit(*block):
        return spec((None, None) + block, lambda b, i: (i, b) + (0,) * len(block))

    def branch(*block):
        return spec((None,) + block, lambda b, i: (b,) + (0,) * len(block))

    def unit_shape(*block, kind=F32):
        return jax.ShapeDtypeStruct((slots, 2) + block, kind)

    act, dsilu, delta, sig, proj, end, back, total, starts, sums = pl.pallas_call(
        first_kernel,
        grid=(2, slots),
        in_specs=[
            unit(HALO + toks, inner), unit(toks, inner), branch(tap_count, inner), branch(1, inner), branch(proj_rows, inner),
            branch(wide_rank, inner), branch(1, inner), branch(states, inner),
        ],
        out_specs=[
            unit(toks, inner), unit(toks, inner), unit(toks, inner), unit(toks, inner), unit(proj_rows, toks),
            unit(states, inner), unit(states, inner), unit(1, inner), unit(blocks, states, inner), unit(blocks, 1, inner),
        ],
        out_shape=[
            unit_shape(toks, inner, kind=BF16), unit_shape(toks, inner), unit_shape(toks, inner), unit_shape(toks, inner),
            unit_shape(proj_rows, toks), unit_shape(states, inner), unit_shape(states, inner), unit_shape(1, inner),
            unit_shape(blocks, states, inner), unit_shape(blocks, 1, inner),
        ],
        scratch_shapes=[
            pltpu.VMEM((HALO + toks, inner), F32), pltpu.VMEM((toks, inner), F32), pltpu.VMEM((toks, inner), F32),
            pltpu.VMEM((BLK, inner), F32), pltpu.VMEM((BLK, inner), F32), pltpu.VMEM((BLK, inner), F32),
            pltpu.VMEM((BLK, states, inner), F32), pltpu.VMEM((8, inner), F32),
        ],
        compiler_params=params(),
        name="first",
    )(xe, dy, conv_weight, vec(conv_bias), xwt, dtw, vec(dt_bias), rate2)

    pairs = int(math.log2(runs))
    units = 2 * slots
    vmem = pl.BlockSpec(memory_space=pltpu.VMEM)
    s_in, lam_in = pl.pallas_call(
        functools.partial(exchange_kernel, runs),
        in_specs=[vmem] * 4,
        out_specs=[vmem] * 2,
        out_shape=[unit_shape(states, inner), unit_shape(states, inner)],
        scratch_shapes=[
            pltpu.VMEM((2, units, states, inner), F32), pltpu.VMEM((2, units, 8, inner), F32),
            pltpu.VMEM((2, units, states, inner), F32), pltpu.VMEM((2, units, 8, inner), F32),
            pltpu.VMEM((2 * pairs, units * (states + 16), inner), BF16),
            pltpu.VMEM((2 * pairs, units * (states + 16), inner), BF16),
            pltpu.SemaphoreType.DMA((2 * pairs,)), pltpu.SemaphoreType.DMA((2 * pairs,)),
        ],
        compiler_params=params(collective_id=2, has_side_effects=True),
        name="exchange",
    )(end, back, total, rate2)

    rim_spec = spec((None, None, 8, inner), lambda b, i: (b, i, 0, 0))
    y, dx, rims, rate_grad, skip_grad, dtb_grad, dtp_grad, xp_grad, tap_grad, tapb_grad = pl.pallas_call(
        second_kernel,
        grid=(2, slots),
        in_specs=[
            unit(states, inner), unit(states, inner), unit(blocks, states, inner),
            unit(blocks, 1, inner), branch(states, inner), branch(states, inner), unit(HALO + toks, inner), unit(toks, inner),
            unit(toks, inner), unit(toks, inner), unit(toks, inner), unit(toks, inner), unit(proj_rows, toks),
            branch(proj_rows, inner), branch(inner, BLK * states), branch(inner, BLK * states), branch(wide_rank, inner),
            branch(tap_count, inner), branch(1, inner),
        ],
        out_specs=[
            unit(toks, inner), unit(toks, inner), rim_spec, branch(states, inner), branch(1, inner), branch(1, inner),
            branch(wide_rank, inner), branch(proj_rows, inner), branch(tap_count, inner), branch(1, inner),
        ],
        out_shape=[
            unit_shape(toks, inner), unit_shape(toks, inner), jax.ShapeDtypeStruct((2, slots, 8, inner), F32),
        ] + [
            jax.ShapeDtypeStruct((2, rows, inner), F32) for rows in (states, 1, 1, wide_rank, proj_rows, tap_count, 1)
        ],
        scratch_shapes=[
            pltpu.VMEM((states, inner), F32), pltpu.VMEM((toks, inner), F32),
            pltpu.VMEM((toks, BLK * states), BF16), pltpu.VMEM((toks, BLK * states), BF16),
            pltpu.VMEM((BLK, inner), F32), pltpu.VMEM((BLK, inner), F32), pltpu.VMEM((BLK, inner), F32),
            pltpu.VMEM((BLK, states, inner), F32), pltpu.VMEM(((BLK + 1) * states, inner), BF16),
            pltpu.VMEM((BLK * states, inner), BF16), pltpu.VMEM((BLK * states, inner), BF16),
            pltpu.VMEM((states, inner), F32), pltpu.VMEM((toks, inner), F32), pltpu.VMEM((toks, inner), F32),
            pltpu.VMEM((toks, BLK * states), BF16), pltpu.VMEM((toks, BLK * states), BF16),
            pltpu.VMEM((toks + 2 * HALO, inner), F32), pltpu.VMEM((toks + HALO, inner), F32),
        ],
        compiler_params=params(),
        name="second",
    )(
        s_in, lam_in, starts, sums, rate2, decay_rate, xe, act, dsilu, delta,
        sig, dy, proj, xwt, bwide, cwide, dtw, conv_weight, vec(skip_gain),
    )

    mixed, d_tokens, d_mod, out_grad, in_grad = pl.pallas_call(
        functools.partial(third_kernel, runs),
        grid=(slots,),
        in_specs=[
            item(toks, dim), item(toks, dim), item(1, 3 * dim), whole(slots, toks), whole(1, 1), item(toks, dim),
            item(toks, inner), item(2, toks, inner), item(2, toks, inner), whole(2, slots, 8, inner), whole(dim, 2 * inner),
            whole(inner, dim),
        ],
        out_specs=[item(toks, dim), item(toks, dim), item(3, dim), whole(inner, dim), whole(dim, 2 * inner)],
        out_shape=[
            jax.ShapeDtypeStruct((slots, toks, dim), BF16), jax.ShapeDtypeStruct((slots, toks, dim), F32),
            jax.ShapeDtypeStruct((slots, 3, dim), F32), jax.ShapeDtypeStruct((inner, dim), F32),
            jax.ShapeDtypeStruct((dim, 2 * inner), F32),
        ],
        scratch_shapes=[
            pltpu.VMEM((slots, 8, inner), F32), pltpu.VMEM((slots, 8, inner), F32), pltpu.SemaphoreType.DMA((2,)),
            pltpu.SemaphoreType.DMA((2,)),
        ],
        compiler_params=params(collective_id=3, has_side_effects=True),
        name="third",
    )(
        tokens, cotangent, modulate, token_mask, counts2, hid, z_gate, y, dx, rims, input_weight, output_weight,
    )

    small = 2 * (proj_rows + wide_rank + states + tap_count) + 8
    rows = reduce_rows(dim, inner, small)
    stages = int(math.log2(runs)) + int(math.log2(groups))
    result, factors = pl.pallas_call(
        functools.partial(reduce_kernel, (runs, groups, rows)),
        in_specs=[vmem] * 11,
        out_specs=[vmem] * 2,
        out_shape=[jax.ShapeDtypeStruct((rows, inner), BF16), jax.ShapeDtypeStruct((16 * groups, dim), BF16)],
        scratch_shapes=[
            pltpu.VMEM((rows, inner), F32), pltpu.VMEM((rows + PARTS * LAST_ROWS * stages, inner), BF16),
            pltpu.VMEM((rows + PARTS * LAST_ROWS * stages, inner), BF16),
            pltpu.VMEM((rows, inner), BF16), pltpu.VMEM((16, dim), F32),
            pltpu.VMEM((max(int(math.log2(runs)), 1), 16, dim), F32), pltpu.VMEM((16 * groups, dim), BF16),
            pltpu.SemaphoreType.DMA((PARTS, 2 * stages)), pltpu.SemaphoreType.DMA((PARTS, 2 * stages)),
            pltpu.SemaphoreType.DMA((stages,)), pltpu.SemaphoreType.DMA((stages,)),
        ],
        compiler_params=params(collective_id=4, has_side_effects=True),
        name="reduce",
    )(
        in_grad, out_grad, xp_grad, dtp_grad, rate_grad, tap_grad, tapb_grad, skip_grad, dtb_grad, d_mod, timestep,
    )

    own = lax.dynamic_slice_in_dim(factors, lax.axis_index("dp") * 16, 16, 0)
    (
        d_time, grad_ada, grad_ada_bias, in_grad, tap_grad, tapb_grad, xp_grad, dtp_grad, dtb_grad, rate_grad, skip_grad,
        out_grad,
    ) = pl.pallas_call(
        functools.partial(finish_kernel, (rank, wide_rank)),
        in_specs=[vmem] * 5,
        out_specs=[vmem] * 12,
        out_shape=[
            jax.ShapeDtypeStruct(shape, F32)
            for shape in (
                (slots, dim), (dim, 3 * dim), (1, 3 * dim), (dim, 2 * inner), (2, tap_count, inner), (2, inner),
                (2, inner, rank + 2 * states), (2, rank, inner), (2, inner), (2, states, inner), (2, inner), (inner, dim),
            )
        ],
        compiler_params=params(),
        name="finish",
    )(result, factors, own, timestep, ada_weight)
    return (
        mixed, d_tokens, d_time, grad_ada, grad_ada_bias[0], in_grad, tap_grad, tapb_grad, xp_grad, dtp_grad, dtb_grad,
        rate_grad, skip_grad, out_grad,
    )


def solution(mesh):
    runs = P("dp", "seq", None)
    return jax.shard_map(
        per_device,
        mesh=mesh,
        in_specs=(runs, P("dp", None), P("dp"), P("dp", "seq")) + (P(),) * 11 + (runs,),
        out_specs=(runs, runs, P("dp", None)) + (P(),) * 11,
        check_vma=False,
    )
```

```python
import functools
import math

import jax
import jax.numpy as jnp
from jax import lax
from jax.experimental import pallas as pl
from jax.experimental.pallas import tpu as pltpu
from jax.sharding import PartitionSpec as P

EPSILON = 1e-06
BLK = 16
HALO = 16
LOG2E = math.log2(math.e)
F32, BF16 = jnp.float32, jnp.bfloat16
NT = (((1,), (1,)), ((), ()))
TN = (((0,), (0,)), ((), ()))
VMEM_LIMIT = 60 << 20
MESH = pl.DeviceIdType.MESH


def dot(a, b):
    return jnp.dot(a, b, preferred_element_type=F32)


def dot_nt(a, b):
    return lax.dot_general(a, b, NT, preferred_element_type=F32)


def dot_tn(a, b):
    return lax.dot_general(a, b, TN, preferred_element_type=F32)


def reversal(size):
    rows = lax.broadcasted_iota(jnp.int32, (size, size), 0)
    cols = lax.broadcasted_iota(jnp.int32, (size, size), 1)
    return (rows + cols == size - 1).astype(BF16)


def flip_low(value):
    return dot(reversal(value.shape[0]), value).astype(BF16)


def flip_full(value):
    order = reversal(value.shape[0])
    high = value.astype(BF16)
    return dot(order, high) + dot(order, (value - high.astype(F32)).astype(BF16))


def normalise(tokens_f):
    centered = tokens_f - jnp.mean(tokens_f, axis=-1, keepdims=True)
    inv_std = lax.rsqrt(jnp.mean(centered * centered, axis=-1, keepdims=True) + EPSILON)
    return centered * inv_std, inv_std


def eye(size):
    rows = lax.broadcasted_iota(jnp.int32, (size, size), 0)
    cols = lax.broadcasted_iota(jnp.int32, (size, size), 1)
    return (rows == cols).astype(BF16)


def as_column(row):
    return dot_nt(eye(row.shape[1]), jnp.broadcast_to(row.astype(F32).astype(BF16), (8, row.shape[1])))[:, :1]


def remote(src, dst, send_sem, recv_sem, target):
    return pltpu.make_async_remote_copy(
        src_ref=src, dst_ref=dst, send_sem=send_sem, recv_sem=recv_sem, device_id=target, device_id_type=MESH
    )


def greet(targets):
    barrier = pltpu.get_barrier_semaphore()
    for target in targets:
        pl.semaphore_signal(barrier, inc=1, device_id=target, device_id_type=MESH)
    pl.semaphore_wait(barrier, len(targets))


def greet_line(me, runs):
    barrier = pltpu.get_barrier_semaphore()

    @pl.when(me > 0)
    def _():
        pl.semaphore_signal(barrier, inc=1, device_id={"seq": me - 1}, device_id_type=MESH)

    @pl.when(me < runs - 1)
    def _():
        pl.semaphore_signal(barrier, inc=1, device_id={"seq": me + 1}, device_id_type=MESH)

    neighbours = (me + runs - 1) // runs + (2 * runs - 2 - me) // runs
    pl.semaphore_wait(barrier, neighbours)


def swap_along_line(me, runs, ups, downs, start):
    up = [remote(src, dst, ss, rs, {"seq": me + 1}) for src, dst, ss, rs in ups]
    down = [remote(src, dst, ss, rs, {"seq": me - 1}) for src, dst, ss, rs in downs]

    @pl.when(me < runs - 1)
    def _():
        for copy in up:
            if start:
                copy.start()
            else:
                copy.wait_send()
        if not start:
            for copy in down:
                copy.wait_recv()

    @pl.when(me > 0)
    def _():
        for copy in down:
            if start:
                copy.start()
            else:
                copy.wait_send()
        if not start:
            for copy in up:
                copy.wait_recv()


def enter_kernel(
    runs, tok, cot, mask, counts, step, ada, ada_bias, win, wout,
    xe, dy, z_out, hid_out, mod_out,
    prev_tok, next_tok, prev_mask, next_mask, send_sem, recv_sem,
):
    slots, toks, dim = tok.shape
    inner = wout.shape[0]
    me = lax.axis_index("seq")
    i = pl.program_id(0)
    ups = [
        (tok.at[:, pl.ds(toks - HALO, HALO), :], prev_tok, send_sem.at[0], recv_sem.at[0]),
        (mask, prev_mask, send_sem.at[1], recv_sem.at[1]),
    ]
    downs = [
        (tok.at[:, pl.ds(0, HALO), :], next_tok, send_sem.at[2], recv_sem.at[2]),
        (mask, next_mask, send_sem.at[3], recv_sem.at[3]),
    ]

    @pl.when(i == 0)
    def _():
        greet_line(me, runs)
        swap_along_line(me, runs, ups, downs, True)

        @pl.when(me == 0)
        def _():
            prev_tok[...] = jnp.zeros(prev_tok.shape, BF16)
            prev_mask[...] = jnp.zeros(prev_mask.shape, jnp.int32)

        @pl.when(me == runs - 1)
        def _():
            next_tok[...] = jnp.zeros(next_tok.shape, BF16)
            next_mask[...] = jnp.zeros(next_mask.shape, jnp.int32)

    live = (counts[...] > i).astype(F32)
    time_f = step[...].astype(F32)
    time_low = (time_f * jax.nn.sigmoid(time_f)).astype(BF16)
    mod = dot(time_low, ada[...]) + ada_bias[...]
    mod_out[...] = mod
    shift, scale, gate = mod[:, :dim], mod[:, dim : 2 * dim], mod[:, 2 * dim :]

    def hidden_of(part):
        normed, _ = normalise(part.astype(F32))
        return (normed * (1.0 + scale) + shift).astype(BF16)

    hid = hidden_of(tok[i])
    hid_out[...] = hid
    xz = dot(hid, win[...]) * (as_column(mask[pl.ds(i, 1), :]) * live)
    x_low = xz[:, :inner].astype(BF16)
    z = xz[:, inner:]
    z_out[...] = z
    d_branch = (cot[...].astype(F32) * gate).astype(BF16)
    d_summed = dot_nt(d_branch, wout[...]) * z * jax.nn.sigmoid(z)
    dy[0] = d_summed
    dy[1] = flip_full(d_summed)
    xe[0, HALO:, :] = x_low
    xe[1, HALO:, :] = flip_low(x_low)

    @pl.when(i == 0)
    def _():
        swap_along_line(me, runs, ups, downs, False)

    rims = jnp.concatenate([prev_tok[i], next_tok[i]], axis=0)
    prev_col = as_column(prev_mask[pl.ds(i, 1), :])[toks - HALO :]
    next_col = as_column(next_mask[pl.ds(i, 1), :])[:HALO]
    rim_x = dot(hidden_of(rims), win[:, :inner]) * (jnp.concatenate([prev_col, next_col], axis=0) * live)
    rim_x = rim_x.astype(BF16)
    xe[0, :HALO, :] = rim_x[:HALO]
    xe[1, :HALO, :] = flip_low(rim_x[HALO:])


def twice(row8):
    return jnp.concatenate([row8, row8], axis=0)


def spread(ref, index):
    return twice(ref[pl.ds(index, 8, stride=0), :])


def lay_out(tiles, rows):
    for t in range(rows.shape[1]):
        tiles[t] = jnp.broadcast_to(rows[:, t : t + 1], (rows.shape[0], 128))


def across_lanes(tile, inner):
    return jnp.concatenate([tile] * (inner // 128), axis=1)


def softplus_parts(pre):
    e = jnp.exp2(-LOG2E * jnp.abs(pre))
    more = jnp.where(e < 1e-3, e - 0.5 * e * e, jnp.log(1.0 + e))
    return jnp.maximum(pre, 0.0) + more, jax.nn.sigmoid(pre)


def first_kernel(
    xe, dy, taps, tap_bias, xwt, dtw, dt_bias, rate2,
    act_out, dsilu_out, delta_out, sig_out, proj_out, end_out, back_out, total_out, starts_out, sums_out, tiles,
    dx, decay, through,
):
    toks, inner = dy.shape
    states = rate2.shape[0]
    blocks = toks // BLK
    rank = dtw.shape[0]
    tap_count = taps.shape[0]
    shifted = xe[...].astype(F32)
    conv = tap_bias[...] + taps[tap_count - 1 : tap_count, :] * shifted[HALO:]
    for k in reversed(range(tap_count - 1)):
        shifted = pltpu.roll(shifted, 1, 0)
        conv = conv + taps[k : k + 1, :] * shifted[HALO:]
    sig = jax.nn.sigmoid(conv)
    act_f = conv * sig
    act = act_f.astype(BF16)
    dsilu_out[...] = sig + act_f * (1.0 - sig)
    act_out[...] = act
    proj = dot_nt(xwt[...], act)
    proj_out[...] = proj
    lay_out(tiles, proj[rank:, :])
    pre = dot_tn(proj[:rank, :].astype(BF16), dtw[...]) + dt_bias[...]
    delta, slope = softplus_parts(pre)
    delta_out[...] = delta
    sig_out[...] = slope
    dx[...] = delta * act.astype(F32)
    end_out[...] = jnp.zeros((states, inner), F32)
    back_out[...] = jnp.zeros((states, inner), F32)
    through[...] = jnp.zeros((8, inner), F32)

    def one_block(j, slot):
        t0 = pl.multiple_of(j * BLK, BLK)
        dr, xr, yr = (ref.at[pl.ds(t0, BLK), :] for ref in (delta_out, dx, dy))
        tile = tiles.at[pl.ds(t0, BLK)]
        rate = rate2[...]
        s = end_out[...]
        starts_out[j] = s
        before = through[...]
        sums_out[j] = before[:1, :]
        for i in range(BLK):
            a = jnp.exp2(spread(dr, i) * rate)
            decay[slot, i] = a
            s = a * s + spread(xr, i) * across_lanes(tile[i, :states], inner)
        end_out[...] = s
        m = jnp.zeros((states, inner), F32)
        for i in reversed(range(BLK)):
            m = decay[slot, i] * (m + spread(yr, i) * across_lanes(tile[i, states:], inner))
        back_out[...] = back_out[...] + m * jnp.exp2(twice(before) * rate)
        through[...] = before + jnp.sum(dr[...], axis=0, keepdims=True)

    def block_step(k, _):
        one_block(2 * k, 0)
        one_block(2 * k + 1, 1)
        return 0

    lax.fori_loop(0, blocks // 2, block_step, 0)
    total_out[...] = through[:1, :]


def second_kernel(
    s_in, lam_in, starts, sums, tiles, rate2, rate, xe, act, dsilu, delta, sig, dy, proj, xwt, dtw, taps, skip,
    y_out, dx_out, rim_out, rate_grad, skip_grad, dtb_grad, dtp_grad, xp_grad, tap_grad, tapb_grad,
    carry, dxs, bdiag, cdiag, decay, states_low, lam_low, rq_low, qd_low, dots, racc, gsum, hsum, db, dc,
):
    toks, inner = dy.shape
    states = rate2.shape[0]
    blocks = toks // BLK
    rank = dtw.shape[0]
    tap_count = taps.shape[0]
    item = pl.program_id(1)
    width = BLK * states

    @pl.when(item == 0)
    def _():
        for ref in (rate_grad, skip_grad, dtb_grad, dtp_grad, xp_grad, tap_grad, tapb_grad):
            ref[...] = jnp.zeros(ref.shape, ref.dtype)

    carry[...] = lam_in[...]
    act_low = act[...]
    dxs[:toks, :] = delta[...] * act_low.astype(F32)
    fold = (
        lax.broadcasted_iota(jnp.int32, (states, width), 1) % states == lax.broadcasted_iota(jnp.int32, (states, width), 0)
    ).astype(BF16)
    own = lax.broadcasted_iota(jnp.int32, (toks, width), 0) % BLK == lax.broadcasted_iota(jnp.int32, (toks, width), 1) // states
    bdiag[:toks, :] = jnp.where(own, dot_tn(proj[rank : rank + states, :].astype(BF16), fold), 0.0).astype(BF16)
    cdiag[...] = jnp.where(own, dot_tn(proj[rank + states :, :].astype(BF16), fold), 0.0).astype(BF16)
    mine = own[:BLK]
    picks = mine.astype(BF16)
    sides = (
        lax.broadcasted_iota(jnp.int32, (2 * BLK, 256), 0) // BLK == lax.broadcasted_iota(jnp.int32, (2 * BLK, 256), 1) // 128
    ).astype(BF16)
    racc[...] = jnp.zeros((states, inner), F32)
    qd_low[1] = jnp.zeros(qd_low.shape[1:], BF16)

    def lane_sum(wide):
        part = [wide[:, at : at + 128] for at in range(0, inner, 128)]
        while len(part) > 1:
            part = [sum(part[at : at + 2]) for at in range(0, len(part), 2)]
        return part[0]

    def products(slot, j):
        t0 = pl.multiple_of(j * BLK, BLK)
        gsum[pl.ds(t0, BLK), :] = dot(bdiag[pl.ds(t0, BLK), :], lam_low[slot])
        hsum[pl.ds(t0, BLK), :] = dot(picks, rq_low[slot])
        racc[...] += dot(fold[:, : BLK // 4 * states], qd_low[slot])
        both = dot_nt(sides, dots[slot])
        dc[pl.ds(t0, BLK), :] = jnp.where(mine, both[:BLK], 0.0).astype(BF16)
        db[pl.ds(t0, BLK), :] = jnp.where(mine, both[BLK:], 0.0).astype(BF16)

    def one_block(slot, j):
        t0 = pl.multiple_of(j * BLK, BLK)
        dr, xr, yr = (ref.at[pl.ds(t0, BLK), :] for ref in (delta, dxs, dy))
        tile = tiles.at[pl.ds(t0, BLK)]
        r2 = rate2[...]
        r_low = rate[...].astype(BF16)
        s = starts[j] + s_in[...] * jnp.exp2(twice(jnp.broadcast_to(sums[j], (8, inner))) * r2)
        states_low[slot, :states, :] = s.astype(BF16)
        for i in range(BLK):
            a = jnp.exp2(spread(dr, i) * r2)
            decay[slot, i] = a
            s = a * s + spread(xr, i) * across_lanes(tile[i, :states], inner)
            s_low = s.astype(BF16)
            states_low[slot, (i + 1) * states : (i + 2) * states, :] = s_low
            dots[slot, i * states : (i + 1) * states, :128] = lane_sum(s_low * spread(yr, i).astype(BF16))
        y_out[pl.ds(t0, BLK), :] = dot(cdiag[pl.ds(t0, BLK), :], states_low[slot, states:, :])
        cr = carry[...]
        qds = []
        for i in reversed(range(BLK)):
            lam = cr + spread(yr, i) * across_lanes(tile[i, states:], inner)
            l_low = lam.astype(BF16)
            lam_low[slot, i * states : (i + 1) * states, :] = l_low
            dots[slot, i * states : (i + 1) * states, 128:] = lane_sum(l_low * spread(xr, i).astype(BF16))
            cr = decay[slot, i] * lam
            q = cr.astype(BF16) * states_low[slot, i * states : (i + 1) * states, :]
            rq_low[slot, i * states : (i + 1) * states, :] = q * r_low
            qds.append(q * spread(dr, i).astype(BF16))
            if i % 4 == 0:
                qd_low[slot, i // 4 * states : (i // 4 + 1) * states, :] = (qds[0] + qds[1]) + (qds[2] + qds[3])
                qds = []
        carry[...] = cr

    def block_step(k, _):
        j = blocks - 1 - 2 * k
        products(1, jnp.where(k == 0, blocks, j + 1))
        one_block(0, j)
        products(0, j)
        one_block(1, j - 1)
        return 0

    lax.fori_loop(0, blocks // 2, block_step, 0)
    products(1, 0)

    rate_grad[...] += -racc[...]
    act_f = act_low.astype(F32)
    d_summed = dy[...]
    g = gsum[:toks, :]
    skip_grad[...] += jnp.sum(d_summed * act_f, axis=0, keepdims=True)
    y_out[...] += skip[...] * act_f
    d_pre = (act_f * g - hsum[:toks, :]) * sig[...]
    dtb_grad[...] += jnp.sum(d_pre, axis=0, keepdims=True)
    d_pre_low = d_pre.astype(BF16)
    dtp_grad[...] += dot(proj[:rank, :].astype(BF16), d_pre_low)
    d_proj = jnp.concatenate(
        [dot_nt(dtw[...], d_pre_low), dot_nt(fold, db[:toks, :]), dot_nt(fold, dc[:toks, :])], axis=0
    ).astype(BF16)
    xp_grad[...] += dot(d_proj, act_low)
    d_act = delta[...] * g + skip[...] * d_summed + dot_tn(d_proj, xwt[...])
    d_conv = d_act * dsilu[...]
    tapb_grad[...] += jnp.sum(d_conv, axis=0, keepdims=True)
    x_f = xe[...].astype(F32)
    moved = jnp.concatenate([jnp.zeros((HALO, inner), F32), d_conv], axis=0)
    window = HALO + toks
    d_window = taps[tap_count - 1 : tap_count, :] * moved
    tap_grad[tap_count - 1 : tap_count, :] += jnp.sum(moved * x_f, axis=0, keepdims=True)
    for k in reversed(range(tap_count - 1)):
        moved = pltpu.roll(moved, window - 1, 0)
        tap_grad[k : k + 1, :] += jnp.sum(moved * x_f, axis=0, keepdims=True)
        d_window = d_window + taps[k : k + 1, :] * moved
    rim_out[...] = d_window[HALO - 8 : HALO]
    dx_out[...] = d_window[HALO:]


def third_kernel(
    runs, tok, cot, mod, mask, counts, hid, z_in, y, dx, rims, win, wout,
    mixed, d_tokens, d_mod, out_grad, in_grad,
    late_up, late_down, send_sem, recv_sem,
):
    dim = tok.shape[-1]
    toks, inner = z_in.shape
    me = lax.axis_index("seq")
    i = pl.program_id(0)
    ups = [(rims.at[1], late_up, send_sem.at[0], recv_sem.at[0])]
    downs = [(rims.at[0], late_down, send_sem.at[1], recv_sem.at[1])]

    @pl.when(i == 0)
    def _():
        greet_line(me, runs)
        swap_along_line(me, runs, ups, downs, True)

        @pl.when(me == 0)
        def _():
            late_up[...] = jnp.zeros(late_up.shape, F32)

        @pl.when(me == runs - 1)
        def _():
            late_down[...] = jnp.zeros(late_down.shape, F32)

        out_grad[...] = jnp.zeros(out_grad.shape, F32)
        in_grad[...] = jnp.zeros(in_grad.shape, F32)

    shift, scale, gate = mod[:, :dim], mod[:, dim : 2 * dim], mod[:, 2 * dim :]
    valid = as_column(mask[pl.ds(i, 1), :]) * (counts[...] > i).astype(F32)
    tok_f = tok[...].astype(F32)
    normed, inv_std = normalise(tok_f)
    cot_f = cot[...].astype(F32)
    z = z_in[...]
    z_sig = jax.nn.sigmoid(z)
    summed = y[0] + flip_full(y[1])
    gated = (summed * z * z_sig).astype(BF16)
    branch_out = dot(gated, wout[...])
    mixed[...] = (tok_f + gate * branch_out).astype(BF16)
    d_branch = (cot_f * gate).astype(BF16)
    d_gated = dot_nt(d_branch, wout[...])
    d_zgate = d_gated * summed * z_sig * (1.0 + z * (1.0 - z_sig))
    out_grad[...] += dot_tn(gated, d_branch)

    @pl.when(i == 0)
    def _():
        swap_along_line(me, runs, ups, downs, False)

    edge = late_up.shape[1]

    def with_late(part, extra):
        return jnp.concatenate([part[: toks - edge], part[toks - edge :] + extra], axis=0)

    d_x = with_late(dx[0], late_down[i]) + flip_full(with_late(dx[1], late_up[i]))
    d_xz = (jnp.concatenate([d_x, d_zgate], axis=1) * valid).astype(BF16)
    d_hidden = dot_nt(d_xz, win[...])
    in_grad[...] += dot_tn(hid[...], d_xz)
    d_mod[0:1, :] = jnp.sum(d_hidden, axis=0, keepdims=True)
    d_mod[1:2, :] = jnp.sum(d_hidden * normed, axis=0, keepdims=True)
    d_mod[2:3, :] = jnp.sum(cot_f * branch_out, axis=0, keepdims=True)
    d_normed = d_hidden * (1.0 + scale)
    d_tokens[...] = cot_f + inv_std * (
        d_normed
        - jnp.mean(d_normed, axis=-1, keepdims=True)
        - normed * jnp.mean(d_normed * normed, axis=-1, keepdims=True)
    )


def bit_of(index, bit):
    return (index // (1 << bit)) % 2


def across(axis, bit):
    me = lax.axis_index(axis)
    mine = bit_of(me, bit)
    return mine, {axis: me + (1 - 2 * mine) * (1 << bit)}


def exchange_kernel(runs, end, back, total, rate2, s_in, lam_in, group, span, pre, pre_span, sends, arrivals, send_sem, recv_sem):
    slots, _, states, inner = end.shape
    bits = int(math.log2(runs))
    links = [across("seq", bit) for bit in range(bits)]
    greet([target for _, target in links])
    flows = (((end, 0), (back, 1)), ((end, 1), (back, 0)))
    units = 2 * slots
    rows = units * states
    pre[...] = jnp.zeros(pre.shape, F32)
    pre_span[...] = jnp.zeros(pre_span.shape, F32)
    for flow in range(2):
        for kind, (array, branch) in enumerate(flows[flow]):
            for i in range(slots):
                group[flow, kind * slots + i] = array[i, branch]
                span[flow, kind * slots + i] = jnp.broadcast_to(total[i, branch], (8, inner))

    def load(flow, slot):
        for unit in range(units):
            sends[slot, unit * states : (unit + 1) * states, :] = group[flow, unit].astype(BF16)
            high = span[flow, unit].astype(BF16)
            low = (span[flow, unit] - high.astype(F32)).astype(BF16)
            at = rows + unit * 16
            sends[slot, at : at + 16, :] = jnp.concatenate([high.astype(F32), low.astype(F32)], axis=0).astype(BF16)

    def join(flow, slot, earlier, last):
        for unit in range(units):
            rate = rate2[flows[flow][unit // slots][1]]
            state = arrivals[slot, unit * states : (unit + 1) * states, :].astype(F32)
            at = rows + unit * 16
            both = arrivals[slot, at : at + 16, :].astype(F32)
            length = both[:8] + both[8:]
            mine, mine_span = pre[flow, unit], pre_span[flow, unit]
            joined = state * jnp.exp2(rate * twice(mine_span)) + mine
            pre[flow, unit] = jnp.where(earlier, joined, mine)
            pre_span[flow, unit] = jnp.where(earlier, length + mine_span, mine_span)
            if not last:
                own, own_span = group[flow, unit], span[flow, unit]
                first = jnp.where(earlier, state, own)
                second = jnp.where(earlier, own, state)
                second_span = jnp.where(earlier, own_span, length)
                group[flow, unit] = first * jnp.exp2(rate * twice(second_span)) + second
                span[flow, unit] = own_span + length

    for stage, (mine, target) in enumerate(links):
        last = stage == bits - 1
        if last:
            slot = 2 * stage

            @pl.when(mine == 0)
            def _():
                load(0, slot)

            @pl.when(mine == 1)
            def _():
                load(1, slot)

            copies = [remote(sends.at[slot], arrivals.at[slot], send_sem.at[slot], recv_sem.at[slot], target)]
        else:
            copies = []
            for flow in range(2):
                slot = 2 * stage + flow
                load(flow, slot)
                copies.append(
                    remote(sends.at[slot], arrivals.at[slot], send_sem.at[slot], recv_sem.at[slot], target)
                )
        for copy in copies:
            copy.start()
        for copy in copies:
            copy.wait()
        if last:

            @pl.when(mine == 1)
            def _():
                join(0, 2 * stage, True, True)

            @pl.when(mine == 0)
            def _():
                join(1, 2 * stage, True, True)
        else:
            join(0, 2 * stage, mine == 1, False)
            join(1, 2 * stage + 1, mine == 0, False)
    for flow in range(2):
        for kind, (_, branch) in enumerate(flows[flow]):
            result = (s_in, lam_in)[kind]
            for i in range(slots):
                result[i, branch] = pre[flow, kind * slots + i]


PARTS = 3
LAST_ROWS = 16


def reduce_rows(dim, inner, small):
    rows = 3 * dim + small
    unit = PARTS * LAST_ROWS * 32
    return -(-rows // unit) * unit


def reduce_kernel(
    plan, in_grad, out_grad, xp_grad, dtp_grad, rate_grad, tap_grad, tapb_grad, skip_grad, dtb_grad, d_mod, step,
    result, factors,
    acc, sends, arrivals, gathered, mod_sum, mod_in, table, send_sem, recv_sem, small_send, small_recv,
):
    runs, groups, total_rows = plan
    dim = in_grad.shape[0]
    inner = out_grad.shape[0]
    slots = step.shape[0]
    seq_bits = [("seq", bit) for bit in range(int(math.log2(runs)))]
    dp_bits = [("dp", bit) for bit in range(int(math.log2(groups)))]
    all_bits = seq_bits + dp_bits
    links = {key: across(*key) for key in all_bits}
    greet([links[key][1] for key in all_bits])
    middle = all_bits[1:-1]
    orders = [
        all_bits[:1] + middle[part % max(len(middle), 1) :] + middle[: part % max(len(middle), 1)] + all_bits[1:][-1:]
        for part in range(PARTS)
    ]
    part_rows = total_rows // PARTS

    mod_sum[...] = jnp.zeros(mod_sum.shape, F32)
    for i in range(slots):
        mod_sum[3 * i : 3 * i + 3, :] = d_mod[i]

    def small_copy(stage):
        axis, bit = all_bits[stage]
        target = links[(axis, bit)][1]
        if axis == "seq":
            return remote(mod_sum, mod_in.at[stage], small_send.at[stage], small_recv.at[stage], target)
        size = 16 << bit
        at = pl.multiple_of(lax.axis_index("dp") // (1 << bit) * size, 16)
        here = table.at[pl.ds(at, size), :]
        return remote(here, here, small_send.at[stage], small_recv.at[stage], target)

    def fill_table():
        time_f = step[...].astype(F32)
        time_low = time_f * jax.nn.sigmoid(time_f)
        at = pl.multiple_of(lax.axis_index("dp") * 16, 16)
        own = jnp.concatenate([mod_sum[: 3 * slots, :], time_low, mod_sum[4 * slots :, :]], axis=0)
        table[pl.ds(at, 16), :] = own.astype(BF16)

    half = dim
    acc[0:dim, :] = in_grad[:, :inner]
    acc[dim : 2 * dim, :] = in_grad[:, inner:]
    acc[2 * dim : 3 * dim, :] = jnp.concatenate([out_grad[:half, :], out_grad[half:, :]], axis=1)
    at = 3 * dim
    for ref in (xp_grad, dtp_grad, rate_grad, tap_grad):
        for branch in range(2):
            size = ref.shape[1]
            acc[at : at + size, :] = ref[branch]
            at += size
    tail = [ref[branch] for ref in (tapb_grad, skip_grad, dtb_grad) for branch in range(2)]
    acc[at : at + 8, :] = jnp.concatenate(tail + [jnp.zeros((2, inner), F32)], axis=0)
    at += 8
    acc[at:, :] = jnp.zeros((total_rows - at, inner), F32)

    starts = [part * part_rows for part in range(PARTS)]
    sizes = [part_rows] * PARTS
    history = [[] for _ in range(PARTS)]
    offsets = [part * part_rows for part in range(PARTS)]
    count = len(all_bits)
    for stage in range(count):
        copies = []
        for part in range(PARTS):
            mine, target = links[orders[part][stage]]
            start, size = starts[part], sizes[part]
            split = size >= 2 * LAST_ROWS
            moved = size // 2 if split else size
            if split:
                away = pl.multiple_of(start + (1 - mine) * moved, LAST_ROWS)
                keep = pl.multiple_of(start + mine * moved, LAST_ROWS)
            else:
                away = keep = start
            history[part].append((start, size, split))
            at = offsets[part]
            offsets[part] += moved
            here = sends.at[pl.ds(at, moved), :]
            sends[at : at + moved, :] = acc[pl.ds(away, moved), :].astype(BF16)
            copy = remote(
                here, arrivals.at[pl.ds(at, moved), :], send_sem.at[part, stage], recv_sem.at[part, stage], target
            )
            copy.start()
            copies.append((copy, part, keep, moved, at, split))
            starts[part], sizes[part] = keep, moved
        if stage == len(seq_bits):
            fill_table()
        small = small_copy(stage)
        small.start()
        for copy, part, keep, moved, at, split in copies:
            copy.wait()
            held = acc[pl.ds(keep, moved), :]
            if not split:
                held = held.astype(BF16).astype(F32)
            acc[pl.ds(keep, moved), :] = held + arrivals[at : at + moved, :].astype(F32)
        small.wait()
        if all_bits[stage][0] == "seq":
            mod_sum[...] += mod_in[stage]
    if not dp_bits:
        fill_table()
    factors[...] = table[...]
    for part in range(PARTS):
        where = pl.ds(starts[part], sizes[part])
        gathered[where, :] = acc[where, :].astype(BF16)
    for stage in reversed(range(count)):
        copies = []
        for part in range(PARTS):
            start, size, split = history[part][stage]
            if not split:
                continue
            target = links[orders[part][stage]][1]
            here = gathered.at[pl.ds(starts[part], sizes[part]), :]
            copy = remote(
                here, here, send_sem.at[part, count + stage], recv_sem.at[part, count + stage], target
            )
            copy.start()
            copies.append(copy)
            starts[part], sizes[part] = start, size
        for copy in copies:
            copy.wait()
    result[...] = gathered[...]


def finish_kernel(
    ranks, result, factors, own, step, ada,
    grad_time, grad_ada, grad_ada_bias, in_grad, tap_grad, tapb_grad, xp_grad, dtp_grad, dtb_grad, rate_grad, skip_grad, out_grad,
):
    rank, wide_rank = ranks
    dim = in_grad.shape[0]
    inner = out_grad.shape[0]
    slots = step.shape[0]
    states = rate_grad.shape[1]
    taps = tap_grad.shape[1]

    def rows(at, size):
        return result[at : at + size, :].astype(F32)

    in_grad[:, :inner] = rows(0, dim)
    in_grad[:, inner:] = rows(dim, dim)
    both = rows(2 * dim, dim)
    out_grad[:dim, :] = both[:, :dim]
    out_grad[dim:, :] = both[:, dim:]
    at = 3 * dim
    wide = wide_rank + 2 * states
    for branch in range(2):
        part = rows(at, wide)
        part = jnp.concatenate([part[:rank], part[wide_rank:], part[rank:wide_rank]], axis=0)
        part = jnp.concatenate([part, jnp.zeros((128 - wide, inner), F32)], axis=0)
        xp_grad[branch] = part.T[:, : rank + 2 * states]
        at += wide
    for branch in range(2):
        dtp_grad[branch] = rows(at, wide_rank)[:rank]
        at += wide_rank
    for branch in range(2):
        rate_grad[branch] = rows(at, states)
        at += states
    tail = rows(at, 16)
    for branch in range(2):
        tap_grad[branch] = tail[branch * taps : (branch + 1) * taps]
    tapb_grad[...] = tail[2 * taps : 2 * taps + 2]
    skip_grad[...] = tail[2 * taps + 2 : 2 * taps + 4]
    dtb_grad[...] = tail[2 * taps + 4 : 2 * taps + 6]

    table = factors[...]
    length = table.shape[0]
    groups = length // 16
    items = groups * 8

    def pick(place):
        row = lax.broadcasted_iota(jnp.int32, (items, length), 0)
        col = lax.broadcasted_iota(jnp.int32, (items, length), 1)
        slot = row % 8
        wanted = row // 8 * 16 + place(slot)
        return dot(((col == wanted) & (slot < slots)).astype(BF16), table)

    times = pick(lambda slot: 3 * slots + slot).astype(BF16)
    time_f = step[...].astype(F32)
    time_sig = jax.nn.sigmoid(time_f)
    d_time = jnp.zeros((slots, dim), F32)
    mine = own[...].astype(F32)
    for part in range(3):
        mods = pick(lambda slot: 3 * slot + part)
        lanes = slice(part * dim, (part + 1) * dim)
        grad_ada[:, lanes] = dot_tn(times, mods.astype(BF16))
        grad_ada_bias[:, lanes] = jnp.sum(mods, axis=0, keepdims=True)
        picked = jnp.concatenate([mine[3 * i + part : 3 * i + part + 1] for i in range(slots)], axis=0)
        d_time = d_time + dot_nt(picked.astype(BF16), ada[:, lanes])
    grad_time[...] = d_time * time_sig * (1.0 + time_f * (1.0 - time_sig))


def params(**more):
    return pltpu.CompilerParams(vmem_limit_bytes=VMEM_LIMIT, **more)


def spec(block, index):
    return pl.BlockSpec(block, index)


def per_device(
    tokens, timestep, counts, token_mask, ada_weight, ada_bias, input_weight, conv_weight, conv_bias, x_weight, dt_weight,
    dt_bias, decay_rate, skip_gain, output_weight, cotangent,
):
    slots, toks, dim = tokens.shape
    inner = output_weight.shape[0]
    rank = dt_weight.shape[1]
    states = decay_rate.shape[1]
    tap_count = conv_weight.shape[1]
    wide_rank = 32
    proj_rows = wide_rank + 2 * states
    blocks = toks // BLK
    runs = lax.axis_size("seq")
    groups = lax.axis_size("dp")
    counts2 = counts[:, None]
    step3 = timestep[:, None, :]
    xwt = jnp.swapaxes(x_weight, 1, 2)
    xwt = jnp.concatenate(
        [xwt[:, :rank], jnp.zeros((2, wide_rank - rank, inner), BF16), xwt[:, rank:]], axis=1
    )
    dtw = jnp.concatenate([dt_weight, jnp.zeros((2, wide_rank - rank, inner), BF16)], axis=1)
    rate2 = -LOG2E * decay_rate
    vec = lambda a: a[:, None, :]

    def item(*block):
        return spec((None,) + block, lambda i: (i,) + (0,) * len(block))

    def whole(*block):
        return spec(block, lambda *_: (0,) * len(block))

    xe, dy, z_gate, hid, modulate = pl.pallas_call(
        functools.partial(enter_kernel, runs),
        grid=(slots,),
        in_specs=[
            whole(slots, toks, dim), item(toks, dim), whole(slots, toks), whole(1, 1), item(1, dim), whole(dim, 3 * dim),
            whole(1, 3 * dim), whole(dim, 2 * inner), whole(inner, dim),
        ],
        out_specs=[
            item(2, HALO + toks, inner), item(2, toks, inner), item(toks, inner), item(toks, dim), item(1, 3 * dim),
        ],
        out_shape=[
            jax.ShapeDtypeStruct((slots, 2, HALO + toks, inner), BF16),
            jax.ShapeDtypeStruct((slots, 2, toks, inner), F32),
            jax.ShapeDtypeStruct((slots, toks, inner), F32),
            jax.ShapeDtypeStruct((slots, toks, dim), BF16),
            jax.ShapeDtypeStruct((slots, 1, 3 * dim), F32),
        ],
        scratch_shapes=[
            pltpu.VMEM((slots, HALO, dim), BF16), pltpu.VMEM((slots, HALO, dim), BF16), pltpu.VMEM((slots, toks), jnp.int32),
            pltpu.VMEM((slots, toks), jnp.int32), pltpu.SemaphoreType.DMA((4,)), pltpu.SemaphoreType.DMA((4,)),
        ],
        compiler_params=params(collective_id=1, has_side_effects=True),
        name="enter",
    )(
        tokens, cotangent, token_mask, counts2, step3, ada_weight, ada_bias[None, :], input_weight, output_weight,
    )

    def unit(*block):
        return spec((None, None) + block, lambda b, i: (i, b) + (0,) * len(block))

    def branch(*block):
        return spec((None,) + block, lambda b, i: (b,) + (0,) * len(block))

    def unit_shape(*block, kind=F32):
        return jax.ShapeDtypeStruct((slots, 2) + block, kind)

    act, dsilu, delta, sig, proj, end, back, total, starts, sums, tiles = pl.pallas_call(
        first_kernel,
        grid=(2, slots),
        in_specs=[
            unit(HALO + toks, inner), unit(toks, inner), branch(tap_count, inner), branch(1, inner), branch(proj_rows, inner),
            branch(wide_rank, inner), branch(1, inner), branch(states, inner),
        ],
        out_specs=[
            unit(toks, inner), unit(toks, inner), unit(toks, inner), unit(toks, inner), unit(proj_rows, toks),
            unit(states, inner), unit(states, inner), unit(1, inner), unit(blocks, states, inner), unit(blocks, 1, inner),
            unit(toks, 2 * states, 128),
        ],
        out_shape=[
            unit_shape(toks, inner, kind=BF16), unit_shape(toks, inner), unit_shape(toks, inner), unit_shape(toks, inner),
            unit_shape(proj_rows, toks), unit_shape(states, inner), unit_shape(states, inner), unit_shape(1, inner),
            unit_shape(blocks, states, inner), unit_shape(blocks, 1, inner), unit_shape(toks, 2 * states, 128),
        ],
        scratch_shapes=[
            pltpu.VMEM((toks, inner), F32), pltpu.VMEM((2, BLK, states, inner), F32), pltpu.VMEM((8, inner), F32),
        ],
        compiler_params=params(),
        name="first",
    )(xe, dy, conv_weight, vec(conv_bias), xwt, dtw, vec(dt_bias), rate2)

    pairs = int(math.log2(runs))
    units = 2 * slots
    vmem = pl.BlockSpec(memory_space=pltpu.VMEM)
    s_in, lam_in = pl.pallas_call(
        functools.partial(exchange_kernel, runs),
        in_specs=[vmem] * 4,
        out_specs=[vmem] * 2,
        out_shape=[unit_shape(states, inner), unit_shape(states, inner)],
        scratch_shapes=[
            pltpu.VMEM((2, units, states, inner), F32), pltpu.VMEM((2, units, 8, inner), F32),
            pltpu.VMEM((2, units, states, inner), F32), pltpu.VMEM((2, units, 8, inner), F32),
            pltpu.VMEM((2 * pairs, units * (states + 16), inner), BF16),
            pltpu.VMEM((2 * pairs, units * (states + 16), inner), BF16),
            pltpu.SemaphoreType.DMA((2 * pairs,)), pltpu.SemaphoreType.DMA((2 * pairs,)),
        ],
        compiler_params=params(collective_id=2, has_side_effects=True),
        name="exchange",
    )(end, back, total, rate2)

    rim_spec = spec((None, None, 8, inner), lambda b, i: (b, i, 0, 0))
    y, dx, rims, rate_grad, skip_grad, dtb_grad, dtp_grad, xp_grad, tap_grad, tapb_grad = pl.pallas_call(
        second_kernel,
        grid=(2, slots),
        in_specs=[
            unit(states, inner), unit(states, inner), unit(blocks, states, inner),
            unit(blocks, 1, inner), unit(toks, 2 * states, 128), branch(states, inner), branch(states, inner), unit(HALO + toks, inner), unit(toks, inner),
            unit(toks, inner), unit(toks, inner), unit(toks, inner), unit(toks, inner), unit(proj_rows, toks),
            branch(proj_rows, inner), branch(wide_rank, inner),
            branch(tap_count, inner), branch(1, inner),
        ],
        out_specs=[
            unit(toks, inner), unit(toks, inner), rim_spec, branch(states, inner), branch(1, inner), branch(1, inner),
            branch(wide_rank, inner), branch(proj_rows, inner), branch(tap_count, inner), branch(1, inner),
        ],
        out_shape=[
            unit_shape(toks, inner), unit_shape(toks, inner), jax.ShapeDtypeStruct((2, slots, 8, inner), F32),
        ] + [
            jax.ShapeDtypeStruct((2, rows, inner), F32) for rows in (states, 1, 1, wide_rank, proj_rows, tap_count, 1)
        ],
        scratch_shapes=[
            pltpu.VMEM((states, inner), F32), pltpu.VMEM((toks + BLK, inner), F32), pltpu.VMEM((toks + BLK, BLK * states), BF16),
            pltpu.VMEM((toks, BLK * states), BF16),
            pltpu.VMEM((2, BLK, states, inner), F32),
            pltpu.VMEM((2, (BLK + 1) * states, inner), BF16), pltpu.VMEM((2, BLK * states, inner), BF16),
            pltpu.VMEM((2, BLK * states, inner), BF16), pltpu.VMEM((2, BLK // 4 * states, inner), BF16),
            pltpu.VMEM((2, BLK * states, 256), BF16), pltpu.VMEM((states, inner), F32),
            pltpu.VMEM((toks + BLK, inner), F32), pltpu.VMEM((toks + BLK, inner), F32),
            pltpu.VMEM((toks + BLK, BLK * states), BF16), pltpu.VMEM((toks + BLK, BLK * states), BF16),
        ],
        compiler_params=params(),
        name="second",
    )(
        s_in, lam_in, starts, sums, tiles, rate2, decay_rate, xe, act, dsilu, delta,
        sig, dy, proj, xwt, dtw, conv_weight, vec(skip_gain),
    )

    mixed, d_tokens, d_mod, out_grad, in_grad = pl.pallas_call(
        functools.partial(third_kernel, runs),
        grid=(slots,),
        in_specs=[
            item(toks, dim), item(toks, dim), item(1, 3 * dim), whole(slots, toks), whole(1, 1), item(toks, dim),
            item(toks, inner), item(2, toks, inner), item(2, toks, inner), whole(2, slots, 8, inner), whole(dim, 2 * inner),
            whole(inner, dim),
        ],
        out_specs=[item(toks, dim), item(toks, dim), item(3, dim), whole(inner, dim), whole(dim, 2 * inner)],
        out_shape=[
            jax.ShapeDtypeStruct((slots, toks, dim), BF16), jax.ShapeDtypeStruct((slots, toks, dim), F32),
            jax.ShapeDtypeStruct((slots, 3, dim), F32), jax.ShapeDtypeStruct((inner, dim), F32),
            jax.ShapeDtypeStruct((dim, 2 * inner), F32),
        ],
        scratch_shapes=[
            pltpu.VMEM((slots, 8, inner), F32), pltpu.VMEM((slots, 8, inner), F32), pltpu.SemaphoreType.DMA((2,)),
            pltpu.SemaphoreType.DMA((2,)),
        ],
        compiler_params=params(collective_id=3, has_side_effects=True),
        name="third",
    )(
        tokens, cotangent, modulate, token_mask, counts2, hid, z_gate, y, dx, rims, input_weight, output_weight,
    )

    small = 2 * (proj_rows + wide_rank + states + tap_count) + 8
    rows = reduce_rows(dim, inner, small)
    stages = int(math.log2(runs)) + int(math.log2(groups))
    result, factors = pl.pallas_call(
        functools.partial(reduce_kernel, (runs, groups, rows)),
        in_specs=[vmem] * 11,
        out_specs=[vmem] * 2,
        out_shape=[jax.ShapeDtypeStruct((rows, inner), BF16), jax.ShapeDtypeStruct((16 * groups, dim), BF16)],
        scratch_shapes=[
            pltpu.VMEM((rows, inner), F32), pltpu.VMEM((rows + PARTS * LAST_ROWS * stages, inner), BF16),
            pltpu.VMEM((rows + PARTS * LAST_ROWS * stages, inner), BF16),
            pltpu.VMEM((rows, inner), BF16), pltpu.VMEM((16, dim), F32),
            pltpu.VMEM((max(int(math.log2(runs)), 1), 16, dim), F32), pltpu.VMEM((16 * groups, dim), BF16),
            pltpu.SemaphoreType.DMA((PARTS, 2 * stages)), pltpu.SemaphoreType.DMA((PARTS, 2 * stages)),
            pltpu.SemaphoreType.DMA((stages,)), pltpu.SemaphoreType.DMA((stages,)),
        ],
        compiler_params=params(collective_id=4, has_side_effects=True),
        name="reduce",
    )(
        in_grad, out_grad, xp_grad, dtp_grad, rate_grad, tap_grad, tapb_grad, skip_grad, dtb_grad, d_mod, timestep,
    )

    own = lax.dynamic_slice_in_dim(factors, lax.axis_index("dp") * 16, 16, 0)
    (
        d_time, grad_ada, grad_ada_bias, in_grad, tap_grad, tapb_grad, xp_grad, dtp_grad, dtb_grad, rate_grad, skip_grad,
        out_grad,
    ) = pl.pallas_call(
        functools.partial(finish_kernel, (rank, wide_rank)),
        in_specs=[vmem] * 5,
        out_specs=[vmem] * 12,
        out_shape=[
            jax.ShapeDtypeStruct(shape, F32)
            for shape in (
                (slots, dim), (dim, 3 * dim), (1, 3 * dim), (dim, 2 * inner), (2, tap_count, inner), (2, inner),
                (2, inner, rank + 2 * states), (2, rank, inner), (2, inner), (2, states, inner), (2, inner), (inner, dim),
            )
        ],
        compiler_params=params(),
        name="finish",
    )(result, factors, own, timestep, ada_weight)
    return (
        mixed, d_tokens, d_time, grad_ada, grad_ada_bias[0], in_grad, tap_grad, tapb_grad, xp_grad, dtp_grad, dtb_grad,
        rate_grad, skip_grad, out_grad,
    )


def solution(mesh):
    runs = P("dp", "seq", None)
    return jax.shard_map(
        per_device,
        mesh=mesh,
        in_specs=(runs, P("dp", None), P("dp"), P("dp", "seq")) + (P(),) * 11 + (runs,),
        out_specs=(runs, runs, P("dp", None)) + (P(),) * 11,
        check_vma=False,
    )
```

```python
import functools
import math

import jax
import jax.numpy as jnp
from jax import lax
from jax.experimental import pallas as pl
from jax.experimental.pallas import tpu as pltpu
from jax.sharding import PartitionSpec as P

EPSILON = 1e-06
BLK = 16
HALO = 16
LOG2E = math.log2(math.e)
F32, BF16 = jnp.float32, jnp.bfloat16
NT = (((1,), (1,)), ((), ()))
TN = (((0,), (0,)), ((), ()))
VMEM_LIMIT = 60 << 20
MESH = pl.DeviceIdType.MESH


def dot(a, b):
    return jnp.dot(a, b, preferred_element_type=F32)


def dot_nt(a, b):
    return lax.dot_general(a, b, NT, preferred_element_type=F32)


def dot_tn(a, b):
    return lax.dot_general(a, b, TN, preferred_element_type=F32)


def reversal(size):
    rows = lax.broadcasted_iota(jnp.int32, (size, size), 0)
    cols = lax.broadcasted_iota(jnp.int32, (size, size), 1)
    return (rows + cols == size - 1).astype(BF16)


def flip_low(value):
    return dot(reversal(value.shape[0]), value).astype(BF16)


def flip_full(value):
    order = reversal(value.shape[0])
    high = value.astype(BF16)
    return dot(order, high) + dot(order, (value - high.astype(F32)).astype(BF16))


def normalise(tokens_f):
    centered = tokens_f - jnp.mean(tokens_f, axis=-1, keepdims=True)
    inv_std = lax.rsqrt(jnp.mean(centered * centered, axis=-1, keepdims=True) + EPSILON)
    return centered * inv_std, inv_std


def eye(size):
    rows = lax.broadcasted_iota(jnp.int32, (size, size), 0)
    cols = lax.broadcasted_iota(jnp.int32, (size, size), 1)
    return (rows == cols).astype(BF16)


def as_column(row):
    return dot_nt(eye(row.shape[1]), jnp.broadcast_to(row.astype(F32).astype(BF16), (8, row.shape[1])))[:, :1]


def remote(src, dst, send_sem, recv_sem, target):
    return pltpu.make_async_remote_copy(
        src_ref=src, dst_ref=dst, send_sem=send_sem, recv_sem=recv_sem, device_id=target, device_id_type=MESH
    )


def greet(targets):
    barrier = pltpu.get_barrier_semaphore()
    for target in targets:
        pl.semaphore_signal(barrier, inc=1, device_id=target, device_id_type=MESH)
    pl.semaphore_wait(barrier, len(targets))


def greet_line(me, runs):
    barrier = pltpu.get_barrier_semaphore()

    @pl.when(me > 0)
    def _():
        pl.semaphore_signal(barrier, inc=1, device_id={"seq": me - 1}, device_id_type=MESH)

    @pl.when(me < runs - 1)
    def _():
        pl.semaphore_signal(barrier, inc=1, device_id={"seq": me + 1}, device_id_type=MESH)

    neighbours = (me + runs - 1) // runs + (2 * runs - 2 - me) // runs
    pl.semaphore_wait(barrier, neighbours)


def swap_along_line(me, runs, ups, downs, start):
    up = [remote(src, dst, ss, rs, {"seq": me + 1}) for src, dst, ss, rs in ups]
    down = [remote(src, dst, ss, rs, {"seq": me - 1}) for src, dst, ss, rs in downs]

    @pl.when(me < runs - 1)
    def _():
        for copy in up:
            if start:
                copy.start()
            else:
                copy.wait_send()
        if not start:
            for copy in down:
                copy.wait_recv()

    @pl.when(me > 0)
    def _():
        for copy in down:
            if start:
                copy.start()
            else:
                copy.wait_send()
        if not start:
            for copy in up:
                copy.wait_recv()


def enter_kernel(
    runs, tok, cot, mask, counts, step, ada, ada_bias, win, wout,
    xe, dy, z_out, hid_out, mod_out,
    prev_tok, next_tok, prev_mask, next_mask, send_sem, recv_sem,
):
    slots, toks, dim = tok.shape
    inner = wout.shape[0]
    me = lax.axis_index("seq")
    i = pl.program_id(0)
    ups = [
        (tok.at[:, pl.ds(toks - HALO, HALO), :], prev_tok, send_sem.at[0], recv_sem.at[0]),
        (mask, prev_mask, send_sem.at[1], recv_sem.at[1]),
    ]
    downs = [
        (tok.at[:, pl.ds(0, HALO), :], next_tok, send_sem.at[2], recv_sem.at[2]),
        (mask, next_mask, send_sem.at[3], recv_sem.at[3]),
    ]

    @pl.when(i == 0)
    def _():
        greet_line(me, runs)
        swap_along_line(me, runs, ups, downs, True)

        @pl.when(me == 0)
        def _():
            prev_tok[...] = jnp.zeros(prev_tok.shape, BF16)
            prev_mask[...] = jnp.zeros(prev_mask.shape, jnp.int32)

        @pl.when(me == runs - 1)
        def _():
            next_tok[...] = jnp.zeros(next_tok.shape, BF16)
            next_mask[...] = jnp.zeros(next_mask.shape, jnp.int32)

    live = (counts[...] > i).astype(F32)
    steps = step[...].astype(F32)
    here = lax.broadcasted_iota(jnp.int32, steps.shape, 0) == i
    time_f = jnp.sum(jnp.where(here, steps, 0.0), axis=0, keepdims=True)
    time_low = (time_f * jax.nn.sigmoid(time_f)).astype(BF16)
    mod = dot(time_low, ada[...]) + ada_bias[...].reshape(1, 3 * dim)
    mod_out[...] = mod
    shift, scale, gate = mod[:, :dim], mod[:, dim : 2 * dim], mod[:, 2 * dim :]

    def hidden_of(part):
        normed, _ = normalise(part.astype(F32))
        return (normed * (1.0 + scale) + shift).astype(BF16)

    hid = hidden_of(tok[i])
    hid_out[...] = hid
    xz = dot(hid, win[...]) * (as_column(mask[pl.ds(i, 1), :]) * live)
    x_low = xz[:, :inner].astype(BF16)
    z = xz[:, inner:]
    z_out[...] = z
    d_branch = (cot[...].astype(F32) * gate).astype(BF16)
    d_summed = dot_nt(d_branch, wout[...]) * z * jax.nn.sigmoid(z)
    dy[0] = d_summed
    dy[1] = flip_full(d_summed)
    xe[0, HALO:, :] = x_low
    xe[1, HALO:, :] = flip_low(x_low)

    @pl.when(i == 0)
    def _():
        swap_along_line(me, runs, ups, downs, False)

    rims = jnp.concatenate([prev_tok[i], next_tok[i]], axis=0)
    prev_col = as_column(prev_mask[pl.ds(i, 1), :])[toks - HALO :]
    next_col = as_column(next_mask[pl.ds(i, 1), :])[:HALO]
    rim_x = dot(hidden_of(rims), win[:, :inner]) * (jnp.concatenate([prev_col, next_col], axis=0) * live)
    rim_x = rim_x.astype(BF16)
    xe[0, :HALO, :] = rim_x[:HALO]
    xe[1, :HALO, :] = flip_low(rim_x[HALO:])


def twice(row8):
    return jnp.concatenate([row8, row8], axis=0)


def spread(ref, index):
    return twice(ref[pl.ds(index, 8, stride=0), :])


def lay_out(wide, rows, picks):
    count, toks = rows.shape
    high = rows.astype(BF16).astype(F32)
    halves = jnp.concatenate([high, rows - high], axis=0).T.astype(BF16)
    for n in range(0, count, 2):
        pair = dot(halves, picks[:, n * 128 : (n + 2) * 128])
        for t in range(0, toks, 8):
            for k in range(2):
                at = 8 * (count * (t // 8) + n + k)
                wide[at : at + 8, :] = pair[t : t + 8, k * 128 : (k + 1) * 128]


def wide_tile(wide, i, count):
    at = 8 * count * (i // 8) + i % 8
    return jnp.concatenate([wide[pl.ds(at + 64 * n, 8, stride=8), :] for n in range(count // 8)], axis=0)


def across_lanes(tile, inner):
    return jnp.concatenate([tile] * (inner // 128), axis=1)


def softplus_parts(pre):
    e = jnp.exp2(-LOG2E * jnp.abs(pre))
    more = jnp.where(e < 1e-3, e - 0.5 * e * e, jnp.log(1.0 + e))
    return jnp.maximum(pre, 0.0) + more, jax.nn.sigmoid(pre)


def first_kernel(
    xe, dy, taps, tap_bias, x_rows, dt_rows, dt_bias, rate,
    act_out, dsilu_out, delta_out, sig_out, proj_out, end_out, back_out, total_out, starts_out, sums_out, tiles, xwt, dtw,
    dx, decay, through, rate2, wide, picks,
):
    toks, inner = dy.shape
    states = rate.shape[0]
    blocks = toks // BLK
    rank = dtw.shape[0]
    tap_count = taps.shape[0]
    branch = pl.program_id(0)

    @pl.when(pl.program_id(1) == 0)
    def _():
        rate2[...] = rate[...] * -LOG2E
        picks[...] = (
            lax.broadcasted_iota(jnp.int32, picks.shape, 0) % (2 * states)
            == lax.broadcasted_iota(jnp.int32, picks.shape, 1) // 128
        ).astype(BF16)
        held = dt_rows.shape[0]
        rows = x_rows[...].astype(F32)
        gap = jnp.zeros((rank - held, inner), F32)
        xwt[...] = jnp.concatenate([rows[:held], gap, rows[held:]], axis=0).astype(BF16)
        dtw[...] = jnp.concatenate([dt_rows[...].astype(F32), gap], axis=0).astype(BF16)

    shifted = xe[...].astype(F32)
    conv = tap_bias[pl.ds(branch, 1), :] + taps[tap_count - 1 : tap_count, :] * shifted[HALO:]
    for k in reversed(range(tap_count - 1)):
        shifted = pltpu.roll(shifted, 1, 0)
        conv = conv + taps[k : k + 1, :] * shifted[HALO:]
    sig = jax.nn.sigmoid(conv)
    act_f = conv * sig
    act = act_f.astype(BF16)
    dsilu_out[...] = sig + act_f * (1.0 - sig)
    act_out[...] = act
    proj = dot_nt(xwt[...], act)
    proj_out[...] = proj
    pre = dot_tn(proj[:rank, :].astype(BF16), dtw[...]) + dt_bias[pl.ds(branch, 1), :]
    delta, slope = softplus_parts(pre)
    delta_out[...] = delta
    sig_out[...] = slope
    dx[...] = delta * act.astype(F32)
    lay_out(wide, proj[rank:, :], picks)
    end_out[...] = jnp.zeros((states, inner), F32)
    back_out[...] = jnp.zeros((states, inner), F32)
    through[...] = jnp.zeros((8, inner), F32)

    def one_block(j, slot):
        t0 = pl.multiple_of(j * BLK, BLK)
        dr, xr, yr = (ref.at[pl.ds(t0, BLK), :] for ref in (delta_out, dx, dy))
        count = 2 * states
        wide_rows = wide.at[pl.ds(pl.multiple_of(j * (BLK * count), BLK * count), BLK * count), :]
        s = end_out[...]
        starts_out[j] = s
        before = through[...]
        sums_out[j] = before[:1, :]
        rates = rate2[...]
        for i in range(BLK):
            a = jnp.exp2(spread(dr, i) * rates)
            decay[slot, i] = a
            tile = wide_tile(wide_rows, i, count)
            tiles[t0 + i] = tile
            s = a * s + spread(xr, i) * across_lanes(tile[:states], inner)
        end_out[...] = s
        m = jnp.zeros((states, inner), F32)
        for i in reversed(range(BLK)):
            m = decay[slot, i] * (m + spread(yr, i) * across_lanes(tiles[t0 + i, states:], inner))
        back_out[...] = back_out[...] + m * jnp.exp2(twice(before) * rates)
        through[...] = before + jnp.sum(dr[...], axis=0, keepdims=True)

    def block_step(k, _):
        one_block(2 * k, 0)
        one_block(2 * k + 1, 1)
        return 0

    lax.fori_loop(0, blocks // 2, block_step, 0)
    total_out[...] = through[:1, :]


def second_kernel(
    s_in, lam_in, starts, sums, tiles, rate, xe, act, dsilu, delta, sig, dy, proj, xwt, dtw, taps, skip,
    y_out, dx_out, rim_out, rate_grad, skip_grad, dtb_grad, dtp_grad, xp_grad, tap_grad, tapb_grad,
    rate2, carry, dxs, bdiag, cdiag, decay, states_low, lam_low, rq_low, qd_low, dots, racc, gsum, hsum, db, dc,
):
    toks, inner = dy.shape
    states = rate.shape[0]
    blocks = toks // BLK
    rank = dtw.shape[0]
    tap_count = taps.shape[0]
    item = pl.program_id(1)
    gain = skip[pl.ds(pl.program_id(0), 1), :]
    rate2[...] = rate[...] * -LOG2E
    width = BLK * states

    @pl.when(item == 0)
    def _():
        for ref in (rate_grad, skip_grad, dtb_grad, dtp_grad, xp_grad, tap_grad, tapb_grad):
            ref[...] = jnp.zeros(ref.shape, ref.dtype)

    carry[...] = lam_in[...]
    act_low = act[...]
    dxs[:toks, :] = delta[...] * act_low.astype(F32)
    fold = (
        lax.broadcasted_iota(jnp.int32, (states, width), 1) % states == lax.broadcasted_iota(jnp.int32, (states, width), 0)
    ).astype(BF16)
    own = lax.broadcasted_iota(jnp.int32, (toks, width), 0) % BLK == lax.broadcasted_iota(jnp.int32, (toks, width), 1) // states
    bdiag[:toks, :] = jnp.where(own, dot_tn(proj[rank : rank + states, :].astype(BF16), fold), 0.0).astype(BF16)
    cdiag[...] = jnp.where(own, dot_tn(proj[rank + states :, :].astype(BF16), fold), 0.0).astype(BF16)
    mine = own[:BLK]
    picks = mine.astype(BF16)
    sides = (
        lax.broadcasted_iota(jnp.int32, (2 * BLK, 256), 0) // BLK == lax.broadcasted_iota(jnp.int32, (2 * BLK, 256), 1) // 128
    ).astype(BF16)
    racc[...] = jnp.zeros((states, inner), F32)
    qd_low[1] = jnp.zeros(qd_low.shape[1:], BF16)

    def lane_sum(wide):
        part = [wide[:, at : at + 128] for at in range(0, inner, 128)]
        while len(part) > 1:
            part = [sum(part[at : at + 2]) for at in range(0, len(part), 2)]
        return part[0]

    def products(slot, j):
        t0 = pl.multiple_of(j * BLK, BLK)
        gsum[pl.ds(t0, BLK), :] = dot(bdiag[pl.ds(t0, BLK), :], lam_low[slot])
        hsum[pl.ds(t0, BLK), :] = dot(picks, rq_low[slot])
        racc[...] += dot(fold[:, : BLK // 4 * states], qd_low[slot])
        both = dot_nt(sides, dots[slot])
        dc[pl.ds(t0, BLK), :] = jnp.where(mine, both[:BLK], 0.0).astype(BF16)
        db[pl.ds(t0, BLK), :] = jnp.where(mine, both[BLK:], 0.0).astype(BF16)

    def one_block(slot, j):
        t0 = pl.multiple_of(j * BLK, BLK)
        dr, xr, yr = (ref.at[pl.ds(t0, BLK), :] for ref in (delta, dxs, dy))
        tile = tiles.at[pl.ds(t0, BLK)]
        r2 = rate2[...]
        r_low = rate[...].astype(BF16)
        s = starts[j] + s_in[...] * jnp.exp2(twice(jnp.broadcast_to(sums[j], (8, inner))) * r2)
        states_low[slot, :states, :] = s.astype(BF16)
        for i in range(BLK):
            a = jnp.exp2(spread(dr, i) * r2)
            decay[slot, i] = a
            s = a * s + spread(xr, i) * across_lanes(tile[i, :states], inner)
            s_low = s.astype(BF16)
            states_low[slot, (i + 1) * states : (i + 2) * states, :] = s_low
            dots[slot, i * states : (i + 1) * states, :128] = lane_sum(s_low * spread(yr, i).astype(BF16))
        y_out[pl.ds(t0, BLK), :] = dot(cdiag[pl.ds(t0, BLK), :], states_low[slot, states:, :])
        cr = carry[...]
        qds = []
        for i in reversed(range(BLK)):
            lam = cr + spread(yr, i) * across_lanes(tile[i, states:], inner)
            l_low = lam.astype(BF16)
            lam_low[slot, i * states : (i + 1) * states, :] = l_low
            dots[slot, i * states : (i + 1) * states, 128:] = lane_sum(l_low * spread(xr, i).astype(BF16))
            cr = decay[slot, i] * lam
            q = cr.astype(BF16) * states_low[slot, i * states : (i + 1) * states, :]
            rq_low[slot, i * states : (i + 1) * states, :] = q * r_low
            qds.append(q * spread(dr, i).astype(BF16))
            if i % 4 == 0:
                qd_low[slot, i // 4 * states : (i // 4 + 1) * states, :] = (qds[0] + qds[1]) + (qds[2] + qds[3])
                qds = []
        carry[...] = cr

    def block_step(k, _):
        j = blocks - 1 - 2 * k
        products(1, jnp.where(k == 0, blocks, j + 1))
        one_block(0, j)
        products(0, j)
        one_block(1, j - 1)
        return 0

    lax.fori_loop(0, blocks // 2, block_step, 0)
    products(1, 0)

    rate_grad[...] += -racc[...]
    act_f = act_low.astype(F32)
    d_summed = dy[...]
    g = gsum[:toks, :]
    skip_grad[...] += jnp.sum(d_summed * act_f, axis=0, keepdims=True)
    y_out[...] += gain * act_f
    d_pre = (act_f * g - hsum[:toks, :]) * sig[...]
    dtb_grad[...] += jnp.sum(d_pre, axis=0, keepdims=True)
    d_pre_low = d_pre.astype(BF16)
    dtp_grad[...] += dot(proj[:rank, :].astype(BF16), d_pre_low)
    d_proj = jnp.concatenate(
        [dot_nt(dtw[...], d_pre_low), dot_nt(fold, db[:toks, :]), dot_nt(fold, dc[:toks, :])], axis=0
    ).astype(BF16)
    xp_grad[...] += dot(d_proj, act_low)
    d_act = delta[...] * g + gain * d_summed + dot_tn(d_proj, xwt[...])
    d_conv = d_act * dsilu[...]
    tapb_grad[...] += jnp.sum(d_conv, axis=0, keepdims=True)
    x_f = xe[...].astype(F32)
    moved = jnp.concatenate([jnp.zeros((HALO, inner), F32), d_conv], axis=0)
    window = HALO + toks
    d_window = taps[tap_count - 1 : tap_count, :] * moved
    tap_grad[tap_count - 1 : tap_count, :] += jnp.sum(moved * x_f, axis=0, keepdims=True)
    for k in reversed(range(tap_count - 1)):
        moved = pltpu.roll(moved, window - 1, 0)
        tap_grad[k : k + 1, :] += jnp.sum(moved * x_f, axis=0, keepdims=True)
        d_window = d_window + taps[k : k + 1, :] * moved
    rim_out[...] = d_window[HALO - 8 : HALO]
    dx_out[...] = d_window[HALO:]


def third_kernel(
    runs, tok, cot, mod, mask, counts, hid, z_in, y, dx, rims, win, wout,
    mixed, d_tokens, d_mod, out_grad, in_grad,
    late_up, late_down, send_sem, recv_sem,
):
    dim = tok.shape[-1]
    toks, inner = z_in.shape
    me = lax.axis_index("seq")
    i = pl.program_id(0)
    ups = [(rims.at[1], late_up, send_sem.at[0], recv_sem.at[0])]
    downs = [(rims.at[0], late_down, send_sem.at[1], recv_sem.at[1])]

    @pl.when(i == 0)
    def _():
        greet_line(me, runs)
        swap_along_line(me, runs, ups, downs, True)

        @pl.when(me == 0)
        def _():
            late_up[...] = jnp.zeros(late_up.shape, F32)

        @pl.when(me == runs - 1)
        def _():
            late_down[...] = jnp.zeros(late_down.shape, F32)

        out_grad[...] = jnp.zeros(out_grad.shape, F32)
        in_grad[...] = jnp.zeros(in_grad.shape, F32)

    shift, scale, gate = mod[:, :dim], mod[:, dim : 2 * dim], mod[:, 2 * dim :]
    valid = as_column(mask[pl.ds(i, 1), :]) * (counts[...] > i).astype(F32)
    tok_f = tok[...].astype(F32)
    normed, inv_std = normalise(tok_f)
    cot_f = cot[...].astype(F32)
    z = z_in[...]
    z_sig = jax.nn.sigmoid(z)
    summed = y[0] + flip_full(y[1])
    gated = (summed * z * z_sig).astype(BF16)
    branch_out = dot(gated, wout[...])
    mixed[...] = (tok_f + gate * branch_out).astype(BF16)
    d_branch = (cot_f * gate).astype(BF16)
    d_gated = dot_nt(d_branch, wout[...])
    d_zgate = d_gated * summed * z_sig * (1.0 + z * (1.0 - z_sig))
    out_grad[...] += dot_tn(gated, d_branch)

    @pl.when(i == 0)
    def _():
        swap_along_line(me, runs, ups, downs, False)

    edge = late_up.shape[1]

    def with_late(part, extra):
        return jnp.concatenate([part[: toks - edge], part[toks - edge :] + extra], axis=0)

    d_x = with_late(dx[0], late_down[i]) + flip_full(with_late(dx[1], late_up[i]))
    d_xz = (jnp.concatenate([d_x, d_zgate], axis=1) * valid).astype(BF16)
    d_hidden = dot_nt(d_xz, win[...])
    in_grad[...] += dot_tn(hid[...], d_xz)
    d_mod[0:1, :] = jnp.sum(d_hidden, axis=0, keepdims=True)
    d_mod[1:2, :] = jnp.sum(d_hidden * normed, axis=0, keepdims=True)
    d_mod[2:3, :] = jnp.sum(cot_f * branch_out, axis=0, keepdims=True)
    d_normed = d_hidden * (1.0 + scale)
    d_tokens[...] = cot_f + inv_std * (
        d_normed
        - jnp.mean(d_normed, axis=-1, keepdims=True)
        - normed * jnp.mean(d_normed * normed, axis=-1, keepdims=True)
    )


def bit_of(index, bit):
    return (index // (1 << bit)) % 2


def across(axis, bit):
    me = lax.axis_index(axis)
    mine = bit_of(me, bit)
    return mine, {axis: me + (1 - 2 * mine) * (1 << bit)}


def exchange_kernel(runs, end, back, total, rates, s_in, lam_in, group, span, pre, pre_span, sends, arrivals, send_sem, recv_sem):
    slots, _, states, inner = end.shape
    bits = int(math.log2(runs))
    links = [across("seq", bit) for bit in range(bits)]
    greet([target for _, target in links])
    flows = (((end, 0), (back, 1)), ((end, 1), (back, 0)))
    units = 2 * slots
    rows = units * states
    pre[...] = jnp.zeros(pre.shape, F32)
    pre_span[...] = jnp.zeros(pre_span.shape, F32)
    span[...] = jnp.zeros(span.shape, F32)
    for flow in range(2):
        for kind, (array, branch) in enumerate(flows[flow]):
            for i in range(slots):
                unit = kind * slots + i
                group[flow, unit] = array[i, branch]
                span[flow, unit : unit + 1, :] = total[i, branch]

    def load(flow, slot):
        for unit in range(units):
            sends[slot, unit * states : (unit + 1) * states, :] = group[flow, unit].astype(BF16)
        high = span[flow].astype(BF16).astype(F32)
        sends[slot, rows:, :] = jnp.concatenate([high, span[flow] - high], axis=0).astype(BF16)

    def join(flow, slot, earlier, last):
        both = arrivals[slot, rows:, :].astype(F32)
        length = both[: both.shape[0] // 2] + both[both.shape[0] // 2 :]
        own_span = span[flow]
        mine_span = pre_span[flow]
        second_span = jnp.where(earlier, own_span, length)
        for unit in range(units):
            rate = rates[flows[flow][unit // slots][1]] * -LOG2E
            state = arrivals[slot, unit * states : (unit + 1) * states, :].astype(F32)
            mine = pre[flow, unit]
            joined = state * jnp.exp2(rate * mine_span[unit : unit + 1]) + mine
            pre[flow, unit] = jnp.where(earlier, joined, mine)
            if not last:
                own = group[flow, unit]
                first = jnp.where(earlier, state, own)
                second = jnp.where(earlier, own, state)
                group[flow, unit] = first * jnp.exp2(rate * second_span[unit : unit + 1]) + second
        pre_span[flow] = jnp.where(earlier, length + mine_span, mine_span)
        if not last:
            span[flow] = own_span + length

    for stage, (mine, target) in enumerate(links):
        last = stage == bits - 1
        if last:
            slot = 2 * stage

            @pl.when(mine == 0)
            def _():
                load(0, slot)

            @pl.when(mine == 1)
            def _():
                load(1, slot)

            copies = [remote(sends.at[slot], arrivals.at[slot], send_sem.at[slot], recv_sem.at[slot], target)]
        else:
            copies = []
            for flow in range(2):
                slot = 2 * stage + flow
                load(flow, slot)
                copies.append(
                    remote(sends.at[slot], arrivals.at[slot], send_sem.at[slot], recv_sem.at[slot], target)
                )
        for copy in copies:
            copy.start()
        for copy in copies:
            copy.wait()
        if last:

            @pl.when(mine == 1)
            def _():
                join(0, 2 * stage, True, True)

            @pl.when(mine == 0)
            def _():
                join(1, 2 * stage, True, True)
        else:
            join(0, 2 * stage, mine == 1, False)
            join(1, 2 * stage + 1, mine == 0, False)
    for flow in range(2):
        for kind, (_, branch) in enumerate(flows[flow]):
            result = (s_in, lam_in)[kind]
            for i in range(slots):
                result[i, branch] = pre[flow, kind * slots + i]


PARTS = 6
LAST_ROWS = 16


def reduce_rows(dim, inner, small):
    rows = inner + (2 * dim + small) * (inner // dim)
    unit = PARTS * LAST_ROWS * 32
    return -(-rows // unit) * unit


def reduce_kernel(
    plan, in_grad, out_grad, xp_grad, dtp_grad, rate_grad, tap_grad, tapb_grad, skip_grad, dtb_grad, d_mod, step,
    result, factors, own_rows,
    acc, sends, arrivals, gathered, mod_sum, mod_in, table, send_sem, recv_sem, small_send, small_recv,
):
    runs, groups, total_rows = plan
    dim = in_grad.shape[0]
    inner = out_grad.shape[0]
    slots = step.shape[0]
    seq_bits = [("seq", bit) for bit in range(int(math.log2(runs)))]
    dp_bits = [("dp", bit) for bit in range(int(math.log2(groups)))]
    all_bits = seq_bits + dp_bits
    count = len(all_bits)
    links = {key: across(*key) for key in all_bits}
    middle = all_bits[1:-1]
    turn = [part % max(len(middle), 1) for part in range(PARTS)]
    orders = [all_bits[:1] + middle[at:] + middle[:at] + all_bits[1:][-1:] for at in turn]
    part_rows = total_rows // PARTS

    def small_copy(stage):
        axis, bit = all_bits[stage]
        target = links[(axis, bit)][1]
        if axis == "seq":
            return remote(mod_sum, mod_in.at[stage], small_send.at[stage], small_recv.at[stage], target)
        size = 16 << bit
        at = pl.multiple_of(lax.axis_index("dp") // (1 << bit) * size, 16)
        here = table.at[pl.ds(at, size), :]
        return remote(here, here, small_send.at[stage], small_recv.at[stage], target)

    def fill_table():
        time_f = step[...].astype(F32)
        time_low = time_f * jax.nn.sigmoid(time_f)
        at = pl.multiple_of(lax.axis_index("dp") * 16, 16)
        own = jnp.concatenate([mod_sum[: 3 * slots, :], time_low, mod_sum[4 * slots :, :]], axis=0)
        own_rows[...] = own.astype(BF16)
        table[pl.ds(at, 16), :] = own.astype(BF16)

    def start_small(stage):
        if stage == len(seq_bits):
            fill_table()
        if stage < count:
            small_copy(stage).start()

    def end_small(stage):
        small_copy(stage).wait()
        if all_bits[stage][0] == "seq":
            mod_sum[...] += mod_in[stage]

    segments = [(lambda at, size: out_grad[at : at + size, :], inner)]
    for lane in range(0, 2 * inner, dim):
        segments.append((lambda at, size, lane=lane: in_grad[at : at + size, lane : lane + dim], dim))
    small = []
    for ref in (xp_grad, dtp_grad, rate_grad, tap_grad):
        small += [(lambda ref=ref, branch=branch: ref[branch], ref.shape[1]) for branch in range(2)]

    def tail():
        rows = [ref[branch] for ref in (tapb_grad, skip_grad, dtb_grad) for branch in range(2)]
        return jnp.concatenate(rows + [jnp.zeros((2, inner), F32)], axis=0)

    small.append((tail, 8))
    for lane in range(0, inner, dim):
        for get, size in small:
            segments.append((lambda at, size, get=get, lane=lane: get()[at : at + size, lane : lane + dim], size))
    total = sum(size for _, size in segments)
    segments.append((lambda at, size: jnp.zeros((size, dim), F32), total_rows - total))

    def assemble(part):
        low, high = part * part_rows, (part + 1) * part_rows
        at = 0
        for get, size in segments:
            first, last = max(at, low), min(at + size, high)
            if first < last:
                acc[first:last, :] = get(first - at, last - first)
            at += size

    starts = [part * part_rows for part in range(PARTS)]
    sizes = [part_rows] * PARTS
    history = [[] for _ in range(PARTS)]
    offsets = [part * (part_rows + LAST_ROWS * count) for part in range(PARTS)]
    flying = [None] * PARTS

    def scatter(part, stage):
        mine, target = links[orders[part][stage]]
        start, size = starts[part], sizes[part]
        split = size >= 2 * LAST_ROWS
        moved = size // 2 if split else size
        away = keep = start
        if split:
            away = pl.multiple_of(start + (1 - mine) * moved, LAST_ROWS)
            keep = pl.multiple_of(start + mine * moved, LAST_ROWS)
        history[part].append((start, size, split))
        at = offsets[part]
        offsets[part] += moved
        sends[at : at + moved, :] = acc[pl.ds(away, moved), :].astype(BF16)
        copy = remote(
            sends.at[pl.ds(at, moved), :], arrivals.at[pl.ds(at, moved), :], send_sem.at[part, stage],
            recv_sem.at[part, stage], target,
        )
        copy.start()
        starts[part], sizes[part] = keep, moved
        flying[part] = (copy, keep, moved, at, split)

    def settle(part):
        copy, keep, moved, at, split = flying[part]
        copy.wait()
        held = acc[pl.ds(keep, moved), :]
        if not split:
            held = held.astype(BF16).astype(F32)
        acc[pl.ds(keep, moved), :] = held + arrivals[at : at + moved, :].astype(F32)

    def gather(part, stage):
        start, size, split = history[part][stage]
        flying[part] = None
        if split:
            here = gathered.at[pl.ds(starts[part], sizes[part]), :]
            target = links[orders[part][stage]][1]
            flying[part] = remote(
                here, here, send_sem.at[part, count + stage], recv_sem.at[part, count + stage], target
            )
            flying[part].start()
            starts[part], sizes[part] = start, size

    mod_sum[...] = jnp.zeros(mod_sum.shape, F32)
    for i in range(slots):
        mod_sum[3 * i : 3 * i + 3, :] = d_mod[i]
    greet([links[key][1] for key in all_bits])
    start_small(0)
    for part in range(PARTS):
        assemble(part)
        scatter(part, 0)
    for stage in range(1, count):
        end_small(stage - 1)
        start_small(stage)
        for part in range(PARTS):
            settle(part)
            scatter(part, stage)
    end_small(count - 1)
    if not dp_bits:
        fill_table()
    for part in range(PARTS):
        settle(part)
        where = pl.ds(starts[part], sizes[part])
        gathered[where, :] = acc[where, :].astype(BF16)
        gather(part, count - 1)
    for stage in reversed(range(count - 1)):
        for part in range(PARTS):
            if flying[part] is not None:
                flying[part].wait()
            gather(part, stage)
    for part in range(PARTS):
        if flying[part] is not None:
            flying[part].wait()
        result[part * part_rows : (part + 1) * part_rows, :] = gathered[part * part_rows : (part + 1) * part_rows, :]
    factors[...] = table[...]


def finish_kernel(
    ranks, result, factors, own, step, ada,
    grad_time, grad_ada, grad_ada_bias, in_grad, tap_grad, tapb_grad, xp_grad, dtp_grad, dtb_grad, rate_grad, skip_grad, out_grad,
):
    rank, wide_rank = ranks
    dim = in_grad.shape[0]
    inner = out_grad.shape[0]
    slots = step.shape[0]
    states = rate_grad.shape[1]
    taps = tap_grad.shape[1]

    def rows(at, size):
        return result[at : at + size, :].astype(F32)

    out_grad[...] = rows(0, inner)
    at = inner
    for lane in range(0, 2 * inner, dim):
        in_grad[:, lane : lane + dim] = rows(at, dim)
        at += dim
    wide = wide_rank + 2 * states
    for first in range(0, inner, dim):
        lanes = slice(first, first + dim)
        for branch in range(2):
            part = rows(at, wide)
            xp_grad[branch, :, lanes] = jnp.concatenate([part[:rank], part[wide_rank:]], axis=0)
            at += wide
        for branch in range(2):
            dtp_grad[branch, :, lanes] = rows(at, wide_rank)[:rank]
            at += wide_rank
        for branch in range(2):
            rate_grad[branch, :, lanes] = rows(at, states)
            at += states
        tail = rows(at, 16)
        for branch in range(2):
            tap_grad[branch, :, lanes] = tail[branch * taps : (branch + 1) * taps]
        tapb_grad[:, lanes] = tail[2 * taps : 2 * taps + 2]
        skip_grad[:, lanes] = tail[2 * taps + 2 : 2 * taps + 4]
        dtb_grad[:, lanes] = tail[2 * taps + 4 : 2 * taps + 6]
        at += 16

    table = factors[...]
    length = table.shape[0]
    groups = length // 16
    items = groups * 8

    def pick(place):
        row = lax.broadcasted_iota(jnp.int32, (items, length), 0)
        col = lax.broadcasted_iota(jnp.int32, (items, length), 1)
        slot = row % 8
        wanted = row // 8 * 16 + place(slot)
        return dot(((col == wanted) & (slot < slots)).astype(BF16), table)

    times = pick(lambda slot: 3 * slots + slot).astype(BF16)
    time_f = step[...].astype(F32)
    time_sig = jax.nn.sigmoid(time_f)
    d_time = jnp.zeros((slots, dim), F32)
    mine = own[...].astype(F32)
    for part in range(3):
        mods = pick(lambda slot: 3 * slot + part)
        lanes = slice(part * dim, (part + 1) * dim)
        grad_ada[:, lanes] = dot_tn(times, mods.astype(BF16))
        grad_ada_bias[lanes] = jnp.sum(mods, axis=0)
        picked = jnp.concatenate([mine[3 * i + part : 3 * i + part + 1] for i in range(slots)], axis=0)
        d_time = d_time + dot_nt(picked.astype(BF16), ada[:, lanes])
    grad_time[...] = d_time * time_sig * (1.0 + time_f * (1.0 - time_sig))


def params(**more):
    return pltpu.CompilerParams(vmem_limit_bytes=VMEM_LIMIT, **more)


def spec(block, index):
    return pl.BlockSpec(block, index)


def per_device(
    tokens, timestep, counts, token_mask, ada_weight, ada_bias, input_weight, conv_weight, conv_bias, x_weight, dt_weight,
    dt_bias, decay_rate, skip_gain, output_weight, cotangent,
):
    slots, toks, dim = tokens.shape
    inner = output_weight.shape[0]
    rank = dt_weight.shape[1]
    states = decay_rate.shape[1]
    tap_count = conv_weight.shape[1]
    wide_rank = 32
    proj_rows = wide_rank + 2 * states
    blocks = toks // BLK
    runs = lax.axis_size("seq")
    groups = lax.axis_size("dp")
    counts2 = counts[:, None]
    x_rows = jnp.swapaxes(x_weight, 1, 2)

    def item(*block):
        return spec((None,) + block, lambda i: (i,) + (0,) * len(block))

    def whole(*block):
        return spec(block, lambda *_: (0,) * len(block))

    xe, dy, z_gate, hid, modulate = pl.pallas_call(
        functools.partial(enter_kernel, runs),
        grid=(slots,),
        in_specs=[
            whole(slots, toks, dim), item(toks, dim), whole(slots, toks), whole(1, 1), whole(slots, dim), whole(dim, 3 * dim),
            whole(3 * dim), whole(dim, 2 * inner), whole(inner, dim),
        ],
        out_specs=[
            item(2, HALO + toks, inner), item(2, toks, inner), item(toks, inner), item(toks, dim), item(1, 3 * dim),
        ],
        out_shape=[
            jax.ShapeDtypeStruct((slots, 2, HALO + toks, inner), BF16),
            jax.ShapeDtypeStruct((slots, 2, toks, inner), F32),
            jax.ShapeDtypeStruct((slots, toks, inner), F32),
            jax.ShapeDtypeStruct((slots, toks, dim), BF16),
            jax.ShapeDtypeStruct((slots, 1, 3 * dim), F32),
        ],
        scratch_shapes=[
            pltpu.VMEM((slots, HALO, dim), BF16), pltpu.VMEM((slots, HALO, dim), BF16), pltpu.VMEM((slots, toks), jnp.int32),
            pltpu.VMEM((slots, toks), jnp.int32), pltpu.SemaphoreType.DMA((4,)), pltpu.SemaphoreType.DMA((4,)),
        ],
        compiler_params=params(collective_id=1, has_side_effects=True),
        name="enter",
    )(
        tokens, cotangent, token_mask, counts2, timestep, ada_weight, ada_bias, input_weight, output_weight,
    )

    def unit(*block):
        return spec((None, None) + block, lambda b, i: (i, b) + (0,) * len(block))

    def branch(*block):
        return spec((None,) + block, lambda b, i: (b,) + (0,) * len(block))

    def unit_shape(*block, kind=F32):
        return jax.ShapeDtypeStruct((slots, 2) + block, kind)

    act, dsilu, delta, sig, proj, end, back, total, starts, sums, tiles, xwt, dtw = pl.pallas_call(
        first_kernel,
        grid=(2, slots),
        in_specs=[
            unit(HALO + toks, inner), unit(toks, inner), branch(tap_count, inner), whole(2, inner),
            branch(rank + 2 * states, inner), branch(rank, inner), whole(2, inner), branch(states, inner),
        ],
        out_specs=[
            unit(toks, inner), unit(toks, inner), unit(toks, inner), unit(toks, inner), unit(proj_rows, toks),
            unit(states, inner), unit(states, inner), unit(1, inner), unit(blocks, states, inner), unit(blocks, 1, inner),
            unit(toks, 2 * states, 128), branch(proj_rows, inner), branch(wide_rank, inner),
        ],
        out_shape=[
            unit_shape(toks, inner, kind=BF16), unit_shape(toks, inner), unit_shape(toks, inner), unit_shape(toks, inner),
            unit_shape(proj_rows, toks), unit_shape(states, inner), unit_shape(states, inner), unit_shape(1, inner),
            unit_shape(blocks, states, inner), unit_shape(blocks, 1, inner), unit_shape(toks, 2 * states, 128),
            jax.ShapeDtypeStruct((2, proj_rows, inner), BF16), jax.ShapeDtypeStruct((2, wide_rank, inner), BF16),
        ],
        scratch_shapes=[
            pltpu.VMEM((toks, inner), F32), pltpu.VMEM((2, BLK, states, inner), F32), pltpu.VMEM((8, inner), F32),
            pltpu.VMEM((states, inner), F32), pltpu.VMEM((2 * states * toks, 128), F32),
            pltpu.VMEM((4 * states, 2 * states * 128), BF16),
        ],
        compiler_params=params(),
        name="first",
    )(xe, dy, conv_weight, conv_bias, x_rows, dt_weight, dt_bias, decay_rate)

    pairs = int(math.log2(runs))
    units = 2 * slots
    span_rows = -(-units // 8) * 8
    vmem = pl.BlockSpec(memory_space=pltpu.VMEM)
    s_in, lam_in = pl.pallas_call(
        functools.partial(exchange_kernel, runs),
        in_specs=[vmem] * 4,
        out_specs=[vmem] * 2,
        out_shape=[unit_shape(states, inner), unit_shape(states, inner)],
        scratch_shapes=[
            pltpu.VMEM((2, units, states, inner), F32), pltpu.VMEM((2, span_rows, inner), F32),
            pltpu.VMEM((2, units, states, inner), F32), pltpu.VMEM((2, span_rows, inner), F32),
            pltpu.VMEM((2 * pairs, units * states + 2 * span_rows, inner), BF16),
            pltpu.VMEM((2 * pairs, units * states + 2 * span_rows, inner), BF16),
            pltpu.SemaphoreType.DMA((2 * pairs,)), pltpu.SemaphoreType.DMA((2 * pairs,)),
        ],
        compiler_params=params(collective_id=2, has_side_effects=True),
        name="exchange",
    )(end, back, total, decay_rate)

    rim_spec = spec((None, None, 8, inner), lambda b, i: (b, i, 0, 0))
    y, dx, rims, rate_grad, skip_grad, dtb_grad, dtp_grad, xp_grad, tap_grad, tapb_grad = pl.pallas_call(
        second_kernel,
        grid=(2, slots),
        in_specs=[
            unit(states, inner), unit(states, inner), unit(blocks, states, inner),
            unit(blocks, 1, inner), unit(toks, 2 * states, 128), branch(states, inner), unit(HALO + toks, inner), unit(toks, inner),
            unit(toks, inner), unit(toks, inner), unit(toks, inner), unit(toks, inner), unit(proj_rows, toks),
            branch(proj_rows, inner), branch(wide_rank, inner),
            branch(tap_count, inner), whole(2, inner),
        ],
        out_specs=[
            unit(toks, inner), unit(toks, inner), rim_spec, branch(states, inner), branch(1, inner), branch(1, inner),
            branch(wide_rank, inner), branch(proj_rows, inner), branch(tap_count, inner), branch(1, inner),
        ],
        out_shape=[
            unit_shape(toks, inner), unit_shape(toks, inner), jax.ShapeDtypeStruct((2, slots, 8, inner), F32),
        ] + [
            jax.ShapeDtypeStruct((2, rows, inner), F32) for rows in (states, 1, 1, wide_rank, proj_rows, tap_count, 1)
        ],
        scratch_shapes=[
            pltpu.VMEM((states, inner), F32), pltpu.VMEM((states, inner), F32), pltpu.VMEM((toks + BLK, inner), F32), pltpu.VMEM((toks + BLK, BLK * states), BF16),
            pltpu.VMEM((toks, BLK * states), BF16),
            pltpu.VMEM((2, BLK, states, inner), F32),
            pltpu.VMEM((2, (BLK + 1) * states, inner), BF16), pltpu.VMEM((2, BLK * states, inner), BF16),
            pltpu.VMEM((2, BLK * states, inner), BF16), pltpu.VMEM((2, BLK // 4 * states, inner), BF16),
            pltpu.VMEM((2, BLK * states, 256), BF16), pltpu.VMEM((states, inner), F32),
            pltpu.VMEM((toks + BLK, inner), F32), pltpu.VMEM((toks + BLK, inner), F32),
            pltpu.VMEM((toks + BLK, BLK * states), BF16), pltpu.VMEM((toks + BLK, BLK * states), BF16),
        ],
        compiler_params=params(),
        name="second",
    )(
        s_in, lam_in, starts, sums, tiles, decay_rate, xe, act, dsilu, delta,
        sig, dy, proj, xwt, dtw, conv_weight, skip_gain,
    )

    mixed, d_tokens, d_mod, out_grad, in_grad = pl.pallas_call(
        functools.partial(third_kernel, runs),
        grid=(slots,),
        in_specs=[
            item(toks, dim), item(toks, dim), item(1, 3 * dim), whole(slots, toks), whole(1, 1), item(toks, dim),
            item(toks, inner), item(2, toks, inner), item(2, toks, inner), whole(2, slots, 8, inner), whole(dim, 2 * inner),
            whole(inner, dim),
        ],
        out_specs=[item(toks, dim), item(toks, dim), item(3, dim), whole(inner, dim), whole(dim, 2 * inner)],
        out_shape=[
            jax.ShapeDtypeStruct((slots, toks, dim), BF16), jax.ShapeDtypeStruct((slots, toks, dim), F32),
            jax.ShapeDtypeStruct((slots, 3, dim), F32), jax.ShapeDtypeStruct((inner, dim), F32),
            jax.ShapeDtypeStruct((dim, 2 * inner), F32),
        ],
        scratch_shapes=[
            pltpu.VMEM((slots, 8, inner), F32), pltpu.VMEM((slots, 8, inner), F32), pltpu.SemaphoreType.DMA((2,)),
            pltpu.SemaphoreType.DMA((2,)),
        ],
        compiler_params=params(collective_id=3, has_side_effects=True),
        name="third",
    )(
        tokens, cotangent, modulate, token_mask, counts2, hid, z_gate, y, dx, rims, input_weight, output_weight,
    )

    small = 2 * (proj_rows + wide_rank + states + tap_count) + 8
    rows = reduce_rows(dim, inner, small)
    stages = int(math.log2(runs)) + int(math.log2(groups))
    result, factors, own = pl.pallas_call(
        functools.partial(reduce_kernel, (runs, groups, rows)),
        in_specs=[vmem] * 11,
        out_specs=[vmem] * 3,
        out_shape=[
            jax.ShapeDtypeStruct((rows, dim), BF16), jax.ShapeDtypeStruct((16 * groups, dim), BF16),
            jax.ShapeDtypeStruct((16, dim), BF16),
        ],
        scratch_shapes=[
            pltpu.VMEM((rows, dim), F32), pltpu.VMEM((rows + PARTS * LAST_ROWS * stages, dim), BF16),
            pltpu.VMEM((rows + PARTS * LAST_ROWS * stages, dim), BF16),
            pltpu.VMEM((rows, dim), BF16), pltpu.VMEM((16, dim), F32),
            pltpu.VMEM((max(int(math.log2(runs)), 1), 16, dim), F32), pltpu.VMEM((16 * groups, dim), BF16),
            pltpu.SemaphoreType.DMA((PARTS, 2 * stages)), pltpu.SemaphoreType.DMA((PARTS, 2 * stages)),
            pltpu.SemaphoreType.DMA((stages,)), pltpu.SemaphoreType.DMA((stages,)),
        ],
        compiler_params=params(collective_id=4, has_side_effects=True),
        name="reduce",
    )(
        in_grad, out_grad, xp_grad, dtp_grad, rate_grad, tap_grad, tapb_grad, skip_grad, dtb_grad, d_mod, timestep,
    )

    (
        d_time, grad_ada, grad_ada_bias, in_grad, tap_grad, tapb_grad, xp_grad, dtp_grad, dtb_grad, rate_grad, skip_grad,
        out_grad,
    ) = pl.pallas_call(
        functools.partial(finish_kernel, (rank, wide_rank)),
        in_specs=[vmem] * 5,
        out_specs=[vmem] * 12,
        out_shape=[
            jax.ShapeDtypeStruct(shape, F32)
            for shape in (
                (slots, dim), (dim, 3 * dim), (3 * dim,), (dim, 2 * inner), (2, tap_count, inner), (2, inner),
                (2, rank + 2 * states, inner), (2, rank, inner), (2, inner), (2, states, inner), (2, inner), (inner, dim),
            )
        ],
        compiler_params=params(),
        name="finish",
    )(result, factors, own, timestep, ada_weight)
    return (
        mixed, d_tokens, d_time, grad_ada, grad_ada_bias, in_grad, tap_grad, tapb_grad, jnp.swapaxes(xp_grad, 1, 2), dtp_grad, dtb_grad,
        rate_grad, skip_grad, out_grad,
    )


def solution(mesh):
    runs = P("dp", "seq", None)
    return jax.shard_map(
        per_device,
        mesh=mesh,
        in_specs=(runs, P("dp", None), P("dp"), P("dp", "seq")) + (P(),) * 11 + (runs,),
        out_specs=(runs, runs, P("dp", None)) + (P(),) * 11,
        check_vma=False,
    )
```

```python
import functools
import math

import jax
import jax.numpy as jnp
from jax import lax
from jax.experimental import pallas as pl
from jax.experimental.pallas import tpu as pltpu
from jax.sharding import PartitionSpec as P

EPSILON = 1e-06
BLK = 16
HALO = 16
LOG2E = math.log2(math.e)
F32, BF16 = jnp.float32, jnp.bfloat16
NT = (((1,), (1,)), ((), ()))
TN = (((0,), (0,)), ((), ()))
VMEM_LIMIT = 60 << 20
MESH = pl.DeviceIdType.MESH


def dot(a, b):
    return jnp.dot(a, b, preferred_element_type=F32)


def dot_nt(a, b):
    return lax.dot_general(a, b, NT, preferred_element_type=F32)


def dot_tn(a, b):
    return lax.dot_general(a, b, TN, preferred_element_type=F32)


def reversal(size):
    rows = lax.broadcasted_iota(jnp.int32, (size, size), 0)
    cols = lax.broadcasted_iota(jnp.int32, (size, size), 1)
    return (rows + cols == size - 1).astype(BF16)


def flip_low(value):
    return dot(reversal(value.shape[0]), value).astype(BF16)


def flip_full(value):
    order = reversal(value.shape[0])
    high = value.astype(BF16)
    return dot(order, high) + dot(order, (value - high.astype(F32)).astype(BF16))


def normalise(tokens_f):
    centered = tokens_f - jnp.mean(tokens_f, axis=-1, keepdims=True)
    inv_std = lax.rsqrt(jnp.mean(centered * centered, axis=-1, keepdims=True) + EPSILON)
    return centered * inv_std, inv_std


def eye(size):
    rows = lax.broadcasted_iota(jnp.int32, (size, size), 0)
    cols = lax.broadcasted_iota(jnp.int32, (size, size), 1)
    return (rows == cols).astype(BF16)


def as_column(row):
    return dot_nt(eye(row.shape[1]), jnp.broadcast_to(row.astype(F32).astype(BF16), (8, row.shape[1])))[:, :1]


def remote(src, dst, send_sem, recv_sem, target):
    return pltpu.make_async_remote_copy(
        src_ref=src, dst_ref=dst, send_sem=send_sem, recv_sem=recv_sem, device_id=target, device_id_type=MESH
    )


def greet(targets):
    barrier = pltpu.get_barrier_semaphore()
    for target in targets:
        pl.semaphore_signal(barrier, inc=1, device_id=target, device_id_type=MESH)
    pl.semaphore_wait(barrier, len(targets))


def greet_line(me, runs):
    barrier = pltpu.get_barrier_semaphore()

    @pl.when(me > 0)
    def _():
        pl.semaphore_signal(barrier, inc=1, device_id={"seq": me - 1}, device_id_type=MESH)

    @pl.when(me < runs - 1)
    def _():
        pl.semaphore_signal(barrier, inc=1, device_id={"seq": me + 1}, device_id_type=MESH)

    neighbours = (me + runs - 1) // runs + (2 * runs - 2 - me) // runs
    pl.semaphore_wait(barrier, neighbours)


def swap_along_line(me, runs, ups, downs, start):
    up = [remote(src, dst, ss, rs, {"seq": me + 1}) for src, dst, ss, rs in ups]
    down = [remote(src, dst, ss, rs, {"seq": me - 1}) for src, dst, ss, rs in downs]

    @pl.when(me < runs - 1)
    def _():
        for copy in up:
            if start:
                copy.start()
            else:
                copy.wait_send()
        if not start:
            for copy in down:
                copy.wait_recv()

    @pl.when(me > 0)
    def _():
        for copy in down:
            if start:
                copy.start()
            else:
                copy.wait_send()
        if not start:
            for copy in up:
                copy.wait_recv()


def enter_kernel(
    runs, tok, cot, mask, counts, step, ada, ada_bias, win, wout,
    xe, dy, z_out, hid_out, mod_out,
    prev_tok, next_tok, prev_mask, next_mask, send_sem, recv_sem,
):
    slots, toks, dim = tok.shape
    inner = wout.shape[0]
    me = lax.axis_index("seq")
    i = pl.program_id(0)
    ups = [
        (tok.at[:, pl.ds(toks - HALO, HALO), :], prev_tok, send_sem.at[0], recv_sem.at[0]),
        (mask, prev_mask, send_sem.at[1], recv_sem.at[1]),
    ]
    downs = [
        (tok.at[:, pl.ds(0, HALO), :], next_tok, send_sem.at[2], recv_sem.at[2]),
        (mask, next_mask, send_sem.at[3], recv_sem.at[3]),
    ]

    @pl.when(i == 0)
    def _():
        greet_line(me, runs)
        swap_along_line(me, runs, ups, downs, True)

        @pl.when(me == 0)
        def _():
            prev_tok[...] = jnp.zeros(prev_tok.shape, BF16)
            prev_mask[...] = jnp.zeros(prev_mask.shape, jnp.int32)

        @pl.when(me == runs - 1)
        def _():
            next_tok[...] = jnp.zeros(next_tok.shape, BF16)
            next_mask[...] = jnp.zeros(next_mask.shape, jnp.int32)

    live = (counts[...] > i).astype(F32)
    steps = step[...].astype(F32)
    here = lax.broadcasted_iota(jnp.int32, steps.shape, 0) == i
    time_f = jnp.sum(jnp.where(here, steps, 0.0), axis=0, keepdims=True)
    time_low = (time_f * jax.nn.sigmoid(time_f)).astype(BF16)
    mod = dot(time_low, ada[...]) + ada_bias[...].reshape(1, 3 * dim)
    mod_out[...] = mod
    shift, scale, gate = mod[:, :dim], mod[:, dim : 2 * dim], mod[:, 2 * dim :]

    def hidden_of(part):
        normed, _ = normalise(part.astype(F32))
        return (normed * (1.0 + scale) + shift).astype(BF16)

    hid = hidden_of(tok[i])
    hid_out[...] = hid
    xz = dot(hid, win[...]) * (as_column(mask[pl.ds(i, 1), :]) * live)
    x_low = xz[:, :inner].astype(BF16)
    z = xz[:, inner:]
    z_out[...] = z
    d_branch = (cot[...].astype(F32) * gate).astype(BF16)
    d_summed = dot_nt(d_branch, wout[...]) * z * jax.nn.sigmoid(z)
    dy[0] = d_summed
    dy[1] = flip_full(d_summed)
    xe[0, HALO:, :] = x_low
    xe[1, HALO:, :] = flip_low(x_low)

    @pl.when(i == 0)
    def _():
        swap_along_line(me, runs, ups, downs, False)

    rims = jnp.concatenate([prev_tok[i], next_tok[i]], axis=0)
    prev_col = as_column(prev_mask[pl.ds(i, 1), :])[toks - HALO :]
    next_col = as_column(next_mask[pl.ds(i, 1), :])[:HALO]
    rim_x = dot(hidden_of(rims), win[:, :inner]) * (jnp.concatenate([prev_col, next_col], axis=0) * live)
    rim_x = rim_x.astype(BF16)
    xe[0, :HALO, :] = rim_x[:HALO]
    xe[1, :HALO, :] = flip_low(rim_x[HALO:])


def twice(row8):
    return jnp.concatenate([row8, row8], axis=0)


def spread(ref, index):
    return twice(ref[pl.ds(index, 8, stride=0), :])


def lay_out(wide, rows, picks):
    count, toks = rows.shape
    high = rows.astype(BF16).astype(F32)
    halves = jnp.concatenate([high, rows - high], axis=0).T.astype(BF16)
    for n in range(0, count, 2):
        pair = dot(halves, picks[:, n * 128 : (n + 2) * 128])
        for t in range(0, toks, 8):
            for k in range(2):
                at = 8 * (count * (t // 8) + n + k)
                wide[at : at + 8, :] = pair[t : t + 8, k * 128 : (k + 1) * 128]


def wide_tile(wide, i, count):
    at = 8 * count * (i // 8) + i % 8
    return jnp.concatenate([wide[pl.ds(at + 64 * n, 8, stride=8), :] for n in range(count // 8)], axis=0)


def across_lanes(tile, inner):
    return jnp.concatenate([tile] * (inner // 128), axis=1)


def softplus_parts(pre):
    e = jnp.exp2(-LOG2E * jnp.abs(pre))
    more = jnp.where(e < 1e-3, e - 0.5 * e * e, jnp.log(1.0 + e))
    return jnp.maximum(pre, 0.0) + more, jax.nn.sigmoid(pre)


def first_kernel(
    xe, dy, taps, tap_bias, x_rows, dt_rows, dt_bias, rate,
    act_out, dsilu_out, delta_out, sig_out, proj_out, end_out, back_out, total_out, starts_out, sums_out, tiles, xwt, dtw,
    dx, decay, through, rate2, wide, picks,
):
    toks, inner = dy.shape
    states = rate.shape[0]
    blocks = toks // BLK
    rank = dtw.shape[0]
    tap_count = taps.shape[0]
    branch = pl.program_id(0)

    @pl.when(pl.program_id(1) == 0)
    def _():
        rate2[...] = rate[...] * -LOG2E
        picks[...] = (
            lax.broadcasted_iota(jnp.int32, picks.shape, 0) % (2 * states)
            == lax.broadcasted_iota(jnp.int32, picks.shape, 1) // 128
        ).astype(BF16)
        held = dt_rows.shape[0]
        rows = x_rows[...].astype(F32)
        gap = jnp.zeros((rank - held, inner), F32)
        xwt[...] = jnp.concatenate([rows[:held], gap, rows[held:]], axis=0).astype(BF16)
        dtw[...] = jnp.concatenate([dt_rows[...].astype(F32), gap], axis=0).astype(BF16)

    shifted = xe[...].astype(F32)
    conv = tap_bias[pl.ds(branch, 1), :] + taps[tap_count - 1 : tap_count, :] * shifted[HALO:]
    for k in reversed(range(tap_count - 1)):
        shifted = pltpu.roll(shifted, 1, 0)
        conv = conv + taps[k : k + 1, :] * shifted[HALO:]
    sig = jax.nn.sigmoid(conv)
    act_f = conv * sig
    act = act_f.astype(BF16)
    dsilu_out[...] = sig + act_f * (1.0 - sig)
    act_out[...] = act
    proj = dot_nt(xwt[...], act)
    proj_out[...] = proj
    pre = dot_tn(proj[:rank, :].astype(BF16), dtw[...]) + dt_bias[pl.ds(branch, 1), :]
    delta, slope = softplus_parts(pre)
    delta_out[...] = delta
    sig_out[...] = slope
    dx[...] = delta * act.astype(F32)
    lay_out(wide, proj[rank:, :], picks)
    end_out[...] = jnp.zeros((states, inner), F32)
    back_out[...] = jnp.zeros((states, inner), F32)
    through[...] = jnp.zeros((8, inner), F32)

    def one_block(j, slot):
        t0 = pl.multiple_of(j * BLK, BLK)
        dr, xr, yr = (ref.at[pl.ds(t0, BLK), :] for ref in (delta_out, dx, dy))
        count = 2 * states
        wide_rows = wide.at[pl.ds(pl.multiple_of(j * (BLK * count), BLK * count), BLK * count), :]
        s = end_out[...]
        starts_out[j] = s
        before = through[...]
        sums_out[j] = before[:1, :]
        rates = rate2[...]
        for i in range(BLK):
            a = jnp.exp2(spread(dr, i) * rates)
            decay[slot, i] = a
            tile = wide_tile(wide_rows, i, count)
            tiles[t0 + i] = tile
            s = a * s + spread(xr, i) * across_lanes(tile[:states], inner)
        end_out[...] = s
        m = jnp.zeros((states, inner), F32)
        for i in reversed(range(BLK)):
            m = decay[slot, i] * (m + spread(yr, i) * across_lanes(tiles[t0 + i, states:], inner))
        back_out[...] = back_out[...] + m * jnp.exp2(twice(before) * rates)
        through[...] = before + jnp.sum(dr[...], axis=0, keepdims=True)

    def block_step(k, _):
        one_block(2 * k, 0)
        one_block(2 * k + 1, 1)
        return 0

    lax.fori_loop(0, blocks // 2, block_step, 0)
    total_out[...] = through[:1, :]


def second_kernel(
    runs, s_in, lam_in, starts, sums, tiles, rate, xe, act, dsilu, delta, sig, dy, proj, xwt, dtw, taps, skip,
    y_out, dx_out, late_out, rate_grad, skip_grad, dtb_grad, dtp_grad, xp_grad, tap_grad, tapb_grad,
    rate2, carry, dxs, bdiag, cdiag, decay, states_low, lam_low, rq_low, qd_low, dots, racc, gsum, hsum, db, dc,
    rims, late, send_sem, recv_sem,
):
    toks, inner = dy.shape
    states = rate.shape[0]
    blocks = toks // BLK
    rank = dtw.shape[0]
    tap_count = taps.shape[0]
    item = pl.program_id(1)
    last_item = item == pl.num_programs(1) - 1
    me = lax.axis_index("seq")
    downs = [(rims.at[0], late.at[0], send_sem.at[0], recv_sem.at[0])]
    ups = [(rims.at[1], late.at[1], send_sem.at[1], recv_sem.at[1])]

    @pl.when((item == 0) & (pl.program_id(0) == 0))
    def _():
        greet_line(me, runs)

    gain = skip[pl.ds(pl.program_id(0), 1), :]
    rate2[...] = rate[...] * -LOG2E
    width = BLK * states

    @pl.when(item == 0)
    def _():
        for ref in (rate_grad, skip_grad, dtb_grad, dtp_grad, xp_grad, tap_grad, tapb_grad):
            ref[...] = jnp.zeros(ref.shape, ref.dtype)

    carry[...] = lam_in[...]
    act_low = act[...]
    dxs[:toks, :] = delta[...] * act_low.astype(F32)
    fold = (
        lax.broadcasted_iota(jnp.int32, (states, width), 1) % states == lax.broadcasted_iota(jnp.int32, (states, width), 0)
    ).astype(BF16)
    own = lax.broadcasted_iota(jnp.int32, (toks, width), 0) % BLK == lax.broadcasted_iota(jnp.int32, (toks, width), 1) // states
    bdiag[:toks, :] = jnp.where(own, dot_tn(proj[rank : rank + states, :].astype(BF16), fold), 0.0).astype(BF16)
    cdiag[...] = jnp.where(own, dot_tn(proj[rank + states :, :].astype(BF16), fold), 0.0).astype(BF16)
    mine = own[:BLK]
    picks = mine.astype(BF16)
    sides = (
        lax.broadcasted_iota(jnp.int32, (2 * BLK, 256), 0) // BLK == lax.broadcasted_iota(jnp.int32, (2 * BLK, 256), 1) // 128
    ).astype(BF16)
    racc[...] = jnp.zeros((states, inner), F32)
    qd_low[1] = jnp.zeros(qd_low.shape[1:], BF16)

    def lane_sum(wide):
        part = [wide[:, at : at + 128] for at in range(0, inner, 128)]
        while len(part) > 1:
            part = [sum(part[at : at + 2]) for at in range(0, len(part), 2)]
        return part[0]

    def products(slot, j):
        t0 = pl.multiple_of(j * BLK, BLK)
        gsum[pl.ds(t0, BLK), :] = dot(bdiag[pl.ds(t0, BLK), :], lam_low[slot])
        hsum[pl.ds(t0, BLK), :] = dot(picks, rq_low[slot])
        racc[...] += dot(fold[:, : BLK // 4 * states], qd_low[slot])
        both = dot_nt(sides, dots[slot])
        dc[pl.ds(t0, BLK), :] = jnp.where(mine, both[:BLK], 0.0).astype(BF16)
        db[pl.ds(t0, BLK), :] = jnp.where(mine, both[BLK:], 0.0).astype(BF16)

    def one_block(slot, j):
        t0 = pl.multiple_of(j * BLK, BLK)
        dr, xr, yr = (ref.at[pl.ds(t0, BLK), :] for ref in (delta, dxs, dy))
        tile = tiles.at[pl.ds(t0, BLK)]
        r2 = rate2[...]
        r_low = rate[...].astype(BF16)
        s = starts[j] + s_in[...] * jnp.exp2(twice(jnp.broadcast_to(sums[j], (8, inner))) * r2)
        states_low[slot, :states, :] = s.astype(BF16)
        for i in range(BLK):
            a = jnp.exp2(spread(dr, i) * r2)
            decay[slot, i] = a
            s = a * s + spread(xr, i) * across_lanes(tile[i, :states], inner)
            s_low = s.astype(BF16)
            states_low[slot, (i + 1) * states : (i + 2) * states, :] = s_low
            dots[slot, i * states : (i + 1) * states, :128] = lane_sum(s_low * spread(yr, i).astype(BF16))
        y_out[pl.ds(t0, BLK), :] = dot(cdiag[pl.ds(t0, BLK), :], states_low[slot, states:, :])
        cr = carry[...]
        qds = []
        for i in reversed(range(BLK)):
            lam = cr + spread(yr, i) * across_lanes(tile[i, states:], inner)
            l_low = lam.astype(BF16)
            lam_low[slot, i * states : (i + 1) * states, :] = l_low
            dots[slot, i * states : (i + 1) * states, 128:] = lane_sum(l_low * spread(xr, i).astype(BF16))
            cr = decay[slot, i] * lam
            q = cr.astype(BF16) * states_low[slot, i * states : (i + 1) * states, :]
            rq_low[slot, i * states : (i + 1) * states, :] = q * r_low
            qds.append(q * spread(dr, i).astype(BF16))
            if i % 4 == 0:
                qd_low[slot, i // 4 * states : (i // 4 + 1) * states, :] = (qds[0] + qds[1]) + (qds[2] + qds[3])
                qds = []
        carry[...] = cr

    def block_step(k, _):
        j = blocks - 1 - 2 * k
        products(1, jnp.where(k == 0, blocks, j + 1))
        one_block(0, j)
        products(0, j)
        one_block(1, j - 1)
        return 0

    lax.fori_loop(0, blocks // 2, block_step, 0)
    products(1, 0)

    rate_grad[...] += -racc[...]
    act_f = act_low.astype(F32)
    d_summed = dy[...]
    g = gsum[:toks, :]
    skip_grad[...] += jnp.sum(d_summed * act_f, axis=0, keepdims=True)
    y_out[...] += gain * act_f
    d_pre = (act_f * g - hsum[:toks, :]) * sig[...]
    dtb_grad[...] += jnp.sum(d_pre, axis=0, keepdims=True)
    d_pre_low = d_pre.astype(BF16)
    dtp_grad[...] += dot(proj[:rank, :].astype(BF16), d_pre_low)
    d_proj = jnp.concatenate(
        [dot_nt(dtw[...], d_pre_low), dot_nt(fold, db[:toks, :]), dot_nt(fold, dc[:toks, :])], axis=0
    ).astype(BF16)
    xp_grad[...] += dot(d_proj, act_low)
    d_act = delta[...] * g + gain * d_summed + dot_tn(d_proj, xwt[...])
    d_conv = d_act * dsilu[...]
    tapb_grad[...] += jnp.sum(d_conv, axis=0, keepdims=True)
    x_f = xe[...].astype(F32)
    moved = jnp.concatenate([jnp.zeros((HALO, inner), F32), d_conv], axis=0)
    window = HALO + toks
    d_window = taps[tap_count - 1 : tap_count, :] * moved
    tap_grad[tap_count - 1 : tap_count, :] += jnp.sum(moved * x_f, axis=0, keepdims=True)
    for k in reversed(range(tap_count - 1)):
        moved = pltpu.roll(moved, window - 1, 0)
        tap_grad[k : k + 1, :] += jnp.sum(moved * x_f, axis=0, keepdims=True)
        d_window = d_window + taps[k : k + 1, :] * moved
    rims[pl.program_id(0), item] = d_window[HALO - 8 : HALO]
    dx_out[...] = d_window[HALO:]

    @pl.when(last_item & (pl.program_id(0) == 0))
    def _():
        swap_along_line(me, runs, [], downs, True)

    @pl.when(last_item & (pl.program_id(0) == 1))
    def _():
        swap_along_line(me, runs, ups, [], True)
        swap_along_line(me, runs, ups, downs, False)

        @pl.when(me == 0)
        def _():
            late[1] = jnp.zeros(late.shape[1:], F32)

        @pl.when(me == runs - 1)
        def _():
            late[0] = jnp.zeros(late.shape[1:], F32)

        late_out[...] = late[...]


def third_kernel(
    tok, cot, mod, mask, counts, hid, z_in, y, dx, late, win, wout,
    mixed, d_tokens, d_mod, out_grad, in_grad,
):
    dim = tok.shape[-1]
    toks, inner = z_in.shape
    i = pl.program_id(0)

    @pl.when(i == 0)
    def _():
        out_grad[...] = jnp.zeros(out_grad.shape, F32)
        in_grad[...] = jnp.zeros(in_grad.shape, F32)

    shift, scale, gate = mod[:, :dim], mod[:, dim : 2 * dim], mod[:, 2 * dim :]
    valid = as_column(mask[pl.ds(i, 1), :]) * (counts[...] > i).astype(F32)
    tok_f = tok[...].astype(F32)
    normed, inv_std = normalise(tok_f)
    cot_f = cot[...].astype(F32)
    z = z_in[...]
    z_sig = jax.nn.sigmoid(z)
    summed = y[0] + flip_full(y[1])
    gated = (summed * z * z_sig).astype(BF16)
    branch_out = dot(gated, wout[...])
    mixed[...] = (tok_f + gate * branch_out).astype(BF16)
    d_branch = (cot_f * gate).astype(BF16)
    d_gated = dot_nt(d_branch, wout[...])
    d_zgate = d_gated * summed * z_sig * (1.0 + z * (1.0 - z_sig))
    out_grad[...] += dot_tn(gated, d_branch)

    edge = late.shape[2]

    def with_late(part, extra):
        return jnp.concatenate([part[: toks - edge], part[toks - edge :] + extra], axis=0)

    d_x = with_late(dx[0], late[0, i]) + flip_full(with_late(dx[1], late[1, i]))
    d_xz = (jnp.concatenate([d_x, d_zgate], axis=1) * valid).astype(BF16)
    d_hidden = dot_nt(d_xz, win[...])
    in_grad[...] += dot_tn(hid[...], d_xz)
    d_mod[0:1, :] = jnp.sum(d_hidden, axis=0, keepdims=True)
    d_mod[1:2, :] = jnp.sum(d_hidden * normed, axis=0, keepdims=True)
    d_mod[2:3, :] = jnp.sum(cot_f * branch_out, axis=0, keepdims=True)
    d_normed = d_hidden * (1.0 + scale)
    d_tokens[...] = cot_f + inv_std * (
        d_normed
        - jnp.mean(d_normed, axis=-1, keepdims=True)
        - normed * jnp.mean(d_normed * normed, axis=-1, keepdims=True)
    )


def bit_of(index, bit):
    return (index // (1 << bit)) % 2


def across(axis, bit):
    me = lax.axis_index(axis)
    mine = bit_of(me, bit)
    return mine, {axis: me + (1 - 2 * mine) * (1 << bit)}


def exchange_kernel(runs, end, back, total, rates, s_in, lam_in, group, span, pre, pre_span, sends, arrivals, send_sem, recv_sem):
    slots, _, states, inner = end.shape
    bits = int(math.log2(runs))
    links = [across("seq", bit) for bit in range(bits)]
    greet([target for _, target in links])
    flows = (((end, 0), (back, 1)), ((end, 1), (back, 0)))
    units = 2 * slots
    rows = units * states
    pre[...] = jnp.zeros(pre.shape, F32)
    pre_span[...] = jnp.zeros(pre_span.shape, F32)
    span[...] = jnp.zeros(span.shape, F32)
    for flow in range(2):
        for kind, (array, branch) in enumerate(flows[flow]):
            for i in range(slots):
                unit = kind * slots + i
                group[flow, unit] = array[i, branch]
                span[flow, unit : unit + 1, :] = total[i, branch]

    def load(flow, slot):
        for unit in range(units):
            sends[slot, unit * states : (unit + 1) * states, :] = group[flow, unit].astype(BF16)
        high = span[flow].astype(BF16).astype(F32)
        sends[slot, rows:, :] = jnp.concatenate([high, span[flow] - high], axis=0).astype(BF16)

    def join(flow, slot, earlier, last):
        both = arrivals[slot, rows:, :].astype(F32)
        length = both[: both.shape[0] // 2] + both[both.shape[0] // 2 :]
        own_span = span[flow]
        mine_span = pre_span[flow]
        second_span = jnp.where(earlier, own_span, length)
        for unit in range(units):
            rate = rates[flows[flow][unit // slots][1]] * -LOG2E
            state = arrivals[slot, unit * states : (unit + 1) * states, :].astype(F32)
            mine = pre[flow, unit]
            joined = state * jnp.exp2(rate * mine_span[unit : unit + 1]) + mine
            pre[flow, unit] = jnp.where(earlier, joined, mine)
            if not last:
                own = group[flow, unit]
                first = jnp.where(earlier, state, own)
                second = jnp.where(earlier, own, state)
                group[flow, unit] = first * jnp.exp2(rate * second_span[unit : unit + 1]) + second
        pre_span[flow] = jnp.where(earlier, length + mine_span, mine_span)
        if not last:
            span[flow] = own_span + length

    for stage, (mine, target) in enumerate(links):
        last = stage == bits - 1
        if last:
            slot = 2 * stage

            @pl.when(mine == 0)
            def _():
                load(0, slot)

            @pl.when(mine == 1)
            def _():
                load(1, slot)

            copies = [remote(sends.at[slot], arrivals.at[slot], send_sem.at[slot], recv_sem.at[slot], target)]
        else:
            copies = []
            for flow in range(2):
                slot = 2 * stage + flow
                load(flow, slot)
                copies.append(
                    remote(sends.at[slot], arrivals.at[slot], send_sem.at[slot], recv_sem.at[slot], target)
                )
        for copy in copies:
            copy.start()
        for copy in copies:
            copy.wait()
        if last:

            @pl.when(mine == 1)
            def _():
                join(0, 2 * stage, True, True)

            @pl.when(mine == 0)
            def _():
                join(1, 2 * stage, True, True)
        else:
            join(0, 2 * stage, mine == 1, False)
            join(1, 2 * stage + 1, mine == 0, False)
    for flow in range(2):
        for kind, (_, branch) in enumerate(flows[flow]):
            result = (s_in, lam_in)[kind]
            for i in range(slots):
                result[i, branch] = pre[flow, kind * slots + i]


PARTS = 6
LAST_ROWS = 16


def reduce_rows(dim, inner, small):
    rows = inner + (2 * dim + small) * (inner // dim)
    unit = PARTS * LAST_ROWS * 32
    return -(-rows // unit) * unit


def reduce_kernel(
    plan, in_grad, out_grad, xp_grad, dtp_grad, rate_grad, tap_grad, tapb_grad, skip_grad, dtb_grad, d_mod, step,
    result, factors, own_rows,
    acc, sends, arrivals, gathered, mod_sum, mod_in, table, send_sem, recv_sem, small_send, small_recv,
):
    runs, groups, total_rows = plan
    dim = in_grad.shape[0]
    inner = out_grad.shape[0]
    slots = step.shape[0]
    seq_bits = [("seq", bit) for bit in range(int(math.log2(runs)))]
    dp_bits = [("dp", bit) for bit in range(int(math.log2(groups)))]
    all_bits = seq_bits + dp_bits
    count = len(all_bits)
    links = {key: across(*key) for key in all_bits}
    middle = all_bits[1:-1]
    turn = [part % max(len(middle), 1) for part in range(PARTS)]
    orders = [all_bits[:1] + middle[at:] + middle[:at] + all_bits[1:][-1:] for at in turn]
    part_rows = total_rows // PARTS

    def small_copy(stage):
        axis, bit = all_bits[stage]
        target = links[(axis, bit)][1]
        if axis == "seq":
            return remote(mod_sum, mod_in.at[stage], small_send.at[stage], small_recv.at[stage], target)
        size = 16 << bit
        at = pl.multiple_of(lax.axis_index("dp") // (1 << bit) * size, 16)
        here = table.at[pl.ds(at, size), :]
        return remote(here, here, small_send.at[stage], small_recv.at[stage], target)

    def fill_table():
        time_f = step[...].astype(F32)
        time_low = time_f * jax.nn.sigmoid(time_f)
        at = pl.multiple_of(lax.axis_index("dp") * 16, 16)
        own = jnp.concatenate([mod_sum[: 3 * slots, :], time_low, mod_sum[4 * slots :, :]], axis=0)
        own_rows[...] = own.astype(BF16)
        table[pl.ds(at, 16), :] = own.astype(BF16)

    def start_small(stage):
        if stage == len(seq_bits):
            fill_table()
        if stage < count:
            small_copy(stage).start()

    def end_small(stage):
        small_copy(stage).wait()
        if all_bits[stage][0] == "seq":
            mod_sum[...] += mod_in[stage]

    segments = [(lambda at, size: out_grad[at : at + size, :], inner)]
    for lane in range(0, 2 * inner, dim):
        segments.append((lambda at, size, lane=lane: in_grad[at : at + size, lane : lane + dim], dim))
    small = []
    for ref in (xp_grad, dtp_grad, rate_grad, tap_grad):
        small += [(lambda ref=ref, branch=branch: ref[branch], ref.shape[1]) for branch in range(2)]

    def tail():
        rows = [ref[branch] for ref in (tapb_grad, skip_grad, dtb_grad) for branch in range(2)]
        return jnp.concatenate(rows + [jnp.zeros((2, inner), F32)], axis=0)

    small.append((tail, 8))
    for lane in range(0, inner, dim):
        for get, size in small:
            segments.append((lambda at, size, get=get, lane=lane: get()[at : at + size, lane : lane + dim], size))
    total = sum(size for _, size in segments)
    segments.append((lambda at, size: jnp.zeros((size, dim), F32), total_rows - total))

    def assemble(part):
        low, high = part * part_rows, (part + 1) * part_rows
        at = 0
        for get, size in segments:
            first, last = max(at, low), min(at + size, high)
            if first < last:
                acc[first:last, :] = get(first - at, last - first)
            at += size

    starts = [part * part_rows for part in range(PARTS)]
    sizes = [part_rows] * PARTS
    history = [[] for _ in range(PARTS)]
    offsets = [part * (part_rows + LAST_ROWS * count) for part in range(PARTS)]
    flying = [None] * PARTS

    def scatter(part, stage):
        mine, target = links[orders[part][stage]]
        start, size = starts[part], sizes[part]
        split = size >= 2 * LAST_ROWS
        moved = size // 2 if split else size
        away = keep = start
        if split:
            away = pl.multiple_of(start + (1 - mine) * moved, LAST_ROWS)
            keep = pl.multiple_of(start + mine * moved, LAST_ROWS)
        history[part].append((start, size, split))
        at = offsets[part]
        offsets[part] += moved
        sends[at : at + moved, :] = acc[pl.ds(away, moved), :].astype(BF16)
        copy = remote(
            sends.at[pl.ds(at, moved), :], arrivals.at[pl.ds(at, moved), :], send_sem.at[part, stage],
            recv_sem.at[part, stage], target,
        )
        copy.start()
        starts[part], sizes[part] = keep, moved
        flying[part] = (copy, keep, moved, at, split)

    def settle(part):
        copy, keep, moved, at, split = flying[part]
        copy.wait()
        held = acc[pl.ds(keep, moved), :]
        if not split:
            held = held.astype(BF16).astype(F32)
        acc[pl.ds(keep, moved), :] = held + arrivals[at : at + moved, :].astype(F32)

    def gather(part, stage):
        start, size, split = history[part][stage]
        flying[part] = None
        if split:
            here = gathered.at[pl.ds(starts[part], sizes[part]), :]
            target = links[orders[part][stage]][1]
            flying[part] = remote(
                here, here, send_sem.at[part, count + stage], recv_sem.at[part, count + stage], target
            )
            flying[part].start()
            starts[part], sizes[part] = start, size

    mod_sum[...] = jnp.zeros(mod_sum.shape, F32)
    for i in range(slots):
        mod_sum[3 * i : 3 * i + 3, :] = d_mod[i]
    greet([links[key][1] for key in all_bits])
    start_small(0)
    for part in range(PARTS):
        assemble(part)
        scatter(part, 0)
    for stage in range(1, count):
        end_small(stage - 1)
        start_small(stage)
        for part in range(PARTS):
            settle(part)
            scatter(part, stage)
    end_small(count - 1)
    if not dp_bits:
        fill_table()
    for part in range(PARTS):
        settle(part)
        where = pl.ds(starts[part], sizes[part])
        gathered[where, :] = acc[where, :].astype(BF16)
        gather(part, count - 1)
    for stage in reversed(range(count - 1)):
        for part in range(PARTS):
            if flying[part] is not None:
                flying[part].wait()
            gather(part, stage)
    for part in range(PARTS):
        if flying[part] is not None:
            flying[part].wait()
        result[part * part_rows : (part + 1) * part_rows, :] = gathered[part * part_rows : (part + 1) * part_rows, :]
    factors[...] = table[...]


def finish_kernel(
    ranks, result, factors, own, step, ada,
    grad_time, grad_ada, grad_ada_bias, in_grad, tap_grad, tapb_grad, xp_grad, dtp_grad, dtb_grad, rate_grad, skip_grad, out_grad,
):
    rank, wide_rank = ranks
    dim = in_grad.shape[0]
    inner = out_grad.shape[0]
    slots = step.shape[0]
    states = rate_grad.shape[1]
    taps = tap_grad.shape[1]

    def rows(at, size):
        return result[at : at + size, :].astype(F32)

    out_grad[...] = rows(0, inner)
    at = inner
    for lane in range(0, 2 * inner, dim):
        in_grad[:, lane : lane + dim] = rows(at, dim)
        at += dim
    wide = wide_rank + 2 * states
    for first in range(0, inner, dim):
        lanes = slice(first, first + dim)
        for branch in range(2):
            part = rows(at, wide)
            xp_grad[branch, :, lanes] = jnp.concatenate([part[:rank], part[wide_rank:]], axis=0)
            at += wide
        for branch in range(2):
            dtp_grad[branch, :, lanes] = rows(at, wide_rank)[:rank]
            at += wide_rank
        for branch in range(2):
            rate_grad[branch, :, lanes] = rows(at, states)
            at += states
        tail = rows(at, 16)
        for branch in range(2):
            tap_grad[branch, :, lanes] = tail[branch * taps : (branch + 1) * taps]
        tapb_grad[:, lanes] = tail[2 * taps : 2 * taps + 2]
        skip_grad[:, lanes] = tail[2 * taps + 2 : 2 * taps + 4]
        dtb_grad[:, lanes] = tail[2 * taps + 4 : 2 * taps + 6]
        at += 16

    table = factors[...]
    length = table.shape[0]
    groups = length // 16
    items = groups * 8

    def pick(place):
        row = lax.broadcasted_iota(jnp.int32, (items, length), 0)
        col = lax.broadcasted_iota(jnp.int32, (items, length), 1)
        slot = row % 8
        wanted = row // 8 * 16 + place(slot)
        return dot(((col == wanted) & (slot < slots)).astype(BF16), table)

    times = pick(lambda slot: 3 * slots + slot).astype(BF16)
    time_f = step[...].astype(F32)
    time_sig = jax.nn.sigmoid(time_f)
    d_time = jnp.zeros((slots, dim), F32)
    mine = own[...].astype(F32)
    for part in range(3):
        mods = pick(lambda slot: 3 * slot + part)
        lanes = slice(part * dim, (part + 1) * dim)
        grad_ada[:, lanes] = dot_tn(times, mods.astype(BF16))
        grad_ada_bias[lanes] = jnp.sum(mods, axis=0)
        picked = jnp.concatenate([mine[3 * i + part : 3 * i + part + 1] for i in range(slots)], axis=0)
        d_time = d_time + dot_nt(picked.astype(BF16), ada[:, lanes])
    grad_time[...] = d_time * time_sig * (1.0 + time_f * (1.0 - time_sig))


def params(**more):
    return pltpu.CompilerParams(vmem_limit_bytes=VMEM_LIMIT, **more)


def spec(block, index):
    return pl.BlockSpec(block, index)


def per_device(
    tokens, timestep, counts, token_mask, ada_weight, ada_bias, input_weight, conv_weight, conv_bias, x_weight, dt_weight,
    dt_bias, decay_rate, skip_gain, output_weight, cotangent,
):
    slots, toks, dim = tokens.shape
    inner = output_weight.shape[0]
    rank = dt_weight.shape[1]
    states = decay_rate.shape[1]
    tap_count = conv_weight.shape[1]
    wide_rank = 32
    proj_rows = wide_rank + 2 * states
    blocks = toks // BLK
    runs = lax.axis_size("seq")
    groups = lax.axis_size("dp")
    counts2 = counts[:, None]
    x_rows = jnp.swapaxes(x_weight, 1, 2)

    def item(*block):
        return spec((None,) + block, lambda i: (i,) + (0,) * len(block))

    def whole(*block):
        return spec(block, lambda *_: (0,) * len(block))

    xe, dy, z_gate, hid, modulate = pl.pallas_call(
        functools.partial(enter_kernel, runs),
        grid=(slots,),
        in_specs=[
            whole(slots, toks, dim), item(toks, dim), whole(slots, toks), whole(1, 1), whole(slots, dim), whole(dim, 3 * dim),
            whole(3 * dim), whole(dim, 2 * inner), whole(inner, dim),
        ],
        out_specs=[
            item(2, HALO + toks, inner), item(2, toks, inner), item(toks, inner), item(toks, dim), item(1, 3 * dim),
        ],
        out_shape=[
            jax.ShapeDtypeStruct((slots, 2, HALO + toks, inner), BF16),
            jax.ShapeDtypeStruct((slots, 2, toks, inner), F32),
            jax.ShapeDtypeStruct((slots, toks, inner), F32),
            jax.ShapeDtypeStruct((slots, toks, dim), BF16),
            jax.ShapeDtypeStruct((slots, 1, 3 * dim), F32),
        ],
        scratch_shapes=[
            pltpu.VMEM((slots, HALO, dim), BF16), pltpu.VMEM((slots, HALO, dim), BF16), pltpu.VMEM((slots, toks), jnp.int32),
            pltpu.VMEM((slots, toks), jnp.int32), pltpu.SemaphoreType.DMA((4,)), pltpu.SemaphoreType.DMA((4,)),
        ],
        compiler_params=params(collective_id=1, has_side_effects=True),
        name="enter",
    )(
        tokens, cotangent, token_mask, counts2, timestep, ada_weight, ada_bias, input_weight, output_weight,
    )

    def unit(*block):
        return spec((None, None) + block, lambda b, i: (i, b) + (0,) * len(block))

    def branch(*block):
        return spec((None,) + block, lambda b, i: (b,) + (0,) * len(block))

    def unit_shape(*block, kind=F32):
        return jax.ShapeDtypeStruct((slots, 2) + block, kind)

    act, dsilu, delta, sig, proj, end, back, total, starts, sums, tiles, xwt, dtw = pl.pallas_call(
        first_kernel,
        grid=(2, slots),
        in_specs=[
            unit(HALO + toks, inner), unit(toks, inner), branch(tap_count, inner), whole(2, inner),
            branch(rank + 2 * states, inner), branch(rank, inner), whole(2, inner), branch(states, inner),
        ],
        out_specs=[
            unit(toks, inner), unit(toks, inner), unit(toks, inner), unit(toks, inner), unit(proj_rows, toks),
            unit(states, inner), unit(states, inner), unit(1, inner), unit(blocks, states, inner), unit(blocks, 1, inner),
            unit(toks, 2 * states, 128), branch(proj_rows, inner), branch(wide_rank, inner),
        ],
        out_shape=[
            unit_shape(toks, inner, kind=BF16), unit_shape(toks, inner), unit_shape(toks, inner), unit_shape(toks, inner),
            unit_shape(proj_rows, toks), unit_shape(states, inner), unit_shape(states, inner), unit_shape(1, inner),
            unit_shape(blocks, states, inner), unit_shape(blocks, 1, inner), unit_shape(toks, 2 * states, 128),
            jax.ShapeDtypeStruct((2, proj_rows, inner), BF16), jax.ShapeDtypeStruct((2, wide_rank, inner), BF16),
        ],
        scratch_shapes=[
            pltpu.VMEM((toks, inner), F32), pltpu.VMEM((2, BLK, states, inner), F32), pltpu.VMEM((8, inner), F32),
            pltpu.VMEM((states, inner), F32), pltpu.VMEM((2 * states * toks, 128), F32),
            pltpu.VMEM((4 * states, 2 * states * 128), BF16),
        ],
        compiler_params=params(),
        name="first",
    )(xe, dy, conv_weight, conv_bias, x_rows, dt_weight, dt_bias, decay_rate)

    pairs = int(math.log2(runs))
    units = 2 * slots
    span_rows = -(-units // 8) * 8
    vmem = pl.BlockSpec(memory_space=pltpu.VMEM)
    s_in, lam_in = pl.pallas_call(
        functools.partial(exchange_kernel, runs),
        in_specs=[vmem] * 4,
        out_specs=[vmem] * 2,
        out_shape=[unit_shape(states, inner), unit_shape(states, inner)],
        scratch_shapes=[
            pltpu.VMEM((2, units, states, inner), F32), pltpu.VMEM((2, span_rows, inner), F32),
            pltpu.VMEM((2, units, states, inner), F32), pltpu.VMEM((2, span_rows, inner), F32),
            pltpu.VMEM((2 * pairs, units * states + 2 * span_rows, inner), BF16),
            pltpu.VMEM((2 * pairs, units * states + 2 * span_rows, inner), BF16),
            pltpu.SemaphoreType.DMA((2 * pairs,)), pltpu.SemaphoreType.DMA((2 * pairs,)),
        ],
        compiler_params=params(collective_id=2, has_side_effects=True),
        name="exchange",
    )(end, back, total, decay_rate)

    y, dx, late, rate_grad, skip_grad, dtb_grad, dtp_grad, xp_grad, tap_grad, tapb_grad = pl.pallas_call(
        functools.partial(second_kernel, runs),
        grid=(2, slots),
        in_specs=[
            unit(states, inner), unit(states, inner), unit(blocks, states, inner),
            unit(blocks, 1, inner), unit(toks, 2 * states, 128), branch(states, inner), unit(HALO + toks, inner), unit(toks, inner),
            unit(toks, inner), unit(toks, inner), unit(toks, inner), unit(toks, inner), unit(proj_rows, toks),
            branch(proj_rows, inner), branch(wide_rank, inner),
            branch(tap_count, inner), whole(2, inner),
        ],
        out_specs=[
            unit(toks, inner), unit(toks, inner), whole(2, slots, 8, inner), branch(states, inner), branch(1, inner), branch(1, inner),
            branch(wide_rank, inner), branch(proj_rows, inner), branch(tap_count, inner), branch(1, inner),
        ],
        out_shape=[
            unit_shape(toks, inner), unit_shape(toks, inner), jax.ShapeDtypeStruct((2, slots, 8, inner), F32),
        ] + [
            jax.ShapeDtypeStruct((2, rows, inner), F32) for rows in (states, 1, 1, wide_rank, proj_rows, tap_count, 1)
        ],
        scratch_shapes=[
            pltpu.VMEM((states, inner), F32), pltpu.VMEM((states, inner), F32), pltpu.VMEM((toks + BLK, inner), F32), pltpu.VMEM((toks + BLK, BLK * states), BF16),
            pltpu.VMEM((toks, BLK * states), BF16),
            pltpu.VMEM((2, BLK, states, inner), F32),
            pltpu.VMEM((2, (BLK + 1) * states, inner), BF16), pltpu.VMEM((2, BLK * states, inner), BF16),
            pltpu.VMEM((2, BLK * states, inner), BF16), pltpu.VMEM((2, BLK // 4 * states, inner), BF16),
            pltpu.VMEM((2, BLK * states, 256), BF16), pltpu.VMEM((states, inner), F32),
            pltpu.VMEM((toks + BLK, inner), F32), pltpu.VMEM((toks + BLK, inner), F32),
            pltpu.VMEM((toks + BLK, BLK * states), BF16), pltpu.VMEM((toks + BLK, BLK * states), BF16),
            pltpu.VMEM((2, slots, 8, inner), F32), pltpu.VMEM((2, slots, 8, inner), F32),
            pltpu.SemaphoreType.DMA((2,)), pltpu.SemaphoreType.DMA((2,)),
        ],
        compiler_params=params(collective_id=3, has_side_effects=True),
        name="second",
    )(
        s_in, lam_in, starts, sums, tiles, decay_rate, xe, act, dsilu, delta,
        sig, dy, proj, xwt, dtw, conv_weight, skip_gain,
    )

    mixed, d_tokens, d_mod, out_grad, in_grad = pl.pallas_call(
        third_kernel,
        grid=(slots,),
        in_specs=[
            item(toks, dim), item(toks, dim), item(1, 3 * dim), whole(slots, toks), whole(1, 1), item(toks, dim),
            item(toks, inner), item(2, toks, inner), item(2, toks, inner), whole(2, slots, 8, inner), whole(dim, 2 * inner),
            whole(inner, dim),
        ],
        out_specs=[item(toks, dim), item(toks, dim), item(3, dim), whole(inner, dim), whole(dim, 2 * inner)],
        out_shape=[
            jax.ShapeDtypeStruct((slots, toks, dim), BF16), jax.ShapeDtypeStruct((slots, toks, dim), F32),
            jax.ShapeDtypeStruct((slots, 3, dim), F32), jax.ShapeDtypeStruct((inner, dim), F32),
            jax.ShapeDtypeStruct((dim, 2 * inner), F32),
        ],
        compiler_params=params(),
        name="third",
    )(
        tokens, cotangent, modulate, token_mask, counts2, hid, z_gate, y, dx, late, input_weight, output_weight,
    )

    small = 2 * (proj_rows + wide_rank + states + tap_count) + 8
    rows = reduce_rows(dim, inner, small)
    stages = int(math.log2(runs)) + int(math.log2(groups))
    result, factors, own = pl.pallas_call(
        functools.partial(reduce_kernel, (runs, groups, rows)),
        in_specs=[vmem] * 11,
        out_specs=[vmem] * 3,
        out_shape=[
            jax.ShapeDtypeStruct((rows, dim), BF16), jax.ShapeDtypeStruct((16 * groups, dim), BF16),
            jax.ShapeDtypeStruct((16, dim), BF16),
        ],
        scratch_shapes=[
            pltpu.VMEM((rows, dim), F32), pltpu.VMEM((rows + PARTS * LAST_ROWS * stages, dim), BF16),
            pltpu.VMEM((rows + PARTS * LAST_ROWS * stages, dim), BF16),
            pltpu.VMEM((rows, dim), BF16), pltpu.VMEM((16, dim), F32),
            pltpu.VMEM((max(int(math.log2(runs)), 1), 16, dim), F32), pltpu.VMEM((16 * groups, dim), BF16),
            pltpu.SemaphoreType.DMA((PARTS, 2 * stages)), pltpu.SemaphoreType.DMA((PARTS, 2 * stages)),
            pltpu.SemaphoreType.DMA((stages,)), pltpu.SemaphoreType.DMA((stages,)),
        ],
        compiler_params=params(collective_id=4, has_side_effects=True),
        name="reduce",
    )(
        in_grad, out_grad, xp_grad, dtp_grad, rate_grad, tap_grad, tapb_grad, skip_grad, dtb_grad, d_mod, timestep,
    )

    (
        d_time, grad_ada, grad_ada_bias, in_grad, tap_grad, tapb_grad, xp_grad, dtp_grad, dtb_grad, rate_grad, skip_grad,
        out_grad,
    ) = pl.pallas_call(
        functools.partial(finish_kernel, (rank, wide_rank)),
        in_specs=[vmem] * 5,
        out_specs=[vmem] * 12,
        out_shape=[
            jax.ShapeDtypeStruct(shape, F32)
            for shape in (
                (slots, dim), (dim, 3 * dim), (3 * dim,), (dim, 2 * inner), (2, tap_count, inner), (2, inner),
                (2, rank + 2 * states, inner), (2, rank, inner), (2, inner), (2, states, inner), (2, inner), (inner, dim),
            )
        ],
        compiler_params=params(),
        name="finish",
    )(result, factors, own, timestep, ada_weight)
    return (
        mixed, d_tokens, d_time, grad_ada, grad_ada_bias, in_grad, tap_grad, tapb_grad, jnp.swapaxes(xp_grad, 1, 2), dtp_grad, dtb_grad,
        rate_grad, skip_grad, out_grad,
    )


def solution(mesh):
    runs = P("dp", "seq", None)
    return jax.shard_map(
        per_device,
        mesh=mesh,
        in_specs=(runs, P("dp", None), P("dp"), P("dp", "seq")) + (P(),) * 11 + (runs,),
        out_specs=(runs, runs, P("dp", None)) + (P(),) * 11,
        check_vma=False,
    )
```

```python
import functools
import math

import jax
import jax.numpy as jnp
from jax import lax
from jax.experimental import pallas as pl
from jax.experimental.pallas import tpu as pltpu
from jax.sharding import PartitionSpec as P

EPSILON = 1e-06
BLK = 16
HALO = 16
LOG2E = math.log2(math.e)
F32, BF16 = jnp.float32, jnp.bfloat16
NT = (((1,), (1,)), ((), ()))
TN = (((0,), (0,)), ((), ()))
VMEM_LIMIT = 60 << 20
MESH = pl.DeviceIdType.MESH


def dot(a, b):
    return jnp.dot(a, b, preferred_element_type=F32)


def dot_nt(a, b):
    return lax.dot_general(a, b, NT, preferred_element_type=F32)


def dot_tn(a, b):
    return lax.dot_general(a, b, TN, preferred_element_type=F32)


def reversal(size):
    rows = lax.broadcasted_iota(jnp.int32, (size, size), 0)
    cols = lax.broadcasted_iota(jnp.int32, (size, size), 1)
    return (rows + cols == size - 1).astype(BF16)


def flip_low(value):
    return dot(reversal(value.shape[0]), value).astype(BF16)


def flip_full(value):
    order = reversal(value.shape[0])
    high = value.astype(BF16)
    return dot(order, high) + dot(order, (value - high.astype(F32)).astype(BF16))


def normalise(tokens_f):
    centered = tokens_f - jnp.mean(tokens_f, axis=-1, keepdims=True)
    inv_std = lax.rsqrt(jnp.mean(centered * centered, axis=-1, keepdims=True) + EPSILON)
    return centered * inv_std, inv_std


def eye(size):
    rows = lax.broadcasted_iota(jnp.int32, (size, size), 0)
    cols = lax.broadcasted_iota(jnp.int32, (size, size), 1)
    return (rows == cols).astype(BF16)


def as_column(row):
    return dot_nt(eye(row.shape[1]), jnp.broadcast_to(row.astype(F32).astype(BF16), (8, row.shape[1])))[:, :1]


def remote(src, dst, send_sem, recv_sem, target):
    return pltpu.make_async_remote_copy(
        src_ref=src, dst_ref=dst, send_sem=send_sem, recv_sem=recv_sem, device_id=target, device_id_type=MESH
    )


def greet(targets):
    barrier = pltpu.get_barrier_semaphore()
    for target in targets:
        pl.semaphore_signal(barrier, inc=1, device_id=target, device_id_type=MESH)
    pl.semaphore_wait(barrier, len(targets))


def greet_line(me, runs, others=()):
    barrier = pltpu.get_barrier_semaphore()
    for target in others:
        pl.semaphore_signal(barrier, inc=1, device_id=target, device_id_type=MESH)

    @pl.when(me > 0)
    def _():
        pl.semaphore_signal(barrier, inc=1, device_id={"seq": me - 1}, device_id_type=MESH)

    @pl.when(me < runs - 1)
    def _():
        pl.semaphore_signal(barrier, inc=1, device_id={"seq": me + 1}, device_id_type=MESH)

    neighbours = (me + runs - 1) // runs + (2 * runs - 2 - me) // runs
    pl.semaphore_wait(barrier, neighbours + len(others))


def swap_along_line(me, runs, ups, downs, start):
    up = [remote(src, dst, ss, rs, {"seq": me + 1}) for src, dst, ss, rs in ups]
    down = [remote(src, dst, ss, rs, {"seq": me - 1}) for src, dst, ss, rs in downs]

    @pl.when(me < runs - 1)
    def _():
        for copy in up:
            if start:
                copy.start()
            else:
                copy.wait_send()
        if not start:
            for copy in down:
                copy.wait_recv()

    @pl.when(me > 0)
    def _():
        for copy in down:
            if start:
                copy.start()
            else:
                copy.wait_send()
        if not start:
            for copy in up:
                copy.wait_recv()


def enter_kernel(
    runs, tok, cot, mask, counts, step, ada, ada_bias, win, wout,
    xe, dy, z_out, hid_out, mod_out,
    prev_tok, next_tok, prev_mask, next_mask, send_sem, recv_sem,
):
    slots, toks, dim = tok.shape
    inner = wout.shape[0]
    me = lax.axis_index("seq")
    i = pl.program_id(0)
    ups = [
        (tok.at[:, pl.ds(toks - HALO, HALO), :], prev_tok, send_sem.at[0], recv_sem.at[0]),
        (mask, prev_mask, send_sem.at[1], recv_sem.at[1]),
    ]
    downs = [
        (tok.at[:, pl.ds(0, HALO), :], next_tok, send_sem.at[2], recv_sem.at[2]),
        (mask, next_mask, send_sem.at[3], recv_sem.at[3]),
    ]

    @pl.when(i == 0)
    def _():
        greet_line(me, runs)
        swap_along_line(me, runs, ups, downs, True)

        @pl.when(me == 0)
        def _():
            prev_tok[...] = jnp.zeros(prev_tok.shape, BF16)
            prev_mask[...] = jnp.zeros(prev_mask.shape, jnp.int32)

        @pl.when(me == runs - 1)
        def _():
            next_tok[...] = jnp.zeros(next_tok.shape, BF16)
            next_mask[...] = jnp.zeros(next_mask.shape, jnp.int32)

    live = (counts[...] > i).astype(F32)
    steps = step[...].astype(F32)
    here = lax.broadcasted_iota(jnp.int32, steps.shape, 0) == i
    time_f = jnp.sum(jnp.where(here, steps, 0.0), axis=0, keepdims=True)
    time_low = (time_f * jax.nn.sigmoid(time_f)).astype(BF16)
    mod = dot(time_low, ada[...]) + ada_bias[...].reshape(1, 3 * dim)
    mod_out[...] = mod
    shift, scale, gate = mod[:, :dim], mod[:, dim : 2 * dim], mod[:, 2 * dim :]

    def hidden_of(part):
        normed, _ = normalise(part.astype(F32))
        return (normed * (1.0 + scale) + shift).astype(BF16)

    hid = hidden_of(tok[i])
    hid_out[...] = hid
    xz = dot(hid, win[...]) * (as_column(mask[pl.ds(i, 1), :]) * live)
    x_low = xz[:, :inner].astype(BF16)
    z = xz[:, inner:]
    z_out[...] = z
    d_branch = (cot[...].astype(F32) * gate).astype(BF16)
    d_summed = dot_nt(d_branch, wout[...]) * z * jax.nn.sigmoid(z)
    dy[0] = d_summed
    dy[1] = flip_full(d_summed)
    xe[0, HALO:, :] = x_low
    xe[1, HALO:, :] = flip_low(x_low)

    @pl.when(i == 0)
    def _():
        swap_along_line(me, runs, ups, downs, False)

    rims = jnp.concatenate([prev_tok[i], next_tok[i]], axis=0)
    prev_col = as_column(prev_mask[pl.ds(i, 1), :])[toks - HALO :]
    next_col = as_column(next_mask[pl.ds(i, 1), :])[:HALO]
    rim_x = dot(hidden_of(rims), win[:, :inner]) * (jnp.concatenate([prev_col, next_col], axis=0) * live)
    rim_x = rim_x.astype(BF16)
    xe[0, :HALO, :] = rim_x[:HALO]
    xe[1, :HALO, :] = flip_low(rim_x[HALO:])


def twice(row8):
    return jnp.concatenate([row8, row8], axis=0)


def spread(ref, index):
    return twice(ref[pl.ds(index, 8, stride=0), :])


def lay_out(wide, rows, picks):
    count, toks = rows.shape
    high = rows.astype(BF16).astype(F32)
    halves = jnp.concatenate([high, rows - high], axis=0).T.astype(BF16)
    for n in range(0, count, 2):
        pair = dot(halves, picks[:, n * 128 : (n + 2) * 128])
        for t in range(0, toks, 8):
            for k in range(2):
                at = 8 * (count * (t // 8) + n + k)
                wide[at : at + 8, :] = pair[t : t + 8, k * 128 : (k + 1) * 128]


def wide_tile(wide, i, count):
    at = 8 * count * (i // 8) + i % 8
    return jnp.concatenate([wide[pl.ds(at + 64 * n, 8, stride=8), :] for n in range(count // 8)], axis=0)


def across_lanes(tile, inner):
    return jnp.concatenate([tile] * (inner // 128), axis=1)


def softplus_parts(pre):
    e = jnp.exp2(-LOG2E * jnp.abs(pre))
    more = jnp.where(e < 1e-3, e - 0.5 * e * e, jnp.log(1.0 + e))
    return jnp.maximum(pre, 0.0) + more, jax.nn.sigmoid(pre)


def bit_of(index, bit):
    return (index // (1 << bit)) % 2


def across(axis, bit):
    me = lax.axis_index(axis)
    mine = bit_of(me, bit)
    return mine, {axis: me + (1 - 2 * mine) * (1 << bit)}


class Exchange:
    def __init__(self, runs, branch, ends, backs, totals, rate, results, group, span, pre, pre_span, sends, arrivals, sems):
        self.branch, self.rate = branch, rate
        self.sources, self.totals, self.results = (ends, backs), totals, results
        self.group, self.span, self.pre, self.pre_span = group, span, pre, pre_span
        self.sends, self.arrivals, self.sems = sends, arrivals, sems
        self.links = [across("seq", bit) for bit in range(int(math.log2(runs)))]
        self.slots, self.states, self.inner = ends.shape

    def flow(self, kind):
        return kind if self.branch == 0 else 1 - kind

    def targets(self):
        return [target for _, target in self.links]

    def copy(self, stage, kind):
        at = 2 * stage + kind
        return remote(
            self.sends.at[at], self.arrivals.at[at], self.sems.at[0, at], self.sems.at[1, at], self.links[stage][1]
        )

    def send(self, stage, kind):
        rows = self.slots * self.states
        at = 2 * stage + kind
        for i in range(self.slots):
            self.sends[at, i * self.states : (i + 1) * self.states, :] = self.group[kind, i].astype(BF16)
        high = self.span[kind].astype(BF16).astype(F32)
        self.sends[at, rows:, :] = jnp.concatenate([high, self.span[kind] - high], axis=0).astype(BF16)
        self.copy(stage, kind).start()

    def join(self, stage, kind, last):
        mine = self.links[stage][0]
        self.copy(stage, kind).wait()
        at = 2 * stage + kind
        earlier = (mine == 1) if self.flow(kind) == 0 else (mine == 0)
        both = self.arrivals[at, self.slots * self.states :, :].astype(F32)
        length = both[: both.shape[0] // 2] + both[both.shape[0] // 2 :]
        own_span, pre_span = self.span[kind], self.pre_span[kind]
        second_span = jnp.where(earlier, own_span, length)
        rate = self.rate[...] * -LOG2E
        for i in range(self.slots):
            state = self.arrivals[at, i * self.states : (i + 1) * self.states, :].astype(F32)
            before = self.pre[kind, i]
            self.pre[kind, i] = jnp.where(earlier, state * jnp.exp2(rate * pre_span[i : i + 1]) + before, before)
            if not last:
                own = self.group[kind, i]
                first, second = jnp.where(earlier, state, own), jnp.where(earlier, own, state)
                self.group[kind, i] = first * jnp.exp2(rate * second_span[i : i + 1]) + second
        self.pre_span[kind] = jnp.where(earlier, length + pre_span, pre_span)
        if not last:
            self.span[kind] = own_span + length

    def points(self):
        count = len(self.links)

        def begin():
            self.pre[...] = jnp.zeros(self.pre.shape, F32)
            self.pre_span[...] = jnp.zeros(self.pre_span.shape, F32)
            self.span[...] = jnp.zeros(self.span.shape, F32)
            for kind in range(2):
                for i in range(self.slots):
                    self.group[kind, i] = self.sources[kind][i]
                    self.span[kind, i : i + 1, :] = self.totals[i]
                if count:
                    self.send(0, kind)

        def step(stage):
            last = stage == count - 1
            for kind in range(2):
                self.join(stage, kind, last)
                if not last:
                    self.send(stage + 1, kind)

        def end():
            for kind in range(2):
                for i in range(self.slots):
                    self.results[kind][i] = self.pre[kind, i]

        return [begin] + [functools.partial(step, stage) for stage in range(count)] + [end]


def exchange_shapes(runs, slots, states, inner):
    pairs = max(int(math.log2(runs)), 1)
    span_rows = -(-slots // 8) * 8
    return [
        pltpu.VMEM((2, slots, states, inner), F32), pltpu.VMEM((2, span_rows, inner), F32),
        pltpu.VMEM((2, slots, states, inner), F32), pltpu.VMEM((2, span_rows, inner), F32),
        pltpu.VMEM((2 * pairs, slots * states + 2 * span_rows, inner), BF16),
        pltpu.VMEM((2 * pairs, slots * states + 2 * span_rows, inner), BF16),
        pltpu.SemaphoreType.DMA((2, 2 * pairs)),
    ]


def beside(points, step, first, count):
    for at in range(min(len(points), count)):
        todo = points[at:] if at == count - 1 else points[at : at + 1]

        @pl.when(step == first + at)
        def _():
            for point in todo:
                point()


def first_kernel(
    runs, slots, xe, dy, taps, tap_bias, x_rows, dt_rows, dt_bias, rate,
    act_out, dsilu_out, delta_out, sig_out, proj_out, end_out, back_out, total_out, starts_out, sums_out, tiles, xwt, dtw, s_in, lam_in,
    dx, decay, through, rate2, wide, picks, ends, backs, totals, first_rate, *exchange_scratch,
):
    toks, inner = dy.shape
    states = rate.shape[0]
    blocks = toks // BLK
    rank = dtw.shape[0]
    tap_count = taps.shape[0]
    branch, item = pl.program_id(0), pl.program_id(1)
    exchange = Exchange(runs, 0, ends, backs, totals, first_rate, (s_in, lam_in), *exchange_scratch)

    @pl.when((branch == 0) & (item == 0))
    def _():
        greet(exchange.targets())
        first_rate[...] = rate[...]

    beside(exchange.points(), branch * slots + item, slots, slots)

    @pl.when(item == 0)
    def _():
        rate2[...] = rate[...] * -LOG2E
        picks[...] = (
            lax.broadcasted_iota(jnp.int32, picks.shape, 0) % (2 * states)
            == lax.broadcasted_iota(jnp.int32, picks.shape, 1) // 128
        ).astype(BF16)
        held = dt_rows.shape[0]
        rows = x_rows[...].astype(F32)
        gap = jnp.zeros((rank - held, inner), F32)
        xwt[...] = jnp.concatenate([rows[:held], gap, rows[held:]], axis=0).astype(BF16)
        dtw[...] = jnp.concatenate([dt_rows[...].astype(F32), gap], axis=0).astype(BF16)

    shifted = xe[...].astype(F32)
    conv = tap_bias[pl.ds(branch, 1), :] + taps[tap_count - 1 : tap_count, :] * shifted[HALO:]
    for k in reversed(range(tap_count - 1)):
        shifted = pltpu.roll(shifted, 1, 0)
        conv = conv + taps[k : k + 1, :] * shifted[HALO:]
    sig = jax.nn.sigmoid(conv)
    act_f = conv * sig
    act = act_f.astype(BF16)
    dsilu_out[...] = sig + act_f * (1.0 - sig)
    act_out[...] = act
    proj = dot_nt(xwt[...], act)
    proj_out[...] = proj
    pre = dot_tn(proj[:rank, :].astype(BF16), dtw[...]) + dt_bias[pl.ds(branch, 1), :]
    delta, slope = softplus_parts(pre)
    delta_out[...] = delta
    sig_out[...] = slope
    dx[...] = delta * act.astype(F32)
    lay_out(wide, proj[rank:, :], picks)
    end_out[...] = jnp.zeros((states, inner), F32)
    back_out[...] = jnp.zeros((states, inner), F32)
    through[...] = jnp.zeros((8, inner), F32)

    def one_block(j, slot):
        t0 = pl.multiple_of(j * BLK, BLK)
        dr, xr, yr = (ref.at[pl.ds(t0, BLK), :] for ref in (delta_out, dx, dy))
        count = 2 * states
        wide_rows = wide.at[pl.ds(pl.multiple_of(j * (BLK * count), BLK * count), BLK * count), :]
        s = end_out[...]
        starts_out[j] = s
        before = through[...]
        sums_out[j] = before[:1, :]
        rates = rate2[...]
        for i in range(BLK):
            a = jnp.exp2(spread(dr, i) * rates)
            decay[slot, i] = a
            tile = wide_tile(wide_rows, i, count)
            tiles[t0 + i] = tile
            s = a * s + spread(xr, i) * across_lanes(tile[:states], inner)
        end_out[...] = s
        m = jnp.zeros((states, inner), F32)
        for i in reversed(range(BLK)):
            m = decay[slot, i] * (m + spread(yr, i) * across_lanes(tiles[t0 + i, states:], inner))
        back_out[...] = back_out[...] + m * jnp.exp2(twice(before) * rates)
        through[...] = before + jnp.sum(dr[...], axis=0, keepdims=True)

    def block_step(k, _):
        one_block(2 * k, 0)
        one_block(2 * k + 1, 1)
        return 0

    lax.fori_loop(0, blocks // 2, block_step, 0)
    total_out[...] = through[:1, :]

    @pl.when(branch == 0)
    def _():
        ends[item] = end_out[...]
        backs[item] = back_out[...]
        totals[item] = through[:1, :]


def second_kernel(
    runs, s_first, lam_first, ends, backs, totals, last_rate, starts, sums, tiles, rate, xe, act, dsilu, delta, sig, dy, proj, xwt, dtw, taps, skip,
    y_out, dx_out, late_out, rate_grad, skip_grad, dtb_grad, dtp_grad, xp_grad, tap_grad, tapb_grad,
    rate2, carry, dxs, bdiag, cdiag, decay, states_low, lam_low, rq_low, qd_low, dots, racc, gsum, hsum, db, dc,
    rims, late, send_sem, recv_sem, s_in, s_last, lam_last, *exchange_scratch,
):
    toks, inner = dy.shape
    states = rate.shape[0]
    blocks = toks // BLK
    rank = dtw.shape[0]
    tap_count = taps.shape[0]
    item = pl.program_id(1)
    last_item = item == pl.num_programs(1) - 1
    me = lax.axis_index("seq")
    downs = [(rims.at[0], late.at[0], send_sem.at[0], recv_sem.at[0])]
    ups = [(rims.at[1], late.at[1], send_sem.at[1], recv_sem.at[1])]

    branch = pl.program_id(0)
    slots = ends.shape[0]
    exchange = Exchange(runs, 1, ends, backs, totals, last_rate, (s_last, lam_last), *exchange_scratch)

    @pl.when((item == 0) & (branch == 0))
    def _():
        greet_line(me, runs, exchange.targets())

    beside(exchange.points(), branch * slots + item, 0, slots)

    @pl.when(branch == 0)
    def _():
        s_in[...] = s_first[item]
        carry[...] = lam_first[item]

    @pl.when(branch == 1)
    def _():
        s_in[...] = s_last[item]
        carry[...] = lam_last[item]

    gain = skip[pl.ds(pl.program_id(0), 1), :]
    rate2[...] = rate[...] * -LOG2E
    width = BLK * states

    @pl.when(item == 0)
    def _():
        for ref in (rate_grad, skip_grad, dtb_grad, dtp_grad, xp_grad, tap_grad, tapb_grad):
            ref[...] = jnp.zeros(ref.shape, ref.dtype)

    act_low = act[...]
    dxs[:toks, :] = delta[...] * act_low.astype(F32)
    fold = (
        lax.broadcasted_iota(jnp.int32, (states, width), 1) % states == lax.broadcasted_iota(jnp.int32, (states, width), 0)
    ).astype(BF16)
    own = lax.broadcasted_iota(jnp.int32, (toks, width), 0) % BLK == lax.broadcasted_iota(jnp.int32, (toks, width), 1) // states
    bdiag[:toks, :] = jnp.where(own, dot_tn(proj[rank : rank + states, :].astype(BF16), fold), 0.0).astype(BF16)
    cdiag[...] = jnp.where(own, dot_tn(proj[rank + states :, :].astype(BF16), fold), 0.0).astype(BF16)
    mine = own[:BLK]
    picks = mine.astype(BF16)
    sides = (
        lax.broadcasted_iota(jnp.int32, (2 * BLK, 256), 0) // BLK == lax.broadcasted_iota(jnp.int32, (2 * BLK, 256), 1) // 128
    ).astype(BF16)
    racc[...] = jnp.zeros((states, inner), F32)
    qd_low[1] = jnp.zeros(qd_low.shape[1:], BF16)

    def lane_sum(wide):
        part = [wide[:, at : at + 128] for at in range(0, inner, 128)]
        while len(part) > 1:
            part = [sum(part[at : at + 2]) for at in range(0, len(part), 2)]
        return part[0]

    def products(slot, j):
        t0 = pl.multiple_of(j * BLK, BLK)
        gsum[pl.ds(t0, BLK), :] = dot(bdiag[pl.ds(t0, BLK), :], lam_low[slot])
        hsum[pl.ds(t0, BLK), :] = dot(picks, rq_low[slot])
        racc[...] += dot(fold[:, : BLK // 4 * states], qd_low[slot])
        both = dot_nt(sides, dots[slot])
        dc[pl.ds(t0, BLK), :] = jnp.where(mine, both[:BLK], 0.0).astype(BF16)
        db[pl.ds(t0, BLK), :] = jnp.where(mine, both[BLK:], 0.0).astype(BF16)

    def one_block(slot, j):
        t0 = pl.multiple_of(j * BLK, BLK)
        dr, xr, yr = (ref.at[pl.ds(t0, BLK), :] for ref in (delta, dxs, dy))
        tile = tiles.at[pl.ds(t0, BLK)]
        r2 = rate2[...]
        r_low = rate[...].astype(BF16)
        s = starts[j] + s_in[...] * jnp.exp2(twice(jnp.broadcast_to(sums[j], (8, inner))) * r2)
        states_low[slot, :states, :] = s.astype(BF16)
        for i in range(BLK):
            a = jnp.exp2(spread(dr, i) * r2)
            decay[slot, i] = a
            s = a * s + spread(xr, i) * across_lanes(tile[i, :states], inner)
            s_low = s.astype(BF16)
            states_low[slot, (i + 1) * states : (i + 2) * states, :] = s_low
            dots[slot, i * states : (i + 1) * states, :128] = lane_sum(s_low * spread(yr, i).astype(BF16))
        y_out[pl.ds(t0, BLK), :] = dot(cdiag[pl.ds(t0, BLK), :], states_low[slot, states:, :])
        cr = carry[...]
        qds = []
        for i in reversed(range(BLK)):
            lam = cr + spread(yr, i) * across_lanes(tile[i, states:], inner)
            l_low = lam.astype(BF16)
            lam_low[slot, i * states : (i + 1) * states, :] = l_low
            dots[slot, i * states : (i + 1) * states, 128:] = lane_sum(l_low * spread(xr, i).astype(BF16))
            cr = decay[slot, i] * lam
            q = cr.astype(BF16) * states_low[slot, i * states : (i + 1) * states, :]
            rq_low[slot, i * states : (i + 1) * states, :] = q * r_low
            qds.append(q * spread(dr, i).astype(BF16))
            if i % 4 == 0:
                qd_low[slot, i // 4 * states : (i // 4 + 1) * states, :] = (qds[0] + qds[1]) + (qds[2] + qds[3])
                qds = []
        carry[...] = cr

    def block_step(k, _):
        j = blocks - 1 - 2 * k
        products(1, jnp.where(k == 0, blocks, j + 1))
        one_block(0, j)
        products(0, j)
        one_block(1, j - 1)
        return 0

    lax.fori_loop(0, blocks // 2, block_step, 0)
    products(1, 0)

    rate_grad[...] += -racc[...]
    act_f = act_low.astype(F32)
    d_summed = dy[...]
    g = gsum[:toks, :]
    skip_grad[...] += jnp.sum(d_summed * act_f, axis=0, keepdims=True)
    y_out[...] += gain * act_f
    d_pre = (act_f * g - hsum[:toks, :]) * sig[...]
    dtb_grad[...] += jnp.sum(d_pre, axis=0, keepdims=True)
    d_pre_low = d_pre.astype(BF16)
    dtp_grad[...] += dot(proj[:rank, :].astype(BF16), d_pre_low)
    d_proj = jnp.concatenate(
        [dot_nt(dtw[...], d_pre_low), dot_nt(fold, db[:toks, :]), dot_nt(fold, dc[:toks, :])], axis=0
    ).astype(BF16)
    xp_grad[...] += dot(d_proj, act_low)
    d_act = delta[...] * g + gain * d_summed + dot_tn(d_proj, xwt[...])
    d_conv = d_act * dsilu[...]
    tapb_grad[...] += jnp.sum(d_conv, axis=0, keepdims=True)
    x_f = xe[...].astype(F32)
    moved = jnp.concatenate([jnp.zeros((HALO, inner), F32), d_conv], axis=0)
    window = HALO + toks
    d_window = taps[tap_count - 1 : tap_count, :] * moved
    tap_grad[tap_count - 1 : tap_count, :] += jnp.sum(moved * x_f, axis=0, keepdims=True)
    for k in reversed(range(tap_count - 1)):
        moved = pltpu.roll(moved, window - 1, 0)
        tap_grad[k : k + 1, :] += jnp.sum(moved * x_f, axis=0, keepdims=True)
        d_window = d_window + taps[k : k + 1, :] * moved
    rims[pl.program_id(0), item] = d_window[HALO - 8 : HALO]
    dx_out[...] = d_window[HALO:]

    @pl.when(last_item & (pl.program_id(0) == 0))
    def _():
        swap_along_line(me, runs, [], downs, True)

    @pl.when(last_item & (pl.program_id(0) == 1))
    def _():
        swap_along_line(me, runs, ups, [], True)
        swap_along_line(me, runs, ups, downs, False)

        @pl.when(me == 0)
        def _():
            late[1] = jnp.zeros(late.shape[1:], F32)

        @pl.when(me == runs - 1)
        def _():
            late[0] = jnp.zeros(late.shape[1:], F32)

        late_out[...] = late[...]


def third_kernel(
    tok, cot, mod, mask, counts, hid, z_in, y, dx, late, win, wout,
    mixed, d_tokens, d_mod, out_grad, in_grad,
):
    dim = tok.shape[-1]
    toks, inner = z_in.shape
    i = pl.program_id(0)

    @pl.when(i == 0)
    def _():
        out_grad[...] = jnp.zeros(out_grad.shape, F32)
        in_grad[...] = jnp.zeros(in_grad.shape, F32)

    shift, scale, gate = mod[:, :dim], mod[:, dim : 2 * dim], mod[:, 2 * dim :]
    valid = as_column(mask[pl.ds(i, 1), :]) * (counts[...] > i).astype(F32)
    tok_f = tok[...].astype(F32)
    normed, inv_std = normalise(tok_f)
    cot_f = cot[...].astype(F32)
    z = z_in[...]
    z_sig = jax.nn.sigmoid(z)
    summed = y[0] + flip_full(y[1])
    gated = (summed * z * z_sig).astype(BF16)
    branch_out = dot(gated, wout[...])
    mixed[...] = (tok_f + gate * branch_out).astype(BF16)
    d_branch = (cot_f * gate).astype(BF16)
    d_gated = dot_nt(d_branch, wout[...])
    d_zgate = d_gated * summed * z_sig * (1.0 + z * (1.0 - z_sig))
    out_grad[...] += dot_tn(gated, d_branch)

    edge = late.shape[2]

    def with_late(part, extra):
        return jnp.concatenate([part[: toks - edge], part[toks - edge :] + extra], axis=0)

    d_x = with_late(dx[0], late[0, i]) + flip_full(with_late(dx[1], late[1, i]))
    d_xz = (jnp.concatenate([d_x, d_zgate], axis=1) * valid).astype(BF16)
    d_hidden = dot_nt(d_xz, win[...])
    in_grad[...] += dot_tn(hid[...], d_xz)
    d_mod[0:1, :] = jnp.sum(d_hidden, axis=0, keepdims=True)
    d_mod[1:2, :] = jnp.sum(d_hidden * normed, axis=0, keepdims=True)
    d_mod[2:3, :] = jnp.sum(cot_f * branch_out, axis=0, keepdims=True)
    d_normed = d_hidden * (1.0 + scale)
    d_tokens[...] = cot_f + inv_std * (
        d_normed
        - jnp.mean(d_normed, axis=-1, keepdims=True)
        - normed * jnp.mean(d_normed * normed, axis=-1, keepdims=True)
    )


PARTS = 6
LAST_ROWS = 16


def reduce_rows(dim, inner, small):
    rows = inner + (2 * dim + small) * (inner // dim)
    unit = PARTS * LAST_ROWS * 32
    return -(-rows // unit) * unit


def reduce_kernel(
    plan, in_grad, out_grad, xp_grad, dtp_grad, rate_grad, tap_grad, tapb_grad, skip_grad, dtb_grad, d_mod, step,
    result, factors, own_rows,
    acc, sends, arrivals, gathered, mod_sum, mod_in, table, send_sem, recv_sem, small_send, small_recv,
):
    runs, groups, total_rows = plan
    dim = in_grad.shape[0]
    inner = out_grad.shape[0]
    slots = step.shape[0]
    seq_bits = [("seq", bit) for bit in range(int(math.log2(runs)))]
    dp_bits = [("dp", bit) for bit in range(int(math.log2(groups)))]
    all_bits = seq_bits + dp_bits
    count = len(all_bits)
    links = {key: across(*key) for key in all_bits}
    middle = all_bits[1:-1]
    turn = [part % max(len(middle), 1) for part in range(PARTS)]
    orders = [all_bits[:1] + middle[at:] + middle[:at] + all_bits[1:][-1:] for at in turn]
    part_rows = total_rows // PARTS

    def small_copy(stage):
        axis, bit = all_bits[stage]
        target = links[(axis, bit)][1]
        if axis == "seq":
            return remote(mod_sum, mod_in.at[stage], small_send.at[stage], small_recv.at[stage], target)
        size = 16 << bit
        at = pl.multiple_of(lax.axis_index("dp") // (1 << bit) * size, 16)
        here = table.at[pl.ds(at, size), :]
        return remote(here, here, small_send.at[stage], small_recv.at[stage], target)

    def fill_table():
        time_f = step[...].astype(F32)
        time_low = time_f * jax.nn.sigmoid(time_f)
        at = pl.multiple_of(lax.axis_index("dp") * 16, 16)
        own = jnp.concatenate([mod_sum[: 3 * slots, :], time_low, mod_sum[4 * slots :, :]], axis=0)
        own_rows[...] = own.astype(BF16)
        table[pl.ds(at, 16), :] = own.astype(BF16)

    def start_small(stage):
        if stage == len(seq_bits):
            fill_table()
        if stage < count:
            small_copy(stage).start()

    def end_small(stage):
        small_copy(stage).wait()
        if all_bits[stage][0] == "seq":
            mod_sum[...] += mod_in[stage]

    segments = [(lambda at, size: out_grad[at : at + size, :], inner)]
    for lane in range(0, 2 * inner, dim):
        segments.append((lambda at, size, lane=lane: in_grad[at : at + size, lane : lane + dim], dim))
    small = []
    for ref in (xp_grad, dtp_grad, rate_grad, tap_grad):
        small += [(lambda ref=ref, branch=branch: ref[branch], ref.shape[1]) for branch in range(2)]

    def tail():
        rows = [ref[branch] for ref in (tapb_grad, skip_grad, dtb_grad) for branch in range(2)]
        return jnp.concatenate(rows + [jnp.zeros((2, inner), F32)], axis=0)

    small.append((tail, 8))
    for lane in range(0, inner, dim):
        for get, size in small:
            segments.append((lambda at, size, get=get, lane=lane: get()[at : at + size, lane : lane + dim], size))
    total = sum(size for _, size in segments)
    segments.append((lambda at, size: jnp.zeros((size, dim), F32), total_rows - total))

    def assemble(part):
        low, high = part * part_rows, (part + 1) * part_rows
        at = 0
        for get, size in segments:
            first, last = max(at, low), min(at + size, high)
            if first < last:
                acc[first:last, :] = get(first - at, last - first)
            at += size

    starts = [part * part_rows for part in range(PARTS)]
    sizes = [part_rows] * PARTS
    history = [[] for _ in range(PARTS)]
    offsets = [part * (part_rows + LAST_ROWS * count) for part in range(PARTS)]
    flying = [None] * PARTS

    def scatter(part, stage):
        mine, target = links[orders[part][stage]]
        start, size = starts[part], sizes[part]
        split = size >= 2 * LAST_ROWS
        moved = size // 2 if split else size
        away = keep = start
        if split:
            away = pl.multiple_of(start + (1 - mine) * moved, LAST_ROWS)
            keep = pl.multiple_of(start + mine * moved, LAST_ROWS)
        history[part].append((start, size, split))
        at = offsets[part]
        offsets[part] += moved
        sends[at : at + moved, :] = acc[pl.ds(away, moved), :].astype(BF16)
        copy = remote(
            sends.at[pl.ds(at, moved), :], arrivals.at[pl.ds(at, moved), :], send_sem.at[part, stage],
            recv_sem.at[part, stage], target,
        )
        copy.start()
        starts[part], sizes[part] = keep, moved
        flying[part] = (copy, keep, moved, at, split)

    def settle(part):
        copy, keep, moved, at, split = flying[part]
        copy.wait()
        held = acc[pl.ds(keep, moved), :]
        if not split:
            held = held.astype(BF16).astype(F32)
        acc[pl.ds(keep, moved), :] = held + arrivals[at : at + moved, :].astype(F32)

    def gather(part, stage):
        start, size, split = history[part][stage]
        flying[part] = None
        if split:
            here = gathered.at[pl.ds(starts[part], sizes[part]), :]
            target = links[orders[part][stage]][1]
            flying[part] = remote(
                here, here, send_sem.at[part, count + stage], recv_sem.at[part, count + stage], target
            )
            flying[part].start()
            starts[part], sizes[part] = start, size

    mod_sum[...] = jnp.zeros(mod_sum.shape, F32)
    for i in range(slots):
        mod_sum[3 * i : 3 * i + 3, :] = d_mod[i]
    greet([links[key][1] for key in all_bits])
    start_small(0)
    for part in range(PARTS):
        assemble(part)
        scatter(part, 0)
    for stage in range(1, count):
        end_small(stage - 1)
        start_small(stage)
        for part in range(PARTS):
            settle(part)
            scatter(part, stage)
    end_small(count - 1)
    if not dp_bits:
        fill_table()
    for part in range(PARTS):
        settle(part)
        where = pl.ds(starts[part], sizes[part])
        gathered[where, :] = acc[where, :].astype(BF16)
        gather(part, count - 1)
    for stage in reversed(range(count - 1)):
        for part in range(PARTS):
            if flying[part] is not None:
                flying[part].wait()
            gather(part, stage)
    for part in range(PARTS):
        if flying[part] is not None:
            flying[part].wait()
        result[part * part_rows : (part + 1) * part_rows, :] = gathered[part * part_rows : (part + 1) * part_rows, :]
    factors[...] = table[...]


def finish_kernel(
    ranks, result, factors, own, step, ada,
    grad_time, grad_ada, grad_ada_bias, in_grad, tap_grad, tapb_grad, xp_grad, dtp_grad, dtb_grad, rate_grad, skip_grad, out_grad,
):
    rank, wide_rank = ranks
    dim = in_grad.shape[0]
    inner = out_grad.shape[0]
    slots = step.shape[0]
    states = rate_grad.shape[1]
    taps = tap_grad.shape[1]

    def rows(at, size):
        return result[at : at + size, :].astype(F32)

    out_grad[...] = rows(0, inner)
    at = inner
    for lane in range(0, 2 * inner, dim):
        in_grad[:, lane : lane + dim] = rows(at, dim)
        at += dim
    wide = wide_rank + 2 * states
    for first in range(0, inner, dim):
        lanes = slice(first, first + dim)
        for branch in range(2):
            part = rows(at, wide)
            xp_grad[branch, :, lanes] = jnp.concatenate([part[:rank], part[wide_rank:]], axis=0)
            at += wide
        for branch in range(2):
            dtp_grad[branch, :, lanes] = rows(at, wide_rank)[:rank]
            at += wide_rank
        for branch in range(2):
            rate_grad[branch, :, lanes] = rows(at, states)
            at += states
        tail = rows(at, 16)
        for branch in range(2):
            tap_grad[branch, :, lanes] = tail[branch * taps : (branch + 1) * taps]
        tapb_grad[:, lanes] = tail[2 * taps : 2 * taps + 2]
        skip_grad[:, lanes] = tail[2 * taps + 2 : 2 * taps + 4]
        dtb_grad[:, lanes] = tail[2 * taps + 4 : 2 * taps + 6]
        at += 16

    table = factors[...]
    length = table.shape[0]
    groups = length // 16
    items = groups * 8

    def pick(place):
        row = lax.broadcasted_iota(jnp.int32, (items, length), 0)
        col = lax.broadcasted_iota(jnp.int32, (items, length), 1)
        slot = row % 8
        wanted = row // 8 * 16 + place(slot)
        return dot(((col == wanted) & (slot < slots)).astype(BF16), table)

    times = pick(lambda slot: 3 * slots + slot).astype(BF16)
    time_f = step[...].astype(F32)
    time_sig = jax.nn.sigmoid(time_f)
    d_time = jnp.zeros((slots, dim), F32)
    mine = own[...].astype(F32)
    for part in range(3):
        mods = pick(lambda slot: 3 * slot + part)
        lanes = slice(part * dim, (part + 1) * dim)
        grad_ada[:, lanes] = dot_tn(times, mods.astype(BF16))
        grad_ada_bias[lanes] = jnp.sum(mods, axis=0)
        picked = jnp.concatenate([mine[3 * i + part : 3 * i + part + 1] for i in range(slots)], axis=0)
        d_time = d_time + dot_nt(picked.astype(BF16), ada[:, lanes])
    grad_time[...] = d_time * time_sig * (1.0 + time_f * (1.0 - time_sig))


def params(**more):
    return pltpu.CompilerParams(vmem_limit_bytes=VMEM_LIMIT, **more)


def spec(block, index):
    return pl.BlockSpec(block, index)


def per_device(
    tokens, timestep, counts, token_mask, ada_weight, ada_bias, input_weight, conv_weight, conv_bias, x_weight, dt_weight,
    dt_bias, decay_rate, skip_gain, output_weight, cotangent,
):
    slots, toks, dim = tokens.shape
    inner = output_weight.shape[0]
    rank = dt_weight.shape[1]
    states = decay_rate.shape[1]
    tap_count = conv_weight.shape[1]
    wide_rank = 32
    proj_rows = wide_rank + 2 * states
    blocks = toks // BLK
    runs = lax.axis_size("seq")
    groups = lax.axis_size("dp")
    counts2 = counts[:, None]
    x_rows = jnp.swapaxes(x_weight, 1, 2)

    def item(*block):
        return spec((None,) + block, lambda i: (i,) + (0,) * len(block))

    def whole(*block):
        return spec(block, lambda *_: (0,) * len(block))

    xe, dy, z_gate, hid, modulate = pl.pallas_call(
        functools.partial(enter_kernel, runs),
        grid=(slots,),
        in_specs=[
            whole(slots, toks, dim), item(toks, dim), whole(slots, toks), whole(1, 1), whole(slots, dim), whole(dim, 3 * dim),
            whole(3 * dim), whole(dim, 2 * inner), whole(inner, dim),
        ],
        out_specs=[
            item(2, HALO + toks, inner), item(2, toks, inner), item(toks, inner), item(toks, dim), item(1, 3 * dim),
        ],
        out_shape=[
            jax.ShapeDtypeStruct((slots, 2, HALO + toks, inner), BF16),
            jax.ShapeDtypeStruct((slots, 2, toks, inner), F32),
            jax.ShapeDtypeStruct((slots, toks, inner), F32),
            jax.ShapeDtypeStruct((slots, toks, dim), BF16),
            jax.ShapeDtypeStruct((slots, 1, 3 * dim), F32),
        ],
        scratch_shapes=[
            pltpu.VMEM((slots, HALO, dim), BF16), pltpu.VMEM((slots, HALO, dim), BF16), pltpu.VMEM((slots, toks), jnp.int32),
            pltpu.VMEM((slots, toks), jnp.int32), pltpu.SemaphoreType.DMA((4,)), pltpu.SemaphoreType.DMA((4,)),
        ],
        compiler_params=params(collective_id=1, has_side_effects=True),
        name="enter",
    )(
        tokens, cotangent, token_mask, counts2, timestep, ada_weight, ada_bias, input_weight, output_weight,
    )

    def unit(*block):
        return spec((None, None) + block, lambda b, i: (i, b) + (0,) * len(block))

    def branch(*block):
        return spec((None,) + block, lambda b, i: (b,) + (0,) * len(block))

    def unit_shape(*block, kind=F32):
        return jax.ShapeDtypeStruct((slots, 2) + block, kind)

    act, dsilu, delta, sig, proj, end, back, total, starts, sums, tiles, xwt, dtw, s_first, lam_first = pl.pallas_call(
        functools.partial(first_kernel, runs, slots),
        grid=(2, slots),
        in_specs=[
            unit(HALO + toks, inner), unit(toks, inner), branch(tap_count, inner), whole(2, inner),
            branch(rank + 2 * states, inner), branch(rank, inner), whole(2, inner), branch(states, inner),
        ],
        out_specs=[
            unit(toks, inner), unit(toks, inner), unit(toks, inner), unit(toks, inner), unit(proj_rows, toks),
            unit(states, inner), unit(states, inner), unit(1, inner), unit(blocks, states, inner), unit(blocks, 1, inner),
            unit(toks, 2 * states, 128), branch(proj_rows, inner), branch(wide_rank, inner),
            whole(slots, states, inner), whole(slots, states, inner),
        ],
        out_shape=[
            unit_shape(toks, inner, kind=BF16), unit_shape(toks, inner), unit_shape(toks, inner), unit_shape(toks, inner),
            unit_shape(proj_rows, toks), unit_shape(states, inner), unit_shape(states, inner), unit_shape(1, inner),
            unit_shape(blocks, states, inner), unit_shape(blocks, 1, inner), unit_shape(toks, 2 * states, 128),
            jax.ShapeDtypeStruct((2, proj_rows, inner), BF16), jax.ShapeDtypeStruct((2, wide_rank, inner), BF16),
            jax.ShapeDtypeStruct((slots, states, inner), F32), jax.ShapeDtypeStruct((slots, states, inner), F32),
        ],
        scratch_shapes=[
            pltpu.VMEM((toks, inner), F32), pltpu.VMEM((2, BLK, states, inner), F32), pltpu.VMEM((8, inner), F32),
            pltpu.VMEM((states, inner), F32), pltpu.VMEM((2 * states * toks, 128), F32),
            pltpu.VMEM((4 * states, 2 * states * 128), BF16), pltpu.VMEM((slots, states, inner), F32),
            pltpu.VMEM((slots, states, inner), F32), pltpu.VMEM((slots, 1, inner), F32), pltpu.VMEM((states, inner), F32),
            *exchange_shapes(runs, slots, states, inner),
        ],
        compiler_params=params(collective_id=2, has_side_effects=True),
        name="first",
    )(xe, dy, conv_weight, conv_bias, x_rows, dt_weight, dt_bias, decay_rate)

    vmem = pl.BlockSpec(memory_space=pltpu.VMEM)
    last = spec((slots, None, states, inner), lambda b, i: (0, 1, 0, 0))
    last_total = spec((slots, None, 1, inner), lambda b, i: (0, 1, 0, 0))
    last_branch = spec((None, states, inner), lambda b, i: (1, 0, 0))

    y, dx, late, rate_grad, skip_grad, dtb_grad, dtp_grad, xp_grad, tap_grad, tapb_grad = pl.pallas_call(
        functools.partial(second_kernel, runs),
        grid=(2, slots),
        in_specs=[
            whole(slots, states, inner), whole(slots, states, inner), last, last, last_total, last_branch,
            unit(blocks, states, inner), unit(blocks, 1, inner), unit(toks, 2 * states, 128), branch(states, inner), unit(HALO + toks, inner), unit(toks, inner),
            unit(toks, inner), unit(toks, inner), unit(toks, inner), unit(toks, inner), unit(proj_rows, toks),
            branch(proj_rows, inner), branch(wide_rank, inner),
            branch(tap_count, inner), whole(2, inner),
        ],
        out_specs=[
            unit(toks, inner), unit(toks, inner), whole(2, slots, 8, inner), branch(states, inner), branch(1, inner), branch(1, inner),
            branch(wide_rank, inner), branch(proj_rows, inner), branch(tap_count, inner), branch(1, inner),
        ],
        out_shape=[
            unit_shape(toks, inner), unit_shape(toks, inner), jax.ShapeDtypeStruct((2, slots, 8, inner), F32),
        ] + [
            jax.ShapeDtypeStruct((2, rows, inner), F32) for rows in (states, 1, 1, wide_rank, proj_rows, tap_count, 1)
        ],
        scratch_shapes=[
            pltpu.VMEM((states, inner), F32), pltpu.VMEM((states, inner), F32), pltpu.VMEM((toks + BLK, inner), F32), pltpu.VMEM((toks + BLK, BLK * states), BF16),
            pltpu.VMEM((toks, BLK * states), BF16),
            pltpu.VMEM((2, BLK, states, inner), F32),
            pltpu.VMEM((2, (BLK + 1) * states, inner), BF16), pltpu.VMEM((2, BLK * states, inner), BF16),
            pltpu.VMEM((2, BLK * states, inner), BF16), pltpu.VMEM((2, BLK // 4 * states, inner), BF16),
            pltpu.VMEM((2, BLK * states, 256), BF16), pltpu.VMEM((states, inner), F32),
            pltpu.VMEM((toks + BLK, inner), F32), pltpu.VMEM((toks + BLK, inner), F32),
            pltpu.VMEM((toks + BLK, BLK * states), BF16), pltpu.VMEM((toks + BLK, BLK * states), BF16),
            pltpu.VMEM((2, slots, 8, inner), F32), pltpu.VMEM((2, slots, 8, inner), F32),
            pltpu.SemaphoreType.DMA((2,)), pltpu.SemaphoreType.DMA((2,)), pltpu.VMEM((states, inner), F32),
            pltpu.VMEM((slots, states, inner), F32), pltpu.VMEM((slots, states, inner), F32),
            *exchange_shapes(runs, slots, states, inner),
        ],
        compiler_params=params(collective_id=3, has_side_effects=True),
        name="second",
    )(
        s_first, lam_first, end, back, total, decay_rate, starts, sums, tiles, decay_rate, xe, act, dsilu, delta,
        sig, dy, proj, xwt, dtw, conv_weight, skip_gain,
    )

    mixed, d_tokens, d_mod, out_grad, in_grad = pl.pallas_call(
        third_kernel,
        grid=(slots,),
        in_specs=[
            item(toks, dim), item(toks, dim), item(1, 3 * dim), whole(slots, toks), whole(1, 1), item(toks, dim),
            item(toks, inner), item(2, toks, inner), item(2, toks, inner), whole(2, slots, 8, inner), whole(dim, 2 * inner),
            whole(inner, dim),
        ],
        out_specs=[item(toks, dim), item(toks, dim), item(3, dim), whole(inner, dim), whole(dim, 2 * inner)],
        out_shape=[
            jax.ShapeDtypeStruct((slots, toks, dim), BF16), jax.ShapeDtypeStruct((slots, toks, dim), F32),
            jax.ShapeDtypeStruct((slots, 3, dim), F32), jax.ShapeDtypeStruct((inner, dim), F32),
            jax.ShapeDtypeStruct((dim, 2 * inner), F32),
        ],
        compiler_params=params(),
        name="third",
    )(
        tokens, cotangent, modulate, token_mask, counts2, hid, z_gate, y, dx, late, input_weight, output_weight,
    )

    small = 2 * (proj_rows + wide_rank + states + tap_count) + 8
    rows = reduce_rows(dim, inner, small)
    stages = int(math.log2(runs)) + int(math.log2(groups))
    result, factors, own = pl.pallas_call(
        functools.partial(reduce_kernel, (runs, groups, rows)),
        in_specs=[vmem] * 11,
        out_specs=[vmem] * 3,
        out_shape=[
            jax.ShapeDtypeStruct((rows, dim), BF16), jax.ShapeDtypeStruct((16 * groups, dim), BF16),
            jax.ShapeDtypeStruct((16, dim), BF16),
        ],
        scratch_shapes=[
            pltpu.VMEM((rows, dim), F32), pltpu.VMEM((rows + PARTS * LAST_ROWS * stages, dim), BF16),
            pltpu.VMEM((rows + PARTS * LAST_ROWS * stages, dim), BF16),
            pltpu.VMEM((rows, dim), BF16), pltpu.VMEM((16, dim), F32),
            pltpu.VMEM((max(int(math.log2(runs)), 1), 16, dim), F32), pltpu.VMEM((16 * groups, dim), BF16),
            pltpu.SemaphoreType.DMA((PARTS, 2 * stages)), pltpu.SemaphoreType.DMA((PARTS, 2 * stages)),
            pltpu.SemaphoreType.DMA((stages,)), pltpu.SemaphoreType.DMA((stages,)),
        ],
        compiler_params=params(collective_id=4, has_side_effects=True),
        name="reduce",
    )(
        in_grad, out_grad, xp_grad, dtp_grad, rate_grad, tap_grad, tapb_grad, skip_grad, dtb_grad, d_mod, timestep,
    )

    (
        d_time, grad_ada, grad_ada_bias, in_grad, tap_grad, tapb_grad, xp_grad, dtp_grad, dtb_grad, rate_grad, skip_grad,
        out_grad,
    ) = pl.pallas_call(
        functools.partial(finish_kernel, (rank, wide_rank)),
        in_specs=[vmem] * 5,
        out_specs=[vmem] * 12,
        out_shape=[
            jax.ShapeDtypeStruct(shape, F32)
            for shape in (
                (slots, dim), (dim, 3 * dim), (3 * dim,), (dim, 2 * inner), (2, tap_count, inner), (2, inner),
                (2, rank + 2 * states, inner), (2, rank, inner), (2, inner), (2, states, inner), (2, inner), (inner, dim),
            )
        ],
        compiler_params=params(),
        name="finish",
    )(result, factors, own, timestep, ada_weight)
    return (
        mixed, d_tokens, d_time, grad_ada, grad_ada_bias, in_grad, tap_grad, tapb_grad, jnp.swapaxes(xp_grad, 1, 2), dtp_grad, dtb_grad,
        rate_grad, skip_grad, out_grad,
    )


def solution(mesh):
    runs = P("dp", "seq", None)
    return jax.shard_map(
        per_device,
        mesh=mesh,
        in_specs=(runs, P("dp", None), P("dp"), P("dp", "seq")) + (P(),) * 11 + (runs,),
        out_specs=(runs, runs, P("dp", None)) + (P(),) * 11,
        check_vma=False,
    )
```

```python
import functools
import math

import jax
import jax.numpy as jnp
from jax import lax
from jax.experimental import pallas as pl
from jax.experimental.pallas import tpu as pltpu
from jax.sharding import PartitionSpec as P

EPSILON = 1e-06
BLK = 16
HALO = 16
LOG2E = math.log2(math.e)
F32, BF16 = jnp.float32, jnp.bfloat16
NT = (((1,), (1,)), ((), ()))
TN = (((0,), (0,)), ((), ()))
VMEM_LIMIT = 60 << 20
MESH = pl.DeviceIdType.MESH


def dot(a, b):
    return jnp.dot(a, b, preferred_element_type=F32)


def dot_nt(a, b):
    return lax.dot_general(a, b, NT, preferred_element_type=F32)


def dot_tn(a, b):
    return lax.dot_general(a, b, TN, preferred_element_type=F32)


def flip_full(value):
    turned = lax.broadcasted_iota(jnp.int32, (8, value.shape[1]), 0)
    groups = [value[at : at + 8] for at in range(0, value.shape[0], 8)]
    return jnp.concatenate([jnp.take_along_axis(group, 7 - turned, axis=0) for group in reversed(groups)], axis=0)


def flip_low(value):
    return flip_full(value.astype(F32)).astype(BF16)


def normalise(tokens_f):
    centered = tokens_f - jnp.mean(tokens_f, axis=-1, keepdims=True)
    inv_std = lax.rsqrt(jnp.mean(centered * centered, axis=-1, keepdims=True) + EPSILON)
    return centered * inv_std, inv_std


def eye(size):
    rows = lax.broadcasted_iota(jnp.int32, (size, size), 0)
    cols = lax.broadcasted_iota(jnp.int32, (size, size), 1)
    return (rows == cols).astype(BF16)


def as_column(row):
    return dot_nt(eye(row.shape[1]), jnp.broadcast_to(row.astype(F32).astype(BF16), (8, row.shape[1])))[:, :1]


def remote(src, dst, send_sem, recv_sem, target):
    return pltpu.make_async_remote_copy(
        src_ref=src, dst_ref=dst, send_sem=send_sem, recv_sem=recv_sem, device_id=target, device_id_type=MESH
    )


def greet(targets):
    barrier = pltpu.get_barrier_semaphore()
    for target in targets:
        pl.semaphore_signal(barrier, inc=1, device_id=target, device_id_type=MESH)
    pl.semaphore_wait(barrier, len(targets))


def greet_line(me, runs, others=()):
    barrier = pltpu.get_barrier_semaphore()
    for target in others:
        pl.semaphore_signal(barrier, inc=1, device_id=target, device_id_type=MESH)

    @pl.when(me > 0)
    def _():
        pl.semaphore_signal(barrier, inc=1, device_id={"seq": me - 1}, device_id_type=MESH)

    @pl.when(me < runs - 1)
    def _():
        pl.semaphore_signal(barrier, inc=1, device_id={"seq": me + 1}, device_id_type=MESH)

    neighbours = (me + runs - 1) // runs + (2 * runs - 2 - me) // runs
    pl.semaphore_wait(barrier, neighbours + len(others))


def swap_along_line(me, runs, ups, downs, start):
    up = [remote(src, dst, ss, rs, {"seq": me + 1}) for src, dst, ss, rs in ups]
    down = [remote(src, dst, ss, rs, {"seq": me - 1}) for src, dst, ss, rs in downs]

    @pl.when(me < runs - 1)
    def _():
        for copy in up:
            if start:
                copy.start()
            else:
                copy.wait_send()
        if not start:
            for copy in down:
                copy.wait_recv()

    @pl.when(me > 0)
    def _():
        for copy in down:
            if start:
                copy.start()
            else:
                copy.wait_send()
        if not start:
            for copy in up:
                copy.wait_recv()


def enter_kernel(
    runs, tok, cot, mask, counts, step, ada, ada_bias, win, wout,
    xe, dy, z_out, hid_out, mod_out,
    mods, prev_tok, next_tok, prev_mask, next_mask, send_sem, recv_sem,
):
    slots, toks, dim = tok.shape
    inner = wout.shape[0]
    me = lax.axis_index("seq")
    i = pl.program_id(0)
    ups = [
        (tok.at[:, pl.ds(toks - HALO, HALO), :], prev_tok, send_sem.at[0], recv_sem.at[0]),
        (mask, prev_mask, send_sem.at[1], recv_sem.at[1]),
    ]
    downs = [
        (tok.at[:, pl.ds(0, HALO), :], next_tok, send_sem.at[2], recv_sem.at[2]),
        (mask, next_mask, send_sem.at[3], recv_sem.at[3]),
    ]

    @pl.when(i == 0)
    def _():
        greet_line(me, runs)
        swap_along_line(me, runs, ups, downs, True)

        @pl.when(me == 0)
        def _():
            prev_tok[...] = jnp.zeros(prev_tok.shape, BF16)
            prev_mask[...] = jnp.zeros(prev_mask.shape, jnp.int32)

        @pl.when(me == runs - 1)
        def _():
            next_tok[...] = jnp.zeros(next_tok.shape, BF16)
            next_mask[...] = jnp.zeros(next_mask.shape, jnp.int32)

    live = (counts[...] > i).astype(F32)

    @pl.when(i == 0)
    def _():
        time_f = step[...].astype(F32)
        time_low = (time_f * jax.nn.sigmoid(time_f)).astype(BF16)
        mods[...] = dot(time_low, ada[...]) + ada_bias[...].reshape(1, 3 * dim)

    mod = mods[pl.ds(i, 1), :]
    mod_out[...] = mod
    shift, scale, gate = mod[:, :dim], mod[:, dim : 2 * dim], mod[:, 2 * dim :]

    def hidden_of(part):
        normed, _ = normalise(part.astype(F32))
        return (normed * (1.0 + scale) + shift).astype(BF16)

    hid = hidden_of(tok[i])
    hid_out[...] = hid
    xz = dot(hid, win[...]) * (as_column(mask[pl.ds(i, 1), :]) * live)
    x_low = xz[:, :inner].astype(BF16)
    z = xz[:, inner:]
    z_out[...] = z
    d_branch = (cot[...].astype(F32) * gate).astype(BF16)
    d_summed = dot_nt(d_branch, wout[...]) * z * jax.nn.sigmoid(z)
    dy[0] = d_summed
    dy[1] = flip_full(d_summed)
    xe[0, HALO:, :] = x_low
    xe[1, HALO:, :] = flip_low(x_low)

    @pl.when(i == 0)
    def _():
        swap_along_line(me, runs, ups, downs, False)

    rims = jnp.concatenate([prev_tok[i], next_tok[i]], axis=0)
    prev_col = as_column(prev_mask[pl.ds(i, 1), :])[toks - HALO :]
    next_col = as_column(next_mask[pl.ds(i, 1), :])[:HALO]
    rim_x = dot(hidden_of(rims), win[:, :inner]) * (jnp.concatenate([prev_col, next_col], axis=0) * live)
    rim_x = rim_x.astype(BF16)
    xe[0, :HALO, :] = rim_x[:HALO]
    xe[1, :HALO, :] = flip_low(rim_x[HALO:])


def columns(inner, width=128):
    return [slice(at, at + width) for at in range(0, inner, width)]


def twice(row8):
    return jnp.concatenate([row8, row8], axis=0)


def spread(ref, index):
    return twice(ref[pl.ds(index, 8, stride=0), :])


def lay_out(wide, rows, picks):
    count, toks = rows.shape
    high = rows.astype(BF16).astype(F32)
    halves = jnp.concatenate([high, rows - high], axis=0).T.astype(BF16)
    for n in range(0, count, 2):
        pair = dot(halves, picks[:, n * 128 : (n + 2) * 128])
        for t in range(0, toks, 8):
            for k in range(2):
                at = 8 * (count * (t // 8) + n + k)
                wide[at : at + 8, :] = pair[t : t + 8, k * 128 : (k + 1) * 128]


def wide_tile(wide, i, count):
    at = 8 * count * (i // 8) + i % 8
    return jnp.concatenate([wide[pl.ds(at + 64 * n, 8, stride=8), :] for n in range(count // 8)], axis=0)


def across_lanes(tile, inner):
    return jnp.concatenate([tile] * (inner // 128), axis=1)


def softplus_parts(pre):
    e = jnp.exp2(-LOG2E * jnp.abs(pre))
    more = jnp.where(e < 1e-3, e - 0.5 * e * e, jnp.log(1.0 + e))
    return jnp.maximum(pre, 0.0) + more, jax.nn.sigmoid(pre)


def bit_of(index, bit):
    return (index // (1 << bit)) % 2


def across(axis, bit):
    me = lax.axis_index(axis)
    mine = bit_of(me, bit)
    return mine, {axis: me + (1 - 2 * mine) * (1 << bit)}


class Exchange:
    def __init__(self, runs, branch, ends, backs, totals, rate, results, group, span, pre, pre_span, sends, arrivals, sems):
        self.branch, self.rate = branch, rate
        self.sources, self.totals, self.results = (ends, backs), totals, results
        self.group, self.span, self.pre, self.pre_span = group, span, pre, pre_span
        self.sends, self.arrivals, self.sems = sends, arrivals, sems
        self.links = [across("seq", bit) for bit in range(int(math.log2(runs)))]
        self.slots, self.states, self.inner = ends.shape

    def flow(self, kind):
        return kind if self.branch == 0 else 1 - kind

    def targets(self):
        return [target for _, target in self.links]

    def copy(self, stage, kind):
        at = 2 * stage + kind
        return remote(
            self.sends.at[at], self.arrivals.at[at], self.sems.at[0, at], self.sems.at[1, at], self.links[stage][1]
        )

    def send(self, stage, kind):
        rows = self.slots * self.states
        at = 2 * stage + kind
        for i in range(self.slots):
            self.sends[at, i * self.states : (i + 1) * self.states, :] = self.group[kind, i].astype(BF16)
        high = self.span[kind].astype(BF16).astype(F32)
        self.sends[at, rows:, :] = jnp.concatenate([high, self.span[kind] - high], axis=0).astype(BF16)
        self.copy(stage, kind).start()

    def join(self, stage, kind, last):
        mine = self.links[stage][0]
        self.copy(stage, kind).wait()
        at = 2 * stage + kind
        earlier = (mine == 1) if self.flow(kind) == 0 else (mine == 0)
        both = self.arrivals[at, self.slots * self.states :, :].astype(F32)
        length = both[: both.shape[0] // 2] + both[both.shape[0] // 2 :]
        own_span, pre_span = self.span[kind], self.pre_span[kind]
        second_span = jnp.where(earlier, own_span, length)
        rate = self.rate[...] * -LOG2E
        for i in range(self.slots):
            state = self.arrivals[at, i * self.states : (i + 1) * self.states, :].astype(F32)
            before = self.pre[kind, i]
            self.pre[kind, i] = jnp.where(earlier, state * jnp.exp2(rate * pre_span[i : i + 1]) + before, before)
            if not last:
                own = self.group[kind, i]
                first, second = jnp.where(earlier, state, own), jnp.where(earlier, own, state)
                self.group[kind, i] = first * jnp.exp2(rate * second_span[i : i + 1]) + second
        self.pre_span[kind] = jnp.where(earlier, length + pre_span, pre_span)
        if not last:
            self.span[kind] = own_span + length

    def points(self):
        count = len(self.links)

        def begin():
            self.pre[...] = jnp.zeros(self.pre.shape, F32)
            self.pre_span[...] = jnp.zeros(self.pre_span.shape, F32)
            self.span[...] = jnp.zeros(self.span.shape, F32)
            for kind in range(2):
                for i in range(self.slots):
                    self.group[kind, i] = self.sources[kind][i]
                    self.span[kind, i : i + 1, :] = self.totals[i]
                if count:
                    self.send(0, kind)

        def step(stage):
            last = stage == count - 1
            for kind in range(2):
                self.join(stage, kind, last)
                if not last:
                    self.send(stage + 1, kind)

        def end():
            for kind in range(2):
                for i in range(self.slots):
                    self.results[kind][i] = self.pre[kind, i]

        return [begin] + [functools.partial(step, stage) for stage in range(count)] + [end]


def exchange_shapes(runs, slots, states, inner):
    pairs = max(int(math.log2(runs)), 1)
    span_rows = -(-slots // 8) * 8
    return [
        pltpu.VMEM((2, slots, states, inner), F32), pltpu.VMEM((2, span_rows, inner), F32),
        pltpu.VMEM((2, slots, states, inner), F32), pltpu.VMEM((2, span_rows, inner), F32),
        pltpu.VMEM((2 * pairs, slots * states + 2 * span_rows, inner), BF16),
        pltpu.VMEM((2 * pairs, slots * states + 2 * span_rows, inner), BF16),
        pltpu.SemaphoreType.DMA((2, 2 * pairs)),
    ]


def beside(points, step, first, count):
    for at in range(min(len(points), count)):
        todo = points[at:] if at == count - 1 else points[at : at + 1]

        @pl.when(step == first + at)
        def _():
            for point in todo:
                point()


def first_kernel(
    runs, slots, xe, dy, taps, tap_bias, x_rows, dt_rows, dt_bias, rate,
    act_out, dsilu_out, delta_out, sig_out, proj_out, end_out, back_out, total_out, starts_out, sums_out, tiles, xwt, dtw, s_in, lam_in,
    dx, decay, through, rate2, wide, picks, ends, backs, totals, first_rate, *exchange_scratch,
):
    toks, inner = dy.shape
    states = rate.shape[0]
    blocks = toks // BLK
    rank = dtw.shape[0]
    tap_count = taps.shape[0]
    branch, item = pl.program_id(0), pl.program_id(1)
    exchange = Exchange(runs, 0, ends, backs, totals, first_rate, (s_in, lam_in), *exchange_scratch)

    @pl.when((branch == 0) & (item == 0))
    def _():
        greet(exchange.targets())
        first_rate[...] = rate[...]

    beside(exchange.points(), branch * slots + item, slots, slots)

    @pl.when(item == 0)
    def _():
        rate2[...] = rate[...] * -LOG2E
        picks[...] = (
            lax.broadcasted_iota(jnp.int32, picks.shape, 0) % (2 * states)
            == lax.broadcasted_iota(jnp.int32, picks.shape, 1) // 128
        ).astype(BF16)
        held = dt_rows.shape[0]
        rows = x_rows[...].astype(F32)
        gap = jnp.zeros((rank - held, inner), F32)
        xwt[...] = jnp.concatenate([rows[:held], gap, rows[held:]], axis=0).astype(BF16)
        dtw[...] = jnp.concatenate([dt_rows[...].astype(F32), gap], axis=0).astype(BF16)

    tap_row, dt_row = tap_bias[pl.ds(branch, 1), :], dt_bias[pl.ds(branch, 1), :]
    for cols in columns(inner):
        x_f = xe[:, cols].astype(F32)
        conv = tap_row[:, cols] + taps[tap_count - 1 : tap_count, cols] * x_f[HALO:]
        for k in range(tap_count - 1):
            conv = conv + taps[k : k + 1, cols] * pltpu.roll(x_f, tap_count - 1 - k, 0)[HALO:]
        open_part = jax.nn.sigmoid(conv)
        act_f = conv * open_part
        act_out[:, cols] = act_f.astype(BF16)
        dsilu_out[:, cols] = open_part + act_f * (1.0 - open_part)
    proj = dot_nt(xwt[...], act_out[...])
    proj_out[...] = proj
    dt_low = proj[:rank, :].astype(BF16)
    for cols in columns(inner, 256):
        pre = dot_tn(dt_low, dtw[:, cols]) + dt_row[:, cols]
        delta, slope = softplus_parts(pre)
        delta_out[:, cols] = delta
        sig_out[:, cols] = slope
        dx[:, cols] = delta * act_out[:, cols].astype(F32)
    lay_out(wide, proj[rank:, :], picks)
    end_out[...] = jnp.zeros((states, inner), F32)
    back_out[...] = jnp.zeros((states, inner), F32)
    through[...] = jnp.zeros((8, inner), F32)

    def one_block(j, slot):
        t0 = pl.multiple_of(j * BLK, BLK)
        dr, xr, yr = (ref.at[pl.ds(t0, BLK), :] for ref in (delta_out, dx, dy))
        count = 2 * states
        wide_rows = wide.at[pl.ds(pl.multiple_of(j * (BLK * count), BLK * count), BLK * count), :]
        s = end_out[...]
        starts_out[j] = s
        before = through[...]
        sums_out[j] = before[:1, :]
        rates = rate2[...]
        for i in range(BLK):
            a = jnp.exp2(spread(dr, i) * rates)
            decay[slot, i] = a
            tile = wide_tile(wide_rows, i, count)
            tiles[t0 + i] = tile
            s = a * s + spread(xr, i) * across_lanes(tile[:states], inner)
        end_out[...] = s
        m = jnp.zeros((states, inner), F32)
        for i in reversed(range(BLK)):
            m = decay[slot, i] * (m + spread(yr, i) * across_lanes(tiles[t0 + i, states:], inner))
        back_out[...] = back_out[...] + m * jnp.exp2(twice(before) * rates)
        through[...] = before + jnp.sum(dr[...], axis=0, keepdims=True)

    def block_step(k, _):
        one_block(2 * k, 0)
        one_block(2 * k + 1, 1)
        return 0

    lax.fori_loop(0, blocks // 2, block_step, 0)
    total_out[...] = through[:1, :]

    @pl.when(branch == 0)
    def _():
        ends[item] = end_out[...]
        backs[item] = back_out[...]
        totals[item] = through[:1, :]


def second_kernel(
    runs, s_first, lam_first, ends, backs, totals, last_rate, starts, sums, tiles, rate, xe, act, dsilu, delta, sig, dy, proj, xwt, dtw, taps, skip,
    y_out, dx_out, late_out, rate_grad, skip_grad, dtb_grad, dtp_grad, xp_grad, tap_grad, tapb_grad,
    rate2, carry, dxs, bdiag, cdiag, decay, states_low, lam_low, rq_low, qd_low, dots, racc, gsum, hsum, db, dc,
    rims, late, send_sem, recv_sem, d_pre_low, s_in, s_last, lam_last, *exchange_scratch,
):
    toks, inner = dy.shape
    states = rate.shape[0]
    blocks = toks // BLK
    rank = dtw.shape[0]
    tap_count = taps.shape[0]
    item = pl.program_id(1)
    last_item = item == pl.num_programs(1) - 1
    me = lax.axis_index("seq")
    downs = [(rims.at[0], late.at[0], send_sem.at[0], recv_sem.at[0])]
    ups = [(rims.at[1], late.at[1], send_sem.at[1], recv_sem.at[1])]

    branch = pl.program_id(0)
    slots = ends.shape[0]
    exchange = Exchange(runs, 1, ends, backs, totals, last_rate, (s_last, lam_last), *exchange_scratch)

    @pl.when((item == 0) & (branch == 0))
    def _():
        greet_line(me, runs, exchange.targets())

    beside(exchange.points(), branch * slots + item, 0, slots)

    @pl.when(branch == 0)
    def _():
        s_in[...] = s_first[item]
        carry[...] = lam_first[item]

    @pl.when(branch == 1)
    def _():
        s_in[...] = s_last[item]
        carry[...] = lam_last[item]

    gain = skip[pl.ds(pl.program_id(0), 1), :]
    rate2[...] = rate[...] * -LOG2E
    width = BLK * states

    @pl.when(item == 0)
    def _():
        for ref in (rate_grad, skip_grad, dtb_grad, dtp_grad, xp_grad, tap_grad, tapb_grad):
            ref[...] = jnp.zeros(ref.shape, ref.dtype)

    for cols in columns(inner):
        dxs[:toks, cols] = delta[:, cols] * act[:, cols].astype(F32)
    fold = (
        lax.broadcasted_iota(jnp.int32, (states, width), 1) % states == lax.broadcasted_iota(jnp.int32, (states, width), 0)
    ).astype(BF16)
    own = lax.broadcasted_iota(jnp.int32, (toks, width), 0) % BLK == lax.broadcasted_iota(jnp.int32, (toks, width), 1) // states
    bdiag[:toks, :] = jnp.where(own, dot_tn(proj[rank : rank + states, :].astype(BF16), fold), 0.0).astype(BF16)
    cdiag[...] = jnp.where(own, dot_tn(proj[rank + states :, :].astype(BF16), fold), 0.0).astype(BF16)
    mine = own[:BLK]
    picks = mine.astype(BF16)
    sides = (
        lax.broadcasted_iota(jnp.int32, (2 * BLK, 256), 0) // BLK == lax.broadcasted_iota(jnp.int32, (2 * BLK, 256), 1) // 128
    ).astype(BF16)
    racc[...] = jnp.zeros((states, inner), F32)
    qd_low[1] = jnp.zeros(qd_low.shape[1:], BF16)

    def lane_sum(wide):
        part = [wide[:, at : at + 128] for at in range(0, inner, 128)]
        while len(part) > 1:
            part = [sum(part[at : at + 2]) for at in range(0, len(part), 2)]
        return part[0]

    def products(slot, j):
        t0 = pl.multiple_of(j * BLK, BLK)
        gsum[pl.ds(t0, BLK), :] = dot(bdiag[pl.ds(t0, BLK), :], lam_low[slot])
        hsum[pl.ds(t0, BLK), :] = dot(picks, rq_low[slot])
        racc[...] += dot(fold[:, : BLK // 4 * states], qd_low[slot])
        both = dot_nt(sides, dots[slot])
        dc[pl.ds(t0, BLK), :] = jnp.where(mine, both[:BLK], 0.0).astype(BF16)
        db[pl.ds(t0, BLK), :] = jnp.where(mine, both[BLK:], 0.0).astype(BF16)

    def one_block(slot, j):
        t0 = pl.multiple_of(j * BLK, BLK)
        dr, xr, yr = (ref.at[pl.ds(t0, BLK), :] for ref in (delta, dxs, dy))
        tile = tiles.at[pl.ds(t0, BLK)]
        r2 = rate2[...]
        r_low = rate[...].astype(BF16)
        s = starts[j] + s_in[...] * jnp.exp2(twice(jnp.broadcast_to(sums[j], (8, inner))) * r2)
        states_low[slot, :states, :] = s.astype(BF16)
        for i in range(BLK):
            a = jnp.exp2(spread(dr, i) * r2)
            decay[slot, i] = a
            s = a * s + spread(xr, i) * across_lanes(tile[i, :states], inner)
            s_low = s.astype(BF16)
            states_low[slot, (i + 1) * states : (i + 2) * states, :] = s_low
            dots[slot, i * states : (i + 1) * states, :128] = lane_sum(s_low * spread(yr, i).astype(BF16))
        y_out[pl.ds(t0, BLK), :] = dot(cdiag[pl.ds(t0, BLK), :], states_low[slot, states:, :])
        cr = carry[...]
        qds = []
        for i in reversed(range(BLK)):
            lam = cr + spread(yr, i) * across_lanes(tile[i, states:], inner)
            l_low = lam.astype(BF16)
            lam_low[slot, i * states : (i + 1) * states, :] = l_low
            dots[slot, i * states : (i + 1) * states, 128:] = lane_sum(l_low * spread(xr, i).astype(BF16))
            cr = decay[slot, i] * lam
            q = cr.astype(BF16) * states_low[slot, i * states : (i + 1) * states, :]
            rq_low[slot, i * states : (i + 1) * states, :] = q * r_low
            qds.append(q * spread(dr, i).astype(BF16))
            if i % 4 == 0:
                qd_low[slot, i // 4 * states : (i // 4 + 1) * states, :] = (qds[0] + qds[1]) + (qds[2] + qds[3])
                qds = []
        carry[...] = cr

    def block_step(k, _):
        j = blocks - 1 - 2 * k
        products(1, jnp.where(k == 0, blocks, j + 1))
        one_block(0, j)
        products(0, j)
        one_block(1, j - 1)
        return 0

    lax.fori_loop(0, blocks // 2, block_step, 0)
    products(1, 0)

    rate_grad[...] += -racc[...]
    for cols in columns(inner):
        act_f = act[:, cols].astype(F32)
        skip_grad[:, cols] += jnp.sum(dy[:, cols] * act_f, axis=0, keepdims=True)
        y_out[:, cols] += gain[:, cols] * act_f
        d_pre = (act_f * gsum[:toks, cols] - hsum[:toks, cols]) * sig[:, cols]
        dtb_grad[:, cols] += jnp.sum(d_pre, axis=0, keepdims=True)
        d_pre_low[:, cols] = d_pre.astype(BF16)
    held = dtp_grad.shape[0]
    dtp_grad[...] += dot(proj[:rank, :].astype(BF16), d_pre_low[...])[:held]
    d_proj = jnp.concatenate(
        [dot_nt(dtw[...], d_pre_low[...]), dot_nt(fold, db[:toks, :]), dot_nt(fold, dc[:toks, :])], axis=0
    ).astype(BF16)
    xp_new = dot(d_proj, act[...])
    xp_grad[:held, :] += xp_new[:held]
    xp_grad[held:, :] += xp_new[rank:]
    window = HALO + toks
    for wide_cols in columns(inner, 256):
        through = dot_tn(d_proj, xwt[:, wide_cols])
        for at in columns(256):
            cols = slice(wide_cols.start + at.start, wide_cols.start + at.stop)
            d_act = delta[:, cols] * gsum[:toks, cols] + gain[:, cols] * dy[:, cols] + through[:, at]
            d_conv = d_act * dsilu[:, cols]
            tapb_grad[:, cols] += jnp.sum(d_conv, axis=0, keepdims=True)
            x_f = xe[:, cols].astype(F32)
            base = jnp.concatenate([jnp.zeros((HALO, 128), F32), d_conv], axis=0)
            d_window = taps[tap_count - 1 : tap_count, cols] * base
            tap_grad[tap_count - 1 : tap_count, cols] += jnp.sum(d_conv * x_f[HALO:], axis=0, keepdims=True)
            for k in range(tap_count - 1):
                moved = pltpu.roll(base, window - (tap_count - 1 - k), 0)
                tap_grad[k : k + 1, cols] += jnp.sum(moved * x_f, axis=0, keepdims=True)
                d_window = d_window + taps[k : k + 1, cols] * moved
            rims[branch, item, :, cols] = d_window[HALO - 8 : HALO]
            dx_out[:, cols] = d_window[HALO:]

    @pl.when(last_item & (pl.program_id(0) == 0))
    def _():
        swap_along_line(me, runs, [], downs, True)

    @pl.when(last_item & (pl.program_id(0) == 1))
    def _():
        swap_along_line(me, runs, ups, [], True)
        swap_along_line(me, runs, ups, downs, False)

        @pl.when(me == 0)
        def _():
            late[1] = jnp.zeros(late.shape[1:], F32)

        @pl.when(me == runs - 1)
        def _():
            late[0] = jnp.zeros(late.shape[1:], F32)

        late_out[...] = late[...]


LAST_ROWS = 16
PART_ROWS = 512


class Ring:
    def __init__(self, bits):
        self.bits = bits
        self.size = 1 << len(bits)
        self.digits = [bit_of(lax.axis_index(axis), bit) for axis, bit in bits]
        self.place = sum(digit * (1 << at) for at, digit in enumerate(self.digits))

    def target(self, ahead):
        place = (self.place + ahead) % self.size
        where = {}
        for at, (axis, bit) in enumerate(self.bits):
            base = where.get(axis, lax.axis_index(axis))
            where[axis] = base + (bit_of(place, at) - self.digits[at]) * (1 << bit)
        return where, place

    def targets(self):
        return [self.target(ahead)[0] for ahead in range(1, self.size)]


def stage_rings(runs, groups):
    bits = [("seq", bit) for bit in range(int(math.log2(runs)))] + [("dp", bit) for bit in range(int(math.log2(groups)))]
    return [Ring(bits[:1])] + [Ring(bits[at : at + 2]) for at in range(1, len(bits), 2)]


def part_count(rows):
    return -(-rows // PART_ROWS)


def buffer_rows(runs, groups):
    bits = int(math.log2(runs)) + int(math.log2(groups))
    size, total = PART_ROWS, 0
    for members in [2] + [1 << min(2, bits - at) for at in range(1, bits, 2)]:
        moved = size // members if size >= members * LAST_ROWS else size
        total += moved * (members - 1)
        size = moved
    return total


def reduce_shapes(parts, dim, runs, groups):
    bits = int(math.log2(runs)) + int(math.log2(groups))
    stages = 1 + bits // 2
    room = parts * buffer_rows(runs, groups)
    sems = pltpu.SemaphoreType.DMA((parts, 2 * stages, 3))
    return [
        pltpu.VMEM((parts * PART_ROWS, dim), F32), pltpu.VMEM((room, dim), BF16), pltpu.VMEM((room, dim), BF16),
        pltpu.VMEM((parts * PART_ROWS, dim), BF16), sems, sems,
    ]


class Reduction:
    def __init__(self, rings, turns, segments, acc, sends, arrivals, gathered, send_sem, recv_sem):
        self.rings = rings
        self.count = len(rings)
        self.parts = len(turns)
        self.segments = segments
        self.acc, self.sends, self.arrivals, self.gathered = acc, sends, arrivals, gathered
        self.send_sem, self.recv_sem = send_sem, recv_sem
        room = sends.shape[0] // self.parts
        self.steps = []
        for part, turn in enumerate(turns):
            later = rings[1:]
            turn = turn % max(len(later), 1)
            order = rings[:1] + later[turn:] + later[:turn]
            start, size, at = part * PART_ROWS, PART_ROWS, part * room
            steps = []
            for ring in order:
                split = size >= ring.size * LAST_ROWS
                moved = size // ring.size if split else size
                keep = pl.multiple_of(start + ring.place * moved, LAST_ROWS) if split else start
                steps.append((ring, start, split, moved, keep, at))
                at += moved * (ring.size - 1)
                start, size = keep, moved
            self.steps.append(steps)

    def assemble(self, part):
        low, high = part * PART_ROWS, (part + 1) * PART_ROWS
        at = 0
        for get, size in self.segments:
            first, last = max(at, low), min(at + size, high)
            if first < last:
                self.acc[first:last, :] = get(first - at, last - first)
            at += size
        if at < high:
            first = max(at, low)
            self.acc[first:high, :] = jnp.zeros((high - first, self.acc.shape[1]), F32)

    def scatter_copy(self, part, stage, ahead):
        ring, _, _, moved, _, at = self.steps[part][stage]
        at += (ahead - 1) * moved
        return remote(
            self.sends.at[pl.ds(at, moved), :], self.arrivals.at[pl.ds(at, moved), :],
            self.send_sem.at[part, stage, ahead - 1], self.recv_sem.at[part, stage, ahead - 1], ring.target(ahead)[0],
        )

    def scatter(self, part, stage):
        ring, start, split, moved, _, at = self.steps[part][stage]
        for ahead in range(1, ring.size):
            place = ring.target(ahead)[1]
            away = pl.multiple_of(start + place * moved, LAST_ROWS) if split else start
            here = at + (ahead - 1) * moved
            self.sends[here : here + moved, :] = self.acc[pl.ds(away, moved), :].astype(BF16)
            self.scatter_copy(part, stage, ahead).start()

    def settle(self, part, stage):
        ring, _, split, moved, keep, at = self.steps[part][stage]
        for ahead in range(1, ring.size):
            self.scatter_copy(part, stage, ahead).wait()
        held = self.acc[pl.ds(keep, moved), :]
        came = [
            self.arrivals[at + (ahead - 1) * moved : at + ahead * moved, :].astype(F32) for ahead in range(1, ring.size)
        ]
        if split:
            held = held + sum(came)
        else:
            values = [held.astype(BF16).astype(F32)] + came
            total = jnp.zeros_like(held)
            for place in range(ring.size):
                behind = (ring.place - place + ring.size) % ring.size
                chosen = values[0]
                for ahead in range(1, ring.size):
                    chosen = jnp.where(behind == ahead, values[ahead], chosen)
                total = total + chosen
            held = total
        self.acc[pl.ds(keep, moved), :] = held

    def gather_copies(self, part, stage):
        ring, _, split, moved, keep, _ = self.steps[part][stage]
        here = self.gathered.at[pl.ds(keep, moved), :]
        return [
            remote(
                here, here, self.send_sem.at[part, self.count + stage, ahead - 1],
                self.recv_sem.at[part, self.count + stage, ahead - 1], ring.target(ahead)[0],
            )
            for ahead in range(1, ring.size)
            if split
        ]

    def points(self):
        def begin():
            for part in range(self.parts):
                self.assemble(part)
                self.scatter(part, 0)

        def split(stage):
            for part in range(self.parts):
                self.settle(part, stage - 1)
                self.scatter(part, stage)

        def turn():
            for part in range(self.parts):
                self.settle(part, self.count - 1)
                _, _, _, moved, keep, _ = self.steps[part][-1]
                self.gathered[pl.ds(keep, moved), :] = self.acc[pl.ds(keep, moved), :].astype(BF16)
                for copy in self.gather_copies(part, self.count - 1):
                    copy.start()

        def join(stage):
            for part in range(self.parts):
                for copy in self.gather_copies(part, stage + 1):
                    copy.wait()
                if stage >= 0:
                    for copy in self.gather_copies(part, stage):
                        copy.start()

        points = [begin]
        points += [functools.partial(split, stage) for stage in range(1, self.count)]
        points += [turn]
        return points + [functools.partial(join, stage) for stage in reversed(range(-1, self.count - 1))]


def big_segments(ref, dim):
    return [
        (lambda at, size, lane=lane: ref[at : at + size, lane : lane + dim], ref.shape[0])
        for lane in range(0, ref.shape[1], dim)
    ]


def small_segments(refs, tails, dim):
    inner = refs[0].shape[2]
    blocks = [(lambda ref=ref, branch=branch: ref[branch], ref.shape[1]) for ref in refs for branch in range(2)]

    def tail():
        lines = [ref[branch] for ref in tails for branch in range(2)]
        return jnp.concatenate(lines + [jnp.zeros((8 - len(lines), inner), F32)], axis=0)

    blocks.append((tail, 8))
    return [
        (lambda at, size, get=get, lane=lane: get()[at : at + size, lane : lane + dim], size)
        for lane in range(0, inner, dim)
        for get, size in blocks
    ]


def tail_kernel(
    plan, tok, cot, mod, mask, counts, hid, z_in, y, dx, late, win, wout, step,
    xp_grad, dtp_grad, rate_grad, tap_grad, tapb_grad, skip_grad, dtb_grad,
    mixed, d_tokens, result, x_result, factors, own_rows,
    dz, out_grad, z_grad, x_grad, mod_sum, mod_in, table, small_send, small_recv, *reduce_scratch,
):
    runs, groups, slots = plan
    dim = tok.shape[-1]
    toks, inner = z_in.shape
    now = pl.program_id(0)
    i = now % slots
    rings = stage_rings(runs, groups)
    seq_ring = Ring([("seq", bit) for bit in range(int(math.log2(runs)))])
    dp_ring = Ring([("dp", bit) for bit in range(int(math.log2(groups)))])
    half = len(reduce_scratch) // 2
    smalls = small_segments((xp_grad, dtp_grad, rate_grad, tap_grad), (tapb_grad, skip_grad, dtb_grad), dim)
    segments = big_segments(out_grad, dim) + big_segments(z_grad, dim) + smalls
    main = Reduction(rings, [part % 3 // 2 for part in range(result.shape[0] // PART_ROWS)], segments, *reduce_scratch[:half])
    rest = Reduction(rings, [part % 2 for part in range(x_result.shape[0] // PART_ROWS)], big_segments(x_grad, dim), *reduce_scratch[half:])
    main_points, rest_points = main.points(), rest.points()

    @pl.when(now == 0)
    def _():
        greet([target for ring in rings + [seq_ring, dp_ring] for target in ring.targets()])
        out_grad[...] = jnp.zeros(out_grad.shape, F32)
        z_grad[...] = jnp.zeros(z_grad.shape, F32)
        x_grad[...] = jnp.zeros(x_grad.shape, F32)
        mod_sum[...] = jnp.zeros(mod_sum.shape, F32)

    scale, gate = mod[:, dim : 2 * dim], mod[:, 2 * dim :]
    valid = as_column(mask[pl.ds(i, 1), :]) * (counts[...] > i).astype(F32)
    mod_rows = pl.ds(pl.multiple_of(8 * i, 8), 8)

    @pl.when(now < slots)
    def _():
        cot_f = cot[...].astype(F32)
        z = z_in[...]
        z_sig = jax.nn.sigmoid(z)
        z_silu = z * z_sig
        summed = y[0] + flip_full(y[1])
        gated = (summed * z_silu).astype(BF16)
        branch_out = dot(gated, wout[...])
        mixed[...] = (tok[...].astype(F32) + gate * branch_out).astype(BF16)
        d_branch = (cot_f * gate).astype(BF16)
        out_grad[...] += dot_tn(gated, d_branch)
        d_zgate = dot_nt(d_branch, wout[...]) * summed * (z_sig + z_silu * (1.0 - z_sig))
        d_low = (d_zgate * valid).astype(BF16)
        dz[i] = d_low
        z_grad[...] += dot_tn(hid[...], d_low)
        d_gate = jnp.sum(cot_f * branch_out, axis=0, keepdims=True)
        mod_sum[mod_rows, :] = jnp.concatenate([jnp.zeros((2, dim), F32), d_gate, jnp.zeros((5, dim), F32)], axis=0)

    @pl.when(now == slots)
    def _():
        main_points[0]()

    @pl.when(now >= slots)
    def _():
        edge = late.shape[2]

        def with_late(part, extra):
            return jnp.concatenate([part[: toks - edge], part[toks - edge :] + extra], axis=0)

        d_x = with_late(dx[0], late[0, i]) + flip_full(with_late(dx[1], late[1, i]))
        d_x = (d_x * valid).astype(BF16)
        x_grad[...] += dot_tn(hid[...], d_x)
        d_hidden = dot_nt(d_x, win[:, :inner]) + dot_nt(dz[i], win[:, inner:])
        normed, inv_std = normalise(tok[...].astype(F32))
        d_shift = jnp.sum(d_hidden, axis=0, keepdims=True)
        d_scale = jnp.sum(d_hidden * normed, axis=0, keepdims=True)
        mod_sum[mod_rows, :] += jnp.concatenate([d_shift, d_scale, jnp.zeros((6, dim), F32)], axis=0)
        d_normed = d_hidden * (1.0 + scale)
        d_tokens[...] = cot[...].astype(F32) + inv_std * (
            d_normed
            - jnp.mean(d_normed, axis=-1, keepdims=True)
            - normed * jnp.mean(d_normed * normed, axis=-1, keepdims=True)
        )

    @pl.when(now == slots)
    def _():
        main_points[1]()

    def sum_copies():
        return [
            remote(mod_sum, mod_in.at[ahead - 1], small_send.at[ahead - 1], small_recv.at[ahead - 1], seq_ring.target(ahead)[0])
            for ahead in range(1, seq_ring.size)
        ]

    def table_copies():
        at = pl.multiple_of(dp_ring.place * 16, 16)
        here = table.at[pl.ds(at, 16), :]
        base = seq_ring.size - 1
        return [
            remote(here, here, small_send.at[base + ahead - 1], small_recv.at[base + ahead - 1], dp_ring.target(ahead)[0])
            for ahead in range(1, dp_ring.size)
        ]

    def start_small():
        for copy in sum_copies():
            copy.start()

    def turn_small():
        for copy in sum_copies():
            copy.wait()
        values = [mod_sum[...]] + [mod_in[ahead - 1] for ahead in range(1, seq_ring.size)]
        total = jnp.zeros(mod_sum.shape, F32)
        for place in range(seq_ring.size):
            behind = (seq_ring.place - place + seq_ring.size) % seq_ring.size
            chosen = values[0]
            for ahead in range(1, seq_ring.size):
                chosen = jnp.where(behind == ahead, values[ahead], chosen)
            total = total + chosen
        time_f = step[...].astype(F32)
        time_low = time_f * jax.nn.sigmoid(time_f)
        lines = [total[8 * item : 8 * item + 3] for item in range(slots)] + [time_low]
        lines.append(jnp.zeros((16 - 4 * slots, dim), F32))
        own = jnp.concatenate(lines, axis=0).astype(BF16)
        own_rows[...] = own
        table[pl.ds(pl.multiple_of(dp_ring.place * 16, 16), 16), :] = own
        for copy in table_copies():
            copy.start()

    def end_small():
        for copy in table_copies():
            copy.wait()
        factors[...] = table[...]

    @pl.when(now == 2 * slots - 1)
    def _():
        start_small()
        rest_points[0]()
        rest_points[1]()
        for at in range(2, len(main_points)):
            main_points[at]()
            if at == 2:
                turn_small()
            rest_points[at]()
        end_small()
        result[...] = main.gathered[...]
        x_result[...] = rest.gathered[...]


def finish_kernel(
    result, x_result, factors, own, step, ada,
    grad_time, grad_ada, grad_ada_bias, in_grad, tap_grad, tapb_grad, xp_grad, dtp_grad, dtb_grad, rate_grad, skip_grad, out_grad,
):
    dim, inner = in_grad.shape[0], rate_grad.shape[2]
    slots = step.shape[0]

    now = pl.program_id(0)

    def rows(at, size):
        return result[at : at + size, :].astype(F32)

    out_rows = out_grad.shape[0]
    out_grad[...] = result[pl.ds(pl.multiple_of(now * out_rows, out_rows), out_rows), :].astype(F32)
    pieces = inner // dim

    @pl.when(now < pieces)
    def _():
        in_grad[...] = x_result[pl.ds(pl.multiple_of(now * dim, dim), dim), :].astype(F32)

    @pl.when(now >= pieces)
    def _():
        in_grad[...] = result[pl.ds(pl.multiple_of(inner + (now - pieces) * dim, dim), dim), :].astype(F32)


    table = factors[...]
    length = table.shape[0]
    items = length // 16 * 8

    def pick(place):
        row = lax.broadcasted_iota(jnp.int32, (items, length), 0)
        col = lax.broadcasted_iota(jnp.int32, (items, length), 1)
        slot = row % 8
        wanted = row // 8 * 16 + place(slot)
        return dot(((col == wanted) & (slot < slots)).astype(BF16), table)

    for part in range(3):

        @pl.when(now == part)
        def _():
            times = pick(lambda slot: 3 * slots + slot).astype(BF16)
            mods = pick(lambda slot: 3 * slot + part)
            lanes = slice(part * dim, (part + 1) * dim)
            grad_ada[...] = dot_tn(times, mods.astype(BF16))
            grad_ada_bias[lanes] = jnp.sum(mods, axis=0)
            mine = own[...].astype(F32)
            picked = jnp.concatenate([mine[3 * i + part : 3 * i + part + 1] for i in range(slots)], axis=0)
            d_time = dot_nt(picked.astype(BF16), ada[:, lanes])
            grad_time[...] = d_time if part == 0 else grad_time[...] + d_time

    @pl.when(now == 3)
    def _():
        time_f = step[...].astype(F32)
        time_sig = jax.nn.sigmoid(time_f)
        grad_time[...] = grad_time[...] * time_sig * (1.0 + time_f * (1.0 - time_sig))
        at = 2 * inner
        for first in range(0, inner, dim):
            lanes = slice(first, first + dim)
            for ref in (xp_grad, dtp_grad, rate_grad, tap_grad):
                size = ref.shape[1]
                for branch in range(2):
                    ref[branch, :, lanes] = rows(at, size)
                    at += size
            tail = rows(at, 8)
            tapb_grad[:, lanes] = tail[0:2]
            skip_grad[:, lanes] = tail[2:4]
            dtb_grad[:, lanes] = tail[4:6]
            at += 8


def params(**more):
    return pltpu.CompilerParams(vmem_limit_bytes=VMEM_LIMIT, **more)


def spec(block, index):
    return pl.BlockSpec(block, index)


def per_device(
    tokens, timestep, counts, token_mask, ada_weight, ada_bias, input_weight, conv_weight, conv_bias, x_weight, dt_weight,
    dt_bias, decay_rate, skip_gain, output_weight, cotangent,
):
    slots, toks, dim = tokens.shape
    inner = output_weight.shape[0]
    rank = dt_weight.shape[1]
    states = decay_rate.shape[1]
    tap_count = conv_weight.shape[1]
    wide_rank = 32
    proj_rows = wide_rank + 2 * states
    blocks = toks // BLK
    runs = lax.axis_size("seq")
    groups = lax.axis_size("dp")
    counts2 = counts[:, None]
    x_rows = jnp.swapaxes(x_weight, 1, 2)

    def item(*block):
        return spec((None,) + block, lambda i: (i,) + (0,) * len(block))

    def whole(*block):
        return spec(block, lambda *_: (0,) * len(block))

    xe, dy, z_gate, hid, modulate = pl.pallas_call(
        functools.partial(enter_kernel, runs),
        grid=(slots,),
        in_specs=[
            whole(slots, toks, dim), item(toks, dim), whole(slots, toks), whole(1, 1), whole(slots, dim), whole(dim, 3 * dim),
            whole(3 * dim), whole(dim, 2 * inner), whole(inner, dim),
        ],
        out_specs=[
            item(2, HALO + toks, inner), item(2, toks, inner), item(toks, inner), item(toks, dim), item(1, 3 * dim),
        ],
        out_shape=[
            jax.ShapeDtypeStruct((slots, 2, HALO + toks, inner), BF16),
            jax.ShapeDtypeStruct((slots, 2, toks, inner), F32),
            jax.ShapeDtypeStruct((slots, toks, inner), F32),
            jax.ShapeDtypeStruct((slots, toks, dim), BF16),
            jax.ShapeDtypeStruct((slots, 1, 3 * dim), F32),
        ],
        scratch_shapes=[
            pltpu.VMEM((slots, 3 * dim), F32),
            pltpu.VMEM((slots, HALO, dim), BF16), pltpu.VMEM((slots, HALO, dim), BF16), pltpu.VMEM((slots, toks), jnp.int32),
            pltpu.VMEM((slots, toks), jnp.int32), pltpu.SemaphoreType.DMA((4,)), pltpu.SemaphoreType.DMA((4,)),
        ],
        compiler_params=params(collective_id=1, has_side_effects=True),
        name="enter",
    )(
        tokens, cotangent, token_mask, counts2, timestep, ada_weight, ada_bias, input_weight, output_weight,
    )

    def unit(*block):
        return spec((None, None) + block, lambda b, i: (i, b) + (0,) * len(block))

    def branch(*block):
        return spec((None,) + block, lambda b, i: (b,) + (0,) * len(block))

    def unit_shape(*block, kind=F32):
        return jax.ShapeDtypeStruct((slots, 2) + block, kind)

    act, dsilu, delta, sig, proj, end, back, total, starts, sums, tiles, xwt, dtw, s_first, lam_first = pl.pallas_call(
        functools.partial(first_kernel, runs, slots),
        grid=(2, slots),
        in_specs=[
            unit(HALO + toks, inner), unit(toks, inner), branch(tap_count, inner), whole(2, inner),
            branch(rank + 2 * states, inner), branch(rank, inner), whole(2, inner), branch(states, inner),
        ],
        out_specs=[
            unit(toks, inner), unit(toks, inner), unit(toks, inner), unit(toks, inner), unit(proj_rows, toks),
            unit(states, inner), unit(states, inner), unit(1, inner), unit(blocks, states, inner), unit(blocks, 1, inner),
            unit(toks, 2 * states, 128), branch(proj_rows, inner), branch(wide_rank, inner),
            whole(slots, states, inner), whole(slots, states, inner),
        ],
        out_shape=[
            unit_shape(toks, inner, kind=BF16), unit_shape(toks, inner), unit_shape(toks, inner), unit_shape(toks, inner),
            unit_shape(proj_rows, toks), unit_shape(states, inner), unit_shape(states, inner), unit_shape(1, inner),
            unit_shape(blocks, states, inner), unit_shape(blocks, 1, inner), unit_shape(toks, 2 * states, 128),
            jax.ShapeDtypeStruct((2, proj_rows, inner), BF16), jax.ShapeDtypeStruct((2, wide_rank, inner), BF16),
            jax.ShapeDtypeStruct((slots, states, inner), F32), jax.ShapeDtypeStruct((slots, states, inner), F32),
        ],
        scratch_shapes=[
            pltpu.VMEM((toks, inner), F32), pltpu.VMEM((2, BLK, states, inner), F32), pltpu.VMEM((8, inner), F32),
            pltpu.VMEM((states, inner), F32), pltpu.VMEM((2 * states * toks, 128), F32),
            pltpu.VMEM((4 * states, 2 * states * 128), BF16), pltpu.VMEM((slots, states, inner), F32),
            pltpu.VMEM((slots, states, inner), F32), pltpu.VMEM((slots, 1, inner), F32), pltpu.VMEM((states, inner), F32),
            *exchange_shapes(runs, slots, states, inner),
        ],
        compiler_params=params(collective_id=2, has_side_effects=True),
        name="first",
    )(xe, dy, conv_weight, conv_bias, x_rows, dt_weight, dt_bias, decay_rate)

    vmem = pl.BlockSpec(memory_space=pltpu.VMEM)
    last = spec((slots, None, states, inner), lambda b, i: (0, 1, 0, 0))
    last_total = spec((slots, None, 1, inner), lambda b, i: (0, 1, 0, 0))
    last_branch = spec((None, states, inner), lambda b, i: (1, 0, 0))

    y, dx, late, rate_grad, skip_grad, dtb_grad, dtp_grad, xp_grad, tap_grad, tapb_grad = pl.pallas_call(
        functools.partial(second_kernel, runs),
        grid=(2, slots),
        in_specs=[
            whole(slots, states, inner), whole(slots, states, inner), last, last, last_total, last_branch,
            unit(blocks, states, inner), unit(blocks, 1, inner), unit(toks, 2 * states, 128), branch(states, inner), unit(HALO + toks, inner), unit(toks, inner),
            unit(toks, inner), unit(toks, inner), unit(toks, inner), unit(toks, inner), unit(proj_rows, toks),
            branch(proj_rows, inner), branch(wide_rank, inner),
            branch(tap_count, inner), whole(2, inner),
        ],
        out_specs=[
            unit(toks, inner), unit(toks, inner), whole(2, slots, 8, inner), branch(states, inner), branch(1, inner), branch(1, inner),
            branch(rank, inner), branch(rank + 2 * states, inner), branch(tap_count, inner), branch(1, inner),
        ],
        out_shape=[
            unit_shape(toks, inner), unit_shape(toks, inner), jax.ShapeDtypeStruct((2, slots, 8, inner), F32),
        ] + [
            jax.ShapeDtypeStruct((2, rows, inner), F32) for rows in (states, 1, 1, rank, rank + 2 * states, tap_count, 1)
        ],
        scratch_shapes=[
            pltpu.VMEM((states, inner), F32), pltpu.VMEM((states, inner), F32), pltpu.VMEM((toks + BLK, inner), F32), pltpu.VMEM((toks + BLK, BLK * states), BF16),
            pltpu.VMEM((toks, BLK * states), BF16),
            pltpu.VMEM((2, BLK, states, inner), F32),
            pltpu.VMEM((2, (BLK + 1) * states, inner), BF16), pltpu.VMEM((2, BLK * states, inner), BF16),
            pltpu.VMEM((2, BLK * states, inner), BF16), pltpu.VMEM((2, BLK // 4 * states, inner), BF16),
            pltpu.VMEM((2, BLK * states, 256), BF16), pltpu.VMEM((states, inner), F32),
            pltpu.VMEM((toks + BLK, inner), F32), pltpu.VMEM((toks + BLK, inner), F32),
            pltpu.VMEM((toks + BLK, BLK * states), BF16), pltpu.VMEM((toks + BLK, BLK * states), BF16),
            pltpu.VMEM((2, slots, 8, inner), F32), pltpu.VMEM((2, slots, 8, inner), F32),
            pltpu.SemaphoreType.DMA((2,)), pltpu.SemaphoreType.DMA((2,)), pltpu.VMEM((toks, inner), BF16),
            pltpu.VMEM((states, inner), F32), pltpu.VMEM((slots, states, inner), F32), pltpu.VMEM((slots, states, inner), F32),
            *exchange_shapes(runs, slots, states, inner),
        ],
        compiler_params=params(collective_id=3, has_side_effects=True),
        name="second",
    )(
        s_first, lam_first, end, back, total, decay_rate, starts, sums, tiles, decay_rate, xe, act, dsilu, delta,
        sig, dy, proj, xwt, dtw, conv_weight, skip_gain,
    )

    def now(*block):
        return spec((None,) + block, lambda s: (s % slots,) + (0,) * len(block))

    def early(*block):
        return spec((None,) + block, lambda s: (jnp.minimum(s, slots - 1),) + (0,) * len(block))

    def after(*block):
        return spec((None,) + block, lambda s: (jnp.maximum(s - slots, 0),) + (0,) * len(block))

    smalls = (xp_grad, dtp_grad, rate_grad, tap_grad, tapb_grad, skip_grad, dtb_grad)
    small_rows = (2 * sum(ref.shape[1] for ref in smalls[:4]) + 8) * (inner // dim)
    main_parts = part_count(inner + dim * (inner // dim) + small_rows)
    rest_parts = part_count(dim * (inner // dim))
    mixed, d_tokens, result, x_result, factors, own = pl.pallas_call(
        functools.partial(tail_kernel, (runs, groups, slots)),
        grid=(2 * slots,),
        in_specs=[
            now(toks, dim), now(toks, dim), now(1, 3 * dim), whole(slots, toks), whole(1, 1), now(toks, dim),
            early(toks, inner), early(2, toks, inner), after(2, toks, inner), whole(2, slots, 8, inner),
            whole(dim, 2 * inner), whole(inner, dim), whole(slots, dim), *[whole(*ref.shape) for ref in smalls],
        ],
        out_specs=[
            early(toks, dim), after(toks, dim), whole(main_parts * PART_ROWS, dim), whole(rest_parts * PART_ROWS, dim),
            whole(16 * groups, dim), whole(16, dim),
        ],
        out_shape=[
            jax.ShapeDtypeStruct((slots, toks, dim), BF16), jax.ShapeDtypeStruct((slots, toks, dim), F32),
            jax.ShapeDtypeStruct((main_parts * PART_ROWS, dim), BF16), jax.ShapeDtypeStruct((rest_parts * PART_ROWS, dim), BF16),
            jax.ShapeDtypeStruct((16 * groups, dim), BF16), jax.ShapeDtypeStruct((16, dim), BF16),
        ],
        scratch_shapes=[
            pltpu.VMEM((slots, toks, inner), BF16), pltpu.VMEM((inner, dim), F32), pltpu.VMEM((dim, inner), F32),
            pltpu.VMEM((dim, inner), F32), pltpu.VMEM((8 * slots, dim), F32), pltpu.VMEM((max(runs - 1, 1), 8 * slots, dim), F32),
            pltpu.VMEM((16 * groups, dim), BF16), pltpu.SemaphoreType.DMA((runs + groups,)),
            pltpu.SemaphoreType.DMA((runs + groups,)), *reduce_shapes(main_parts, dim, runs, groups),
            *reduce_shapes(rest_parts, dim, runs, groups),
        ],
        compiler_params=params(collective_id=4, has_side_effects=True),
        name="tail",
    )(
        tokens, cotangent, modulate, token_mask, counts2, hid, z_gate, y, dx, late, input_weight, output_weight, timestep,
        *smalls,
    )

    (
        d_time, grad_ada, grad_ada_bias, in_grad, tap_grad, tapb_grad, xp_grad, dtp_grad, dtb_grad, rate_grad, skip_grad,
        out_grad,
    ) = pl.pallas_call(
        finish_kernel,
        grid=(4,),
        in_specs=[
            whole(main_parts * PART_ROWS, dim), whole(rest_parts * PART_ROWS, dim), whole(16 * groups, dim), whole(16, dim),
            whole(slots, dim), whole(dim, 3 * dim),
        ],
        out_specs=[
            whole(slots, dim), spec((dim, dim), lambda s: (0, jnp.minimum(s, 2))), whole(3 * dim),
            spec((dim, 2 * inner // 4), lambda s: (0, s)), whole(2, tap_count, inner), whole(2, inner),
            whole(2, rank + 2 * states, inner), whole(2, rank, inner), whole(2, inner), whole(2, states, inner), whole(2, inner),
            spec((inner // 4, dim), lambda s: (s, 0)),
        ],
        out_shape=[
            jax.ShapeDtypeStruct(shape, F32)
            for shape in (
                (slots, dim), (dim, 3 * dim), (3 * dim,), (dim, 2 * inner), (2, tap_count, inner), (2, inner),
                (2, rank + 2 * states, inner), (2, rank, inner), (2, inner), (2, states, inner), (2, inner), (inner, dim),
            )
        ],
        compiler_params=params(),
        name="finish",
    )(result, x_result, factors, own, timestep, ada_weight)
    return (
        mixed, d_tokens, d_time, grad_ada, grad_ada_bias, in_grad, tap_grad, tapb_grad, jnp.swapaxes(xp_grad, 1, 2), dtp_grad, dtb_grad,
        rate_grad, skip_grad, out_grad,
    )


def solution(mesh):
    runs = P("dp", "seq", None)
    return jax.shard_map(
        per_device,
        mesh=mesh,
        in_specs=(runs, P("dp", None), P("dp"), P("dp", "seq")) + (P(),) * 11 + (runs,),
        out_specs=(runs, runs, P("dp", None)) + (P(),) * 11,
        check_vma=False,
    )
```

```python
import functools
import math

import jax
import jax.numpy as jnp
from jax import lax
from jax.experimental import pallas as pl
from jax.experimental.pallas import tpu as pltpu
from jax.sharding import PartitionSpec as P

EPSILON = 1e-06
BLK = 16
WIDE_RANK = 32
HALO = 16
LOG2E = math.log2(math.e)
F32, BF16 = jnp.float32, jnp.bfloat16
NT = (((1,), (1,)), ((), ()))
TN = (((0,), (0,)), ((), ()))
VMEM_LIMIT = 60 << 20
MESH = pl.DeviceIdType.MESH


def dot(a, b):
    return jnp.dot(a, b, preferred_element_type=F32)


def dot_nt(a, b):
    return lax.dot_general(a, b, NT, preferred_element_type=F32)


def dot_tn(a, b):
    return lax.dot_general(a, b, TN, preferred_element_type=F32)


def flip_full(value):
    turned = lax.broadcasted_iota(jnp.int32, (8, value.shape[1]), 0)
    groups = [value[at : at + 8] for at in range(0, value.shape[0], 8)]
    return jnp.concatenate([jnp.take_along_axis(group, 7 - turned, axis=0) for group in reversed(groups)], axis=0)


def flip_low(value):
    return flip_full(value.astype(F32)).astype(BF16)


def normalise(tokens_f):
    centered = tokens_f - jnp.mean(tokens_f, axis=-1, keepdims=True)
    inv_std = lax.rsqrt(jnp.mean(centered * centered, axis=-1, keepdims=True) + EPSILON)
    return centered * inv_std, inv_std


def eye(size):
    rows = lax.broadcasted_iota(jnp.int32, (size, size), 0)
    cols = lax.broadcasted_iota(jnp.int32, (size, size), 1)
    return (rows == cols).astype(BF16)


def as_column(row):
    return dot_nt(eye(row.shape[1]), jnp.broadcast_to(row.astype(F32).astype(BF16), (8, row.shape[1])))[:, :1]


def remote(src, dst, send_sem, recv_sem, target):
    return pltpu.make_async_remote_copy(
        src_ref=src, dst_ref=dst, send_sem=send_sem, recv_sem=recv_sem, device_id=target, device_id_type=MESH
    )


def greet(targets):
    barrier = pltpu.get_barrier_semaphore()
    for target in targets:
        pl.semaphore_signal(barrier, inc=1, device_id=target, device_id_type=MESH)
    pl.semaphore_wait(barrier, len(targets))


def greet_line(me, runs, others=()):
    barrier = pltpu.get_barrier_semaphore()
    for target in others:
        pl.semaphore_signal(barrier, inc=1, device_id=target, device_id_type=MESH)

    @pl.when(me > 0)
    def _():
        pl.semaphore_signal(barrier, inc=1, device_id={"seq": me - 1}, device_id_type=MESH)

    @pl.when(me < runs - 1)
    def _():
        pl.semaphore_signal(barrier, inc=1, device_id={"seq": me + 1}, device_id_type=MESH)

    neighbours = lax.div(me + runs - 1, runs) + lax.div(2 * runs - 2 - me, runs)
    pl.semaphore_wait(barrier, neighbours + len(others))


def swap_along_line(me, runs, ups, downs, start):
    up = [remote(src, dst, ss, rs, {"seq": me + 1}) for src, dst, ss, rs in ups]
    down = [remote(src, dst, ss, rs, {"seq": me - 1}) for src, dst, ss, rs in downs]

    @pl.when(me < runs - 1)
    def _():
        for copy in up:
            if start:
                copy.start()
            else:
                copy.wait_send()
        if not start:
            for copy in down:
                copy.wait_recv()

    @pl.when(me > 0)
    def _():
        for copy in down:
            if start:
                copy.start()
            else:
                copy.wait_send()
        if not start:
            for copy in up:
                copy.wait_recv()


def enter_kernel(
    runs, tok, cot, mask, counts, step, ada, ada_bias, win, wout,
    xe, dy, z_out, hid_out, mod_out,
    mods, prev_tok, next_tok, prev_mask, next_mask, send_sem, recv_sem,
):
    slots, toks, dim = tok.shape
    inner = wout.shape[0]
    me = lax.axis_index("seq")
    i = pl.program_id(0)
    ups = [
        (tok.at[:, pl.ds(toks - HALO, HALO), :], prev_tok, send_sem.at[0], recv_sem.at[0]),
        (mask, prev_mask, send_sem.at[1], recv_sem.at[1]),
    ]
    downs = [
        (tok.at[:, pl.ds(0, HALO), :], next_tok, send_sem.at[2], recv_sem.at[2]),
        (mask, next_mask, send_sem.at[3], recv_sem.at[3]),
    ]

    @pl.when(i == 0)
    def _():
        greet_line(me, runs)
        swap_along_line(me, runs, ups, downs, True)

        @pl.when(me == 0)
        def _():
            prev_tok[...] = jnp.zeros(prev_tok.shape, BF16)
            prev_mask[...] = jnp.zeros(prev_mask.shape, jnp.int32)

        @pl.when(me == runs - 1)
        def _():
            next_tok[...] = jnp.zeros(next_tok.shape, BF16)
            next_mask[...] = jnp.zeros(next_mask.shape, jnp.int32)

    live = (counts[...] > i).astype(F32)

    @pl.when(i == 0)
    def _():
        time_f = step[...].astype(F32)
        time_low = (time_f * jax.nn.sigmoid(time_f)).astype(BF16)
        mods[...] = dot(time_low, ada[...]) + ada_bias[...].reshape(1, 3 * dim)

    mod = mods[pl.ds(i, 1), :]
    mod_out[...] = mod
    shift, scale, gate = mod[:, :dim], mod[:, dim : 2 * dim], mod[:, 2 * dim :]

    def hidden_of(part):
        normed, _ = normalise(part.astype(F32))
        return (normed * (1.0 + scale) + shift).astype(BF16)

    hid = hidden_of(tok[i])
    hid_out[...] = hid
    xz = dot(hid, win[...]) * (as_column(mask[pl.ds(i, 1), :]) * live)
    x_low = xz[:, :inner].astype(BF16)
    z = xz[:, inner:]
    z_out[...] = z
    d_branch = (cot[...].astype(F32) * gate).astype(BF16)
    d_summed = dot_nt(d_branch, wout[...]) * z * jax.nn.sigmoid(z)
    dy[0] = d_summed
    dy[1] = flip_full(d_summed)
    xe[0, HALO:, :] = x_low
    xe[1, HALO:, :] = flip_low(x_low)

    @pl.when(i == 0)
    def _():
        swap_along_line(me, runs, ups, downs, False)

    rims = jnp.concatenate([prev_tok[i], next_tok[i]], axis=0)
    prev_col = as_column(prev_mask[pl.ds(i, 1), :])[toks - HALO :]
    next_col = as_column(next_mask[pl.ds(i, 1), :])[:HALO]
    rim_x = dot(hidden_of(rims), win[:, :inner]) * (jnp.concatenate([prev_col, next_col], axis=0) * live)
    rim_x = rim_x.astype(BF16)
    xe[0, :HALO, :] = rim_x[:HALO]
    xe[1, :HALO, :] = flip_low(rim_x[HALO:])


def columns(inner, width=128):
    return [slice(at, at + width) for at in range(0, inner, width)]


def twice(row8):
    return jnp.concatenate([row8, row8], axis=0)


def spread(ref, index):
    return twice(ref[pl.ds(index, 8, stride=0), :])


def lay_out(wide, rows, picks):
    count, toks = rows.shape
    high = rows.astype(BF16).astype(F32)
    halves = jnp.concatenate([high, rows - high], axis=0).T.astype(BF16)
    for n in range(0, count, 2):
        pair = dot(halves, picks[:, n * 128 : (n + 2) * 128])
        for t in range(0, toks, 8):
            for k in range(2):
                at = 8 * (count * (t // 8) + n + k)
                wide[at : at + 8, :] = pair[t : t + 8, k * 128 : (k + 1) * 128]


def wide_tile(wide, i, count):
    at = 8 * count * (i // 8) + i % 8
    return jnp.concatenate([wide[pl.ds(at + 64 * n, 8, stride=8), :] for n in range(count // 8)], axis=0)


def across_lanes(tile, inner):
    return jnp.concatenate([tile] * (inner // 128), axis=1)


def softplus_parts(pre):
    e = jnp.exp2(-LOG2E * jnp.abs(pre))
    more = jnp.where(e < 1e-3, e - 0.5 * e * e, jnp.log(1.0 + e))
    return jnp.maximum(pre, 0.0) + more, jax.nn.sigmoid(pre)


def bit_of(index, bit):
    return lax.rem(lax.div(index, 1 << bit), 2)


def across(axis, bit):
    me = lax.axis_index(axis)
    mine = bit_of(me, bit)
    return mine, {axis: me + (1 - 2 * mine) * (1 << bit)}


class Exchange:
    def __init__(self, runs, branch, ends, backs, totals, rate, results, group, span, pre, pre_span, sends, arrivals, sems):
        self.branch, self.rate = branch, rate
        self.sources, self.totals, self.results = (ends, backs), totals, results
        self.group, self.span, self.pre, self.pre_span = group, span, pre, pre_span
        self.sends, self.arrivals, self.sems = sends, arrivals, sems
        self.links = [across("seq", bit) for bit in range(int(math.log2(runs)))]
        self.slots = ends.shape[0]
        self.states, self.inner = rate.shape

    def flow(self, kind):
        return kind if self.branch == 0 else 1 - kind

    def targets(self):
        return [target for _, target in self.links]

    def copy(self, stage, kind):
        at = 2 * stage + kind
        return remote(
            self.sends.at[at], self.arrivals.at[at], self.sems.at[0, at], self.sems.at[1, at], self.links[stage][1]
        )

    def send(self, stage, kind):
        rows = self.slots * self.states
        at = 2 * stage + kind
        for i in range(self.slots):
            self.sends[at, i * self.states : (i + 1) * self.states, :] = self.group[kind, i].astype(BF16)
        high = self.span[kind].astype(BF16).astype(F32)
        self.sends[at, rows:, :] = jnp.concatenate([high, self.span[kind] - high], axis=0).astype(BF16)
        self.copy(stage, kind).start()

    def join(self, stage, kind, last):
        mine = self.links[stage][0]
        self.copy(stage, kind).wait()
        at = 2 * stage + kind
        earlier = (mine == 1) if self.flow(kind) == 0 else (mine == 0)
        both = self.arrivals[at, self.slots * self.states :, :].astype(F32)
        length = both[: both.shape[0] // 2] + both[both.shape[0] // 2 :]
        own_span, pre_span = self.span[kind], self.pre_span[kind]
        second_span = jnp.where(earlier, own_span, length)
        rate = self.rate[...] * -LOG2E
        for i in range(self.slots):
            state = self.arrivals[at, i * self.states : (i + 1) * self.states, :].astype(F32)
            before = self.pre[kind, i]
            self.pre[kind, i] = jnp.where(earlier, state * jnp.exp2(rate * pre_span[i : i + 1]) + before, before)
            if not last:
                own = self.group[kind, i]
                first, second = jnp.where(earlier, state, own), jnp.where(earlier, own, state)
                self.group[kind, i] = first * jnp.exp2(rate * second_span[i : i + 1]) + second
        self.pre_span[kind] = jnp.where(earlier, length + pre_span, pre_span)
        if not last:
            self.span[kind] = own_span + length

    def points(self):
        count = len(self.links)

        def begin():
            self.pre[...] = jnp.zeros(self.pre.shape, F32)
            self.pre_span[...] = jnp.zeros(self.pre_span.shape, F32)
            self.span[...] = jnp.zeros(self.span.shape, F32)
            for kind in range(2):
                for i in range(self.slots):
                    self.group[kind, i] = self.sources[kind][i]
                    self.span[kind, i : i + 1, :] = self.totals[i][:1]
                if count:
                    self.send(0, kind)

        def step(stage):
            last = stage == count - 1
            for kind in range(2):
                self.join(stage, kind, last)
                if not last:
                    self.send(stage + 1, kind)

        def end():
            for kind in range(2):
                for i in range(self.slots):
                    self.results[kind][i] = self.pre[kind, i]

        return [begin] + [functools.partial(step, stage) for stage in range(count)] + [end]


def exchange_shapes(runs, slots, states, inner):
    pairs = max(int(math.log2(runs)), 1)
    span_rows = -(-slots // 8) * 8
    return [
        pltpu.VMEM((2, slots, states, inner), F32), pltpu.VMEM((2, span_rows, inner), F32),
        pltpu.VMEM((2, slots, states, inner), F32), pltpu.VMEM((2, span_rows, inner), F32),
        pltpu.VMEM((2 * pairs, slots * states + 2 * span_rows, inner), BF16),
        pltpu.VMEM((2 * pairs, slots * states + 2 * span_rows, inner), BF16),
        pltpu.SemaphoreType.DMA((2, 2 * pairs)),
    ]


def beside(points, step, first, count):
    for at in range(min(len(points), count)):
        todo = points[at:] if at == count - 1 else points[at : at + 1]

        @pl.when(step == first + at)
        def _():
            for point in todo:
                point()


def first_kernel(
    runs, slots, xe, dy, taps, tap_bias, x_rows, dt_rows, dt_bias, rate,
    act_out, planes, proj_out, last_out, starts_out, tiles, weights, first_in,
    dx, decay, through, rate2, wide, picks, ends, backs, totals, first_rate, *exchange_scratch,
):
    toks, inner = dy.shape
    states = rate.shape[0]
    blocks = toks // BLK
    rank = WIDE_RANK
    xwt, dtw = weights.at[: weights.shape[0] - rank], weights.at[weights.shape[0] - rank :]
    delta_out, sig_out, dsilu_out = (planes.at[at] for at in range(3))
    end_out, back_out = last_out.at[:states], last_out.at[states : 2 * states]
    tap_count = taps.shape[0]
    branch, item = pl.program_id(0), pl.program_id(1)
    results = (first_in.at[0], first_in.at[1])
    exchange = Exchange(runs, 0, ends, backs, totals, first_rate, results, *exchange_scratch)

    @pl.when((branch == 0) & (item == 0))
    def _():
        greet(exchange.targets())
        first_rate[...] = rate[...]

    beside(exchange.points(), branch * slots + item, slots, slots)

    @pl.when(item == 0)
    def _():
        rate2[...] = rate[...] * -LOG2E
        picks[...] = (
            lax.broadcasted_iota(jnp.int32, picks.shape, 0) % (2 * states)
            == lax.broadcasted_iota(jnp.int32, picks.shape, 1) // 128
        ).astype(BF16)
        held = dt_rows.shape[0]
        rows = x_rows[...].astype(F32)
        gap = jnp.zeros((rank - held, inner), F32)
        wide = [rows[:held], gap, rows[held:], dt_rows[...].astype(F32), gap]
        weights[...] = jnp.concatenate(wide, axis=0).astype(BF16)

    tap_row, dt_row = tap_bias[pl.ds(branch, 1), :], dt_bias[pl.ds(branch, 1), :]
    for cols in columns(inner):
        x_f = xe[:, cols].astype(F32)
        conv = tap_row[:, cols] + taps[tap_count - 1 : tap_count, cols] * x_f[HALO:]
        for k in range(tap_count - 1):
            conv = conv + taps[k : k + 1, cols] * pltpu.roll(x_f, tap_count - 1 - k, 0)[HALO:]
        open_part = jax.nn.sigmoid(conv)
        act_f = conv * open_part
        act_out[:, cols] = act_f.astype(BF16)
        dsilu_out[:, cols] = open_part + act_f * (1.0 - open_part)
    proj = dot_nt(xwt[...], act_out[...])
    proj_out[...] = proj
    dt_low = proj[:rank, :].astype(BF16)
    for cols in columns(inner, 256):
        pre = dot_tn(dt_low, dtw[:, cols]) + dt_row[:, cols]
        delta, slope = softplus_parts(pre)
        delta_out[:, cols] = delta
        sig_out[:, cols] = slope
        dx[:, cols] = delta * act_out[:, cols].astype(F32)
    lay_out(wide, proj[rank:, :], picks)
    end_out[...] = jnp.zeros((states, inner), F32)
    back_out[...] = jnp.zeros((states, inner), F32)
    through[...] = jnp.zeros((8, inner), F32)

    def one_block(j, slot):
        t0 = pl.multiple_of(j * BLK, BLK)
        dr, xr, yr = (ref.at[pl.ds(t0, BLK), :] for ref in (delta_out, dx, dy))
        count = 2 * states
        wide_rows = wide.at[pl.ds(pl.multiple_of(j * (BLK * count), BLK * count), BLK * count), :]
        s = end_out[...]
        before = through[...]
        starts_out[j] = jnp.concatenate([s, before], axis=0)
        rates = rate2[...]
        for i in range(BLK):
            a = jnp.exp2(spread(dr, i) * rates)
            decay[slot, i] = a
            tile = wide_tile(wide_rows, i, count)
            tiles[t0 + i] = tile
            s = a * s + spread(xr, i) * across_lanes(tile[:states], inner)
        end_out[...] = s
        m = jnp.zeros((states, inner), F32)
        for i in reversed(range(BLK)):
            m = decay[slot, i] * (m + spread(yr, i) * across_lanes(tiles[t0 + i, states:], inner))
        back_out[...] = back_out[...] + m * jnp.exp2(twice(before) * rates)
        through[...] = before + jnp.sum(dr[...], axis=0, keepdims=True)

    def block_step(k, _):
        one_block(2 * k, 0)
        one_block(2 * k + 1, 1)
        return 0

    lax.fori_loop(0, blocks // 2, block_step, 0)
    last_out[2 * states :, :] = through[...]

    @pl.when(branch == 0)
    def _():
        ends[item] = end_out[...]
        backs[item] = back_out[...]
        totals[item] = through[:1, :]


def second_kernel(
    runs, first_in, lasts, last_rate, starts, tiles, rate, xe, act, planes, dy, proj, weights, taps, skip,
    y_out, dx_out, late_out, grads,
    rate2, carry, dxs, bdiag, cdiag, decay, states_low, lam_low, rq_low, qd_low, dots, racc, gsum, hsum, db, dc,
    rims, late, send_sem, recv_sem, d_pre_low, s_in, s_last, lam_last, *exchange_scratch,
):
    toks, inner = dy.shape
    states = rate.shape[0]
    blocks = toks // BLK
    rank = WIDE_RANK
    xwt, dtw = weights.at[: weights.shape[0] - rank], weights.at[weights.shape[0] - rank :]
    delta, sig, dsilu = (planes.at[at] for at in range(3))
    tap_count = taps.shape[0]
    held = (grads.shape[0] - 3 * states - 8) // 2
    xp_grad, dtp_grad = grads.at[: held + 2 * states], grads.at[held + 2 * states : 2 * held + 2 * states]
    at = 2 * held + 2 * states
    rate_grad, row_grads = grads.at[at : at + states], grads.at[at + states : at + states + 8]
    tapb_at, skip_at, dtb_at = (slice(tap_count + row, tap_count + row + 1) for row in range(3))
    item = pl.program_id(1)
    last_item = item == pl.num_programs(1) - 1
    me = lax.axis_index("seq")
    downs = [(rims.at[0], late.at[0], send_sem.at[0], recv_sem.at[0])]
    ups = [(rims.at[1], late.at[1], send_sem.at[1], recv_sem.at[1])]

    branch = pl.program_id(0)
    slots = lasts.shape[0]
    ends, backs = lasts.at[:, :states], lasts.at[:, states : 2 * states]
    totals = lasts.at[:, 2 * states :]
    exchange = Exchange(runs, 1, ends, backs, totals, last_rate, (s_last, lam_last), *exchange_scratch)

    @pl.when((item == 0) & (branch == 0))
    def _():
        greet_line(me, runs, exchange.targets())

    beside(exchange.points(), branch * slots + item, 0, slots)

    @pl.when(branch == 0)
    def _():
        s_in[...] = first_in[0, item]
        carry[...] = first_in[1, item]

    @pl.when(branch == 1)
    def _():
        s_in[...] = s_last[item]
        carry[...] = lam_last[item]

    gain = skip[pl.ds(pl.program_id(0), 1), :]
    rate2[...] = rate[...] * -LOG2E
    width = BLK * states

    @pl.when(item == 0)
    def _():
        grads[...] = jnp.zeros(grads.shape, F32)

    for cols in columns(inner):
        dxs[:toks, cols] = delta[:, cols] * act[:, cols].astype(F32)
    fold = (
        lax.broadcasted_iota(jnp.int32, (states, width), 1) % states == lax.broadcasted_iota(jnp.int32, (states, width), 0)
    ).astype(BF16)
    own = lax.broadcasted_iota(jnp.int32, (toks, width), 0) % BLK == lax.broadcasted_iota(jnp.int32, (toks, width), 1) // states
    bdiag[:toks, :] = jnp.where(own, dot_tn(proj[rank : rank + states, :].astype(BF16), fold), 0.0).astype(BF16)
    cdiag[...] = jnp.where(own, dot_tn(proj[rank + states :, :].astype(BF16), fold), 0.0).astype(BF16)
    mine = own[:BLK]
    picks = mine.astype(BF16)
    sides = (
        lax.broadcasted_iota(jnp.int32, (2 * BLK, 256), 0) // BLK == lax.broadcasted_iota(jnp.int32, (2 * BLK, 256), 1) // 128
    ).astype(BF16)
    racc[...] = jnp.zeros((states, inner), F32)
    qd_low[1] = jnp.zeros(qd_low.shape[1:], BF16)

    def lane_sum(wide):
        part = [wide[:, at : at + 128] for at in range(0, inner, 128)]
        while len(part) > 1:
            part = [sum(part[at : at + 2]) for at in range(0, len(part), 2)]
        return part[0]

    def products(slot, j):
        t0 = pl.multiple_of(j * BLK, BLK)
        gsum[pl.ds(t0, BLK), :] = dot(bdiag[pl.ds(t0, BLK), :], lam_low[slot])
        hsum[pl.ds(t0, BLK), :] = dot(picks, rq_low[slot])
        racc[...] += dot(fold[:, : BLK // 4 * states], qd_low[slot])
        both = dot_nt(sides, dots[slot])
        dc[pl.ds(t0, BLK), :] = jnp.where(mine, both[:BLK], 0.0).astype(BF16)
        db[pl.ds(t0, BLK), :] = jnp.where(mine, both[BLK:], 0.0).astype(BF16)

    def one_block(slot, j):
        t0 = pl.multiple_of(j * BLK, BLK)
        dr, xr, yr = (ref.at[pl.ds(t0, BLK), :] for ref in (delta, dxs, dy))
        tile = tiles.at[pl.ds(t0, BLK)]
        r2 = rate2[...]
        r_low = rate[...].astype(BF16)
        begin = starts[j]
        s = begin[:states] + s_in[...] * jnp.exp2(twice(begin[states:]) * r2)
        states_low[slot, :states, :] = s.astype(BF16)
        for i in range(BLK):
            a = jnp.exp2(spread(dr, i) * r2)
            decay[slot, i] = a
            s = a * s + spread(xr, i) * across_lanes(tile[i, :states], inner)
            s_low = s.astype(BF16)
            states_low[slot, (i + 1) * states : (i + 2) * states, :] = s_low
            dots[slot, i * states : (i + 1) * states, :128] = lane_sum(s_low * spread(yr, i).astype(BF16))
        y_out[pl.ds(t0, BLK), :] = dot(cdiag[pl.ds(t0, BLK), :], states_low[slot, states:, :])
        cr = carry[...]
        qds = []
        for i in reversed(range(BLK)):
            lam = cr + spread(yr, i) * across_lanes(tile[i, states:], inner)
            l_low = lam.astype(BF16)
            lam_low[slot, i * states : (i + 1) * states, :] = l_low
            dots[slot, i * states : (i + 1) * states, 128:] = lane_sum(l_low * spread(xr, i).astype(BF16))
            cr = decay[slot, i] * lam
            q = cr.astype(BF16) * states_low[slot, i * states : (i + 1) * states, :]
            rq_low[slot, i * states : (i + 1) * states, :] = q * r_low
            qds.append(q * spread(dr, i).astype(BF16))
            if i % 4 == 0:
                qd_low[slot, i // 4 * states : (i // 4 + 1) * states, :] = (qds[0] + qds[1]) + (qds[2] + qds[3])
                qds = []
        carry[...] = cr

    def block_step(k, _):
        j = blocks - 1 - 2 * k
        products(1, jnp.where(k == 0, blocks, j + 1))
        one_block(0, j)
        products(0, j)
        one_block(1, j - 1)
        return 0

    lax.fori_loop(0, blocks // 2, block_step, 0)
    products(1, 0)

    rate_grad[...] += -racc[...]
    for cols in columns(inner):
        act_f = act[:, cols].astype(F32)
        row_grads[skip_at, cols] += jnp.sum(dy[:, cols] * act_f, axis=0, keepdims=True)
        y_out[:, cols] += gain[:, cols] * act_f
        d_pre = (act_f * gsum[:toks, cols] - hsum[:toks, cols]) * sig[:, cols]
        row_grads[dtb_at, cols] += jnp.sum(d_pre, axis=0, keepdims=True)
        d_pre_low[:, cols] = d_pre.astype(BF16)
    dtp_grad[...] += dot(proj[:rank, :].astype(BF16), d_pre_low[...])[:held]
    d_proj = jnp.concatenate(
        [dot_nt(dtw[...], d_pre_low[...]), dot_nt(fold, db[:toks, :]), dot_nt(fold, dc[:toks, :])], axis=0
    ).astype(BF16)
    xp_new = dot(d_proj, act[...])
    xp_grad[:held, :] += xp_new[:held]
    xp_grad[held:, :] += xp_new[rank:]
    window = HALO + toks
    for wide_cols in columns(inner, 256):
        through = dot_tn(d_proj, xwt[:, wide_cols])
        for at in columns(256):
            cols = slice(wide_cols.start + at.start, wide_cols.start + at.stop)
            d_act = delta[:, cols] * gsum[:toks, cols] + gain[:, cols] * dy[:, cols] + through[:, at]
            d_conv = d_act * dsilu[:, cols]
            row_grads[tapb_at, cols] += jnp.sum(d_conv, axis=0, keepdims=True)
            x_f = xe[:, cols].astype(F32)
            base = jnp.concatenate([jnp.zeros((HALO, 128), F32), d_conv], axis=0)
            d_window = taps[tap_count - 1 : tap_count, cols] * base
            row_grads[tap_count - 1 : tap_count, cols] += jnp.sum(d_conv * x_f[HALO:], axis=0, keepdims=True)
            for k in range(tap_count - 1):
                moved = pltpu.roll(base, window - (tap_count - 1 - k), 0)
                row_grads[k : k + 1, cols] += jnp.sum(moved * x_f, axis=0, keepdims=True)
                d_window = d_window + taps[k : k + 1, cols] * moved
            rims[branch, item, :, cols] = d_window[HALO - 8 : HALO]
            dx_out[:, cols] = d_window[HALO:]

    @pl.when(last_item & (pl.program_id(0) == 0))
    def _():
        swap_along_line(me, runs, [], downs, True)

    @pl.when(last_item & (pl.program_id(0) == 1))
    def _():
        swap_along_line(me, runs, ups, [], True)
        swap_along_line(me, runs, ups, downs, False)

        @pl.when(me == 0)
        def _():
            late[1] = jnp.zeros(late.shape[1:], F32)

        @pl.when(me == runs - 1)
        def _():
            late[0] = jnp.zeros(late.shape[1:], F32)

        late_out[...] = late[...]


LAST_ROWS = 16
PART_ROWS = 512


class Ring:
    def __init__(self, bits):
        self.bits = bits
        self.size = 1 << len(bits)
        self.digits = [bit_of(lax.axis_index(axis), bit) for axis, bit in bits]
        self.place = sum(digit * (1 << at) for at, digit in enumerate(self.digits))

    def target(self, ahead):
        place = lax.rem(self.place + ahead, self.size)
        where = {}
        for at, (axis, bit) in enumerate(self.bits):
            base = where.get(axis, lax.axis_index(axis))
            where[axis] = base + (bit_of(place, at) - self.digits[at]) * (1 << bit)
        return where, place

    def targets(self):
        return [self.target(ahead)[0] for ahead in range(1, self.size)]


def stage_rings(runs, groups):
    bits = [("seq", bit) for bit in range(int(math.log2(runs)))] + [("dp", bit) for bit in range(int(math.log2(groups)))]
    return [Ring(bits[:1])] + [Ring(bits[at : at + 2]) for at in range(1, len(bits), 2)]


def part_count(rows):
    return -(-rows // PART_ROWS)


def buffer_rows(runs, groups):
    bits = int(math.log2(runs)) + int(math.log2(groups))
    size, total = PART_ROWS, 0
    for members in [2] + [1 << min(2, bits - at) for at in range(1, bits, 2)]:
        moved = size // members if size >= members * LAST_ROWS else size
        total += moved * (members - 1)
        size = moved
    return total


def reduce_shapes(parts, dim, runs, groups):
    bits = int(math.log2(runs)) + int(math.log2(groups))
    stages = 1 + bits // 2
    room = parts * buffer_rows(runs, groups)
    sems = pltpu.SemaphoreType.DMA((parts, 2 * stages, 3))
    return [
        pltpu.VMEM((parts * PART_ROWS, dim), F32), pltpu.VMEM((room, dim), BF16), pltpu.VMEM((room, dim), BF16),
        pltpu.VMEM((parts * PART_ROWS, dim), BF16), sems, sems,
    ]


class Reduction:
    def __init__(self, rings, turns, segments, acc, sends, arrivals, gathered, send_sem, recv_sem):
        self.rings = rings
        self.count = len(rings)
        self.parts = len(turns)
        self.segments = segments
        self.acc, self.sends, self.arrivals, self.gathered = acc, sends, arrivals, gathered
        self.send_sem, self.recv_sem = send_sem, recv_sem
        room = sends.shape[0] // self.parts
        self.steps = []
        for part, turn in enumerate(turns):
            later = rings[1:]
            turn = turn % max(len(later), 1)
            order = rings[:1] + later[turn:] + later[:turn]
            start, size, at = part * PART_ROWS, PART_ROWS, part * room
            steps = []
            for ring in order:
                split = size >= ring.size * LAST_ROWS
                moved = size // ring.size if split else size
                keep = pl.multiple_of(start + ring.place * moved, LAST_ROWS) if split else start
                steps.append((ring, start, split, moved, keep, at))
                at += moved * (ring.size - 1)
                start, size = keep, moved
            self.steps.append(steps)

    def assemble(self, part):
        low, high = part * PART_ROWS, (part + 1) * PART_ROWS
        at = 0
        for get, size in self.segments:
            first, last = max(at, low), min(at + size, high)
            if first < last:
                self.acc[first:last, :] = get(first - at, last - first)
            at += size
        if at < high:
            first = max(at, low)
            self.acc[first:high, :] = jnp.zeros((high - first, self.acc.shape[1]), F32)

    def scatter_copy(self, part, stage, ahead):
        ring, _, _, moved, _, at = self.steps[part][stage]
        at += (ahead - 1) * moved
        return remote(
            self.sends.at[pl.ds(at, moved), :], self.arrivals.at[pl.ds(at, moved), :],
            self.send_sem.at[part, stage, ahead - 1], self.recv_sem.at[part, stage, ahead - 1], ring.target(ahead)[0],
        )

    def scatter(self, part, stage):
        ring, start, split, moved, _, at = self.steps[part][stage]
        for ahead in range(1, ring.size):
            place = ring.target(ahead)[1]
            away = pl.multiple_of(start + place * moved, LAST_ROWS) if split else start
            here = at + (ahead - 1) * moved
            self.sends[here : here + moved, :] = self.acc[pl.ds(away, moved), :].astype(BF16)
            self.scatter_copy(part, stage, ahead).start()

    def settle(self, part, stage):
        ring, _, split, moved, keep, at = self.steps[part][stage]
        for ahead in range(1, ring.size):
            self.scatter_copy(part, stage, ahead).wait()
        held = self.acc[pl.ds(keep, moved), :]
        came = [
            self.arrivals[at + (ahead - 1) * moved : at + ahead * moved, :].astype(F32) for ahead in range(1, ring.size)
        ]
        if split:
            held = held + sum(came)
        else:
            values = [held.astype(BF16).astype(F32)] + came
            total = jnp.zeros_like(held)
            for place in range(ring.size):
                behind = lax.rem(ring.place - place + ring.size, ring.size)
                chosen = values[0]
                for ahead in range(1, ring.size):
                    chosen = jnp.where(behind == ahead, values[ahead], chosen)
                total = total + chosen
            held = total
        self.acc[pl.ds(keep, moved), :] = held

    def gather_copies(self, part, stage):
        ring, _, split, moved, keep, _ = self.steps[part][stage]
        here = self.gathered.at[pl.ds(keep, moved), :]
        return [
            remote(
                here, here, self.send_sem.at[part, self.count + stage, ahead - 1],
                self.recv_sem.at[part, self.count + stage, ahead - 1], ring.target(ahead)[0],
            )
            for ahead in range(1, ring.size)
            if split
        ]

    def points(self):
        def begin():
            for part in range(self.parts):
                self.assemble(part)
                self.scatter(part, 0)

        def split(stage):
            for part in range(self.parts):
                self.settle(part, stage - 1)
                self.scatter(part, stage)

        def turn():
            for part in range(self.parts):
                self.settle(part, self.count - 1)
                _, _, _, moved, keep, _ = self.steps[part][-1]
                self.gathered[pl.ds(keep, moved), :] = self.acc[pl.ds(keep, moved), :].astype(BF16)
                for copy in self.gather_copies(part, self.count - 1):
                    copy.start()

        def join(stage):
            for part in range(self.parts):
                for copy in self.gather_copies(part, stage + 1):
                    copy.wait()
                if stage >= 0:
                    for copy in self.gather_copies(part, stage):
                        copy.start()

        points = [begin]
        points += [functools.partial(split, stage) for stage in range(1, self.count)]
        points += [turn]
        return points + [functools.partial(join, stage) for stage in reversed(range(-1, self.count - 1))]


def big_segments(ref, dim):
    return [
        (lambda at, size, lane=lane: ref[at : at + size, lane : lane + dim], ref.shape[0])
        for lane in range(0, ref.shape[1], dim)
    ]


def small_segments(ref, dim):
    return [
        (lambda at, size, branch=branch, lane=lane: ref[branch, at : at + size, lane : lane + dim], ref.shape[1])
        for lane in range(0, ref.shape[2], dim)
        for branch in range(2)
    ]


def tail_kernel(
    plan, tok, cot, mod, mask, counts, hid, z_in, y, dx, late, win, wout, step,
    grads,
    mixed, d_tokens, result, x_result, factors, own_rows,
    dz, out_grad, z_grad, x_grad, mod_sum, mod_in, table, small_send, small_recv, *reduce_scratch,
):
    runs, groups, slots = plan
    dim = tok.shape[-1]
    toks, inner = z_in.shape
    now = pl.program_id(0)
    i = lax.rem(now, slots)
    rings = stage_rings(runs, groups)
    seq_ring = Ring([("seq", bit) for bit in range(int(math.log2(runs)))])
    dp_ring = Ring([("dp", bit) for bit in range(int(math.log2(groups)))])
    half = len(reduce_scratch) // 2
    smalls = small_segments(grads, dim)
    segments = big_segments(out_grad, dim) + big_segments(z_grad, dim) + smalls
    main = Reduction(rings, [part % 3 // 2 for part in range(result.shape[0] // PART_ROWS)], segments, *reduce_scratch[:half])
    rest = Reduction(rings, [part % 2 for part in range(x_result.shape[0] // PART_ROWS)], big_segments(x_grad, dim), *reduce_scratch[half:])
    main_points, rest_points = main.points(), rest.points()

    @pl.when(now == 0)
    def _():
        greet([target for ring in rings + [seq_ring, dp_ring] for target in ring.targets()])
        out_grad[...] = jnp.zeros(out_grad.shape, F32)
        z_grad[...] = jnp.zeros(z_grad.shape, F32)
        x_grad[...] = jnp.zeros(x_grad.shape, F32)
        mod_sum[...] = jnp.zeros(mod_sum.shape, F32)

    scale, gate = mod[:, dim : 2 * dim], mod[:, 2 * dim :]
    valid = as_column(mask[pl.ds(i, 1), :]) * (counts[...] > i).astype(F32)
    mod_rows = pl.ds(pl.multiple_of(8 * i, 8), 8)

    @pl.when(now < slots)
    def _():
        cot_f = cot[...].astype(F32)
        z = z_in[...]
        z_sig = jax.nn.sigmoid(z)
        z_silu = z * z_sig
        summed = y[0] + flip_full(y[1])
        gated = (summed * z_silu).astype(BF16)
        branch_out = dot(gated, wout[...])
        mixed[...] = (tok[...].astype(F32) + gate * branch_out).astype(BF16)
        d_branch = (cot_f * gate).astype(BF16)
        out_grad[...] += dot_tn(gated, d_branch)
        d_zgate = dot_nt(d_branch, wout[...]) * summed * (z_sig + z_silu * (1.0 - z_sig))
        d_low = (d_zgate * valid).astype(BF16)
        dz[i] = d_low
        z_grad[...] += dot_tn(hid[...], d_low)
        d_gate = jnp.sum(cot_f * branch_out, axis=0, keepdims=True)
        mod_sum[mod_rows, :] = jnp.concatenate([jnp.zeros((2, dim), F32), d_gate, jnp.zeros((5, dim), F32)], axis=0)

    @pl.when(now == slots)
    def _():
        main_points[0]()

    @pl.when(now >= slots)
    def _():
        edge = late.shape[2]

        def with_late(part, extra):
            return jnp.concatenate([part[: toks - edge], part[toks - edge :] + extra], axis=0)

        d_x = with_late(dx[0], late[0, i]) + flip_full(with_late(dx[1], late[1, i]))
        d_x = (d_x * valid).astype(BF16)
        x_grad[...] += dot_tn(hid[...], d_x)
        d_hidden = dot_nt(d_x, win[:, :inner]) + dot_nt(dz[i], win[:, inner:])
        normed, inv_std = normalise(tok[...].astype(F32))
        d_shift = jnp.sum(d_hidden, axis=0, keepdims=True)
        d_scale = jnp.sum(d_hidden * normed, axis=0, keepdims=True)
        mod_sum[mod_rows, :] += jnp.concatenate([d_shift, d_scale, jnp.zeros((6, dim), F32)], axis=0)
        d_normed = d_hidden * (1.0 + scale)
        d_tokens[...] = cot[...].astype(F32) + inv_std * (
            d_normed
            - jnp.mean(d_normed, axis=-1, keepdims=True)
            - normed * jnp.mean(d_normed * normed, axis=-1, keepdims=True)
        )

    @pl.when(now == slots)
    def _():
        main_points[1]()

    def sum_copies():
        return [
            remote(mod_sum, mod_in.at[ahead - 1], small_send.at[ahead - 1], small_recv.at[ahead - 1], seq_ring.target(ahead)[0])
            for ahead in range(1, seq_ring.size)
        ]

    def table_copies():
        at = pl.multiple_of(dp_ring.place * 16, 16)
        here = table.at[pl.ds(at, 16), :]
        base = seq_ring.size - 1
        return [
            remote(here, here, small_send.at[base + ahead - 1], small_recv.at[base + ahead - 1], dp_ring.target(ahead)[0])
            for ahead in range(1, dp_ring.size)
        ]

    def start_small():
        for copy in sum_copies():
            copy.start()

    def turn_small():
        for copy in sum_copies():
            copy.wait()
        values = [mod_sum[...]] + [mod_in[ahead - 1] for ahead in range(1, seq_ring.size)]
        total = jnp.zeros(mod_sum.shape, F32)
        for place in range(seq_ring.size):
            behind = lax.rem(seq_ring.place - place + seq_ring.size, seq_ring.size)
            chosen = values[0]
            for ahead in range(1, seq_ring.size):
                chosen = jnp.where(behind == ahead, values[ahead], chosen)
            total = total + chosen
        time_f = step[...].astype(F32)
        time_low = time_f * jax.nn.sigmoid(time_f)
        lines = [total[8 * item : 8 * item + 3] for item in range(slots)] + [time_low]
        lines.append(jnp.zeros((16 - 4 * slots, dim), F32))
        own = jnp.concatenate(lines, axis=0).astype(BF16)
        own_rows[...] = own
        table[pl.ds(pl.multiple_of(dp_ring.place * 16, 16), 16), :] = own
        for copy in table_copies():
            copy.start()

    def end_small():
        for copy in table_copies():
            copy.wait()
        factors[...] = table[...]

    @pl.when(now == 2 * slots - 1)
    def _():
        start_small()
        rest_points[0]()
        rest_points[1]()
        for at in range(2, len(main_points)):
            main_points[at]()
            if at == 2:
                turn_small()
            rest_points[at]()
        end_small()
        result[...] = main.gathered[...]
        x_result[...] = rest.gathered[...]


def finish_kernel(
    outs, zs, xs, smalls, factors, own, step, ada,
    grad_time, grad_ada, grad_ada_bias, in_grad, tap_grad, tapb_grad, xp_grad, dtp_grad, dtb_grad, rate_grad, skip_grad, out_grad,
):
    dim, inner = in_grad.shape[0], rate_grad.shape[2]
    slots = step.shape[0]
    now = pl.program_id(0)
    out_grad[...] = outs[...].astype(F32)
    in_grad[...] = jnp.where(now < inner // dim, xs[...], zs[...]).astype(F32)
    table = factors[...]
    length = table.shape[0]

    for part in range(3):

        @pl.when(now == part)
        def _():
            row = lax.broadcasted_iota(jnp.int32, (length, length), 0)
            col = lax.broadcasted_iota(jnp.int32, (length, length), 1)
            item = row % 16 - 3 * slots
            wanted = row // 16 * 16 + 3 * item + part
            mods = dot(((col == wanted) & (item >= 0) & (item < slots)).astype(BF16), table)
            lanes = slice(part * dim, (part + 1) * dim)
            grad_ada[...] = dot_tn(table, mods.astype(BF16))
            grad_ada_bias[lanes] = jnp.sum(mods, axis=0)
            mine = own[...].astype(F32)
            picked = jnp.concatenate([mine[3 * i + part : 3 * i + part + 1] for i in range(slots)], axis=0)
            d_time = dot_nt(picked.astype(BF16), ada[...])
            grad_time[...] = d_time if part == 0 else grad_time[...] + d_time

    @pl.when(now == 3)
    def _():
        time_f = step[...].astype(F32)
        time_sig = jax.nn.sigmoid(time_f)
        grad_time[...] = grad_time[...] * time_sig * (1.0 + time_f * (1.0 - time_sig))
        at = 0
        for first in range(0, inner, dim):
            lanes = slice(first, first + dim)
            for branch in range(2):
                for ref in (xp_grad, dtp_grad, rate_grad, tap_grad):
                    size = ref.shape[1]
                    ref[branch, :, lanes] = smalls[at : at + size, :].astype(F32)
                    at += size
                for ref in (tapb_grad, skip_grad, dtb_grad):
                    ref[branch : branch + 1, lanes] = smalls[at : at + 1, :].astype(F32)
                    at += 1
                at += 1


def params(**more):
    return pltpu.CompilerParams(vmem_limit_bytes=VMEM_LIMIT, **more)


def spec(block, index):
    return pl.BlockSpec(block, index)


def per_device(
    tokens, timestep, counts, token_mask, ada_weight, ada_bias, input_weight, conv_weight, conv_bias, x_weight, dt_weight,
    dt_bias, decay_rate, skip_gain, output_weight, cotangent,
):
    slots, toks, dim = tokens.shape
    inner = output_weight.shape[0]
    rank = dt_weight.shape[1]
    states = decay_rate.shape[1]
    tap_count = conv_weight.shape[1]
    wide_rank = WIDE_RANK
    proj_rows = wide_rank + 2 * states
    blocks = toks // BLK
    runs = lax.axis_size("seq")
    groups = lax.axis_size("dp")
    counts2 = counts[:, None]
    x_rows = jnp.swapaxes(x_weight, 1, 2)

    def item(*block):
        return spec((None,) + block, lambda i: (i,) + (0,) * len(block))

    def whole(*block):
        return spec(block, lambda *_: (0,) * len(block))

    xe, dy, z_gate, hid, modulate = pl.pallas_call(
        functools.partial(enter_kernel, runs),
        grid=(slots,),
        in_specs=[
            whole(slots, toks, dim), item(toks, dim), whole(slots, toks), whole(1, 1), whole(slots, dim), whole(dim, 3 * dim),
            whole(3 * dim), whole(dim, 2 * inner), whole(inner, dim),
        ],
        out_specs=[
            item(2, HALO + toks, inner), item(2, toks, inner), item(toks, inner), item(toks, dim), item(1, 3 * dim),
        ],
        out_shape=[
            jax.ShapeDtypeStruct((slots, 2, HALO + toks, inner), BF16),
            jax.ShapeDtypeStruct((slots, 2, toks, inner), F32),
            jax.ShapeDtypeStruct((slots, toks, inner), F32),
            jax.ShapeDtypeStruct((slots, toks, dim), BF16),
            jax.ShapeDtypeStruct((slots, 1, 3 * dim), F32),
        ],
        scratch_shapes=[
            pltpu.VMEM((slots, 3 * dim), F32),
            pltpu.VMEM((slots, HALO, dim), BF16), pltpu.VMEM((slots, HALO, dim), BF16), pltpu.VMEM((slots, toks), jnp.int32),
            pltpu.VMEM((slots, toks), jnp.int32), pltpu.SemaphoreType.DMA((4,)), pltpu.SemaphoreType.DMA((4,)),
        ],
        compiler_params=params(collective_id=1, has_side_effects=True),
        name="enter",
    )(
        tokens, cotangent, token_mask, counts2, timestep, ada_weight, ada_bias, input_weight, output_weight,
    )

    def unit(*block):
        return spec((None, None) + block, lambda b, i: (i, b) + (0,) * len(block))

    def branch(*block):
        return spec((None,) + block, lambda b, i: (b,) + (0,) * len(block))

    def unit_shape(*block, kind=F32):
        return jax.ShapeDtypeStruct((slots, 2) + block, kind)

    act, planes, proj, lasts, starts, tiles, weights, first_in = pl.pallas_call(
        functools.partial(first_kernel, runs, slots),
        grid=(2, slots),
        in_specs=[
            unit(HALO + toks, inner), unit(toks, inner), branch(tap_count, inner), whole(2, inner),
            branch(rank + 2 * states, inner), branch(rank, inner), whole(2, inner), branch(states, inner),
        ],
        out_specs=[
            unit(toks, inner), unit(3, toks, inner), unit(proj_rows, toks), unit(2 * states + 8, inner),
            unit(blocks, states + 8, inner), unit(toks, 2 * states, 128), branch(proj_rows + wide_rank, inner),
            whole(2, slots, states, inner),
        ],
        out_shape=[
            unit_shape(toks, inner, kind=BF16), unit_shape(3, toks, inner), unit_shape(proj_rows, toks),
            unit_shape(2 * states + 8, inner), unit_shape(blocks, states + 8, inner), unit_shape(toks, 2 * states, 128),
            jax.ShapeDtypeStruct((2, proj_rows + wide_rank, inner), BF16),
            jax.ShapeDtypeStruct((2, slots, states, inner), F32),
        ],
        scratch_shapes=[
            pltpu.VMEM((toks, inner), F32), pltpu.VMEM((2, BLK, states, inner), F32), pltpu.VMEM((8, inner), F32),
            pltpu.VMEM((states, inner), F32), pltpu.VMEM((2 * states * toks, 128), F32),
            pltpu.VMEM((4 * states, 2 * states * 128), BF16), pltpu.VMEM((slots, states, inner), F32),
            pltpu.VMEM((slots, states, inner), F32), pltpu.VMEM((slots, 1, inner), F32), pltpu.VMEM((states, inner), F32),
            *exchange_shapes(runs, slots, states, inner),
        ],
        compiler_params=params(collective_id=2, has_side_effects=True),
        name="first",
    )(xe, dy, conv_weight, conv_bias, x_rows, dt_weight, dt_bias, decay_rate)

    vmem = pl.BlockSpec(memory_space=pltpu.VMEM)
    last = spec((slots, None, 2 * states + 8, inner), lambda b, i: (0, 1, 0, 0))
    last_branch = spec((None, states, inner), lambda b, i: (1, 0, 0))

    grad_rows = 2 * rank + 3 * states + 8
    y, dx, late, grads = pl.pallas_call(
        functools.partial(second_kernel, runs),
        grid=(2, slots),
        in_specs=[
            whole(2, slots, states, inner), last, last_branch, unit(blocks, states + 8, inner), unit(toks, 2 * states, 128),
            branch(states, inner), unit(HALO + toks, inner), unit(toks, inner), unit(3, toks, inner), unit(toks, inner),
            unit(proj_rows, toks), branch(proj_rows + wide_rank, inner), branch(tap_count, inner), whole(2, inner),
        ],
        out_specs=[unit(toks, inner), unit(toks, inner), whole(2, slots, 8, inner), branch(grad_rows, inner)],
        out_shape=[
            unit_shape(toks, inner), unit_shape(toks, inner), jax.ShapeDtypeStruct((2, slots, 8, inner), F32),
            jax.ShapeDtypeStruct((2, grad_rows, inner), F32),
        ],
        scratch_shapes=[
            pltpu.VMEM((states, inner), F32), pltpu.VMEM((states, inner), F32), pltpu.VMEM((toks + BLK, inner), F32), pltpu.VMEM((toks + BLK, BLK * states), BF16),
            pltpu.VMEM((toks, BLK * states), BF16),
            pltpu.VMEM((2, BLK, states, inner), F32),
            pltpu.VMEM((2, (BLK + 1) * states, inner), BF16), pltpu.VMEM((2, BLK * states, inner), BF16),
            pltpu.VMEM((2, BLK * states, inner), BF16), pltpu.VMEM((2, BLK // 4 * states, inner), BF16),
            pltpu.VMEM((2, BLK * states, 256), BF16), pltpu.VMEM((states, inner), F32),
            pltpu.VMEM((toks + BLK, inner), F32), pltpu.VMEM((toks + BLK, inner), F32),
            pltpu.VMEM((toks + BLK, BLK * states), BF16), pltpu.VMEM((toks + BLK, BLK * states), BF16),
            pltpu.VMEM((2, slots, 8, inner), F32), pltpu.VMEM((2, slots, 8, inner), F32),
            pltpu.SemaphoreType.DMA((2,)), pltpu.SemaphoreType.DMA((2,)), pltpu.VMEM((toks, inner), BF16),
            pltpu.VMEM((states, inner), F32), pltpu.VMEM((slots, states, inner), F32), pltpu.VMEM((slots, states, inner), F32),
            *exchange_shapes(runs, slots, states, inner),
        ],
        compiler_params=params(collective_id=3, has_side_effects=True),
        name="second",
    )(
        first_in, lasts, decay_rate, starts, tiles, decay_rate, xe, act, planes, dy, proj, weights, conv_weight, skip_gain,
    )

    def now(*block):
        return spec((None,) + block, lambda s: (s % slots,) + (0,) * len(block))

    def early(*block):
        return spec((None,) + block, lambda s: (jnp.minimum(s, slots - 1),) + (0,) * len(block))

    def after(*block):
        return spec((None,) + block, lambda s: (jnp.maximum(s - slots, 0),) + (0,) * len(block))

    small_rows = 2 * grad_rows * (inner // dim)
    main_parts = part_count(inner + dim * (inner // dim) + small_rows)
    rest_parts = part_count(dim * (inner // dim))
    mixed, d_tokens, result, x_result, factors, own = pl.pallas_call(
        functools.partial(tail_kernel, (runs, groups, slots)),
        grid=(2 * slots,),
        in_specs=[
            now(toks, dim), now(toks, dim), now(1, 3 * dim), whole(slots, toks), whole(1, 1), now(toks, dim),
            early(toks, inner), early(2, toks, inner), after(2, toks, inner), whole(2, slots, 8, inner),
            whole(dim, 2 * inner), whole(inner, dim), whole(slots, dim), whole(2, grad_rows, inner),
        ],
        out_specs=[
            early(toks, dim), after(toks, dim), whole(main_parts * PART_ROWS, dim), whole(rest_parts * PART_ROWS, dim),
            whole(16 * groups, dim), whole(16, dim),
        ],
        out_shape=[
            jax.ShapeDtypeStruct((slots, toks, dim), BF16), jax.ShapeDtypeStruct((slots, toks, dim), F32),
            jax.ShapeDtypeStruct((main_parts * PART_ROWS, dim), BF16), jax.ShapeDtypeStruct((rest_parts * PART_ROWS, dim), BF16),
            jax.ShapeDtypeStruct((16 * groups, dim), BF16), jax.ShapeDtypeStruct((16, dim), BF16),
        ],
        scratch_shapes=[
            pltpu.VMEM((slots, toks, inner), BF16), pltpu.VMEM((inner, dim), F32), pltpu.VMEM((dim, inner), F32),
            pltpu.VMEM((dim, inner), F32), pltpu.VMEM((8 * slots, dim), F32), pltpu.VMEM((max(runs - 1, 1), 8 * slots, dim), F32),
            pltpu.VMEM((16 * groups, dim), BF16), pltpu.SemaphoreType.DMA((runs + groups,)),
            pltpu.SemaphoreType.DMA((runs + groups,)), *reduce_shapes(main_parts, dim, runs, groups),
            *reduce_shapes(rest_parts, dim, runs, groups),
        ],
        compiler_params=params(collective_id=4, has_side_effects=True),
        name="tail",
    )(
        tokens, cotangent, modulate, token_mask, counts2, hid, z_gate, y, dx, late, input_weight, output_weight, timestep, grads,
    )

    (
        d_time, grad_ada, grad_ada_bias, in_grad, tap_grad, tapb_grad, xp_grad, dtp_grad, dtb_grad, rate_grad, skip_grad,
        out_grad,
    ) = pl.pallas_call(
        finish_kernel,
        grid=(4,),
        in_specs=[
            spec((inner // 4, dim), lambda s: (s, 0)),
            spec((dim, dim), lambda s: (inner // dim + jnp.maximum(s - inner // dim, 0), 0)),
            spec((dim, dim), lambda s: (jnp.minimum(s, inner // dim - 1), 0)),
            spec((PART_ROWS, dim), lambda s: (2 * inner // PART_ROWS, 0)),
            whole(16 * groups, dim), whole(16, dim), whole(slots, dim), spec((dim, dim), lambda s: (0, jnp.minimum(s, 2))),
        ],
        out_specs=[
            whole(slots, dim), spec((dim, dim), lambda s: (0, jnp.minimum(s, 2))), whole(3 * dim),
            spec((dim, 2 * inner // 4), lambda s: (0, s)), whole(2, tap_count, inner), whole(2, inner),
            whole(2, rank + 2 * states, inner), whole(2, rank, inner), whole(2, inner), whole(2, states, inner), whole(2, inner),
            spec((inner // 4, dim), lambda s: (s, 0)),
        ],
        out_shape=[
            jax.ShapeDtypeStruct(shape, F32)
            for shape in (
                (slots, dim), (dim, 3 * dim), (3 * dim,), (dim, 2 * inner), (2, tap_count, inner), (2, inner),
                (2, rank + 2 * states, inner), (2, rank, inner), (2, inner), (2, states, inner), (2, inner), (inner, dim),
            )
        ],
        compiler_params=params(),
        name="finish",
    )(result, result, x_result, result, factors, own, timestep, ada_weight)
    return (
        mixed, d_tokens, d_time, grad_ada, grad_ada_bias, in_grad, tap_grad, tapb_grad, jnp.swapaxes(xp_grad, 1, 2), dtp_grad, dtb_grad,
        rate_grad, skip_grad, out_grad,
    )


def solution(mesh):
    runs = P("dp", "seq", None)
    return jax.shard_map(
        per_device,
        mesh=mesh,
        in_specs=(runs, P("dp", None), P("dp"), P("dp", "seq")) + (P(),) * 11 + (runs,),
        out_specs=(runs, runs, P("dp", None)) + (P(),) * 11,
        check_vma=False,
    )
```

```python
import functools
import math

import jax
import jax.numpy as jnp
from jax import lax
from jax.experimental import pallas as pl
from jax.experimental.pallas import tpu as pltpu
from jax.sharding import PartitionSpec as P

EPSILON = 1e-06
BLK = 16
WIDE_RANK = 32
HALO = 16
LOG2E = math.log2(math.e)
F32, BF16 = jnp.float32, jnp.bfloat16
NT = (((1,), (1,)), ((), ()))
TN = (((0,), (0,)), ((), ()))
VMEM_LIMIT = 60 << 20
MESH = pl.DeviceIdType.MESH


def dot(a, b):
    return jnp.dot(a, b, preferred_element_type=F32)


def dot_nt(a, b):
    return lax.dot_general(a, b, NT, preferred_element_type=F32)


def dot_tn(a, b):
    return lax.dot_general(a, b, TN, preferred_element_type=F32)


def flip_full(value):
    turned = lax.broadcasted_iota(jnp.int32, (8, value.shape[1]), 0)
    groups = [value[at : at + 8] for at in range(0, value.shape[0], 8)]
    return jnp.concatenate([jnp.take_along_axis(group, 7 - turned, axis=0) for group in reversed(groups)], axis=0)


def flip_low(value):
    return flip_full(value.astype(F32)).astype(BF16)


def normalise(tokens_f):
    centered = tokens_f - jnp.mean(tokens_f, axis=-1, keepdims=True)
    inv_std = lax.rsqrt(jnp.mean(centered * centered, axis=-1, keepdims=True) + EPSILON)
    return centered * inv_std, inv_std


def eye(size):
    rows = lax.broadcasted_iota(jnp.int32, (size, size), 0)
    cols = lax.broadcasted_iota(jnp.int32, (size, size), 1)
    return (rows == cols).astype(BF16)


def as_column(row):
    return dot_nt(eye(row.shape[1]), jnp.broadcast_to(row.astype(F32).astype(BF16), (8, row.shape[1])))[:, :1]


def remote(src, dst, send_sem, recv_sem, target):
    return pltpu.make_async_remote_copy(
        src_ref=src, dst_ref=dst, send_sem=send_sem, recv_sem=recv_sem, device_id=target, device_id_type=MESH
    )


def greet(targets):
    barrier = pltpu.get_barrier_semaphore()
    for target in targets:
        pl.semaphore_signal(barrier, inc=1, device_id=target, device_id_type=MESH)
    pl.semaphore_wait(barrier, len(targets))


def greet_line(me, runs, others=()):
    barrier = pltpu.get_barrier_semaphore()
    for target in others:
        pl.semaphore_signal(barrier, inc=1, device_id=target, device_id_type=MESH)

    @pl.when(me > 0)
    def _():
        pl.semaphore_signal(barrier, inc=1, device_id={"seq": me - 1}, device_id_type=MESH)

    @pl.when(me < runs - 1)
    def _():
        pl.semaphore_signal(barrier, inc=1, device_id={"seq": me + 1}, device_id_type=MESH)

    neighbours = lax.div(me + runs - 1, runs) + lax.div(2 * runs - 2 - me, runs)
    pl.semaphore_wait(barrier, neighbours + len(others))


def swap_along_line(me, runs, ups, downs, start):
    up = [remote(src, dst, ss, rs, {"seq": me + 1}) for src, dst, ss, rs in ups]
    down = [remote(src, dst, ss, rs, {"seq": me - 1}) for src, dst, ss, rs in downs]

    @pl.when(me < runs - 1)
    def _():
        for copy in up:
            if start:
                copy.start()
            else:
                copy.wait_send()
        if not start:
            for copy in down:
                copy.wait_recv()

    @pl.when(me > 0)
    def _():
        for copy in down:
            if start:
                copy.start()
            else:
                copy.wait_send()
        if not start:
            for copy in up:
                copy.wait_recv()


def enter_kernel(
    runs, tok, cot, mask, counts, step, ada, ada_bias, win, wout,
    xe, dy, z_out, hid_out, mod_out,
    mods, prev_tok, next_tok, prev_mask, next_mask, send_sem, recv_sem,
):
    slots, toks, dim = tok.shape
    inner = wout.shape[0]
    me = lax.axis_index("seq")
    i = pl.program_id(0)
    ups = [
        (tok.at[:, pl.ds(toks - HALO, HALO), :], prev_tok, send_sem.at[0], recv_sem.at[0]),
        (mask, prev_mask, send_sem.at[1], recv_sem.at[1]),
    ]
    downs = [
        (tok.at[:, pl.ds(0, HALO), :], next_tok, send_sem.at[2], recv_sem.at[2]),
        (mask, next_mask, send_sem.at[3], recv_sem.at[3]),
    ]

    @pl.when(i == 0)
    def _():
        greet_line(me, runs)
        swap_along_line(me, runs, ups, downs, True)

        @pl.when(me == 0)
        def _():
            prev_tok[...] = jnp.zeros(prev_tok.shape, BF16)
            prev_mask[...] = jnp.zeros(prev_mask.shape, jnp.int32)

        @pl.when(me == runs - 1)
        def _():
            next_tok[...] = jnp.zeros(next_tok.shape, BF16)
            next_mask[...] = jnp.zeros(next_mask.shape, jnp.int32)

    live = (counts[...] > i).astype(F32)

    @pl.when(i == 0)
    def _():
        time_f = step[...].astype(F32)
        time_low = (time_f * jax.nn.sigmoid(time_f)).astype(BF16)
        mods[...] = dot(time_low, ada[...]) + ada_bias[...].reshape(1, 3 * dim)

    mod = mods[pl.ds(i, 1), :]
    mod_out[...] = mod
    shift, scale, gate = mod[:, :dim], mod[:, dim : 2 * dim], mod[:, 2 * dim :]

    def hidden_of(part):
        normed, _ = normalise(part.astype(F32))
        return (normed * (1.0 + scale) + shift).astype(BF16)

    hid = hidden_of(tok[i])
    hid_out[...] = hid
    xz = dot(hid, win[...]) * (as_column(mask[pl.ds(i, 1), :]) * live)
    x_low = xz[:, :inner].astype(BF16)
    z = xz[:, inner:]
    z_out[...] = z
    d_branch = (cot[...].astype(F32) * gate).astype(BF16)
    d_summed = dot_nt(d_branch, wout[...]) * z * jax.nn.sigmoid(z)
    dy[0] = d_summed
    dy[1] = flip_full(d_summed)
    xe[0, HALO:, :] = x_low
    xe[1, HALO:, :] = flip_low(x_low)

    @pl.when(i == 0)
    def _():
        swap_along_line(me, runs, ups, downs, False)

    rims = jnp.concatenate([prev_tok[i], next_tok[i]], axis=0)
    prev_col = as_column(prev_mask[pl.ds(i, 1), :])[toks - HALO :]
    next_col = as_column(next_mask[pl.ds(i, 1), :])[:HALO]
    rim_x = dot(hidden_of(rims), win[:, :inner]) * (jnp.concatenate([prev_col, next_col], axis=0) * live)
    rim_x = rim_x.astype(BF16)
    xe[0, :HALO, :] = rim_x[:HALO]
    xe[1, :HALO, :] = flip_low(rim_x[HALO:])


def columns(inner, width=128):
    return [slice(at, at + width) for at in range(0, inner, width)]


def twice(row8):
    return jnp.concatenate([row8, row8], axis=0)


def spread(ref, index):
    return twice(ref[pl.ds(index, 8, stride=0), :])


def lay_out(wide, rows, picks):
    count, toks = rows.shape
    high = rows.astype(BF16).astype(F32)
    halves = jnp.concatenate([high, rows - high], axis=0).T.astype(BF16)
    for n in range(0, count, 2):
        pair = dot(halves, picks[:, n * 128 : (n + 2) * 128])
        for t in range(0, toks, 8):
            for k in range(2):
                at = 8 * (count * (t // 8) + n + k)
                wide[at : at + 8, :] = pair[t : t + 8, k * 128 : (k + 1) * 128]


def wide_tile(wide, i, count):
    at = 8 * count * (i // 8) + i % 8
    return jnp.concatenate([wide[pl.ds(at + 64 * n, 8, stride=8), :] for n in range(count // 8)], axis=0)


def across_lanes(tile, inner):
    return jnp.concatenate([tile] * (inner // 128), axis=1)


def softplus_parts(pre):
    e = jnp.exp2(-LOG2E * jnp.abs(pre))
    more = jnp.where(e < 1e-3, e - 0.5 * e * e, jnp.log(1.0 + e))
    return jnp.maximum(pre, 0.0) + more, jax.nn.sigmoid(pre)


def bit_of(index, bit):
    return lax.rem(lax.div(index, 1 << bit), 2)


def across(axis, bit):
    me = lax.axis_index(axis)
    mine = bit_of(me, bit)
    return mine, {axis: me + (1 - 2 * mine) * (1 << bit)}


class Exchange:
    def __init__(self, runs, branch, ends, backs, totals, rate, results, group, span, pre, pre_span, sends, arrivals, sems):
        self.branch, self.rate = branch, rate
        self.sources, self.totals, self.results = (ends, backs), totals, results
        self.group, self.span, self.pre, self.pre_span = group, span, pre, pre_span
        self.sends, self.arrivals, self.sems = sends, arrivals, sems
        self.links = [across("seq", bit) for bit in range(int(math.log2(runs)))]
        self.slots = ends.shape[0]
        self.states, self.inner = rate.shape

    def flow(self, kind):
        return kind if self.branch == 0 else 1 - kind

    def targets(self):
        return [target for _, target in self.links]

    def copy(self, stage, kind):
        at = 2 * stage + kind
        return remote(
            self.sends.at[at], self.arrivals.at[at], self.sems.at[0, at], self.sems.at[1, at], self.links[stage][1]
        )

    def send(self, stage, kind):
        rows = self.slots * self.states
        at = 2 * stage + kind
        for i in range(self.slots):
            self.sends[at, i * self.states : (i + 1) * self.states, :] = self.group[kind, i].astype(BF16)
        high = self.span[kind].astype(BF16).astype(F32)
        self.sends[at, rows:, :] = jnp.concatenate([high, self.span[kind] - high], axis=0).astype(BF16)
        self.copy(stage, kind).start()

    def join(self, stage, kind, last):
        mine = self.links[stage][0]
        self.copy(stage, kind).wait()
        at = 2 * stage + kind
        earlier = (mine == 1) if self.flow(kind) == 0 else (mine == 0)
        both = self.arrivals[at, self.slots * self.states :, :].astype(F32)
        length = both[: both.shape[0] // 2] + both[both.shape[0] // 2 :]
        own_span, pre_span = self.span[kind], self.pre_span[kind]
        second_span = jnp.where(earlier, own_span, length)
        rate = self.rate[...] * -LOG2E
        for i in range(self.slots):
            state = self.arrivals[at, i * self.states : (i + 1) * self.states, :].astype(F32)
            before = self.pre[kind, i]
            self.pre[kind, i] = jnp.where(earlier, state * jnp.exp2(rate * pre_span[i : i + 1]) + before, before)
            if not last:
                own = self.group[kind, i]
                first, second = jnp.where(earlier, state, own), jnp.where(earlier, own, state)
                self.group[kind, i] = first * jnp.exp2(rate * second_span[i : i + 1]) + second
        self.pre_span[kind] = jnp.where(earlier, length + pre_span, pre_span)
        if not last:
            self.span[kind] = own_span + length

    def points(self):
        count = len(self.links)

        def begin():
            self.pre[...] = jnp.zeros(self.pre.shape, F32)
            self.pre_span[...] = jnp.zeros(self.pre_span.shape, F32)
            self.span[...] = jnp.zeros(self.span.shape, F32)
            for kind in range(2):
                for i in range(self.slots):
                    self.group[kind, i] = self.sources[kind][i]
                    self.span[kind, i : i + 1, :] = self.totals[i][:1]
                if count:
                    self.send(0, kind)

        def step(stage):
            last = stage == count - 1
            for kind in range(2):
                self.join(stage, kind, last)
                if not last:
                    self.send(stage + 1, kind)

        def end():
            for kind in range(2):
                for i in range(self.slots):
                    self.results[kind][i] = self.pre[kind, i]

        return [begin] + [functools.partial(step, stage) for stage in range(count)] + [end]


def exchange_shapes(runs, slots, states, inner):
    pairs = max(int(math.log2(runs)), 1)
    span_rows = -(-slots // 8) * 8
    return [
        pltpu.VMEM((2, slots, states, inner), F32), pltpu.VMEM((2, span_rows, inner), F32),
        pltpu.VMEM((2, slots, states, inner), F32), pltpu.VMEM((2, span_rows, inner), F32),
        pltpu.VMEM((2 * pairs, slots * states + 2 * span_rows, inner), BF16),
        pltpu.VMEM((2 * pairs, slots * states + 2 * span_rows, inner), BF16),
        pltpu.SemaphoreType.DMA((2, 2 * pairs)),
    ]


def beside(points, step, first, count):
    for at in range(min(len(points), count)):
        todo = points[at:] if at == count - 1 else points[at : at + 1]

        @pl.when(step == first + at)
        def _():
            for point in todo:
                point()


def first_kernel(
    runs, slots, xe, dy, taps, tap_bias, x_rows, dt_rows, dt_bias, rate,
    act_out, planes, proj_out, last_out, starts_out, tiles, weights, first_in,
    dx, decay, through, rate2, wide, picks, ends, backs, totals, first_rate, *exchange_scratch,
):
    toks, inner = dy.shape
    states = rate.shape[0]
    blocks = toks // BLK
    rank = WIDE_RANK
    xwt, dtw = weights.at[: weights.shape[0] - rank], weights.at[weights.shape[0] - rank :]
    delta_out, sig_out, dsilu_out = (planes.at[at] for at in range(3))
    end_out, back_out = last_out.at[:states], last_out.at[states : 2 * states]
    tap_count = taps.shape[0]
    branch, item = pl.program_id(0), pl.program_id(1)
    results = (first_in.at[0], first_in.at[1])
    exchange = Exchange(runs, 0, ends, backs, totals, first_rate, results, *exchange_scratch)

    @pl.when((branch == 0) & (item == 0))
    def _():
        greet(exchange.targets())
        first_rate[...] = rate[...]

    beside(exchange.points(), branch * slots + item, slots, slots)

    @pl.when(item == 0)
    def _():
        rate2[...] = rate[...] * -LOG2E
        picks[...] = (
            lax.broadcasted_iota(jnp.int32, picks.shape, 0) % (2 * states)
            == lax.broadcasted_iota(jnp.int32, picks.shape, 1) // 128
        ).astype(BF16)
        held = dt_rows.shape[0]
        rows = x_rows[...].astype(F32)
        gap = jnp.zeros((rank - held, inner), F32)
        wide = [rows[:held], gap, rows[held:], dt_rows[...].astype(F32), gap]
        weights[...] = jnp.concatenate(wide, axis=0).astype(BF16)

    tap_row, dt_row = tap_bias[pl.ds(branch, 1), :], dt_bias[pl.ds(branch, 1), :]
    for cols in columns(inner):
        x_f = xe[:, cols].astype(F32)
        conv = tap_row[:, cols] + taps[tap_count - 1 : tap_count, cols] * x_f[HALO:]
        for k in range(tap_count - 1):
            conv = conv + taps[k : k + 1, cols] * pltpu.roll(x_f, tap_count - 1 - k, 0)[HALO:]
        open_part = jax.nn.sigmoid(conv)
        act_f = conv * open_part
        act_out[:, cols] = act_f.astype(BF16)
        dsilu_out[:, cols] = open_part + act_f * (1.0 - open_part)
    proj = dot_nt(xwt[...], act_out[...])
    proj_out[...] = proj
    dt_low = proj[:rank, :].astype(BF16)
    for cols in columns(inner, 256):
        pre = dot_tn(dt_low, dtw[:, cols]) + dt_row[:, cols]
        delta, slope = softplus_parts(pre)
        delta_out[:, cols] = delta
        sig_out[:, cols] = slope
        dx[:, cols] = delta * act_out[:, cols].astype(F32)
    lay_out(wide, proj[rank:, :], picks)
    end_out[...] = jnp.zeros((states, inner), F32)
    back_out[...] = jnp.zeros((states, inner), F32)
    through[...] = jnp.zeros((8, inner), F32)

    def one_block(j, slot):
        t0 = pl.multiple_of(j * BLK, BLK)
        dr, xr, yr = (ref.at[pl.ds(t0, BLK), :] for ref in (delta_out, dx, dy))
        count = 2 * states
        wide_rows = wide.at[pl.ds(pl.multiple_of(j * (BLK * count), BLK * count), BLK * count), :]
        s = end_out[...]
        before = through[...]
        starts_out[j] = jnp.concatenate([s, before], axis=0)
        rates = rate2[...]
        for i in range(BLK):
            a = jnp.exp2(spread(dr, i) * rates)
            decay[slot, i] = a
            tile = wide_tile(wide_rows, i, count)
            tiles[t0 + i] = tile
            s = a * s + spread(xr, i) * across_lanes(tile[:states], inner)
        end_out[...] = s
        m = jnp.zeros((states, inner), F32)
        for i in reversed(range(BLK)):
            m = decay[slot, i] * (m + spread(yr, i) * across_lanes(tiles[t0 + i, states:], inner))
        back_out[...] = back_out[...] + m * jnp.exp2(twice(before) * rates)
        through[...] = before + jnp.sum(dr[...], axis=0, keepdims=True)

    def block_step(k, _):
        one_block(2 * k, 0)
        one_block(2 * k + 1, 1)
        return 0

    lax.fori_loop(0, blocks // 2, block_step, 0)
    last_out[2 * states :, :] = through[...]

    @pl.when(branch == 0)
    def _():
        ends[item] = end_out[...]
        backs[item] = back_out[...]
        totals[item] = through[:1, :]


def second_kernel(
    runs, first_in, lasts, last_rate, starts, tiles, rate, xe, act, planes, dy, proj, weights, taps, skip,
    y_out, dx_out, late_out, grads,
    rate2, carry, dxs, bdiag, cdiag, decay, states_low, lam_low, rq_low, qd_low, dots, racc, gsum, hsum, db, dc,
    rims, late, send_sem, recv_sem, d_pre_low, s_in, s_last, lam_last, *exchange_scratch,
):
    toks, inner = dy.shape
    states = rate.shape[0]
    blocks = toks // BLK
    rank = WIDE_RANK
    xwt, dtw = weights.at[: weights.shape[0] - rank], weights.at[weights.shape[0] - rank :]
    delta, sig, dsilu = (planes.at[at] for at in range(3))
    tap_count = taps.shape[0]
    held = (grads.shape[0] - 3 * states - 8) // 2
    xp_grad, dtp_grad = grads.at[: held + 2 * states], grads.at[held + 2 * states : 2 * held + 2 * states]
    at = 2 * held + 2 * states
    rate_grad, row_grads = grads.at[at : at + states], grads.at[at + states : at + states + 8]
    tapb_at, skip_at, dtb_at = (slice(tap_count + row, tap_count + row + 1) for row in range(3))
    item = pl.program_id(1)
    last_item = item == pl.num_programs(1) - 1
    me = lax.axis_index("seq")
    downs = [(rims.at[0], late.at[0], send_sem.at[0], recv_sem.at[0])]
    ups = [(rims.at[1], late.at[1], send_sem.at[1], recv_sem.at[1])]

    branch = pl.program_id(0)
    slots = lasts.shape[0]
    ends, backs = lasts.at[:, :states], lasts.at[:, states : 2 * states]
    totals = lasts.at[:, 2 * states :]
    exchange = Exchange(runs, 1, ends, backs, totals, last_rate, (s_last, lam_last), *exchange_scratch)

    @pl.when((item == 0) & (branch == 0))
    def _():
        greet_line(me, runs, exchange.targets())

    beside(exchange.points(), branch * slots + item, 0, slots)

    @pl.when(branch == 0)
    def _():
        s_in[...] = first_in[0, item]
        carry[...] = first_in[1, item]

    @pl.when(branch == 1)
    def _():
        s_in[...] = s_last[item]
        carry[...] = lam_last[item]

    gain = skip[pl.ds(pl.program_id(0), 1), :]
    rate2[...] = rate[...] * -LOG2E
    width = BLK * states

    @pl.when(item == 0)
    def _():
        grads[...] = jnp.zeros(grads.shape, F32)

    for cols in columns(inner):
        dxs[:toks, cols] = delta[:, cols] * act[:, cols].astype(F32)
    fold = (
        lax.broadcasted_iota(jnp.int32, (states, width), 1) % states == lax.broadcasted_iota(jnp.int32, (states, width), 0)
    ).astype(BF16)
    own = lax.broadcasted_iota(jnp.int32, (toks, width), 0) % BLK == lax.broadcasted_iota(jnp.int32, (toks, width), 1) // states
    bdiag[:toks, :] = jnp.where(own, dot_tn(proj[rank : rank + states, :].astype(BF16), fold), 0.0).astype(BF16)
    cdiag[...] = jnp.where(own, dot_tn(proj[rank + states :, :].astype(BF16), fold), 0.0).astype(BF16)
    mine = own[:BLK]
    picks = mine.astype(BF16)
    sides = (
        lax.broadcasted_iota(jnp.int32, (2 * BLK, 256), 0) // BLK == lax.broadcasted_iota(jnp.int32, (2 * BLK, 256), 1) // 128
    ).astype(BF16)
    racc[...] = jnp.zeros((states, inner), F32)

    def lane_sum(wide):
        part = [wide[:, at : at + 128] for at in range(0, inner, 128)]
        while len(part) > 1:
            part = [sum(part[at : at + 2]) for at in range(0, len(part), 2)]
        return part[0]

    def products(slot, j):
        t0 = pl.multiple_of(j * BLK, BLK)
        y_out[pl.ds(t0, BLK), :] = dot(cdiag[pl.ds(t0, BLK), :], states_low[slot, states:, :])
        gsum[pl.ds(t0, BLK), :] = dot(bdiag[pl.ds(t0, BLK), :], lam_low[slot])
        hsum[pl.ds(t0, BLK), :] = dot(picks, rq_low[slot])
        racc[...] += dot(fold[:, : BLK // 4 * states], qd_low[slot])
        both = dot_nt(sides, dots[slot])
        dc[pl.ds(t0, BLK), :] = jnp.where(mine, both[:BLK], 0.0).astype(BF16)
        db[pl.ds(t0, BLK), :] = jnp.where(mine, both[BLK:], 0.0).astype(BF16)

    def one_block(slot, j):
        t0 = pl.multiple_of(j * BLK, BLK)
        dr, xr, yr = (ref.at[pl.ds(t0, BLK), :] for ref in (delta, dxs, dy))
        tile = tiles.at[pl.ds(t0, BLK)]
        r2 = rate2[...]
        r_low = rate[...].astype(BF16)
        begin = starts[j]
        s = begin[:states] + s_in[...] * jnp.exp2(twice(begin[states:]) * r2)
        states_low[slot, :states, :] = s.astype(BF16)
        for i in range(BLK):
            a = jnp.exp2(spread(dr, i) * r2)
            decay[slot, i] = a
            s = a * s + spread(xr, i) * across_lanes(tile[i, :states], inner)
            s_low = s.astype(BF16)
            states_low[slot, (i + 1) * states : (i + 2) * states, :] = s_low
            dots[slot, i * states : (i + 1) * states, :128] = lane_sum(s_low * spread(yr, i).astype(BF16))
        cr = carry[...]
        qds = []
        for i in reversed(range(BLK)):
            lam = cr + spread(yr, i) * across_lanes(tile[i, states:], inner)
            l_low = lam.astype(BF16)
            lam_low[slot, i * states : (i + 1) * states, :] = l_low
            dots[slot, i * states : (i + 1) * states, 128:] = lane_sum(l_low * spread(xr, i).astype(BF16))
            cr = decay[slot, i] * lam
            q = cr.astype(BF16) * states_low[slot, i * states : (i + 1) * states, :]
            rq_low[slot, i * states : (i + 1) * states, :] = q * r_low
            qds.append(q * spread(dr, i).astype(BF16))
            if i % 4 == 0:
                qd_low[slot, i // 4 * states : (i // 4 + 1) * states, :] = (qds[0] + qds[1]) + (qds[2] + qds[3])
                qds = []
        carry[...] = cr

    def block_step(k, _):
        j = blocks - 1 - 2 * k
        for slot in range(2):
            one_block(slot, j - slot)
            products(slot, j - slot)
        return 0

    lax.fori_loop(0, blocks // 2, block_step, 0)
    rate_grad[...] += -racc[...]
    for cols in columns(inner):
        act_f = act[:, cols].astype(F32)
        row_grads[skip_at, cols] += jnp.sum(dy[:, cols] * act_f, axis=0, keepdims=True)
        y_out[:, cols] += gain[:, cols] * act_f
        d_pre = (act_f * gsum[:toks, cols] - hsum[:toks, cols]) * sig[:, cols]
        row_grads[dtb_at, cols] += jnp.sum(d_pre, axis=0, keepdims=True)
        d_pre_low[:, cols] = d_pre.astype(BF16)
    dtp_grad[...] += dot(proj[:rank, :].astype(BF16), d_pre_low[...])[:held]
    d_proj = jnp.concatenate(
        [dot_nt(dtw[...], d_pre_low[...]), dot_nt(fold, db[:toks, :]), dot_nt(fold, dc[:toks, :])], axis=0
    ).astype(BF16)
    xp_new = dot(d_proj, act[...])
    xp_grad[:held, :] += xp_new[:held]
    xp_grad[held:, :] += xp_new[rank:]
    window = HALO + toks
    for wide_cols in columns(inner, 256):
        through = dot_tn(d_proj, xwt[:, wide_cols])
        for at in columns(256):
            cols = slice(wide_cols.start + at.start, wide_cols.start + at.stop)
            d_act = delta[:, cols] * gsum[:toks, cols] + gain[:, cols] * dy[:, cols] + through[:, at]
            d_conv = d_act * dsilu[:, cols]
            row_grads[tapb_at, cols] += jnp.sum(d_conv, axis=0, keepdims=True)
            x_f = xe[:, cols].astype(F32)
            base = jnp.concatenate([jnp.zeros((HALO, 128), F32), d_conv], axis=0)
            d_window = taps[tap_count - 1 : tap_count, cols] * base
            row_grads[tap_count - 1 : tap_count, cols] += jnp.sum(d_conv * x_f[HALO:], axis=0, keepdims=True)
            for k in range(tap_count - 1):
                moved = pltpu.roll(base, window - (tap_count - 1 - k), 0)
                row_grads[k : k + 1, cols] += jnp.sum(moved * x_f, axis=0, keepdims=True)
                d_window = d_window + taps[k : k + 1, cols] * moved
            rims[branch, item, :, cols] = d_window[HALO - 8 : HALO]
            dx_out[:, cols] = d_window[HALO:]

    @pl.when(last_item & (pl.program_id(0) == 0))
    def _():
        swap_along_line(me, runs, [], downs, True)

    @pl.when(last_item & (pl.program_id(0) == 1))
    def _():
        swap_along_line(me, runs, ups, [], True)
        swap_along_line(me, runs, ups, downs, False)

        @pl.when(me == 0)
        def _():
            late[1] = jnp.zeros(late.shape[1:], F32)

        @pl.when(me == runs - 1)
        def _():
            late[0] = jnp.zeros(late.shape[1:], F32)

        late_out[...] = late[...]


LAST_ROWS = 16
PART_ROWS = 512


class Ring:
    def __init__(self, bits):
        self.bits = bits
        self.size = 1 << len(bits)
        self.digits = [bit_of(lax.axis_index(axis), bit) for axis, bit in bits]
        self.place = sum(digit * (1 << at) for at, digit in enumerate(self.digits))

    def target(self, ahead):
        place = lax.rem(self.place + ahead, self.size)
        where = {}
        for at, (axis, bit) in enumerate(self.bits):
            base = where.get(axis, lax.axis_index(axis))
            where[axis] = base + (bit_of(place, at) - self.digits[at]) * (1 << bit)
        return where, place

    def targets(self):
        return [self.target(ahead)[0] for ahead in range(1, self.size)]


def stage_rings(runs, groups):
    bits = [("seq", bit) for bit in range(int(math.log2(runs)))] + [("dp", bit) for bit in range(int(math.log2(groups)))]
    return [Ring(bits[:1])] + [Ring(bits[at : at + 2]) for at in range(1, len(bits), 2)]


def part_count(rows):
    return -(-rows // PART_ROWS)


def buffer_rows(runs, groups):
    bits = int(math.log2(runs)) + int(math.log2(groups))
    size, total = PART_ROWS, 0
    for members in [2] + [1 << min(2, bits - at) for at in range(1, bits, 2)]:
        moved = size // members if size >= members * LAST_ROWS else size
        total += moved * (members - 1)
        size = moved
    return total


def reduce_shapes(parts, dim, runs, groups):
    bits = int(math.log2(runs)) + int(math.log2(groups))
    stages = 1 + bits // 2
    room = parts * buffer_rows(runs, groups)
    sems = pltpu.SemaphoreType.DMA((parts, 2 * stages, 3))
    return [
        pltpu.VMEM((parts * PART_ROWS, dim), F32), pltpu.VMEM((room, dim), BF16), pltpu.VMEM((room, dim), BF16),
        pltpu.VMEM((parts * PART_ROWS, dim), BF16), sems, sems,
    ]


class Reduction:
    def __init__(self, rings, turns, segments, acc, sends, arrivals, gathered, send_sem, recv_sem):
        self.rings = rings
        self.count = len(rings)
        self.parts = len(turns)
        self.segments = segments
        self.acc, self.sends, self.arrivals, self.gathered = acc, sends, arrivals, gathered
        self.send_sem, self.recv_sem = send_sem, recv_sem
        room = sends.shape[0] // self.parts
        self.steps = []
        for part, turn in enumerate(turns):
            later = rings[1:]
            turn = turn % max(len(later), 1)
            order = rings[:1] + later[turn:] + later[:turn]
            start, size, at = part * PART_ROWS, PART_ROWS, part * room
            steps = []
            for ring in order:
                split = size >= ring.size * LAST_ROWS
                moved = size // ring.size if split else size
                keep = pl.multiple_of(start + ring.place * moved, LAST_ROWS) if split else start
                steps.append((ring, start, split, moved, keep, at))
                at += moved * (ring.size - 1)
                start, size = keep, moved
            self.steps.append(steps)

    def assemble(self, part):
        low, high = part * PART_ROWS, (part + 1) * PART_ROWS
        at = 0
        for get, size in self.segments:
            first, last = max(at, low), min(at + size, high)
            if first < last:
                self.acc[first:last, :] = get(first - at, last - first)
            at += size
        if at < high:
            first = max(at, low)
            self.acc[first:high, :] = jnp.zeros((high - first, self.acc.shape[1]), F32)

    def scatter_copy(self, part, stage, ahead):
        ring, _, _, moved, _, at = self.steps[part][stage]
        at += (ahead - 1) * moved
        return remote(
            self.sends.at[pl.ds(at, moved), :], self.arrivals.at[pl.ds(at, moved), :],
            self.send_sem.at[part, stage, ahead - 1], self.recv_sem.at[part, stage, ahead - 1], ring.target(ahead)[0],
        )

    def scatter(self, part, stage):
        ring, start, split, moved, _, at = self.steps[part][stage]
        for ahead in range(1, ring.size):
            place = ring.target(ahead)[1]
            away = pl.multiple_of(start + place * moved, LAST_ROWS) if split else start
            here = at + (ahead - 1) * moved
            self.sends[here : here + moved, :] = self.acc[pl.ds(away, moved), :].astype(BF16)
            self.scatter_copy(part, stage, ahead).start()

    def settle(self, part, stage):
        ring, _, split, moved, keep, at = self.steps[part][stage]
        for ahead in range(1, ring.size):
            self.scatter_copy(part, stage, ahead).wait()
        held = self.acc[pl.ds(keep, moved), :]
        came = [
            self.arrivals[at + (ahead - 1) * moved : at + ahead * moved, :].astype(F32) for ahead in range(1, ring.size)
        ]
        if split:
            held = held + sum(came)
        else:
            values = [held.astype(BF16).astype(F32)] + came
            total = jnp.zeros_like(held)
            for place in range(ring.size):
                behind = lax.rem(ring.place - place + ring.size, ring.size)
                chosen = values[0]
                for ahead in range(1, ring.size):
                    chosen = jnp.where(behind == ahead, values[ahead], chosen)
                total = total + chosen
            held = total
        self.acc[pl.ds(keep, moved), :] = held

    def gather_copies(self, part, stage):
        ring, _, split, moved, keep, _ = self.steps[part][stage]
        here = self.gathered.at[pl.ds(keep, moved), :]
        return [
            remote(
                here, here, self.send_sem.at[part, self.count + stage, ahead - 1],
                self.recv_sem.at[part, self.count + stage, ahead - 1], ring.target(ahead)[0],
            )
            for ahead in range(1, ring.size)
            if split
        ]

    def points(self):
        def begin():
            for part in range(self.parts):
                self.assemble(part)
                self.scatter(part, 0)

        def split(stage):
            for part in range(self.parts):
                self.settle(part, stage - 1)
                self.scatter(part, stage)

        def turn():
            for part in range(self.parts):
                self.settle(part, self.count - 1)
                _, _, _, moved, keep, _ = self.steps[part][-1]
                self.gathered[pl.ds(keep, moved), :] = self.acc[pl.ds(keep, moved), :].astype(BF16)
                for copy in self.gather_copies(part, self.count - 1):
                    copy.start()

        def join(stage):
            for part in range(self.parts):
                for copy in self.gather_copies(part, stage + 1):
                    copy.wait()
                if stage >= 0:
                    for copy in self.gather_copies(part, stage):
                        copy.start()

        points = [begin]
        points += [functools.partial(split, stage) for stage in range(1, self.count)]
        points += [turn]
        return points + [functools.partial(join, stage) for stage in reversed(range(-1, self.count - 1))]


def big_segments(ref, dim):
    return [
        (lambda at, size, lane=lane: ref[at : at + size, lane : lane + dim], ref.shape[0])
        for lane in range(0, ref.shape[1], dim)
    ]


def small_segments(ref, dim):
    return [
        (lambda at, size, branch=branch, lane=lane: ref[branch, at : at + size, lane : lane + dim], ref.shape[1])
        for lane in range(0, ref.shape[2], dim)
        for branch in range(2)
    ]


def tail_kernel(
    plan, tok, cot, mod, mask, counts, hid, z_in, y, dx, late, win, wout, step,
    grads,
    mixed, d_tokens, result, x_result, factors, own_rows,
    dz, out_grad, z_grad, x_grad, mod_sum, mod_in, table, small_send, small_recv, *reduce_scratch,
):
    runs, groups, slots = plan
    dim = tok.shape[-1]
    toks, inner = z_in.shape
    now = pl.program_id(0)
    i = lax.rem(now, slots)
    rings = stage_rings(runs, groups)
    seq_ring = Ring([("seq", bit) for bit in range(int(math.log2(runs)))])
    dp_ring = Ring([("dp", bit) for bit in range(int(math.log2(groups)))])
    half = len(reduce_scratch) // 2
    smalls = small_segments(grads, dim)
    segments = big_segments(out_grad, dim) + big_segments(z_grad, dim) + smalls
    main = Reduction(rings, [part % 3 // 2 for part in range(result.shape[0] // PART_ROWS)], segments, *reduce_scratch[:half])
    rest = Reduction(rings, [part % 2 for part in range(x_result.shape[0] // PART_ROWS)], big_segments(x_grad, dim), *reduce_scratch[half:])
    main_points, rest_points = main.points(), rest.points()

    @pl.when(now == 0)
    def _():
        greet([target for ring in rings + [seq_ring, dp_ring] for target in ring.targets()])
        out_grad[...] = jnp.zeros(out_grad.shape, F32)
        z_grad[...] = jnp.zeros(z_grad.shape, F32)
        x_grad[...] = jnp.zeros(x_grad.shape, F32)
        mod_sum[...] = jnp.zeros(mod_sum.shape, F32)

    scale, gate = mod[:, dim : 2 * dim], mod[:, 2 * dim :]
    valid = as_column(mask[pl.ds(i, 1), :]) * (counts[...] > i).astype(F32)
    mod_rows = pl.ds(pl.multiple_of(8 * i, 8), 8)

    @pl.when(now < slots)
    def _():
        cot_f = cot[...].astype(F32)
        z = z_in[...]
        z_sig = jax.nn.sigmoid(z)
        z_silu = z * z_sig
        summed = y[0] + flip_full(y[1])
        gated = (summed * z_silu).astype(BF16)
        branch_out = dot(gated, wout[...])
        mixed[...] = (tok[...].astype(F32) + gate * branch_out).astype(BF16)
        d_branch = (cot_f * gate).astype(BF16)
        out_grad[...] += dot_tn(gated, d_branch)
        d_zgate = dot_nt(d_branch, wout[...]) * summed * (z_sig + z_silu * (1.0 - z_sig))
        d_low = (d_zgate * valid).astype(BF16)
        dz[i] = d_low
        z_grad[...] += dot_tn(hid[...], d_low)
        d_gate = jnp.sum(cot_f * branch_out, axis=0, keepdims=True)
        mod_sum[mod_rows, :] = jnp.concatenate([jnp.zeros((2, dim), F32), d_gate, jnp.zeros((5, dim), F32)], axis=0)

    @pl.when(now == slots)
    def _():
        main_points[0]()

    @pl.when(now >= slots)
    def _():
        edge = late.shape[2]

        def with_late(part, extra):
            return jnp.concatenate([part[: toks - edge], part[toks - edge :] + extra], axis=0)

        d_x = with_late(dx[0], late[0, i]) + flip_full(with_late(dx[1], late[1, i]))
        d_x = (d_x * valid).astype(BF16)
        x_grad[...] += dot_tn(hid[...], d_x)
        d_hidden = dot_nt(d_x, win[:, :inner]) + dot_nt(dz[i], win[:, inner:])
        normed, inv_std = normalise(tok[...].astype(F32))
        d_shift = jnp.sum(d_hidden, axis=0, keepdims=True)
        d_scale = jnp.sum(d_hidden * normed, axis=0, keepdims=True)
        mod_sum[mod_rows, :] += jnp.concatenate([d_shift, d_scale, jnp.zeros((6, dim), F32)], axis=0)
        d_normed = d_hidden * (1.0 + scale)
        d_tokens[...] = cot[...].astype(F32) + inv_std * (
            d_normed
            - jnp.mean(d_normed, axis=-1, keepdims=True)
            - normed * jnp.mean(d_normed * normed, axis=-1, keepdims=True)
        )

    @pl.when(now == slots)
    def _():
        main_points[1]()

    def sum_copies():
        return [
            remote(mod_sum, mod_in.at[ahead - 1], small_send.at[ahead - 1], small_recv.at[ahead - 1], seq_ring.target(ahead)[0])
            for ahead in range(1, seq_ring.size)
        ]

    def table_copies():
        at = pl.multiple_of(dp_ring.place * 16, 16)
        here = table.at[pl.ds(at, 16), :]
        base = seq_ring.size - 1
        return [
            remote(here, here, small_send.at[base + ahead - 1], small_recv.at[base + ahead - 1], dp_ring.target(ahead)[0])
            for ahead in range(1, dp_ring.size)
        ]

    def start_small():
        for copy in sum_copies():
            copy.start()

    def turn_small():
        for copy in sum_copies():
            copy.wait()
        values = [mod_sum[...]] + [mod_in[ahead - 1] for ahead in range(1, seq_ring.size)]
        total = jnp.zeros(mod_sum.shape, F32)
        for place in range(seq_ring.size):
            behind = lax.rem(seq_ring.place - place + seq_ring.size, seq_ring.size)
            chosen = values[0]
            for ahead in range(1, seq_ring.size):
                chosen = jnp.where(behind == ahead, values[ahead], chosen)
            total = total + chosen
        time_f = step[...].astype(F32)
        time_low = time_f * jax.nn.sigmoid(time_f)
        lines = [total[8 * item : 8 * item + 3] for item in range(slots)] + [time_low]
        lines.append(jnp.zeros((16 - 4 * slots, dim), F32))
        own = jnp.concatenate(lines, axis=0).astype(BF16)
        own_rows[...] = own
        table[pl.ds(pl.multiple_of(dp_ring.place * 16, 16), 16), :] = own
        for copy in table_copies():
            copy.start()

    def end_small():
        for copy in table_copies():
            copy.wait()
        factors[...] = table[...]

    @pl.when(now == 2 * slots - 1)
    def _():
        start_small()
        rest_points[0]()
        rest_points[1]()
        for at in range(2, len(main_points)):
            main_points[at]()
            if at == 2:
                turn_small()
            rest_points[at]()
        end_small()
        result[...] = main.gathered[...]
        x_result[...] = rest.gathered[...]


def finish_kernel(
    outs, zs, xs, smalls, factors, own, step, ada,
    grad_time, grad_ada, grad_ada_bias, in_grad, tap_grad, tapb_grad, xp_grad, dtp_grad, dtb_grad, rate_grad, skip_grad, out_grad,
):
    dim, inner = in_grad.shape[0], rate_grad.shape[2]
    slots = step.shape[0]
    now = pl.program_id(0)
    out_grad[...] = outs[...].astype(F32)
    in_grad[...] = jnp.where(now < inner // dim, xs[...], zs[...]).astype(F32)
    table = factors[...]
    length = table.shape[0]

    for part in range(3):

        @pl.when(now == part)
        def _():
            row = lax.broadcasted_iota(jnp.int32, (length, length), 0)
            col = lax.broadcasted_iota(jnp.int32, (length, length), 1)
            item = row % 16 - 3 * slots
            wanted = row // 16 * 16 + 3 * item + part
            mods = dot(((col == wanted) & (item >= 0) & (item < slots)).astype(BF16), table)
            lanes = slice(part * dim, (part + 1) * dim)
            grad_ada[...] = dot_tn(table, mods.astype(BF16))
            grad_ada_bias[lanes] = jnp.sum(mods, axis=0)
            mine = own[...].astype(F32)
            picked = jnp.concatenate([mine[3 * i + part : 3 * i + part + 1] for i in range(slots)], axis=0)
            d_time = dot_nt(picked.astype(BF16), ada[...])
            grad_time[...] = d_time if part == 0 else grad_time[...] + d_time

    @pl.when(now == 3)
    def _():
        time_f = step[...].astype(F32)
        time_sig = jax.nn.sigmoid(time_f)
        grad_time[...] = grad_time[...] * time_sig * (1.0 + time_f * (1.0 - time_sig))
        at = 0
        for first in range(0, inner, dim):
            lanes = slice(first, first + dim)
            for branch in range(2):
                for ref in (xp_grad, dtp_grad, rate_grad, tap_grad):
                    size = ref.shape[1]
                    ref[branch, :, lanes] = smalls[at : at + size, :].astype(F32)
                    at += size
                for ref in (tapb_grad, skip_grad, dtb_grad):
                    ref[branch : branch + 1, lanes] = smalls[at : at + 1, :].astype(F32)
                    at += 1
                at += 1


def params(**more):
    return pltpu.CompilerParams(vmem_limit_bytes=VMEM_LIMIT, **more)


def spec(block, index):
    return pl.BlockSpec(block, index)


def per_device(
    tokens, timestep, counts, token_mask, ada_weight, ada_bias, input_weight, conv_weight, conv_bias, x_weight, dt_weight,
    dt_bias, decay_rate, skip_gain, output_weight, cotangent,
):
    slots, toks, dim = tokens.shape
    inner = output_weight.shape[0]
    rank = dt_weight.shape[1]
    states = decay_rate.shape[1]
    tap_count = conv_weight.shape[1]
    wide_rank = WIDE_RANK
    proj_rows = wide_rank + 2 * states
    blocks = toks // BLK
    runs = lax.axis_size("seq")
    groups = lax.axis_size("dp")
    counts2 = counts[:, None]
    x_rows = jnp.swapaxes(x_weight, 1, 2)

    def item(*block):
        return spec((None,) + block, lambda i: (i,) + (0,) * len(block))

    def whole(*block):
        return spec(block, lambda *_: (0,) * len(block))

    xe, dy, z_gate, hid, modulate = pl.pallas_call(
        functools.partial(enter_kernel, runs),
        grid=(slots,),
        in_specs=[
            whole(slots, toks, dim), item(toks, dim), whole(slots, toks), whole(1, 1), whole(slots, dim), whole(dim, 3 * dim),
            whole(3 * dim), whole(dim, 2 * inner), whole(inner, dim),
        ],
        out_specs=[
            item(2, HALO + toks, inner), item(2, toks, inner), item(toks, inner), item(toks, dim), item(1, 3 * dim),
        ],
        out_shape=[
            jax.ShapeDtypeStruct((slots, 2, HALO + toks, inner), BF16),
            jax.ShapeDtypeStruct((slots, 2, toks, inner), F32),
            jax.ShapeDtypeStruct((slots, toks, inner), F32),
            jax.ShapeDtypeStruct((slots, toks, dim), BF16),
            jax.ShapeDtypeStruct((slots, 1, 3 * dim), F32),
        ],
        scratch_shapes=[
            pltpu.VMEM((slots, 3 * dim), F32),
            pltpu.VMEM((slots, HALO, dim), BF16), pltpu.VMEM((slots, HALO, dim), BF16), pltpu.VMEM((slots, toks), jnp.int32),
            pltpu.VMEM((slots, toks), jnp.int32), pltpu.SemaphoreType.DMA((4,)), pltpu.SemaphoreType.DMA((4,)),
        ],
        compiler_params=params(collective_id=1, has_side_effects=True),
        name="enter",
    )(
        tokens, cotangent, token_mask, counts2, timestep, ada_weight, ada_bias, input_weight, output_weight,
    )

    def unit(*block):
        return spec((None, None) + block, lambda b, i: (i, b) + (0,) * len(block))

    def branch(*block):
        return spec((None,) + block, lambda b, i: (b,) + (0,) * len(block))

    def unit_shape(*block, kind=F32):
        return jax.ShapeDtypeStruct((slots, 2) + block, kind)

    act, planes, proj, lasts, starts, tiles, weights, first_in = pl.pallas_call(
        functools.partial(first_kernel, runs, slots),
        grid=(2, slots),
        in_specs=[
            unit(HALO + toks, inner), unit(toks, inner), branch(tap_count, inner), whole(2, inner),
            branch(rank + 2 * states, inner), branch(rank, inner), whole(2, inner), branch(states, inner),
        ],
        out_specs=[
            unit(toks, inner), unit(3, toks, inner), unit(proj_rows, toks), unit(2 * states + 8, inner),
            unit(blocks, states + 8, inner), unit(toks, 2 * states, 128), branch(proj_rows + wide_rank, inner),
            whole(2, slots, states, inner),
        ],
        out_shape=[
            unit_shape(toks, inner, kind=BF16), unit_shape(3, toks, inner), unit_shape(proj_rows, toks),
            unit_shape(2 * states + 8, inner), unit_shape(blocks, states + 8, inner), unit_shape(toks, 2 * states, 128),
            jax.ShapeDtypeStruct((2, proj_rows + wide_rank, inner), BF16),
            jax.ShapeDtypeStruct((2, slots, states, inner), F32),
        ],
        scratch_shapes=[
            pltpu.VMEM((toks, inner), F32), pltpu.VMEM((2, BLK, states, inner), F32), pltpu.VMEM((8, inner), F32),
            pltpu.VMEM((states, inner), F32), pltpu.VMEM((2 * states * toks, 128), F32),
            pltpu.VMEM((4 * states, 2 * states * 128), BF16), pltpu.VMEM((slots, states, inner), F32),
            pltpu.VMEM((slots, states, inner), F32), pltpu.VMEM((slots, 1, inner), F32), pltpu.VMEM((states, inner), F32),
            *exchange_shapes(runs, slots, states, inner),
        ],
        compiler_params=params(collective_id=2, has_side_effects=True),
        name="first",
    )(xe, dy, conv_weight, conv_bias, x_rows, dt_weight, dt_bias, decay_rate)

    vmem = pl.BlockSpec(memory_space=pltpu.VMEM)
    last = spec((slots, None, 2 * states + 8, inner), lambda b, i: (0, 1, 0, 0))
    last_branch = spec((None, states, inner), lambda b, i: (1, 0, 0))

    grad_rows = 2 * rank + 3 * states + 8
    y, dx, late, grads = pl.pallas_call(
        functools.partial(second_kernel, runs),
        grid=(2, slots),
        in_specs=[
            whole(2, slots, states, inner), last, last_branch, unit(blocks, states + 8, inner), unit(toks, 2 * states, 128),
            branch(states, inner), unit(HALO + toks, inner), unit(toks, inner), unit(3, toks, inner), unit(toks, inner),
            unit(proj_rows, toks), branch(proj_rows + wide_rank, inner), branch(tap_count, inner), whole(2, inner),
        ],
        out_specs=[unit(toks, inner), unit(toks, inner), whole(2, slots, 8, inner), branch(grad_rows, inner)],
        out_shape=[
            unit_shape(toks, inner), unit_shape(toks, inner), jax.ShapeDtypeStruct((2, slots, 8, inner), F32),
            jax.ShapeDtypeStruct((2, grad_rows, inner), F32),
        ],
        scratch_shapes=[
            pltpu.VMEM((states, inner), F32), pltpu.VMEM((states, inner), F32), pltpu.VMEM((toks + BLK, inner), F32), pltpu.VMEM((toks + BLK, BLK * states), BF16),
            pltpu.VMEM((toks, BLK * states), BF16),
            pltpu.VMEM((2, BLK, states, inner), F32),
            pltpu.VMEM((2, (BLK + 1) * states, inner), BF16), pltpu.VMEM((2, BLK * states, inner), BF16),
            pltpu.VMEM((2, BLK * states, inner), BF16), pltpu.VMEM((2, BLK // 4 * states, inner), BF16),
            pltpu.VMEM((2, BLK * states, 256), BF16), pltpu.VMEM((states, inner), F32),
            pltpu.VMEM((toks + BLK, inner), F32), pltpu.VMEM((toks + BLK, inner), F32),
            pltpu.VMEM((toks + BLK, BLK * states), BF16), pltpu.VMEM((toks + BLK, BLK * states), BF16),
            pltpu.VMEM((2, slots, 8, inner), F32), pltpu.VMEM((2, slots, 8, inner), F32),
            pltpu.SemaphoreType.DMA((2,)), pltpu.SemaphoreType.DMA((2,)), pltpu.VMEM((toks, inner), BF16),
            pltpu.VMEM((states, inner), F32), pltpu.VMEM((slots, states, inner), F32), pltpu.VMEM((slots, states, inner), F32),
            *exchange_shapes(runs, slots, states, inner),
        ],
        compiler_params=params(collective_id=3, has_side_effects=True),
        name="second",
    )(
        first_in, lasts, decay_rate, starts, tiles, decay_rate, xe, act, planes, dy, proj, weights, conv_weight, skip_gain,
    )

    def now(*block):
        return spec((None,) + block, lambda s: (s % slots,) + (0,) * len(block))

    def early(*block):
        return spec((None,) + block, lambda s: (jnp.minimum(s, slots - 1),) + (0,) * len(block))

    def after(*block):
        return spec((None,) + block, lambda s: (jnp.maximum(s - slots, 0),) + (0,) * len(block))

    small_rows = 2 * grad_rows * (inner // dim)
    main_parts = part_count(inner + dim * (inner // dim) + small_rows)
    rest_parts = part_count(dim * (inner // dim))
    mixed, d_tokens, result, x_result, factors, own = pl.pallas_call(
        functools.partial(tail_kernel, (runs, groups, slots)),
        grid=(2 * slots,),
        in_specs=[
            now(toks, dim), now(toks, dim), now(1, 3 * dim), whole(slots, toks), whole(1, 1), now(toks, dim),
            early(toks, inner), early(2, toks, inner), after(2, toks, inner), whole(2, slots, 8, inner),
            whole(dim, 2 * inner), whole(inner, dim), whole(slots, dim), whole(2, grad_rows, inner),
        ],
        out_specs=[
            early(toks, dim), after(toks, dim), whole(main_parts * PART_ROWS, dim), whole(rest_parts * PART_ROWS, dim),
            whole(16 * groups, dim), whole(16, dim),
        ],
        out_shape=[
            jax.ShapeDtypeStruct((slots, toks, dim), BF16), jax.ShapeDtypeStruct((slots, toks, dim), F32),
            jax.ShapeDtypeStruct((main_parts * PART_ROWS, dim), BF16), jax.ShapeDtypeStruct((rest_parts * PART_ROWS, dim), BF16),
            jax.ShapeDtypeStruct((16 * groups, dim), BF16), jax.ShapeDtypeStruct((16, dim), BF16),
        ],
        scratch_shapes=[
            pltpu.VMEM((slots, toks, inner), BF16), pltpu.VMEM((inner, dim), F32), pltpu.VMEM((dim, inner), F32),
            pltpu.VMEM((dim, inner), F32), pltpu.VMEM((8 * slots, dim), F32), pltpu.VMEM((max(runs - 1, 1), 8 * slots, dim), F32),
            pltpu.VMEM((16 * groups, dim), BF16), pltpu.SemaphoreType.DMA((runs + groups,)),
            pltpu.SemaphoreType.DMA((runs + groups,)), *reduce_shapes(main_parts, dim, runs, groups),
            *reduce_shapes(rest_parts, dim, runs, groups),
        ],
        compiler_params=params(collective_id=4, has_side_effects=True),
        name="tail",
    )(
        tokens, cotangent, modulate, token_mask, counts2, hid, z_gate, y, dx, late, input_weight, output_weight, timestep, grads,
    )

    (
        d_time, grad_ada, grad_ada_bias, in_grad, tap_grad, tapb_grad, xp_grad, dtp_grad, dtb_grad, rate_grad, skip_grad,
        out_grad,
    ) = pl.pallas_call(
        finish_kernel,
        grid=(4,),
        in_specs=[
            spec((inner // 4, dim), lambda s: (s, 0)),
            spec((dim, dim), lambda s: (inner // dim + jnp.maximum(s - inner // dim, 0), 0)),
            spec((dim, dim), lambda s: (jnp.minimum(s, inner // dim - 1), 0)),
            spec((PART_ROWS, dim), lambda s: (2 * inner // PART_ROWS, 0)),
            whole(16 * groups, dim), whole(16, dim), whole(slots, dim), spec((dim, dim), lambda s: (0, jnp.minimum(s, 2))),
        ],
        out_specs=[
            whole(slots, dim), spec((dim, dim), lambda s: (0, jnp.minimum(s, 2))), whole(3 * dim),
            spec((dim, 2 * inner // 4), lambda s: (0, s)), whole(2, tap_count, inner), whole(2, inner),
            whole(2, rank + 2 * states, inner), whole(2, rank, inner), whole(2, inner), whole(2, states, inner), whole(2, inner),
            spec((inner // 4, dim), lambda s: (s, 0)),
        ],
        out_shape=[
            jax.ShapeDtypeStruct(shape, F32)
            for shape in (
                (slots, dim), (dim, 3 * dim), (3 * dim,), (dim, 2 * inner), (2, tap_count, inner), (2, inner),
                (2, rank + 2 * states, inner), (2, rank, inner), (2, inner), (2, states, inner), (2, inner), (inner, dim),
            )
        ],
        compiler_params=params(),
        name="finish",
    )(result, result, x_result, result, factors, own, timestep, ada_weight)
    return (
        mixed, d_tokens, d_time, grad_ada, grad_ada_bias, in_grad, tap_grad, tapb_grad, jnp.swapaxes(xp_grad, 1, 2), dtp_grad, dtb_grad,
        rate_grad, skip_grad, out_grad,
    )


def solution(mesh):
    runs = P("dp", "seq", None)
    return jax.shard_map(
        per_device,
        mesh=mesh,
        in_specs=(runs, P("dp", None), P("dp"), P("dp", "seq")) + (P(),) * 11 + (runs,),
        out_specs=(runs, runs, P("dp", None)) + (P(),) * 11,
        check_vma=False,
    )
```

```python
import functools
import math

import jax
import jax.numpy as jnp
from jax import lax
from jax.experimental import pallas as pl
from jax.experimental.pallas import tpu as pltpu
from jax.sharding import PartitionSpec as P

EPSILON = 1e-06
BLK = 16
WIDE_RANK = 32
HALO = 16
LOG2E = math.log2(math.e)
F32, BF16 = jnp.float32, jnp.bfloat16
NT = (((1,), (1,)), ((), ()))
TN = (((0,), (0,)), ((), ()))
VMEM_LIMIT = 60 << 20
MESH = pl.DeviceIdType.MESH


def dot(a, b):
    return jnp.dot(a, b, preferred_element_type=F32)


def dot_nt(a, b):
    return lax.dot_general(a, b, NT, preferred_element_type=F32)


def dot_tn(a, b):
    return lax.dot_general(a, b, TN, preferred_element_type=F32)


def flip_full(value):
    turned = lax.broadcasted_iota(jnp.int32, (8, value.shape[1]), 0)
    groups = [value[at : at + 8] for at in range(0, value.shape[0], 8)]
    return jnp.concatenate([jnp.take_along_axis(group, 7 - turned, axis=0) for group in reversed(groups)], axis=0)


def flip_low(value):
    return flip_full(value.astype(F32)).astype(BF16)


def normalise(tokens_f):
    centered = tokens_f - jnp.mean(tokens_f, axis=-1, keepdims=True)
    inv_std = lax.rsqrt(jnp.mean(centered * centered, axis=-1, keepdims=True) + EPSILON)
    return centered * inv_std, inv_std


def eye(size):
    rows = lax.broadcasted_iota(jnp.int32, (size, size), 0)
    cols = lax.broadcasted_iota(jnp.int32, (size, size), 1)
    return (rows == cols).astype(BF16)


def as_column(row):
    return dot_nt(eye(row.shape[1]), jnp.broadcast_to(row.astype(F32).astype(BF16), (8, row.shape[1])))[:, :1]


def remote(src, dst, send_sem, recv_sem, target):
    return pltpu.make_async_remote_copy(
        src_ref=src, dst_ref=dst, send_sem=send_sem, recv_sem=recv_sem, device_id=target, device_id_type=MESH
    )


def greet(targets):
    barrier = pltpu.get_barrier_semaphore()
    for target in targets:
        pl.semaphore_signal(barrier, inc=1, device_id=target, device_id_type=MESH)
    pl.semaphore_wait(barrier, len(targets))


def greet_line(me, runs, others=()):
    barrier = pltpu.get_barrier_semaphore()
    for target in others:
        pl.semaphore_signal(barrier, inc=1, device_id=target, device_id_type=MESH)

    @pl.when(me > 0)
    def _():
        pl.semaphore_signal(barrier, inc=1, device_id={"seq": me - 1}, device_id_type=MESH)

    @pl.when(me < runs - 1)
    def _():
        pl.semaphore_signal(barrier, inc=1, device_id={"seq": me + 1}, device_id_type=MESH)

    neighbours = lax.div(me + runs - 1, runs) + lax.div(2 * runs - 2 - me, runs)
    pl.semaphore_wait(barrier, neighbours + len(others))


def swap_along_line(me, runs, ups, downs, start):
    up = [remote(src, dst, ss, rs, {"seq": me + 1}) for src, dst, ss, rs in ups]
    down = [remote(src, dst, ss, rs, {"seq": me - 1}) for src, dst, ss, rs in downs]

    @pl.when(me < runs - 1)
    def _():
        for copy in up:
            if start:
                copy.start()
            else:
                copy.wait_send()
        if not start:
            for copy in down:
                copy.wait_recv()

    @pl.when(me > 0)
    def _():
        for copy in down:
            if start:
                copy.start()
            else:
                copy.wait_send()
        if not start:
            for copy in up:
                copy.wait_recv()


def enter_kernel(
    runs, tok, cot, mask, counts, step, ada, ada_bias, win, wout,
    xe, dy, z_out, hid_out, mod_out, rim_out,
    mods, prev_tok, next_tok, prev_mask, next_mask, send_sem, recv_sem,
):
    slots, toks, dim = tok.shape
    inner = wout.shape[0]
    me = lax.axis_index("seq")
    i = pl.program_id(0)
    ups = [
        (tok.at[:, pl.ds(toks - HALO, HALO), :], prev_tok, send_sem.at[0], recv_sem.at[0]),
        (mask, prev_mask, send_sem.at[1], recv_sem.at[1]),
    ]
    downs = [
        (tok.at[:, pl.ds(0, HALO), :], next_tok, send_sem.at[2], recv_sem.at[2]),
        (mask, next_mask, send_sem.at[3], recv_sem.at[3]),
    ]

    @pl.when(i == 0)
    def _():
        greet_line(me, runs)
        swap_along_line(me, runs, ups, downs, True)

        @pl.when(me == 0)
        def _():
            prev_tok[...] = jnp.zeros(prev_tok.shape, BF16)
            prev_mask[...] = jnp.zeros(prev_mask.shape, jnp.int32)

        @pl.when(me == runs - 1)
        def _():
            next_tok[...] = jnp.zeros(next_tok.shape, BF16)
            next_mask[...] = jnp.zeros(next_mask.shape, jnp.int32)

    live = jnp.where(counts[0] > i, 1.0, 0.0)

    @pl.when(i == 0)
    def _():
        time_f = step[...].astype(F32)
        time_low = (time_f * jax.nn.sigmoid(time_f)).astype(BF16)
        mods[...] = dot(time_low, ada[...]) + ada_bias[...].reshape(1, 3 * dim)

    mod = mods[pl.ds(i, 1), :]
    mod_out[...] = mod
    shift, scale, gate = mod[:, :dim], mod[:, dim : 2 * dim], mod[:, 2 * dim :]

    def hidden_of(part, scale, shift):
        normed, _ = normalise(part.astype(F32))
        return (normed * (1.0 + scale) + shift).astype(BF16)

    hid = hidden_of(tok[i], scale, shift)
    hid_out[...] = hid
    xz = dot(hid, win[...]) * (as_column(mask[pl.ds(i, 1), :]) * live)
    x_low = xz[:, :inner].astype(BF16)
    z = xz[:, inner:]
    z_out[...] = z
    d_branch = (cot[...].astype(F32) * gate).astype(BF16)
    d_summed = dot_nt(d_branch, wout[...]) * z * jax.nn.sigmoid(z)
    dy[0] = d_summed
    dy[1] = flip_full(d_summed)
    xe[0] = x_low
    xe[1] = flip_low(x_low)

    @pl.when(i == slots - 1)
    def _():
        swap_along_line(me, runs, ups, downs, False)
        hidden, seen = [], []
        for item in range(slots):
            row = mods[item : item + 1, :]
            rims = jnp.concatenate([prev_tok[item], next_tok[item]], axis=0)
            hidden.append(hidden_of(rims, row[:, dim : 2 * dim], row[:, :dim]))
            prev_col = as_column(prev_mask[item : item + 1, :])[toks - HALO :]
            next_col = as_column(next_mask[item : item + 1, :])[:HALO]
            live = jnp.where(counts[0] > item, 1.0, 0.0)
            seen.append(jnp.concatenate([prev_col, next_col], axis=0) * live)
        rim_x = dot(jnp.concatenate(hidden, axis=0), win[:, :inner]) * jnp.concatenate(seen, axis=0)
        for item in range(slots):
            part = rim_x[2 * HALO * item : 2 * HALO * (item + 1)]
            rim_out[item, 0] = part[:HALO].astype(BF16)
            rim_out[item, 1] = flip_full(part[HALO:]).astype(BF16)


def columns(inner, width=128):
    return [slice(at, at + width) for at in range(0, inner, width)]


def twice(row8):
    return jnp.concatenate([row8, row8], axis=0)


def spread(ref, index):
    return twice(ref[pl.ds(index, 8, stride=0), :])


def lay_out(wide, rows, picks):
    count, toks = rows.shape
    high = rows.astype(BF16).astype(F32)
    halves = jnp.concatenate([high, rows - high], axis=0).T.astype(BF16)
    for n in range(0, count, 2):
        pair = dot(halves, picks[:, n * 128 : (n + 2) * 128])
        for t in range(0, toks, 8):
            for k in range(2):
                at = 8 * (count * (t // 8) + n + k)
                wide[at : at + 8, :] = pair[t : t + 8, k * 128 : (k + 1) * 128]


def wide_tile(wide, i, count):
    at = 8 * count * (i // 8) + i % 8
    return jnp.concatenate([wide[pl.ds(at + 64 * n, 8, stride=8), :] for n in range(count // 8)], axis=0)


def across_lanes(tile, inner):
    return jnp.concatenate([tile] * (inner // 128), axis=1)


def softplus_parts(pre):
    e = jnp.exp2(-LOG2E * jnp.abs(pre))
    more = jnp.where(e < 1e-3, e - 0.5 * e * e, jnp.log(1.0 + e))
    return jnp.maximum(pre, 0.0) + more, jax.nn.sigmoid(pre)


def bit_of(index, bit):
    return lax.rem(lax.div(index, 1 << bit), 2)


def across(axis, bit):
    me = lax.axis_index(axis)
    mine = bit_of(me, bit)
    return mine, {axis: me + (1 - 2 * mine) * (1 << bit)}


class Exchange:
    def __init__(self, runs, branch, ends, backs, totals, rate, results, group, span, pre, pre_span, sends, arrivals, sems):
        self.branch, self.rate = branch, rate
        self.sources, self.totals, self.results = (ends, backs), totals, results
        self.group, self.span, self.pre, self.pre_span = group, span, pre, pre_span
        self.sends, self.arrivals, self.sems = sends, arrivals, sems
        self.links = [across("seq", bit) for bit in range(int(math.log2(runs)))]
        self.slots = ends.shape[0]
        self.states, self.inner = rate.shape

    def flow(self, kind):
        return kind if self.branch == 0 else 1 - kind

    def targets(self):
        return [target for _, target in self.links]

    def copy(self, stage, kind):
        at = 2 * stage + kind
        return remote(
            self.sends.at[at], self.arrivals.at[at], self.sems.at[0, at], self.sems.at[1, at], self.links[stage][1]
        )

    def send(self, stage, kind):
        rows = self.slots * self.states
        at = 2 * stage + kind
        for i in range(self.slots):
            self.sends[at, i * self.states : (i + 1) * self.states, :] = self.group[kind, i].astype(BF16)
        high = self.span[kind].astype(BF16).astype(F32)
        self.sends[at, rows:, :] = jnp.concatenate([high, self.span[kind] - high], axis=0).astype(BF16)
        self.copy(stage, kind).start()

    def join(self, stage, kind, last):
        mine = self.links[stage][0]
        self.copy(stage, kind).wait()
        at = 2 * stage + kind
        earlier = (mine == 1) if self.flow(kind) == 0 else (mine == 0)
        both = self.arrivals[at, self.slots * self.states :, :].astype(F32)
        length = both[: both.shape[0] // 2] + both[both.shape[0] // 2 :]
        own_span, pre_span = self.span[kind], self.pre_span[kind]
        second_span = jnp.where(earlier, own_span, length)
        rate = self.rate[...] * -LOG2E
        for i in range(self.slots):
            state = self.arrivals[at, i * self.states : (i + 1) * self.states, :].astype(F32)
            before = self.pre[kind, i]
            self.pre[kind, i] = jnp.where(earlier, state * jnp.exp2(rate * pre_span[i : i + 1]) + before, before)
            if not last:
                own = self.group[kind, i]
                first, second = jnp.where(earlier, state, own), jnp.where(earlier, own, state)
                self.group[kind, i] = first * jnp.exp2(rate * second_span[i : i + 1]) + second
        self.pre_span[kind] = jnp.where(earlier, length + pre_span, pre_span)
        if not last:
            self.span[kind] = own_span + length

    def points(self):
        count = len(self.links)

        def begin():
            self.pre[...] = jnp.zeros(self.pre.shape, F32)
            self.pre_span[...] = jnp.zeros(self.pre_span.shape, F32)
            self.span[...] = jnp.zeros(self.span.shape, F32)
            for kind in range(2):
                for i in range(self.slots):
                    self.group[kind, i] = self.sources[kind][i]
                    self.span[kind, i : i + 1, :] = self.totals[i][:1]
                if count:
                    self.send(0, kind)

        def step(stage):
            last = stage == count - 1
            for kind in range(2):
                self.join(stage, kind, last)
                if not last:
                    self.send(stage + 1, kind)

        def end():
            for kind in range(2):
                for i in range(self.slots):
                    self.results[kind][i] = self.pre[kind, i]

        return [begin] + [functools.partial(step, stage) for stage in range(count)] + [end]


def exchange_shapes(runs, slots, states, inner):
    pairs = max(int(math.log2(runs)), 1)
    span_rows = -(-slots // 8) * 8
    return [
        pltpu.VMEM((2, slots, states, inner), F32), pltpu.VMEM((2, span_rows, inner), F32),
        pltpu.VMEM((2, slots, states, inner), F32), pltpu.VMEM((2, span_rows, inner), F32),
        pltpu.VMEM((2 * pairs, slots * states + 2 * span_rows, inner), BF16),
        pltpu.VMEM((2 * pairs, slots * states + 2 * span_rows, inner), BF16),
        pltpu.SemaphoreType.DMA((2, 2 * pairs)),
    ]


def beside(points, step, first, count):
    for at in range(min(len(points), count)):
        todo = points[at:] if at == count - 1 else points[at : at + 1]

        @pl.when(step == first + at)
        def _():
            for point in todo:
                point()


def first_kernel(
    runs, slots, ahead, xe, dy, taps, tap_bias, x_rows, dt_rows, dt_bias, rate,
    act_out, planes, proj_out, last_out, starts_out, tiles, weights, first_in,
    dx, decay, through, rate2, wide, picks, ends, backs, totals, first_rate, *exchange_scratch,
):
    toks, inner = dy.shape
    states = rate.shape[0]
    blocks = toks // BLK
    rank = WIDE_RANK
    xwt, dtw = weights.at[: weights.shape[0] - rank], weights.at[weights.shape[0] - rank :]
    delta_out, sig_out, dsilu_out = (planes.at[at] for at in range(3))
    end_out, back_out = last_out.at[:states], last_out.at[states : 2 * states]
    tap_count = taps.shape[0]
    branch, item = pl.program_id(0), pl.program_id(1)
    results = (first_in.at[0], first_in.at[1])
    exchange = Exchange(runs, 0, ends, backs, totals, first_rate, results, *exchange_scratch)

    @pl.when((branch == 0) & (item == 0))
    def _():
        greet(exchange.targets())
        first_rate[...] = rate[...]

    beside(exchange.points(), branch * slots + item, slots, slots)

    @pl.when(item == 0)
    def _():
        rate2[...] = rate[...] * -LOG2E
        picks[...] = (
            lax.broadcasted_iota(jnp.int32, picks.shape, 0) % (2 * states)
            == lax.broadcasted_iota(jnp.int32, picks.shape, 1) // 128
        ).astype(BF16)
        held = dt_rows.shape[0]
        rows = x_rows[...].astype(F32)
        gap = jnp.zeros((rank - held, inner), F32)
        wide = [rows[:held], gap, rows[held:], dt_rows[...].astype(F32), gap]
        weights[...] = jnp.concatenate(wide, axis=0).astype(BF16)

    tap_row, dt_row = tap_bias[pl.ds(branch, 1), :], dt_bias[pl.ds(branch, 1), :]
    for cols in columns(inner):
        x_f = jnp.concatenate([ahead[:, cols], xe[:, cols]], axis=0).astype(F32)
        conv = tap_row[:, cols] + taps[tap_count - 1 : tap_count, cols] * x_f[HALO:]
        for k in range(tap_count - 1):
            conv = conv + taps[k : k + 1, cols] * pltpu.roll(x_f, tap_count - 1 - k, 0)[HALO:]
        open_part = jax.nn.sigmoid(conv)
        act_f = conv * open_part
        act_out[:, cols] = act_f.astype(BF16)
        dsilu_out[:, cols] = open_part + act_f * (1.0 - open_part)
    proj = dot_nt(xwt[...], act_out[...])
    proj_out[...] = proj
    dt_low = proj[:rank, :].astype(BF16)
    for cols in columns(inner, 256):
        pre = dot_tn(dt_low, dtw[:, cols]) + dt_row[:, cols]
        delta, slope = softplus_parts(pre)
        delta_out[:, cols] = delta
        sig_out[:, cols] = slope
        dx[:, cols] = delta * act_out[:, cols].astype(F32)
    lay_out(wide, proj[rank:, :], picks)
    end_out[...] = jnp.zeros((states, inner), F32)
    back_out[...] = jnp.zeros((states, inner), F32)
    through[...] = jnp.zeros((8, inner), F32)

    def one_block(j, slot):
        t0 = pl.multiple_of(j * BLK, BLK)
        dr, xr, yr = (ref.at[pl.ds(t0, BLK), :] for ref in (delta_out, dx, dy))
        count = 2 * states
        wide_rows = wide.at[pl.ds(pl.multiple_of(j * (BLK * count), BLK * count), BLK * count), :]
        s = end_out[...]
        before = through[...]
        starts_out[j] = jnp.concatenate([s, before], axis=0)
        rates = rate2[...]
        for i in range(BLK):
            a = jnp.exp2(spread(dr, i) * rates)
            decay[slot, i] = a
            tile = wide_tile(wide_rows, i, count)
            tiles[t0 + i] = tile
            s = a * s + spread(xr, i) * across_lanes(tile[:states], inner)
        end_out[...] = s
        m = jnp.zeros((states, inner), F32)
        for i in reversed(range(BLK)):
            m = decay[slot, i] * (m + spread(yr, i) * across_lanes(tiles[t0 + i, states:], inner))
        back_out[...] = back_out[...] + m * jnp.exp2(twice(before) * rates)
        through[...] = before + jnp.sum(dr[...], axis=0, keepdims=True)

    def block_step(k, _):
        one_block(2 * k, 0)
        one_block(2 * k + 1, 1)
        return 0

    lax.fori_loop(0, blocks // 2, block_step, 0)
    last_out[2 * states :, :] = through[...]

    @pl.when(branch == 0)
    def _():
        ends[item] = end_out[...]
        backs[item] = back_out[...]
        totals[item] = through[:1, :]


def second_kernel(
    runs, first_in, lasts, last_rate, starts, tiles, rate, ahead, xe, act, planes, dy, proj, weights, taps, skip,
    y_out, dx_out, rims, grads,
    rate2, carry, dxs, bdiag, cdiag, decay, states_low, lam_low, rq_low, qd_low, dots, racc, gsum, hsum, db, dc,
    d_pre_low, s_in, s_last, lam_last, *exchange_scratch,
):
    toks, inner = dy.shape
    states = rate.shape[0]
    blocks = toks // BLK
    rank = WIDE_RANK
    xwt, dtw = weights.at[: weights.shape[0] - rank], weights.at[weights.shape[0] - rank :]
    delta, sig, dsilu = (planes.at[at] for at in range(3))
    tap_count = taps.shape[0]
    held = (grads.shape[0] - 3 * states - 8) // 2
    xp_grad, dtp_grad = grads.at[: held + 2 * states], grads.at[held + 2 * states : 2 * held + 2 * states]
    at = 2 * held + 2 * states
    rate_grad, row_grads = grads.at[at : at + states], grads.at[at + states : at + states + 8]
    tapb_at, skip_at, dtb_at = (slice(tap_count + row, tap_count + row + 1) for row in range(3))
    item = pl.program_id(1)
    branch = pl.program_id(0)
    slots = lasts.shape[0]
    ends, backs = lasts.at[:, :states], lasts.at[:, states : 2 * states]
    totals = lasts.at[:, 2 * states :]
    exchange = Exchange(runs, 1, ends, backs, totals, last_rate, (s_last, lam_last), *exchange_scratch)

    @pl.when((item == 0) & (branch == 0))
    def _():
        greet(exchange.targets())

    beside(exchange.points(), branch * slots + item, 0, slots)

    @pl.when(branch == 0)
    def _():
        s_in[...] = first_in[0, item]
        carry[...] = first_in[1, item]

    @pl.when(branch == 1)
    def _():
        s_in[...] = s_last[item]
        carry[...] = lam_last[item]

    gain = skip[pl.ds(pl.program_id(0), 1), :]
    rate2[...] = rate[...] * -LOG2E
    width = BLK * states

    @pl.when(item == 0)
    def _():
        grads[...] = jnp.zeros(grads.shape, F32)

    for cols in columns(inner):
        dxs[:toks, cols] = delta[:, cols] * act[:, cols].astype(F32)
    fold = (
        lax.broadcasted_iota(jnp.int32, (states, width), 1) % states == lax.broadcasted_iota(jnp.int32, (states, width), 0)
    ).astype(BF16)
    own = lax.broadcasted_iota(jnp.int32, (toks, width), 0) % BLK == lax.broadcasted_iota(jnp.int32, (toks, width), 1) // states
    bdiag[:toks, :] = jnp.where(own, dot_tn(proj[rank : rank + states, :].astype(BF16), fold), 0.0).astype(BF16)
    cdiag[...] = jnp.where(own, dot_tn(proj[rank + states :, :].astype(BF16), fold), 0.0).astype(BF16)
    mine = own[:BLK]
    picks = mine.astype(BF16)
    sides = (
        lax.broadcasted_iota(jnp.int32, (2 * BLK, 256), 0) // BLK == lax.broadcasted_iota(jnp.int32, (2 * BLK, 256), 1) // 128
    ).astype(BF16)
    racc[...] = jnp.zeros((states, inner), F32)

    def lane_sum(wide):
        part = [wide[:, at : at + 128] for at in range(0, inner, 128)]
        while len(part) > 1:
            part = [sum(part[at : at + 2]) for at in range(0, len(part), 2)]
        return part[0]

    def products(slot, j):
        t0 = pl.multiple_of(j * BLK, BLK)
        y_out[pl.ds(t0, BLK), :] = dot(cdiag[pl.ds(t0, BLK), :], states_low[slot, states:, :])
        gsum[pl.ds(t0, BLK), :] = dot(bdiag[pl.ds(t0, BLK), :], lam_low[slot])
        hsum[pl.ds(t0, BLK), :] = dot(picks, rq_low[slot])
        racc[...] += dot(fold[:, : BLK // 4 * states], qd_low[slot])
        both = dot_nt(sides, dots[slot])
        dc[pl.ds(t0, BLK), :] = jnp.where(mine, both[:BLK], 0.0).astype(BF16)
        db[pl.ds(t0, BLK), :] = jnp.where(mine, both[BLK:], 0.0).astype(BF16)

    def one_block(slot, j):
        t0 = pl.multiple_of(j * BLK, BLK)
        dr, xr, yr = (ref.at[pl.ds(t0, BLK), :] for ref in (delta, dxs, dy))
        tile = tiles.at[pl.ds(t0, BLK)]
        r2 = rate2[...]
        r_low = rate[...].astype(BF16)
        begin = starts[j]
        s = begin[:states] + s_in[...] * jnp.exp2(twice(begin[states:]) * r2)
        states_low[slot, :states, :] = s.astype(BF16)
        for i in range(BLK):
            a = jnp.exp2(spread(dr, i) * r2)
            decay[slot, i] = a
            s = a * s + spread(xr, i) * across_lanes(tile[i, :states], inner)
            s_low = s.astype(BF16)
            states_low[slot, (i + 1) * states : (i + 2) * states, :] = s_low
            dots[slot, i * states : (i + 1) * states, :128] = lane_sum(s_low * spread(yr, i).astype(BF16))
        cr = carry[...]
        qds = []
        for i in reversed(range(BLK)):
            lam = cr + spread(yr, i) * across_lanes(tile[i, states:], inner)
            l_low = lam.astype(BF16)
            lam_low[slot, i * states : (i + 1) * states, :] = l_low
            dots[slot, i * states : (i + 1) * states, 128:] = lane_sum(l_low * spread(xr, i).astype(BF16))
            cr = decay[slot, i] * lam
            q = cr.astype(BF16) * states_low[slot, i * states : (i + 1) * states, :]
            rq_low[slot, i * states : (i + 1) * states, :] = q * r_low
            qds.append(q * spread(dr, i).astype(BF16))
            if i % 4 == 0:
                qd_low[slot, i // 4 * states : (i // 4 + 1) * states, :] = (qds[0] + qds[1]) + (qds[2] + qds[3])
                qds = []
        carry[...] = cr

    def block_step(k, _):
        j = blocks - 1 - 2 * k
        for slot in range(2):
            one_block(slot, j - slot)
            products(slot, j - slot)
        return 0

    lax.fori_loop(0, blocks // 2, block_step, 0)
    rate_grad[...] += -racc[...]
    for cols in columns(inner):
        act_f = act[:, cols].astype(F32)
        row_grads[skip_at, cols] += jnp.sum(dy[:, cols] * act_f, axis=0, keepdims=True)
        y_out[:, cols] += gain[:, cols] * act_f
        d_pre = (act_f * gsum[:toks, cols] - hsum[:toks, cols]) * sig[:, cols]
        row_grads[dtb_at, cols] += jnp.sum(d_pre, axis=0, keepdims=True)
        d_pre_low[:, cols] = d_pre.astype(BF16)
    dtp_grad[...] += dot(proj[:rank, :].astype(BF16), d_pre_low[...])[:held]
    d_proj = jnp.concatenate(
        [dot_nt(dtw[...], d_pre_low[...]), dot_nt(fold, db[:toks, :]), dot_nt(fold, dc[:toks, :])], axis=0
    ).astype(BF16)
    xp_new = dot(d_proj, act[...])
    xp_grad[:held, :] += xp_new[:held]
    xp_grad[held:, :] += xp_new[rank:]
    window = HALO + toks
    for wide_cols in columns(inner, 256):
        through = dot_tn(d_proj, xwt[:, wide_cols])
        for at in columns(256):
            cols = slice(wide_cols.start + at.start, wide_cols.start + at.stop)
            d_act = delta[:, cols] * gsum[:toks, cols] + gain[:, cols] * dy[:, cols] + through[:, at]
            d_conv = d_act * dsilu[:, cols]
            row_grads[tapb_at, cols] += jnp.sum(d_conv, axis=0, keepdims=True)
            x_f = jnp.concatenate([ahead[:, cols], xe[:, cols]], axis=0).astype(F32)
            base = jnp.concatenate([jnp.zeros((HALO, 128), F32), d_conv], axis=0)
            d_window = taps[tap_count - 1 : tap_count, cols] * base
            row_grads[tap_count - 1 : tap_count, cols] += jnp.sum(d_conv * x_f[HALO:], axis=0, keepdims=True)
            for k in range(tap_count - 1):
                moved = pltpu.roll(base, window - (tap_count - 1 - k), 0)
                row_grads[k : k + 1, cols] += jnp.sum(moved * x_f, axis=0, keepdims=True)
                d_window = d_window + taps[k : k + 1, cols] * moved
            rims[branch, item, :, cols] = d_window[HALO - 8 : HALO]
            dx_out[:, cols] = d_window[HALO:]


LAST_ROWS = 16
PART_ROWS = 512


class Ring:
    def __init__(self, bits):
        self.bits = bits
        self.size = 1 << len(bits)
        self.digits = [bit_of(lax.axis_index(axis), bit) for axis, bit in bits]
        self.place = sum(digit * (1 << at) for at, digit in enumerate(self.digits))

    def target(self, ahead):
        place = lax.rem(self.place + ahead, self.size)
        where = {}
        for at, (axis, bit) in enumerate(self.bits):
            base = where.get(axis, lax.axis_index(axis))
            where[axis] = base + (bit_of(place, at) - self.digits[at]) * (1 << bit)
        return where, place

    def targets(self):
        return [self.target(ahead)[0] for ahead in range(1, self.size)]


def stage_rings(runs, groups):
    bits = [("seq", bit) for bit in range(int(math.log2(runs)))] + [("dp", bit) for bit in range(int(math.log2(groups)))]
    return [Ring(bits[:1])] + [Ring(bits[at : at + 2]) for at in range(1, len(bits), 2)]


def part_count(rows):
    return -(-rows // PART_ROWS)


def buffer_rows(runs, groups):
    bits = int(math.log2(runs)) + int(math.log2(groups))
    size, total = PART_ROWS, 0
    for members in [2] + [1 << min(2, bits - at) for at in range(1, bits, 2)]:
        moved = size // members if size >= members * LAST_ROWS else size
        total += moved * (members - 1)
        size = moved
    return total


def reduce_shapes(parts, dim, runs, groups):
    bits = int(math.log2(runs)) + int(math.log2(groups))
    stages = 1 + bits // 2
    room = parts * buffer_rows(runs, groups)
    sems = pltpu.SemaphoreType.DMA((parts, 2 * stages, 3))
    return [
        pltpu.VMEM((parts * PART_ROWS, dim), F32), pltpu.VMEM((room, dim), BF16), pltpu.VMEM((room, dim), BF16),
        pltpu.VMEM((parts * PART_ROWS, dim), BF16), sems, sems,
    ]


class Reduction:
    def __init__(self, rings, turns, segments, acc, sends, arrivals, gathered, send_sem, recv_sem):
        self.rings = rings
        self.count = len(rings)
        self.parts = len(turns)
        self.segments = segments
        self.acc, self.sends, self.arrivals, self.gathered = acc, sends, arrivals, gathered
        self.send_sem, self.recv_sem = send_sem, recv_sem
        room = sends.shape[0] // self.parts
        self.steps = []
        for part, turn in enumerate(turns):
            later = rings[1:]
            turn = turn % max(len(later), 1)
            order = rings[:1] + later[turn:] + later[:turn]
            start, size, at = part * PART_ROWS, PART_ROWS, part * room
            steps = []
            for ring in order:
                split = size >= ring.size * LAST_ROWS
                moved = size // ring.size if split else size
                keep = pl.multiple_of(start + ring.place * moved, LAST_ROWS) if split else start
                steps.append((ring, start, split, moved, keep, at))
                at += moved * (ring.size - 1)
                start, size = keep, moved
            self.steps.append(steps)

    def assemble(self, part):
        low, high = part * PART_ROWS, (part + 1) * PART_ROWS
        at = 0
        for get, size in self.segments:
            first, last = max(at, low), min(at + size, high)
            if first < last:
                self.acc[first:last, :] = get(first - at, last - first)
            at += size
        if at < high:
            first = max(at, low)
            self.acc[first:high, :] = jnp.zeros((high - first, self.acc.shape[1]), F32)

    def scatter_copy(self, part, stage, ahead):
        ring, _, _, moved, _, at = self.steps[part][stage]
        at += (ahead - 1) * moved
        return remote(
            self.sends.at[pl.ds(at, moved), :], self.arrivals.at[pl.ds(at, moved), :],
            self.send_sem.at[part, stage, ahead - 1], self.recv_sem.at[part, stage, ahead - 1], ring.target(ahead)[0],
        )

    def scatter(self, part, stage):
        ring, start, split, moved, _, at = self.steps[part][stage]
        for ahead in range(1, ring.size):
            place = ring.target(ahead)[1]
            away = pl.multiple_of(start + place * moved, LAST_ROWS) if split else start
            here = at + (ahead - 1) * moved
            self.sends[here : here + moved, :] = self.acc[pl.ds(away, moved), :].astype(BF16)
            self.scatter_copy(part, stage, ahead).start()

    def settle(self, part, stage):
        ring, _, split, moved, keep, at = self.steps[part][stage]
        for ahead in range(1, ring.size):
            self.scatter_copy(part, stage, ahead).wait()
        held = self.acc[pl.ds(keep, moved), :]
        came = [
            self.arrivals[at + (ahead - 1) * moved : at + ahead * moved, :].astype(F32) for ahead in range(1, ring.size)
        ]
        if split:
            held = held + sum(came)
        else:
            values = [held.astype(BF16).astype(F32)] + came
            total = jnp.zeros_like(held)
            for place in range(ring.size):
                behind = lax.rem(ring.place - place + ring.size, ring.size)
                chosen = values[0]
                for ahead in range(1, ring.size):
                    chosen = jnp.where(behind == ahead, values[ahead], chosen)
                total = total + chosen
            held = total
        self.acc[pl.ds(keep, moved), :] = held

    def gather_copies(self, part, stage):
        ring, _, split, moved, keep, _ = self.steps[part][stage]
        here = self.gathered.at[pl.ds(keep, moved), :]
        return [
            remote(
                here, here, self.send_sem.at[part, self.count + stage, ahead - 1],
                self.recv_sem.at[part, self.count + stage, ahead - 1], ring.target(ahead)[0],
            )
            for ahead in range(1, ring.size)
            if split
        ]

    def points(self):
        def begin():
            for part in range(self.parts):
                self.assemble(part)
                self.scatter(part, 0)

        def split(stage):
            for part in range(self.parts):
                self.settle(part, stage - 1)
                self.scatter(part, stage)

        def turn():
            for part in range(self.parts):
                self.settle(part, self.count - 1)
                _, _, _, moved, keep, _ = self.steps[part][-1]
                self.gathered[pl.ds(keep, moved), :] = self.acc[pl.ds(keep, moved), :].astype(BF16)
                for copy in self.gather_copies(part, self.count - 1):
                    copy.start()

        def join(stage):
            for part in range(self.parts):
                for copy in self.gather_copies(part, stage + 1):
                    copy.wait()
                if stage >= 0:
                    for copy in self.gather_copies(part, stage):
                        copy.start()

        points = [begin]
        points += [functools.partial(split, stage) for stage in range(1, self.count)]
        points += [turn]
        return points + [functools.partial(join, stage) for stage in reversed(range(-1, self.count - 1))]


def big_segments(ref, dim):
    return [
        (lambda at, size, lane=lane: ref[at : at + size, lane : lane + dim], ref.shape[0])
        for lane in range(0, ref.shape[1], dim)
    ]


def small_segments(ref, dim):
    return [
        (lambda at, size, branch=branch, lane=lane: ref[branch, at : at + size, lane : lane + dim], ref.shape[1])
        for lane in range(0, ref.shape[2], dim)
        for branch in range(2)
    ]


def tail_kernel(
    plan, tok, cot, mod, mask, counts, hid, z_in, y, dx, rims, win, wout, step,
    grads,
    mixed, d_tokens, result, x_result, factors, own_rows,
    late, rim_send, rim_recv, dz, out_grad, z_grad, x_grad, mod_sum, mod_in, table, small_send, small_recv, *reduce_scratch,
):
    runs, groups, slots = plan
    me = lax.axis_index("seq")
    downs = [(rims.at[0], late.at[0], rim_send.at[0], rim_recv.at[0])]
    ups = [(rims.at[1], late.at[1], rim_send.at[1], rim_recv.at[1])]
    dim = tok.shape[-1]
    toks, inner = z_in.shape
    now = pl.program_id(0)
    i = lax.rem(now, slots)
    rings = stage_rings(runs, groups)
    seq_ring = Ring([("seq", bit) for bit in range(int(math.log2(runs)))])
    dp_ring = Ring([("dp", bit) for bit in range(int(math.log2(groups)))])
    half = len(reduce_scratch) // 2
    smalls = small_segments(grads, dim)
    segments = big_segments(out_grad, dim) + big_segments(z_grad, dim) + smalls
    main = Reduction(rings, [part % 3 // 2 for part in range(result.shape[0] // PART_ROWS)], segments, *reduce_scratch[:half])
    rest = Reduction(rings, [part % 2 for part in range(x_result.shape[0] // PART_ROWS)], big_segments(x_grad, dim), *reduce_scratch[half:])
    main_points, rest_points = main.points(), rest.points()

    @pl.when(now == 0)
    def _():
        greet_line(me, runs, [target for ring in rings + [seq_ring, dp_ring] for target in ring.targets()])
        swap_along_line(me, runs, ups, downs, True)

        @pl.when(me == 0)
        def _():
            late[1] = jnp.zeros(late.shape[1:], F32)

        @pl.when(me == runs - 1)
        def _():
            late[0] = jnp.zeros(late.shape[1:], F32)

        out_grad[...] = jnp.zeros(out_grad.shape, F32)
        z_grad[...] = jnp.zeros(z_grad.shape, F32)
        x_grad[...] = jnp.zeros(x_grad.shape, F32)
        mod_sum[...] = jnp.zeros(mod_sum.shape, F32)

    scale, gate = mod[:, dim : 2 * dim], mod[:, 2 * dim :]
    valid = as_column(mask[pl.ds(i, 1), :]) * jnp.where(counts[0] > i, 1.0, 0.0)
    mod_rows = pl.ds(pl.multiple_of(8 * i, 8), 8)

    @pl.when(now < slots)
    def _():
        cot_f = cot[...].astype(F32)
        z = z_in[...]
        z_sig = jax.nn.sigmoid(z)
        z_silu = z * z_sig
        summed = y[0] + flip_full(y[1])
        gated = (summed * z_silu).astype(BF16)
        branch_out = dot(gated, wout[...])
        mixed[...] = (tok[...].astype(F32) + gate * branch_out).astype(BF16)
        d_branch = (cot_f * gate).astype(BF16)
        out_grad[...] += dot_tn(gated, d_branch)
        d_zgate = dot_nt(d_branch, wout[...]) * summed * (z_sig + z_silu * (1.0 - z_sig))
        d_low = (d_zgate * valid).astype(BF16)
        dz[i] = d_low
        z_grad[...] += dot_tn(hid[...], d_low)
        d_gate = jnp.sum(cot_f * branch_out, axis=0, keepdims=True)
        mod_sum[mod_rows, :] = jnp.concatenate([jnp.zeros((2, dim), F32), d_gate, jnp.zeros((5, dim), F32)], axis=0)

    @pl.when(now == slots)
    def _():
        main_points[0]()
        swap_along_line(me, runs, ups, downs, False)

    @pl.when(now >= slots)
    def _():
        edge = late.shape[2]

        def with_late(part, extra):
            return jnp.concatenate([part[: toks - edge], part[toks - edge :] + extra], axis=0)

        d_x = with_late(dx[0], late[0, i]) + flip_full(with_late(dx[1], late[1, i]))
        d_x = (d_x * valid).astype(BF16)
        x_grad[...] += dot_tn(hid[...], d_x)
        d_hidden = dot_nt(d_x, win[:, :inner]) + dot_nt(dz[i], win[:, inner:])
        normed, inv_std = normalise(tok[...].astype(F32))
        d_shift = jnp.sum(d_hidden, axis=0, keepdims=True)
        d_scale = jnp.sum(d_hidden * normed, axis=0, keepdims=True)
        mod_sum[mod_rows, :] += jnp.concatenate([d_shift, d_scale, jnp.zeros((6, dim), F32)], axis=0)
        d_normed = d_hidden * (1.0 + scale)
        d_tokens[...] = cot[...].astype(F32) + inv_std * (
            d_normed
            - jnp.mean(d_normed, axis=-1, keepdims=True)
            - normed * jnp.mean(d_normed * normed, axis=-1, keepdims=True)
        )

    @pl.when(now == slots)
    def _():
        main_points[1]()

    def sum_copies():
        return [
            remote(mod_sum, mod_in.at[ahead - 1], small_send.at[ahead - 1], small_recv.at[ahead - 1], seq_ring.target(ahead)[0])
            for ahead in range(1, seq_ring.size)
        ]

    def table_copies():
        at = pl.multiple_of(dp_ring.place * 16, 16)
        here = table.at[pl.ds(at, 16), :]
        base = seq_ring.size - 1
        return [
            remote(here, here, small_send.at[base + ahead - 1], small_recv.at[base + ahead - 1], dp_ring.target(ahead)[0])
            for ahead in range(1, dp_ring.size)
        ]

    def start_small():
        for copy in sum_copies():
            copy.start()

    def turn_small():
        for copy in sum_copies():
            copy.wait()
        values = [mod_sum[...]] + [mod_in[ahead - 1] for ahead in range(1, seq_ring.size)]
        total = jnp.zeros(mod_sum.shape, F32)
        for place in range(seq_ring.size):
            behind = lax.rem(seq_ring.place - place + seq_ring.size, seq_ring.size)
            chosen = values[0]
            for ahead in range(1, seq_ring.size):
                chosen = jnp.where(behind == ahead, values[ahead], chosen)
            total = total + chosen
        time_f = step[...].astype(F32)
        time_low = time_f * jax.nn.sigmoid(time_f)
        lines = [total[8 * item : 8 * item + 3] for item in range(slots)] + [time_low]
        lines.append(jnp.zeros((16 - 4 * slots, dim), F32))
        own = jnp.concatenate(lines, axis=0).astype(BF16)
        own_rows[...] = own
        table[pl.ds(pl.multiple_of(dp_ring.place * 16, 16), 16), :] = own
        for copy in table_copies():
            copy.start()

    def end_small():
        for copy in table_copies():
            copy.wait()
        factors[...] = table[...]

    @pl.when(now == 2 * slots - 1)
    def _():
        start_small()
        rest_points[0]()
        rest_points[1]()
        for at in range(2, len(main_points)):
            main_points[at]()
            if at == 2:
                turn_small()
            rest_points[at]()
        end_small()
        result[...] = main.gathered[...]
        x_result[...] = rest.gathered[...]


def finish_kernel(
    outs, zs, xs, smalls, factors, own, step, ada,
    grad_time, grad_ada, grad_ada_bias, in_grad, tap_grad, tapb_grad, xp_grad, dtp_grad, dtb_grad, rate_grad, skip_grad, out_grad,
):
    dim, inner = in_grad.shape[0], rate_grad.shape[2]
    slots = step.shape[0]
    now = pl.program_id(0)
    out_grad[...] = outs[...].astype(F32)
    in_grad[...] = jnp.where(now < inner // dim, xs[...], zs[...]).astype(F32)
    table = factors[...]
    length = table.shape[0]

    for part in range(3):

        @pl.when(now == part)
        def _():
            row = lax.broadcasted_iota(jnp.int32, (length, length), 0)
            col = lax.broadcasted_iota(jnp.int32, (length, length), 1)
            item = row % 16 - 3 * slots
            wanted = row // 16 * 16 + 3 * item + part
            mods = dot(((col == wanted) & (item >= 0) & (item < slots)).astype(BF16), table)
            lanes = slice(part * dim, (part + 1) * dim)
            grad_ada[...] = dot_tn(table, mods.astype(BF16))
            grad_ada_bias[lanes] = jnp.sum(mods, axis=0)
            mine = own[...].astype(F32)
            picked = jnp.concatenate([mine[3 * i + part : 3 * i + part + 1] for i in range(slots)], axis=0)
            d_time = dot_nt(picked.astype(BF16), ada[...])
            grad_time[...] = d_time if part == 0 else grad_time[...] + d_time

    @pl.when(now == 3)
    def _():
        time_f = step[...].astype(F32)
        time_sig = jax.nn.sigmoid(time_f)
        grad_time[...] = grad_time[...] * time_sig * (1.0 + time_f * (1.0 - time_sig))
        at = 0
        for first in range(0, inner, dim):
            lanes = slice(first, first + dim)
            for branch in range(2):
                for ref in (xp_grad, dtp_grad, rate_grad, tap_grad):
                    size = ref.shape[1]
                    ref[branch, :, lanes] = smalls[at : at + size, :].astype(F32)
                    at += size
                for ref in (tapb_grad, skip_grad, dtb_grad):
                    ref[branch : branch + 1, lanes] = smalls[at : at + 1, :].astype(F32)
                    at += 1
                at += 1


def params(**more):
    return pltpu.CompilerParams(vmem_limit_bytes=VMEM_LIMIT, **more)


def spec(block, index):
    return pl.BlockSpec(block, index)


def per_device(
    tokens, timestep, counts, token_mask, ada_weight, ada_bias, input_weight, conv_weight, conv_bias, x_weight, dt_weight,
    dt_bias, decay_rate, skip_gain, output_weight, cotangent,
):
    slots, toks, dim = tokens.shape
    inner = output_weight.shape[0]
    rank = dt_weight.shape[1]
    states = decay_rate.shape[1]
    tap_count = conv_weight.shape[1]
    wide_rank = WIDE_RANK
    proj_rows = wide_rank + 2 * states
    blocks = toks // BLK
    runs = lax.axis_size("seq")
    groups = lax.axis_size("dp")
    x_rows = jnp.swapaxes(x_weight, 1, 2)

    def item(*block):
        return spec((None,) + block, lambda i: (i,) + (0,) * len(block))

    def whole(*block):
        return spec(block, lambda *_: (0,) * len(block))

    xe, dy, z_gate, hid, modulate, ahead = pl.pallas_call(
        functools.partial(enter_kernel, runs),
        grid=(slots,),
        in_specs=[
            whole(slots, toks, dim), item(toks, dim), whole(slots, toks), pl.BlockSpec(memory_space=pltpu.SMEM), whole(slots, dim), whole(dim, 3 * dim),
            whole(3 * dim), whole(dim, 2 * inner), whole(inner, dim),
        ],
        out_specs=[
            item(2, toks, inner), item(2, toks, inner), item(toks, inner), item(toks, dim), item(1, 3 * dim),
            whole(slots, 2, HALO, inner),
        ],
        out_shape=[
            jax.ShapeDtypeStruct((slots, 2, toks, inner), BF16),
            jax.ShapeDtypeStruct((slots, 2, toks, inner), F32),
            jax.ShapeDtypeStruct((slots, toks, inner), F32),
            jax.ShapeDtypeStruct((slots, toks, dim), BF16),
            jax.ShapeDtypeStruct((slots, 1, 3 * dim), F32),
            jax.ShapeDtypeStruct((slots, 2, HALO, inner), BF16),
        ],
        scratch_shapes=[
            pltpu.VMEM((slots, 3 * dim), F32),
            pltpu.VMEM((slots, HALO, dim), BF16), pltpu.VMEM((slots, HALO, dim), BF16), pltpu.VMEM((slots, toks), jnp.int32),
            pltpu.VMEM((slots, toks), jnp.int32), pltpu.SemaphoreType.DMA((4,)), pltpu.SemaphoreType.DMA((4,)),
        ],
        compiler_params=params(collective_id=1, has_side_effects=True),
        name="enter",
    )(
        tokens, cotangent, token_mask, counts, timestep, ada_weight, ada_bias, input_weight, output_weight,
    )

    def unit(*block):
        return spec((None, None) + block, lambda b, i: (i, b) + (0,) * len(block))

    def branch(*block):
        return spec((None,) + block, lambda b, i: (b,) + (0,) * len(block))

    def unit_shape(*block, kind=F32):
        return jax.ShapeDtypeStruct((slots, 2) + block, kind)

    act, planes, proj, lasts, starts, tiles, weights, first_in = pl.pallas_call(
        functools.partial(first_kernel, runs, slots),
        grid=(2, slots),
        in_specs=[
            unit(HALO, inner), unit(toks, inner), unit(toks, inner), branch(tap_count, inner), whole(2, inner),
            branch(rank + 2 * states, inner), branch(rank, inner), whole(2, inner), branch(states, inner),
        ],
        out_specs=[
            unit(toks, inner), unit(3, toks, inner), unit(proj_rows, toks), unit(2 * states + 8, inner),
            unit(blocks, states + 8, inner), unit(toks, 2 * states, 128), branch(proj_rows + wide_rank, inner),
            whole(2, slots, states, inner),
        ],
        out_shape=[
            unit_shape(toks, inner, kind=BF16), unit_shape(3, toks, inner), unit_shape(proj_rows, toks),
            unit_shape(2 * states + 8, inner), unit_shape(blocks, states + 8, inner), unit_shape(toks, 2 * states, 128),
            jax.ShapeDtypeStruct((2, proj_rows + wide_rank, inner), BF16),
            jax.ShapeDtypeStruct((2, slots, states, inner), F32),
        ],
        scratch_shapes=[
            pltpu.VMEM((toks, inner), F32), pltpu.VMEM((2, BLK, states, inner), F32), pltpu.VMEM((8, inner), F32),
            pltpu.VMEM((states, inner), F32), pltpu.VMEM((2 * states * toks, 128), F32),
            pltpu.VMEM((4 * states, 2 * states * 128), BF16), pltpu.VMEM((slots, states, inner), F32),
            pltpu.VMEM((slots, states, inner), F32), pltpu.VMEM((slots, 1, inner), F32), pltpu.VMEM((states, inner), F32),
            *exchange_shapes(runs, slots, states, inner),
        ],
        compiler_params=params(collective_id=2, has_side_effects=True),
        name="first",
    )(ahead, xe, dy, conv_weight, conv_bias, x_rows, dt_weight, dt_bias, decay_rate)

    vmem = pl.BlockSpec(memory_space=pltpu.VMEM)
    last = spec((slots, None, 2 * states + 8, inner), lambda b, i: (0, 1, 0, 0))
    last_branch = spec((None, states, inner), lambda b, i: (1, 0, 0))

    grad_rows = 2 * rank + 3 * states + 8
    y, dx, rims, grads = pl.pallas_call(
        functools.partial(second_kernel, runs),
        grid=(2, slots),
        in_specs=[
            whole(2, slots, states, inner), last, last_branch, unit(blocks, states + 8, inner), unit(toks, 2 * states, 128),
            branch(states, inner), unit(HALO, inner), unit(toks, inner), unit(toks, inner), unit(3, toks, inner), unit(toks, inner),
            unit(proj_rows, toks), branch(proj_rows + wide_rank, inner), branch(tap_count, inner), whole(2, inner),
        ],
        out_specs=[unit(toks, inner), unit(toks, inner), whole(2, slots, 8, inner), branch(grad_rows, inner)],
        out_shape=[
            unit_shape(toks, inner), unit_shape(toks, inner), jax.ShapeDtypeStruct((2, slots, 8, inner), F32),
            jax.ShapeDtypeStruct((2, grad_rows, inner), F32),
        ],
        scratch_shapes=[
            pltpu.VMEM((states, inner), F32), pltpu.VMEM((states, inner), F32), pltpu.VMEM((toks + BLK, inner), F32), pltpu.VMEM((toks + BLK, BLK * states), BF16),
            pltpu.VMEM((toks, BLK * states), BF16),
            pltpu.VMEM((2, BLK, states, inner), F32),
            pltpu.VMEM((2, (BLK + 1) * states, inner), BF16), pltpu.VMEM((2, BLK * states, inner), BF16),
            pltpu.VMEM((2, BLK * states, inner), BF16), pltpu.VMEM((2, BLK // 4 * states, inner), BF16),
            pltpu.VMEM((2, BLK * states, 256), BF16), pltpu.VMEM((states, inner), F32),
            pltpu.VMEM((toks + BLK, inner), F32), pltpu.VMEM((toks + BLK, inner), F32),
            pltpu.VMEM((toks + BLK, BLK * states), BF16), pltpu.VMEM((toks + BLK, BLK * states), BF16),
            pltpu.VMEM((toks, inner), BF16),
            pltpu.VMEM((states, inner), F32), pltpu.VMEM((slots, states, inner), F32), pltpu.VMEM((slots, states, inner), F32),
            *exchange_shapes(runs, slots, states, inner),
        ],
        compiler_params=params(collective_id=3, has_side_effects=True),
        name="second",
    )(
        first_in, lasts, decay_rate, starts, tiles, decay_rate, ahead, xe, act, planes, dy, proj, weights, conv_weight, skip_gain,
    )

    def now(*block):
        return spec((None,) + block, lambda s: (s % slots,) + (0,) * len(block))

    def early(*block):
        return spec((None,) + block, lambda s: (jnp.minimum(s, slots - 1),) + (0,) * len(block))

    def after(*block):
        return spec((None,) + block, lambda s: (jnp.maximum(s - slots, 0),) + (0,) * len(block))

    small_rows = 2 * grad_rows * (inner // dim)
    main_parts = part_count(inner + dim * (inner // dim) + small_rows)
    rest_parts = part_count(dim * (inner // dim))
    mixed, d_tokens, result, x_result, factors, own = pl.pallas_call(
        functools.partial(tail_kernel, (runs, groups, slots)),
        grid=(2 * slots,),
        in_specs=[
            now(toks, dim), now(toks, dim), now(1, 3 * dim), whole(slots, toks), pl.BlockSpec(memory_space=pltpu.SMEM), now(toks, dim),
            early(toks, inner), early(2, toks, inner), after(2, toks, inner), whole(2, slots, 8, inner),
            whole(dim, 2 * inner), whole(inner, dim), whole(slots, dim), whole(2, grad_rows, inner),
        ],
        out_specs=[
            early(toks, dim), after(toks, dim), whole(main_parts * PART_ROWS, dim), whole(rest_parts * PART_ROWS, dim),
            whole(16 * groups, dim), whole(16, dim),
        ],
        out_shape=[
            jax.ShapeDtypeStruct((slots, toks, dim), BF16), jax.ShapeDtypeStruct((slots, toks, dim), F32),
            jax.ShapeDtypeStruct((main_parts * PART_ROWS, dim), BF16), jax.ShapeDtypeStruct((rest_parts * PART_ROWS, dim), BF16),
            jax.ShapeDtypeStruct((16 * groups, dim), BF16), jax.ShapeDtypeStruct((16, dim), BF16),
        ],
        scratch_shapes=[
            pltpu.VMEM((2, slots, 8, inner), F32), pltpu.SemaphoreType.DMA((2,)), pltpu.SemaphoreType.DMA((2,)),
            pltpu.VMEM((slots, toks, inner), BF16), pltpu.VMEM((inner, dim), F32), pltpu.VMEM((dim, inner), F32),
            pltpu.VMEM((dim, inner), F32), pltpu.VMEM((8 * slots, dim), F32), pltpu.VMEM((max(runs - 1, 1), 8 * slots, dim), F32),
            pltpu.VMEM((16 * groups, dim), BF16), pltpu.SemaphoreType.DMA((runs + groups,)),
            pltpu.SemaphoreType.DMA((runs + groups,)), *reduce_shapes(main_parts, dim, runs, groups),
            *reduce_shapes(rest_parts, dim, runs, groups),
        ],
        compiler_params=params(collective_id=4, has_side_effects=True),
        name="tail",
    )(
        tokens, cotangent, modulate, token_mask, counts, hid, z_gate, y, dx, rims, input_weight, output_weight, timestep, grads,
    )

    (
        d_time, grad_ada, grad_ada_bias, in_grad, tap_grad, tapb_grad, xp_grad, dtp_grad, dtb_grad, rate_grad, skip_grad,
        out_grad,
    ) = pl.pallas_call(
        finish_kernel,
        grid=(4,),
        in_specs=[
            spec((inner // 4, dim), lambda s: (s, 0)),
            spec((dim, dim), lambda s: (inner // dim + jnp.maximum(s - inner // dim, 0), 0)),
            spec((dim, dim), lambda s: (jnp.minimum(s, inner // dim - 1), 0)),
            spec((PART_ROWS, dim), lambda s: (2 * inner // PART_ROWS, 0)),
            whole(16 * groups, dim), whole(16, dim), whole(slots, dim), spec((dim, dim), lambda s: (0, jnp.minimum(s, 2))),
        ],
        out_specs=[
            whole(slots, dim), spec((dim, dim), lambda s: (0, jnp.minimum(s, 2))), whole(3 * dim),
            spec((dim, 2 * inner // 4), lambda s: (0, s)), whole(2, tap_count, inner), whole(2, inner),
            whole(2, rank + 2 * states, inner), whole(2, rank, inner), whole(2, inner), whole(2, states, inner), whole(2, inner),
            spec((inner // 4, dim), lambda s: (s, 0)),
        ],
        out_shape=[
            jax.ShapeDtypeStruct(shape, F32)
            for shape in (
                (slots, dim), (dim, 3 * dim), (3 * dim,), (dim, 2 * inner), (2, tap_count, inner), (2, inner),
                (2, rank + 2 * states, inner), (2, rank, inner), (2, inner), (2, states, inner), (2, inner), (inner, dim),
            )
        ],
        compiler_params=params(),
        name="finish",
    )(result, result, x_result, result, factors, own, timestep, ada_weight)
    return (
        mixed, d_tokens, d_time, grad_ada, grad_ada_bias, in_grad, tap_grad, tapb_grad, jnp.swapaxes(xp_grad, 1, 2), dtp_grad, dtb_grad,
        rate_grad, skip_grad, out_grad,
    )


def solution(mesh):
    runs = P("dp", "seq", None)
    return jax.shard_map(
        per_device,
        mesh=mesh,
        in_specs=(runs, P("dp", None), P("dp"), P("dp", "seq")) + (P(),) * 11 + (runs,),
        out_specs=(runs, runs, P("dp", None)) + (P(),) * 11,
        check_vma=False,
    )
```

```python
import functools
import math

import jax
import jax.numpy as jnp
from jax import lax
from jax.experimental import pallas as pl
from jax.experimental.pallas import tpu as pltpu
from jax.sharding import PartitionSpec as P

EPSILON = 1e-06
BLK = 16
WIDE_RANK = 32
HALO = 16
LOG2E = math.log2(math.e)
F32, BF16 = jnp.float32, jnp.bfloat16
NT = (((1,), (1,)), ((), ()))
TN = (((0,), (0,)), ((), ()))
VMEM_LIMIT = 60 << 20
MESH = pl.DeviceIdType.MESH


def dot(a, b):
    return jnp.dot(a, b, preferred_element_type=F32)


def dot_nt(a, b):
    return lax.dot_general(a, b, NT, preferred_element_type=F32)


def dot_tn(a, b):
    return lax.dot_general(a, b, TN, preferred_element_type=F32)


def flip_full(value):
    turned = lax.broadcasted_iota(jnp.int32, (8, value.shape[1]), 0)
    groups = [value[at : at + 8] for at in range(0, value.shape[0], 8)]
    return jnp.concatenate([jnp.take_along_axis(group, 7 - turned, axis=0) for group in reversed(groups)], axis=0)


def flip_low(value):
    return flip_full(value.astype(F32)).astype(BF16)


def normalise(tokens_f):
    centered = tokens_f - jnp.mean(tokens_f, axis=-1, keepdims=True)
    inv_std = lax.rsqrt(jnp.mean(centered * centered, axis=-1, keepdims=True) + EPSILON)
    return centered * inv_std, inv_std


def eye(size):
    rows = lax.broadcasted_iota(jnp.int32, (size, size), 0)
    cols = lax.broadcasted_iota(jnp.int32, (size, size), 1)
    return (rows == cols).astype(BF16)


def as_column(row):
    return dot_nt(eye(row.shape[1]), jnp.broadcast_to(row.astype(F32).astype(BF16), (8, row.shape[1])))[:, :1]


def remote(src, dst, send_sem, recv_sem, target):
    return pltpu.make_async_remote_copy(
        src_ref=src, dst_ref=dst, send_sem=send_sem, recv_sem=recv_sem, device_id=target, device_id_type=MESH
    )


def greet(targets):
    barrier = pltpu.get_barrier_semaphore()
    for target in targets:
        pl.semaphore_signal(barrier, inc=1, device_id=target, device_id_type=MESH)
    pl.semaphore_wait(barrier, len(targets))


def greet_line(me, runs, others=()):
    barrier = pltpu.get_barrier_semaphore()
    for target in others:
        pl.semaphore_signal(barrier, inc=1, device_id=target, device_id_type=MESH)

    @pl.when(me > 0)
    def _():
        pl.semaphore_signal(barrier, inc=1, device_id={"seq": me - 1}, device_id_type=MESH)

    @pl.when(me < runs - 1)
    def _():
        pl.semaphore_signal(barrier, inc=1, device_id={"seq": me + 1}, device_id_type=MESH)

    neighbours = lax.div(me + runs - 1, runs) + lax.div(2 * runs - 2 - me, runs)
    pl.semaphore_wait(barrier, neighbours + len(others))


def swap_along_line(me, runs, ups, downs, start):
    up = [remote(src, dst, ss, rs, {"seq": me + 1}) for src, dst, ss, rs in ups]
    down = [remote(src, dst, ss, rs, {"seq": me - 1}) for src, dst, ss, rs in downs]

    @pl.when(me < runs - 1)
    def _():
        for copy in up:
            if start:
                copy.start()
            else:
                copy.wait_send()
        if not start:
            for copy in down:
                copy.wait_recv()

    @pl.when(me > 0)
    def _():
        for copy in down:
            if start:
                copy.start()
            else:
                copy.wait_send()
        if not start:
            for copy in up:
                copy.wait_recv()


def enter_kernel(
    runs, tok, cot, mask, counts, step, ada, ada_bias, win, wout,
    xe, dy, z_out, hid_out, mod_out, rim_out,
    mods, prev_tok, next_tok, prev_mask, next_mask, send_sem, recv_sem,
):
    slots, toks, dim = tok.shape
    inner = wout.shape[0]
    me = lax.axis_index("seq")
    i = pl.program_id(0)
    ups = [
        (tok.at[:, pl.ds(toks - HALO, HALO), :], prev_tok, send_sem.at[0], recv_sem.at[0]),
        (mask, prev_mask, send_sem.at[1], recv_sem.at[1]),
    ]
    downs = [
        (tok.at[:, pl.ds(0, HALO), :], next_tok, send_sem.at[2], recv_sem.at[2]),
        (mask, next_mask, send_sem.at[3], recv_sem.at[3]),
    ]

    @pl.when(i == 0)
    def _():
        greet_line(me, runs)
        swap_along_line(me, runs, ups, downs, True)

        @pl.when(me == 0)
        def _():
            prev_tok[...] = jnp.zeros(prev_tok.shape, BF16)
            prev_mask[...] = jnp.zeros(prev_mask.shape, jnp.int32)

        @pl.when(me == runs - 1)
        def _():
            next_tok[...] = jnp.zeros(next_tok.shape, BF16)
            next_mask[...] = jnp.zeros(next_mask.shape, jnp.int32)

    live = jnp.where(counts[0] > i, 1.0, 0.0)

    @pl.when(i == 0)
    def _():
        time_f = step[...].astype(F32)
        time_low = (time_f * jax.nn.sigmoid(time_f)).astype(BF16)
        mods[...] = dot(time_low, ada[...]) + ada_bias[...].reshape(1, 3 * dim)

    mod = mods[pl.ds(i, 1), :]
    mod_out[...] = mod
    shift, scale, gate = mod[:, :dim], mod[:, dim : 2 * dim], mod[:, 2 * dim :]

    def hidden_of(part, scale, shift):
        normed, _ = normalise(part.astype(F32))
        return (normed * (1.0 + scale) + shift).astype(BF16)

    hid = hidden_of(tok[i], scale, shift)
    hid_out[...] = hid
    xz = dot(hid, win[...]) * (as_column(mask[pl.ds(i, 1), :]) * live)
    x_low = xz[:, :inner].astype(BF16)
    z = xz[:, inner:]
    z_out[...] = z
    d_branch = (cot[...].astype(F32) * gate).astype(BF16)
    d_summed = dot_nt(d_branch, wout[...]) * z * jax.nn.sigmoid(z)
    dy[0] = d_summed
    dy[1] = flip_full(d_summed)
    xe[0] = x_low
    xe[1] = flip_low(x_low)

    @pl.when(i == slots - 1)
    def _():
        swap_along_line(me, runs, ups, downs, False)
        hidden, seen = [], []
        for item in range(slots):
            row = mods[item : item + 1, :]
            rims = jnp.concatenate([prev_tok[item], next_tok[item]], axis=0)
            hidden.append(hidden_of(rims, row[:, dim : 2 * dim], row[:, :dim]))
            prev_col = as_column(prev_mask[item : item + 1, :])[toks - HALO :]
            next_col = as_column(next_mask[item : item + 1, :])[:HALO]
            live = jnp.where(counts[0] > item, 1.0, 0.0)
            seen.append(jnp.concatenate([prev_col, next_col], axis=0) * live)
        rim_x = dot(jnp.concatenate(hidden, axis=0), win[:, :inner]) * jnp.concatenate(seen, axis=0)
        for item in range(slots):
            part = rim_x[2 * HALO * item : 2 * HALO * (item + 1)]
            rim_out[item, 0] = part[:HALO].astype(BF16)
            rim_out[item, 1] = flip_full(part[HALO:]).astype(BF16)


def columns(inner, width=128):
    return [slice(at, at + width) for at in range(0, inner, width)]


def twice(row8):
    return jnp.concatenate([row8, row8], axis=0)


def spread(ref, index):
    return twice(ref[pl.ds(index, 8, stride=0), :])


def lay_out(wide, rows, picks):
    count, toks = rows.shape
    high = rows.astype(BF16).astype(F32)
    halves = jnp.concatenate([high, rows - high], axis=0).T.astype(BF16)
    for n in range(0, count, 2):
        pair = dot(halves, picks[:, n * 128 : (n + 2) * 128])
        for t in range(0, toks, 8):
            for k in range(2):
                at = 8 * (count * (t // 8) + n + k)
                wide[at : at + 8, :] = pair[t : t + 8, k * 128 : (k + 1) * 128]


def wide_tile(wide, i, count):
    at = 8 * count * (i // 8) + i % 8
    return jnp.concatenate([wide[pl.ds(at + 64 * n, 8, stride=8), :] for n in range(count // 8)], axis=0)


def across_lanes(tile, inner):
    return jnp.concatenate([tile] * (inner // 128), axis=1)


def softplus_parts(pre):
    e = jnp.exp2(-LOG2E * jnp.abs(pre))
    more = jnp.where(e < 1e-3, e - 0.5 * e * e, jnp.log(1.0 + e))
    return jnp.maximum(pre, 0.0) + more, jax.nn.sigmoid(pre)


def bit_of(index, bit):
    return lax.rem(lax.div(index, 1 << bit), 2)


def across(axis, bit):
    me = lax.axis_index(axis)
    mine = bit_of(me, bit)
    return mine, {axis: me + (1 - 2 * mine) * (1 << bit)}


class Exchange:
    def __init__(self, runs, branch, ends, backs, totals, rate, results, group, span, pre, pre_span, sends, arrivals, sems):
        self.branch, self.rate = branch, rate
        self.sources, self.totals, self.results = (ends, backs), totals, results
        self.group, self.span, self.pre, self.pre_span = group, span, pre, pre_span
        self.sends, self.arrivals, self.sems = sends, arrivals, sems
        self.links = [across("seq", bit) for bit in range(int(math.log2(runs)))]
        self.slots = ends.shape[0]
        self.states, self.inner = rate.shape

    def flow(self, kind):
        return kind if self.branch == 0 else 1 - kind

    def targets(self):
        return [target for _, target in self.links]

    def copy(self, stage, kind):
        at = 2 * stage + kind
        return remote(
            self.sends.at[at], self.arrivals.at[at], self.sems.at[0, at], self.sems.at[1, at], self.links[stage][1]
        )

    def send(self, stage, kind):
        rows = self.slots * self.states
        at = 2 * stage + kind
        for i in range(self.slots):
            self.sends[at, i * self.states : (i + 1) * self.states, :] = self.group[kind, i].astype(BF16)
        high = self.span[kind].astype(BF16).astype(F32)
        self.sends[at, rows:, :] = jnp.concatenate([high, self.span[kind] - high], axis=0).astype(BF16)
        self.copy(stage, kind).start()

    def join(self, stage, kind, last):
        mine = self.links[stage][0]
        self.copy(stage, kind).wait()
        at = 2 * stage + kind
        earlier = (mine == 1) if self.flow(kind) == 0 else (mine == 0)
        both = self.arrivals[at, self.slots * self.states :, :].astype(F32)
        length = both[: both.shape[0] // 2] + both[both.shape[0] // 2 :]
        own_span, pre_span = self.span[kind], self.pre_span[kind]
        second_span = jnp.where(earlier, own_span, length)
        rate = self.rate[...] * -LOG2E
        for i in range(self.slots):
            state = self.arrivals[at, i * self.states : (i + 1) * self.states, :].astype(F32)
            before = self.pre[kind, i]
            self.pre[kind, i] = jnp.where(earlier, state * jnp.exp2(rate * pre_span[i : i + 1]) + before, before)
            if not last:
                own = self.group[kind, i]
                first, second = jnp.where(earlier, state, own), jnp.where(earlier, own, state)
                self.group[kind, i] = first * jnp.exp2(rate * second_span[i : i + 1]) + second
        self.pre_span[kind] = jnp.where(earlier, length + pre_span, pre_span)
        if not last:
            self.span[kind] = own_span + length

    def points(self):
        count = len(self.links)

        def begin():
            self.pre[...] = jnp.zeros(self.pre.shape, F32)
            self.pre_span[...] = jnp.zeros(self.pre_span.shape, F32)
            self.span[...] = jnp.zeros(self.span.shape, F32)
            for kind in range(2):
                for i in range(self.slots):
                    self.group[kind, i] = self.sources[kind][i]
                    self.span[kind, i : i + 1, :] = self.totals[i][:1]
                if count:
                    self.send(0, kind)

        def step(stage):
            last = stage == count - 1
            for kind in range(2):
                self.join(stage, kind, last)
                if not last:
                    self.send(stage + 1, kind)

        def end():
            for kind in range(2):
                for i in range(self.slots):
                    self.results[kind][i] = self.pre[kind, i]

        return [begin] + [functools.partial(step, stage) for stage in range(count)] + [end]


def exchange_shapes(runs, slots, states, inner):
    pairs = max(int(math.log2(runs)), 1)
    span_rows = -(-slots // 8) * 8
    return [
        pltpu.VMEM((2, slots, states, inner), F32), pltpu.VMEM((2, span_rows, inner), F32),
        pltpu.VMEM((2, slots, states, inner), F32), pltpu.VMEM((2, span_rows, inner), F32),
        pltpu.VMEM((2 * pairs, slots * states + 2 * span_rows, inner), BF16),
        pltpu.VMEM((2 * pairs, slots * states + 2 * span_rows, inner), BF16),
        pltpu.SemaphoreType.DMA((2, 2 * pairs)),
    ]


def beside(points, step, first, count):
    for at in range(min(len(points), count)):
        todo = points[at:] if at == count - 1 else points[at : at + 1]

        @pl.when(step == first + at)
        def _():
            for point in todo:
                point()


def first_kernel(
    runs, slots, ahead, xe, dy, taps, tap_bias, x_rows, dt_rows, dt_bias, rate,
    act_out, planes, proj_out, last_out, starts_out, tiles, weights, first_in,
    x_cols, dx, decay, through, rate2, wide, picks, ends, backs, totals, first_rate, *exchange_scratch,
):
    toks, inner = dy.shape
    states = rate.shape[0]
    blocks = toks // BLK
    rank = WIDE_RANK
    xwt, dtw = weights.at[: weights.shape[0] - rank], weights.at[weights.shape[0] - rank :]
    delta_out, sig_out, dsilu_out = (planes.at[at] for at in range(3))
    end_out, back_out = last_out.at[:states], last_out.at[states : 2 * states]
    tap_count = taps.shape[0]
    branch, item = pl.program_id(0), pl.program_id(1)
    results = (first_in.at[0], first_in.at[1])
    exchange = Exchange(runs, 0, ends, backs, totals, first_rate, results, *exchange_scratch)

    @pl.when((branch == 0) & (item == 0))
    def _():
        greet(exchange.targets())
        first_rate[...] = rate[...]

    beside(exchange.points(), branch * slots + item, slots, slots)

    @pl.when(item == 0)
    def _():
        rate2[...] = rate[...] * -LOG2E
        picks[...] = (
            lax.broadcasted_iota(jnp.int32, picks.shape, 0) % (2 * states)
            == lax.broadcasted_iota(jnp.int32, picks.shape, 1) // 128
        ).astype(BF16)
        held = dt_rows.shape[0]
        rows = x_rows[...].astype(F32)
        gap = jnp.zeros((rank - held, inner), F32)
        wide = [rows[:held], gap, rows[held:], dt_rows[...].astype(F32), gap]
        weights[...] = jnp.concatenate(wide, axis=0).astype(BF16)

    tap_row, dt_row = tap_bias[pl.ds(branch, 1), :], dt_bias[pl.ds(branch, 1), :]
    for cols in columns(inner):
        at_col = cols.start // 128
        x_cols[at_col] = jnp.concatenate([ahead[:, cols], xe[:, cols]], axis=0).astype(F32)
        parts = []
        for row in range(0, toks, 8):
            part = tap_row[:, cols]
            for k in range(tap_count):
                part = part + taps[k : k + 1, cols] * x_cols[at_col, pl.ds(HALO - tap_count + 1 + k + row, 8), :]
            parts.append(part)
        conv = jnp.concatenate(parts, axis=0)
        open_part = jax.nn.sigmoid(conv)
        act_f = conv * open_part
        act_out[:, cols] = act_f.astype(BF16)
        dsilu_out[:, cols] = open_part + act_f * (1.0 - open_part)
    proj = dot_nt(xwt[...], act_out[...])
    proj_out[...] = proj
    dt_low = proj[:rank, :].astype(BF16)
    for cols in columns(inner, 256):
        pre = dot_tn(dt_low, dtw[:, cols]) + dt_row[:, cols]
        delta, slope = softplus_parts(pre)
        delta_out[:, cols] = delta
        sig_out[:, cols] = slope
        dx[:, cols] = delta * act_out[:, cols].astype(F32)
    lay_out(wide, proj[rank:, :], picks)
    end_out[...] = jnp.zeros((states, inner), F32)
    back_out[...] = jnp.zeros((states, inner), F32)
    through[...] = jnp.zeros((8, inner), F32)

    def one_block(j, slot):
        t0 = pl.multiple_of(j * BLK, BLK)
        dr, xr, yr = (ref.at[pl.ds(t0, BLK), :] for ref in (delta_out, dx, dy))
        count = 2 * states
        wide_rows = wide.at[pl.ds(pl.multiple_of(j * (BLK * count), BLK * count), BLK * count), :]
        s = end_out[...]
        before = through[...]
        starts_out[j] = jnp.concatenate([s, before], axis=0)
        rates = rate2[...]
        for i in range(BLK):
            a = jnp.exp2(spread(dr, i) * rates)
            decay[slot, i] = a
            tile = wide_tile(wide_rows, i, count)
            tiles[t0 + i] = tile
            s = a * s + spread(xr, i) * across_lanes(tile[:states], inner)
        end_out[...] = s
        m = jnp.zeros((states, inner), F32)
        for i in reversed(range(BLK)):
            m = decay[slot, i] * (m + spread(yr, i) * across_lanes(tiles[t0 + i, states:], inner))
        back_out[...] = back_out[...] + m * jnp.exp2(twice(before) * rates)
        through[...] = before + jnp.sum(dr[...], axis=0, keepdims=True)

    def block_step(k, _):
        one_block(2 * k, 0)
        one_block(2 * k + 1, 1)
        return 0

    lax.fori_loop(0, blocks // 2, block_step, 0)
    last_out[2 * states :, :] = through[...]

    @pl.when(branch == 0)
    def _():
        ends[item] = end_out[...]
        backs[item] = back_out[...]
        totals[item] = through[:1, :]


def second_kernel(
    runs, first_in, lasts, last_rate, starts, tiles, rate, ahead, xe, act, planes, dy, proj, weights, taps, skip,
    y_out, dx_out, rims, grads,
    rate2, carry, dxs, bdiag, cdiag, decay, states_low, lam_low, rq_low, qd_low, dots, racc, gsum, hsum, db, dc,
    d_cols, d_pre_low, s_in, s_last, lam_last, *exchange_scratch,
):
    toks, inner = dy.shape
    states = rate.shape[0]
    blocks = toks // BLK
    rank = WIDE_RANK
    xwt, dtw = weights.at[: weights.shape[0] - rank], weights.at[weights.shape[0] - rank :]
    delta, sig, dsilu = (planes.at[at] for at in range(3))
    tap_count = taps.shape[0]
    held = (grads.shape[0] - 3 * states - 8) // 2
    xp_grad, dtp_grad = grads.at[: held + 2 * states], grads.at[held + 2 * states : 2 * held + 2 * states]
    at = 2 * held + 2 * states
    rate_grad, row_grads = grads.at[at : at + states], grads.at[at + states : at + states + 8]
    tapb_at, skip_at, dtb_at = (slice(tap_count + row, tap_count + row + 1) for row in range(3))
    item = pl.program_id(1)
    branch = pl.program_id(0)
    slots = lasts.shape[0]
    ends, backs = lasts.at[:, :states], lasts.at[:, states : 2 * states]
    totals = lasts.at[:, 2 * states :]
    exchange = Exchange(runs, 1, ends, backs, totals, last_rate, (s_last, lam_last), *exchange_scratch)

    @pl.when((item == 0) & (branch == 0))
    def _():
        greet(exchange.targets())

    beside(exchange.points(), branch * slots + item, 0, slots)

    @pl.when(branch == 0)
    def _():
        s_in[...] = first_in[0, item]
        carry[...] = first_in[1, item]

    @pl.when(branch == 1)
    def _():
        s_in[...] = s_last[item]
        carry[...] = lam_last[item]

    gain = skip[pl.ds(pl.program_id(0), 1), :]
    rate2[...] = rate[...] * -LOG2E
    width = BLK * states

    @pl.when(item == 0)
    def _():
        grads[...] = jnp.zeros(grads.shape, F32)

    for cols in columns(inner):
        dxs[:toks, cols] = delta[:, cols] * act[:, cols].astype(F32)
    fold = (
        lax.broadcasted_iota(jnp.int32, (states, width), 1) % states == lax.broadcasted_iota(jnp.int32, (states, width), 0)
    ).astype(BF16)
    own = lax.broadcasted_iota(jnp.int32, (toks, width), 0) % BLK == lax.broadcasted_iota(jnp.int32, (toks, width), 1) // states
    bdiag[:toks, :] = jnp.where(own, dot_tn(proj[rank : rank + states, :].astype(BF16), fold), 0.0).astype(BF16)
    cdiag[...] = jnp.where(own, dot_tn(proj[rank + states :, :].astype(BF16), fold), 0.0).astype(BF16)
    mine = own[:BLK]
    picks = mine.astype(BF16)
    sides = (
        lax.broadcasted_iota(jnp.int32, (2 * BLK, 256), 0) // BLK == lax.broadcasted_iota(jnp.int32, (2 * BLK, 256), 1) // 128
    ).astype(BF16)
    racc[...] = jnp.zeros((states, inner), F32)

    def lane_sum(wide):
        part = [wide[:, at : at + 128] for at in range(0, inner, 128)]
        while len(part) > 1:
            part = [sum(part[at : at + 2]) for at in range(0, len(part), 2)]
        return part[0]

    def products(slot, j):
        t0 = pl.multiple_of(j * BLK, BLK)
        y_out[pl.ds(t0, BLK), :] = dot(cdiag[pl.ds(t0, BLK), :], states_low[slot, states:, :])
        gsum[pl.ds(t0, BLK), :] = dot(bdiag[pl.ds(t0, BLK), :], lam_low[slot])
        hsum[pl.ds(t0, BLK), :] = dot(picks, rq_low[slot])
        racc[...] += dot(fold[:, : BLK // 4 * states], qd_low[slot])
        both = dot_nt(sides, dots[slot])
        dc[pl.ds(t0, BLK), :] = jnp.where(mine, both[:BLK], 0.0).astype(BF16)
        db[pl.ds(t0, BLK), :] = jnp.where(mine, both[BLK:], 0.0).astype(BF16)

    def one_block(slot, j):
        t0 = pl.multiple_of(j * BLK, BLK)
        dr, xr, yr = (ref.at[pl.ds(t0, BLK), :] for ref in (delta, dxs, dy))
        tile = tiles.at[pl.ds(t0, BLK)]
        r2 = rate2[...]
        r_low = rate[...].astype(BF16)
        begin = starts[j]
        s = begin[:states] + s_in[...] * jnp.exp2(twice(begin[states:]) * r2)
        states_low[slot, :states, :] = s.astype(BF16)
        for i in range(BLK):
            a = jnp.exp2(spread(dr, i) * r2)
            decay[slot, i] = a
            s = a * s + spread(xr, i) * across_lanes(tile[i, :states], inner)
            s_low = s.astype(BF16)
            states_low[slot, (i + 1) * states : (i + 2) * states, :] = s_low
            dots[slot, i * states : (i + 1) * states, :128] = lane_sum(s_low * spread(yr, i).astype(BF16))
        cr = carry[...]
        qds = []
        for i in reversed(range(BLK)):
            lam = cr + spread(yr, i) * across_lanes(tile[i, states:], inner)
            l_low = lam.astype(BF16)
            lam_low[slot, i * states : (i + 1) * states, :] = l_low
            dots[slot, i * states : (i + 1) * states, 128:] = lane_sum(l_low * spread(xr, i).astype(BF16))
            cr = decay[slot, i] * lam
            q = cr.astype(BF16) * states_low[slot, i * states : (i + 1) * states, :]
            rq_low[slot, i * states : (i + 1) * states, :] = q * r_low
            qds.append(q * spread(dr, i).astype(BF16))
            if i % 4 == 0:
                qd_low[slot, i // 4 * states : (i // 4 + 1) * states, :] = (qds[0] + qds[1]) + (qds[2] + qds[3])
                qds = []
        carry[...] = cr

    def block_step(k, _):
        j = blocks - 1 - 2 * k
        for slot in range(2):
            one_block(slot, j - slot)
            products(slot, j - slot)
        return 0

    lax.fori_loop(0, blocks // 2, block_step, 0)
    rate_grad[...] += -racc[...]
    for cols in columns(inner):
        act_f = act[:, cols].astype(F32)
        row_grads[skip_at, cols] += jnp.sum(dy[:, cols] * act_f, axis=0, keepdims=True)
        y_out[:, cols] += gain[:, cols] * act_f
        d_pre = (act_f * gsum[:toks, cols] - hsum[:toks, cols]) * sig[:, cols]
        row_grads[dtb_at, cols] += jnp.sum(d_pre, axis=0, keepdims=True)
        d_pre_low[:, cols] = d_pre.astype(BF16)
    dtp_grad[...] += dot(proj[:rank, :].astype(BF16), d_pre_low[...])[:held]
    d_proj = jnp.concatenate(
        [dot_nt(dtw[...], d_pre_low[...]), dot_nt(fold, db[:toks, :]), dot_nt(fold, dc[:toks, :])], axis=0
    ).astype(BF16)
    xp_new = dot(d_proj, act[...])
    xp_grad[:held, :] += xp_new[:held]
    xp_grad[held:, :] += xp_new[rank:]
    d_cols[:, :HALO, :] = jnp.zeros((inner // 128, HALO, 128), F32)
    d_cols[:, HALO + toks :, :] = jnp.zeros((inner // 128, HALO, 128), F32)
    for wide_cols in columns(inner, 256):
        through = dot_tn(d_proj, xwt[:, wide_cols])
        for at in columns(256):
            cols = slice(wide_cols.start + at.start, wide_cols.start + at.stop)
            d_act = delta[:, cols] * gsum[:toks, cols] + gain[:, cols] * dy[:, cols] + through[:, at]
            d_conv = d_act * dsilu[:, cols]
            row_grads[tapb_at, cols] += jnp.sum(d_conv, axis=0, keepdims=True)
            x_f = jnp.concatenate([ahead[:, cols], xe[:, cols]], axis=0).astype(F32)
            at_col = cols.start // 128
            d_cols[at_col, HALO : HALO + toks, :] = d_conv
            sums = [jnp.zeros((8, 128), F32) for _ in range(tap_count)]
            for row in range(HALO - 8, HALO + toks, 8):
                part = jnp.zeros((8, 128), F32)
                for k in range(tap_count):
                    moved = d_cols[at_col, pl.ds(row + tap_count - 1 - k, 8), :]
                    part = part + taps[k : k + 1, cols] * moved
                    sums[k] = sums[k] + moved * x_f[row : row + 8]
                if row < HALO:
                    rims[branch, item, :, cols] = part
                else:
                    dx_out[row - HALO : row - HALO + 8, cols] = part
            for k in range(tap_count):
                row_grads[k : k + 1, cols] += jnp.sum(sums[k], axis=0, keepdims=True)


LAST_ROWS = 16
PART_ROWS = 512


class Ring:
    def __init__(self, bits):
        self.bits = bits
        self.size = 1 << len(bits)
        self.digits = [bit_of(lax.axis_index(axis), bit) for axis, bit in bits]
        self.place = sum(digit * (1 << at) for at, digit in enumerate(self.digits))

    def target(self, ahead):
        place = lax.rem(self.place + ahead, self.size)
        where = {}
        for at, (axis, bit) in enumerate(self.bits):
            base = where.get(axis, lax.axis_index(axis))
            where[axis] = base + (bit_of(place, at) - self.digits[at]) * (1 << bit)
        return where, place

    def targets(self):
        return [self.target(ahead)[0] for ahead in range(1, self.size)]


def stage_rings(runs, groups):
    bits = [("seq", bit) for bit in range(int(math.log2(runs)))] + [("dp", bit) for bit in range(int(math.log2(groups)))]
    return [Ring(bits[:1])] + [Ring(bits[at : at + 2]) for at in range(1, len(bits), 2)]


def part_count(rows):
    return -(-rows // PART_ROWS)


def buffer_rows(runs, groups):
    bits = int(math.log2(runs)) + int(math.log2(groups))
    size, total = PART_ROWS, 0
    for members in [2] + [1 << min(2, bits - at) for at in range(1, bits, 2)]:
        moved = size // members if size >= members * LAST_ROWS else size
        total += moved * (members - 1)
        size = moved
    return total


def reduce_shapes(parts, dim, runs, groups):
    bits = int(math.log2(runs)) + int(math.log2(groups))
    stages = 1 + bits // 2
    room = parts * buffer_rows(runs, groups)
    sems = pltpu.SemaphoreType.DMA((parts, 2 * stages, 3))
    return [
        pltpu.VMEM((parts * PART_ROWS, dim), F32), pltpu.VMEM((room, dim), BF16), pltpu.VMEM((room, dim), BF16),
        pltpu.VMEM((parts * PART_ROWS, dim), BF16), sems, sems,
    ]


class Reduction:
    def __init__(self, rings, turns, segments, acc, sends, arrivals, gathered, send_sem, recv_sem):
        self.rings = rings
        self.count = len(rings)
        self.parts = len(turns)
        self.segments = segments
        self.acc, self.sends, self.arrivals, self.gathered = acc, sends, arrivals, gathered
        self.send_sem, self.recv_sem = send_sem, recv_sem
        room = sends.shape[0] // self.parts
        self.steps = []
        for part, turn in enumerate(turns):
            later = rings[1:]
            turn = turn % max(len(later), 1)
            order = rings[:1] + later[turn:] + later[:turn]
            start, size, at = part * PART_ROWS, PART_ROWS, part * room
            steps = []
            for ring in order:
                split = size >= ring.size * LAST_ROWS
                moved = size // ring.size if split else size
                keep = pl.multiple_of(start + ring.place * moved, LAST_ROWS) if split else start
                steps.append((ring, start, split, moved, keep, at))
                at += moved * (ring.size - 1)
                start, size = keep, moved
            self.steps.append(steps)

    def assemble(self, part):
        low, high = part * PART_ROWS, (part + 1) * PART_ROWS
        at = 0
        for get, size in self.segments:
            first, last = max(at, low), min(at + size, high)
            if first < last:
                self.acc[first:last, :] = get(first - at, last - first)
            at += size
        if at < high:
            first = max(at, low)
            self.acc[first:high, :] = jnp.zeros((high - first, self.acc.shape[1]), F32)

    def scatter_copy(self, part, stage, ahead):
        ring, _, _, moved, _, at = self.steps[part][stage]
        at += (ahead - 1) * moved
        return remote(
            self.sends.at[pl.ds(at, moved), :], self.arrivals.at[pl.ds(at, moved), :],
            self.send_sem.at[part, stage, ahead - 1], self.recv_sem.at[part, stage, ahead - 1], ring.target(ahead)[0],
        )

    def scatter(self, part, stage):
        ring, start, split, moved, _, at = self.steps[part][stage]
        for ahead in range(1, ring.size):
            place = ring.target(ahead)[1]
            away = pl.multiple_of(start + place * moved, LAST_ROWS) if split else start
            here = at + (ahead - 1) * moved
            self.sends[here : here + moved, :] = self.acc[pl.ds(away, moved), :].astype(BF16)
            self.scatter_copy(part, stage, ahead).start()

    def settle(self, part, stage):
        ring, _, split, moved, keep, at = self.steps[part][stage]
        for ahead in range(1, ring.size):
            self.scatter_copy(part, stage, ahead).wait()
        held = self.acc[pl.ds(keep, moved), :]
        came = [
            self.arrivals[at + (ahead - 1) * moved : at + ahead * moved, :].astype(F32) for ahead in range(1, ring.size)
        ]
        if split:
            held = held + sum(came)
        else:
            values = [held.astype(BF16).astype(F32)] + came
            total = jnp.zeros_like(held)
            for place in range(ring.size):
                behind = lax.rem(ring.place - place + ring.size, ring.size)
                chosen = values[0]
                for ahead in range(1, ring.size):
                    chosen = jnp.where(behind == ahead, values[ahead], chosen)
                total = total + chosen
            held = total
        self.acc[pl.ds(keep, moved), :] = held

    def gather_copies(self, part, stage):
        ring, _, split, moved, keep, _ = self.steps[part][stage]
        here = self.gathered.at[pl.ds(keep, moved), :]
        return [
            remote(
                here, here, self.send_sem.at[part, self.count + stage, ahead - 1],
                self.recv_sem.at[part, self.count + stage, ahead - 1], ring.target(ahead)[0],
            )
            for ahead in range(1, ring.size)
            if split
        ]

    def points(self):
        def begin():
            for part in range(self.parts):
                self.assemble(part)
                self.scatter(part, 0)

        def split(stage):
            for part in range(self.parts):
                self.settle(part, stage - 1)
                self.scatter(part, stage)

        def turn():
            for part in range(self.parts):
                self.settle(part, self.count - 1)
                _, _, _, moved, keep, _ = self.steps[part][-1]
                self.gathered[pl.ds(keep, moved), :] = self.acc[pl.ds(keep, moved), :].astype(BF16)
                for copy in self.gather_copies(part, self.count - 1):
                    copy.start()

        def join(stage):
            for part in range(self.parts):
                for copy in self.gather_copies(part, stage + 1):
                    copy.wait()
                if stage >= 0:
                    for copy in self.gather_copies(part, stage):
                        copy.start()

        points = [begin]
        points += [functools.partial(split, stage) for stage in range(1, self.count)]
        points += [turn]
        return points + [functools.partial(join, stage) for stage in reversed(range(-1, self.count - 1))]


def big_segments(ref, dim):
    return [
        (lambda at, size, lane=lane: ref[at : at + size, lane : lane + dim], ref.shape[0])
        for lane in range(0, ref.shape[1], dim)
    ]


def small_segments(ref, dim):
    return [
        (lambda at, size, branch=branch, lane=lane: ref[branch, at : at + size, lane : lane + dim], ref.shape[1])
        for lane in range(0, ref.shape[2], dim)
        for branch in range(2)
    ]


def tail_kernel(
    plan, tok, cot, mod, mask, counts, hid, z_in, y, dx, rims, win, wout, step,
    grads,
    mixed, d_tokens, result, x_result, factors, own_rows,
    late, rim_send, rim_recv, dz, d_xs, hids, out_grad, z_grad, x_grad, mod_sum, mod_in, table, small_send, small_recv, *reduce_scratch,
):
    runs, groups, slots = plan
    me = lax.axis_index("seq")
    downs = [(rims.at[0], late.at[0], rim_send.at[0], rim_recv.at[0])]
    ups = [(rims.at[1], late.at[1], rim_send.at[1], rim_recv.at[1])]
    dim = tok.shape[-1]
    toks, inner = z_in.shape
    now = pl.program_id(0)
    i = lax.rem(now, slots)
    rings = stage_rings(runs, groups)
    seq_ring = Ring([("seq", bit) for bit in range(int(math.log2(runs)))])
    dp_ring = Ring([("dp", bit) for bit in range(int(math.log2(groups)))])
    half = len(reduce_scratch) // 2
    smalls = small_segments(grads, dim)
    segments = big_segments(out_grad, dim) + big_segments(z_grad, dim) + smalls
    main = Reduction(rings, [part % 3 // 2 for part in range(result.shape[0] // PART_ROWS)], segments, *reduce_scratch[:half])
    rest = Reduction(rings, [part % 2 for part in range(x_result.shape[0] // PART_ROWS)], big_segments(x_grad, dim), *reduce_scratch[half:])
    main_points, rest_points = main.points(), rest.points()

    @pl.when(now == 0)
    def _():
        greet_line(me, runs, [target for ring in rings + [seq_ring, dp_ring] for target in ring.targets()])
        swap_along_line(me, runs, ups, downs, True)

        @pl.when(me == 0)
        def _():
            late[1] = jnp.zeros(late.shape[1:], F32)

        @pl.when(me == runs - 1)
        def _():
            late[0] = jnp.zeros(late.shape[1:], F32)

        out_grad[...] = jnp.zeros(out_grad.shape, F32)
        z_grad[...] = jnp.zeros(z_grad.shape, F32)
        x_grad[...] = jnp.zeros(x_grad.shape, F32)
        mod_sum[...] = jnp.zeros(mod_sum.shape, F32)

    scale, gate = mod[:, dim : 2 * dim], mod[:, 2 * dim :]
    valid = as_column(mask[pl.ds(i, 1), :]) * jnp.where(counts[0] > i, 1.0, 0.0)
    mod_rows = pl.ds(pl.multiple_of(8 * i, 8), 8)

    @pl.when(now < slots)
    def _():
        cot_f = cot[...].astype(F32)
        z = z_in[...]
        z_sig = jax.nn.sigmoid(z)
        z_silu = z * z_sig
        summed = y[0] + flip_full(y[1])
        gated = (summed * z_silu).astype(BF16)
        branch_out = dot(gated, wout[...])
        mixed[...] = (tok[...].astype(F32) + gate * branch_out).astype(BF16)
        d_branch = (cot_f * gate).astype(BF16)
        out_grad[...] += dot_tn(gated, d_branch)
        d_zgate = dot_nt(d_branch, wout[...]) * summed * (z_sig + z_silu * (1.0 - z_sig))
        d_low = (d_zgate * valid).astype(BF16)
        dz[i] = d_low
        z_grad[...] += dot_tn(hid[...], d_low)
        hids[i] = hid[...]
        d_gate = jnp.sum(cot_f * branch_out, axis=0, keepdims=True)
        mod_sum[mod_rows, :] = jnp.concatenate([jnp.zeros((2, dim), F32), d_gate, jnp.zeros((5, dim), F32)], axis=0)

    @pl.when(now == slots)
    def _():
        main_points[0]()
        swap_along_line(me, runs, ups, downs, False)
        edge = late.shape[2]

        def with_late(part, extra):
            return jnp.concatenate([part[: toks - edge], part[toks - edge :] + extra], axis=0)

        for item in range(slots):
            seen = as_column(mask[item : item + 1, :]) * jnp.where(counts[0] > item, 1.0, 0.0)
            d_x = with_late(dx[item, 0], late[0, item]) + flip_full(with_late(dx[item, 1], late[1, item]))
            d_low = (d_x * seen).astype(BF16)
            d_xs[item] = d_low
            x_grad[...] += dot_tn(hids[item], d_low)
        rest_points[0]()
        main_points[1]()

    @pl.when(now >= slots)
    def _():
        d_hidden = dot_nt(d_xs[i], win[:, :inner]) + dot_nt(dz[i], win[:, inner:])
        normed, inv_std = normalise(tok[...].astype(F32))
        d_shift = jnp.sum(d_hidden, axis=0, keepdims=True)
        d_scale = jnp.sum(d_hidden * normed, axis=0, keepdims=True)
        mod_sum[mod_rows, :] += jnp.concatenate([d_shift, d_scale, jnp.zeros((6, dim), F32)], axis=0)
        d_normed = d_hidden * (1.0 + scale)
        d_tokens[...] = cot[...].astype(F32) + inv_std * (
            d_normed
            - jnp.mean(d_normed, axis=-1, keepdims=True)
            - normed * jnp.mean(d_normed * normed, axis=-1, keepdims=True)
        )

    @pl.when(now == slots)
    def _():
        rest_points[1]()

    def sum_copies():
        return [
            remote(mod_sum, mod_in.at[ahead - 1], small_send.at[ahead - 1], small_recv.at[ahead - 1], seq_ring.target(ahead)[0])
            for ahead in range(1, seq_ring.size)
        ]

    def table_copies():
        at = pl.multiple_of(dp_ring.place * 16, 16)
        here = table.at[pl.ds(at, 16), :]
        base = seq_ring.size - 1
        return [
            remote(here, here, small_send.at[base + ahead - 1], small_recv.at[base + ahead - 1], dp_ring.target(ahead)[0])
            for ahead in range(1, dp_ring.size)
        ]

    def start_small():
        for copy in sum_copies():
            copy.start()

    def turn_small():
        for copy in sum_copies():
            copy.wait()
        values = [mod_sum[...]] + [mod_in[ahead - 1] for ahead in range(1, seq_ring.size)]
        total = jnp.zeros(mod_sum.shape, F32)
        for place in range(seq_ring.size):
            behind = lax.rem(seq_ring.place - place + seq_ring.size, seq_ring.size)
            chosen = values[0]
            for ahead in range(1, seq_ring.size):
                chosen = jnp.where(behind == ahead, values[ahead], chosen)
            total = total + chosen
        time_f = step[...].astype(F32)
        time_low = time_f * jax.nn.sigmoid(time_f)
        lines = [total[8 * item : 8 * item + 3] for item in range(slots)] + [time_low]
        lines.append(jnp.zeros((16 - 4 * slots, dim), F32))
        own = jnp.concatenate(lines, axis=0).astype(BF16)
        own_rows[...] = own
        table[pl.ds(pl.multiple_of(dp_ring.place * 16, 16), 16), :] = own
        for copy in table_copies():
            copy.start()

    def end_small():
        for copy in table_copies():
            copy.wait()
        factors[...] = table[...]

    @pl.when(now == 2 * slots - 1)
    def _():
        start_small()
        for at in range(2, len(main_points)):
            main_points[at]()
            if at == 2:
                turn_small()
            rest_points[at]()
        end_small()
        result[...] = main.gathered[...]
        x_result[...] = rest.gathered[...]


def finish_kernel(
    mixed_in, tokens_in, outs, zs, xs, smalls, factors, own, step, ada,
    mixed, d_tokens, grad_time, grad_ada, grad_ada_bias, in_grad, tap_grad, tapb_grad, xp_grad, dtp_grad, dtb_grad, rate_grad, skip_grad, out_grad,
):
    dim, inner = in_grad.shape[0], rate_grad.shape[2]
    slots = step.shape[0]
    now = pl.program_id(0)
    mixed[...] = mixed_in[...]
    d_tokens[...] = tokens_in[...]
    out_grad[...] = outs[...].astype(F32)
    in_grad[...] = jnp.where(now < inner // dim, xs[...], zs[...]).astype(F32)
    table = factors[...]
    length = table.shape[0]

    for part in range(3):

        @pl.when(now == part)
        def _():
            row = lax.broadcasted_iota(jnp.int32, (length, length), 0)
            col = lax.broadcasted_iota(jnp.int32, (length, length), 1)
            item = row % 16 - 3 * slots
            wanted = row // 16 * 16 + 3 * item + part
            mods = dot(((col == wanted) & (item >= 0) & (item < slots)).astype(BF16), table)
            lanes = slice(part * dim, (part + 1) * dim)
            grad_ada[...] = dot_tn(table, mods.astype(BF16))
            grad_ada_bias[lanes] = jnp.sum(mods, axis=0)
            mine = own[...].astype(F32)
            picked = jnp.concatenate([mine[3 * i + part : 3 * i + part + 1] for i in range(slots)], axis=0)
            d_time = dot_nt(picked.astype(BF16), ada[...])
            grad_time[...] = d_time if part == 0 else grad_time[...] + d_time

    @pl.when(now == 3)
    def _():
        time_f = step[...].astype(F32)
        time_sig = jax.nn.sigmoid(time_f)
        grad_time[...] = grad_time[...] * time_sig * (1.0 + time_f * (1.0 - time_sig))
        at = 0
        for first in range(0, inner, dim):
            lanes = slice(first, first + dim)
            for branch in range(2):
                for ref in (xp_grad, dtp_grad, rate_grad, tap_grad):
                    size = ref.shape[1]
                    ref[branch, :, lanes] = smalls[at : at + size, :].astype(F32)
                    at += size
                for ref in (tapb_grad, skip_grad, dtb_grad):
                    ref[branch : branch + 1, lanes] = smalls[at : at + 1, :].astype(F32)
                    at += 1
                at += 1


def params(**more):
    return pltpu.CompilerParams(vmem_limit_bytes=VMEM_LIMIT, **more)


def spec(block, index):
    return pl.BlockSpec(block, index)


def per_device(
    tokens, timestep, counts, token_mask, ada_weight, ada_bias, input_weight, conv_weight, conv_bias, x_weight, dt_weight,
    dt_bias, decay_rate, skip_gain, output_weight, cotangent,
):
    slots, toks, dim = tokens.shape
    inner = output_weight.shape[0]
    rank = dt_weight.shape[1]
    states = decay_rate.shape[1]
    tap_count = conv_weight.shape[1]
    wide_rank = WIDE_RANK
    proj_rows = wide_rank + 2 * states
    blocks = toks // BLK
    runs = lax.axis_size("seq")
    groups = lax.axis_size("dp")
    x_rows = jnp.swapaxes(x_weight, 1, 2)

    def item(*block):
        return spec((None,) + block, lambda i: (i,) + (0,) * len(block))

    def whole(*block):
        return spec(block, lambda *_: (0,) * len(block))

    xe, dy, z_gate, hid, modulate, ahead = pl.pallas_call(
        functools.partial(enter_kernel, runs),
        grid=(slots,),
        in_specs=[
            whole(slots, toks, dim), item(toks, dim), whole(slots, toks), pl.BlockSpec(memory_space=pltpu.SMEM), whole(slots, dim), whole(dim, 3 * dim),
            whole(3 * dim), whole(dim, 2 * inner), whole(inner, dim),
        ],
        out_specs=[
            item(2, toks, inner), item(2, toks, inner), item(toks, inner), item(toks, dim), item(1, 3 * dim),
            whole(slots, 2, HALO, inner),
        ],
        out_shape=[
            jax.ShapeDtypeStruct((slots, 2, toks, inner), BF16),
            jax.ShapeDtypeStruct((slots, 2, toks, inner), F32),
            jax.ShapeDtypeStruct((slots, toks, inner), F32),
            jax.ShapeDtypeStruct((slots, toks, dim), BF16),
            jax.ShapeDtypeStruct((slots, 1, 3 * dim), F32),
            jax.ShapeDtypeStruct((slots, 2, HALO, inner), BF16),
        ],
        scratch_shapes=[
            pltpu.VMEM((slots, 3 * dim), F32),
            pltpu.VMEM((slots, HALO, dim), BF16), pltpu.VMEM((slots, HALO, dim), BF16), pltpu.VMEM((slots, toks), jnp.int32),
            pltpu.VMEM((slots, toks), jnp.int32), pltpu.SemaphoreType.DMA((4,)), pltpu.SemaphoreType.DMA((4,)),
        ],
        compiler_params=params(collective_id=1, has_side_effects=True),
        name="enter",
    )(
        tokens, cotangent, token_mask, counts, timestep, ada_weight, ada_bias, input_weight, output_weight,
    )

    def unit(*block):
        return spec((None, None) + block, lambda b, i: (i, b) + (0,) * len(block))

    def branch(*block):
        return spec((None,) + block, lambda b, i: (b,) + (0,) * len(block))

    def unit_shape(*block, kind=F32):
        return jax.ShapeDtypeStruct((slots, 2) + block, kind)

    act, planes, proj, lasts, starts, tiles, weights, first_in = pl.pallas_call(
        functools.partial(first_kernel, runs, slots),
        grid=(2, slots),
        in_specs=[
            unit(HALO, inner), unit(toks, inner), unit(toks, inner), branch(tap_count, inner), whole(2, inner),
            branch(rank + 2 * states, inner), branch(rank, inner), whole(2, inner), branch(states, inner),
        ],
        out_specs=[
            unit(toks, inner), unit(3, toks, inner), unit(proj_rows, toks), unit(2 * states + 8, inner),
            unit(blocks, states + 8, inner), unit(toks, 2 * states, 128), branch(proj_rows + wide_rank, inner),
            whole(2, slots, states, inner),
        ],
        out_shape=[
            unit_shape(toks, inner, kind=BF16), unit_shape(3, toks, inner), unit_shape(proj_rows, toks),
            unit_shape(2 * states + 8, inner), unit_shape(blocks, states + 8, inner), unit_shape(toks, 2 * states, 128),
            jax.ShapeDtypeStruct((2, proj_rows + wide_rank, inner), BF16),
            jax.ShapeDtypeStruct((2, slots, states, inner), F32),
        ],
        scratch_shapes=[
            pltpu.VMEM((inner // 128, HALO + toks, 128), F32), pltpu.VMEM((toks, inner), F32),
            pltpu.VMEM((2, BLK, states, inner), F32), pltpu.VMEM((8, inner), F32),
            pltpu.VMEM((states, inner), F32), pltpu.VMEM((2 * states * toks, 128), F32),
            pltpu.VMEM((4 * states, 2 * states * 128), BF16), pltpu.VMEM((slots, states, inner), F32),
            pltpu.VMEM((slots, states, inner), F32), pltpu.VMEM((slots, 1, inner), F32), pltpu.VMEM((states, inner), F32),
            *exchange_shapes(runs, slots, states, inner),
        ],
        compiler_params=params(collective_id=2, has_side_effects=True),
        name="first",
    )(ahead, xe, dy, conv_weight, conv_bias, x_rows, dt_weight, dt_bias, decay_rate)

    vmem = pl.BlockSpec(memory_space=pltpu.VMEM)
    last = spec((slots, None, 2 * states + 8, inner), lambda b, i: (0, 1, 0, 0))
    last_branch = spec((None, states, inner), lambda b, i: (1, 0, 0))

    grad_rows = 2 * rank + 3 * states + 8
    y, dx, rims, grads = pl.pallas_call(
        functools.partial(second_kernel, runs),
        grid=(2, slots),
        in_specs=[
            whole(2, slots, states, inner), last, last_branch, unit(blocks, states + 8, inner), unit(toks, 2 * states, 128),
            branch(states, inner), unit(HALO, inner), unit(toks, inner), unit(toks, inner), unit(3, toks, inner), unit(toks, inner),
            unit(proj_rows, toks), branch(proj_rows + wide_rank, inner), branch(tap_count, inner), whole(2, inner),
        ],
        out_specs=[unit(toks, inner), unit(toks, inner), whole(2, slots, 8, inner), branch(grad_rows, inner)],
        out_shape=[
            unit_shape(toks, inner), unit_shape(toks, inner), jax.ShapeDtypeStruct((2, slots, 8, inner), F32),
            jax.ShapeDtypeStruct((2, grad_rows, inner), F32),
        ],
        scratch_shapes=[
            pltpu.VMEM((states, inner), F32), pltpu.VMEM((states, inner), F32), pltpu.VMEM((toks + BLK, inner), F32), pltpu.VMEM((toks + BLK, BLK * states), BF16),
            pltpu.VMEM((toks, BLK * states), BF16),
            pltpu.VMEM((2, BLK, states, inner), F32),
            pltpu.VMEM((2, (BLK + 1) * states, inner), BF16), pltpu.VMEM((2, BLK * states, inner), BF16),
            pltpu.VMEM((2, BLK * states, inner), BF16), pltpu.VMEM((2, BLK // 4 * states, inner), BF16),
            pltpu.VMEM((2, BLK * states, 256), BF16), pltpu.VMEM((states, inner), F32),
            pltpu.VMEM((toks + BLK, inner), F32), pltpu.VMEM((toks + BLK, inner), F32),
            pltpu.VMEM((toks + BLK, BLK * states), BF16), pltpu.VMEM((toks + BLK, BLK * states), BF16),
            pltpu.VMEM((inner // 128, toks + 2 * HALO, 128), F32), pltpu.VMEM((toks, inner), BF16),
            pltpu.VMEM((states, inner), F32), pltpu.VMEM((slots, states, inner), F32), pltpu.VMEM((slots, states, inner), F32),
            *exchange_shapes(runs, slots, states, inner),
        ],
        compiler_params=params(collective_id=3, has_side_effects=True),
        name="second",
    )(
        first_in, lasts, decay_rate, starts, tiles, decay_rate, ahead, xe, act, planes, dy, proj, weights, conv_weight, skip_gain,
    )

    def now(*block):
        return spec((None,) + block, lambda s: (s % slots,) + (0,) * len(block))

    def early(*block):
        return spec((None,) + block, lambda s: (jnp.minimum(s, slots - 1),) + (0,) * len(block))

    def after(*block):
        return spec((None,) + block, lambda s: (jnp.maximum(s - slots, 0),) + (0,) * len(block))

    small_rows = 2 * grad_rows * (inner // dim)
    main_parts = part_count(inner + dim * (inner // dim) + small_rows)
    rest_parts = part_count(dim * (inner // dim))
    mixed, d_tokens, result, x_result, factors, own = pl.pallas_call(
        functools.partial(tail_kernel, (runs, groups, slots)),
        grid=(2 * slots,),
        in_specs=[
            now(toks, dim), now(toks, dim), now(1, 3 * dim), whole(slots, toks), pl.BlockSpec(memory_space=pltpu.SMEM), now(toks, dim),
            early(toks, inner), early(2, toks, inner), whole(slots, 2, toks, inner), whole(2, slots, 8, inner),
            whole(dim, 2 * inner), whole(inner, dim), whole(slots, dim), whole(2, grad_rows, inner),
        ],
        out_specs=[
            early(toks, dim), after(toks, dim), whole(main_parts * PART_ROWS, dim), whole(rest_parts * PART_ROWS, dim),
            whole(16 * groups, dim), whole(16, dim),
        ],
        out_shape=[
            jax.ShapeDtypeStruct((slots, toks, dim), BF16), jax.ShapeDtypeStruct((slots, toks, dim), F32),
            jax.ShapeDtypeStruct((main_parts * PART_ROWS, dim), BF16), jax.ShapeDtypeStruct((rest_parts * PART_ROWS, dim), BF16),
            jax.ShapeDtypeStruct((16 * groups, dim), BF16), jax.ShapeDtypeStruct((16, dim), BF16),
        ],
        scratch_shapes=[
            pltpu.VMEM((2, slots, 8, inner), F32), pltpu.SemaphoreType.DMA((2,)), pltpu.SemaphoreType.DMA((2,)),
            pltpu.VMEM((slots, toks, inner), BF16), pltpu.VMEM((slots, toks, inner), BF16), pltpu.VMEM((slots, toks, dim), BF16),
            pltpu.VMEM((inner, dim), F32), pltpu.VMEM((dim, inner), F32),
            pltpu.VMEM((dim, inner), F32), pltpu.VMEM((8 * slots, dim), F32), pltpu.VMEM((max(runs - 1, 1), 8 * slots, dim), F32),
            pltpu.VMEM((16 * groups, dim), BF16), pltpu.SemaphoreType.DMA((runs + groups,)),
            pltpu.SemaphoreType.DMA((runs + groups,)), *reduce_shapes(main_parts, dim, runs, groups),
            *reduce_shapes(rest_parts, dim, runs, groups),
        ],
        compiler_params=params(collective_id=4, has_side_effects=True),
        name="tail",
    )(
        tokens, cotangent, modulate, token_mask, counts, hid, z_gate, y, dx, rims, input_weight, output_weight, timestep, grads,
    )

    def part(*block):
        return spec((None,) + block, lambda s: (jnp.minimum(s, slots - 1),) + (0,) * len(block))

    (
        mixed, d_tokens, d_time, grad_ada, grad_ada_bias, in_grad, tap_grad, tapb_grad, xp_grad, dtp_grad, dtb_grad, rate_grad, skip_grad,
        out_grad,
    ) = pl.pallas_call(
        finish_kernel,
        grid=(4,),
        in_specs=[
            part(toks, dim), part(toks, dim), spec((inner // 4, dim), lambda s: (s, 0)),
            spec((dim, dim), lambda s: (inner // dim + jnp.maximum(s - inner // dim, 0), 0)),
            spec((dim, dim), lambda s: (jnp.minimum(s, inner // dim - 1), 0)),
            spec((PART_ROWS, dim), lambda s: (2 * inner // PART_ROWS, 0)),
            whole(16 * groups, dim), whole(16, dim), whole(slots, dim), spec((dim, dim), lambda s: (0, jnp.minimum(s, 2))),
        ],
        out_specs=[
            part(toks, dim), part(toks, dim), whole(slots, dim), spec((dim, dim), lambda s: (0, jnp.minimum(s, 2))), whole(3 * dim),
            spec((dim, 2 * inner // 4), lambda s: (0, s)), whole(2, tap_count, inner), whole(2, inner),
            whole(2, rank + 2 * states, inner), whole(2, rank, inner), whole(2, inner), whole(2, states, inner), whole(2, inner),
            spec((inner // 4, dim), lambda s: (s, 0)),
        ],
        out_shape=[jax.ShapeDtypeStruct((slots, toks, dim), BF16)]
        + [
            jax.ShapeDtypeStruct(shape, F32)
            for shape in (
                (slots, toks, dim), (slots, dim), (dim, 3 * dim), (3 * dim,), (dim, 2 * inner), (2, tap_count, inner), (2, inner),
                (2, rank + 2 * states, inner), (2, rank, inner), (2, inner), (2, states, inner), (2, inner), (inner, dim),
            )
        ],
        compiler_params=params(),
        name="finish",
    )(mixed, d_tokens, result, result, x_result, result, factors, own, timestep, ada_weight)
    return (
        mixed, d_tokens, d_time, grad_ada, grad_ada_bias, in_grad, tap_grad, tapb_grad, jnp.swapaxes(xp_grad, 1, 2), dtp_grad, dtb_grad,
        rate_grad, skip_grad, out_grad,
    )


def solution(mesh):
    runs = P("dp", "seq", None)
    return jax.shard_map(
        per_device,
        mesh=mesh,
        in_specs=(runs, P("dp", None), P("dp"), P("dp", "seq")) + (P(),) * 11 + (runs,),
        out_specs=(runs, runs, P("dp", None)) + (P(),) * 11,
        check_vma=False,
    )
```

```python
import functools
import math

import jax
import jax.numpy as jnp
from jax import lax
from jax.experimental import pallas as pl
from jax.experimental.pallas import tpu as pltpu
from jax.sharding import PartitionSpec as P

EPSILON = 1e-06
BLK = 16
WIDE_RANK = 32
HALO = 16
LOG2E = math.log2(math.e)
F32, BF16 = jnp.float32, jnp.bfloat16
NT = (((1,), (1,)), ((), ()))
TN = (((0,), (0,)), ((), ()))
VMEM_LIMIT = 60 << 20
MESH = pl.DeviceIdType.MESH


def dot(a, b):
    return jnp.dot(a, b, preferred_element_type=F32)


def dot_nt(a, b):
    return lax.dot_general(a, b, NT, preferred_element_type=F32)


def dot_tn(a, b):
    return lax.dot_general(a, b, TN, preferred_element_type=F32)


def flip_full(value):
    turned = lax.broadcasted_iota(jnp.int32, (8, value.shape[1]), 0)
    groups = [value[at : at + 8] for at in range(0, value.shape[0], 8)]
    return jnp.concatenate([jnp.take_along_axis(group, 7 - turned, axis=0) for group in reversed(groups)], axis=0)


def flip_low(value):
    return flip_full(value.astype(F32)).astype(BF16)


def normalise(tokens_f):
    centered = tokens_f - jnp.mean(tokens_f, axis=-1, keepdims=True)
    inv_std = lax.rsqrt(jnp.mean(centered * centered, axis=-1, keepdims=True) + EPSILON)
    return centered * inv_std, inv_std


def eye(size):
    rows = lax.broadcasted_iota(jnp.int32, (size, size), 0)
    cols = lax.broadcasted_iota(jnp.int32, (size, size), 1)
    return (rows == cols).astype(BF16)


def as_column(row):
    return dot_nt(eye(row.shape[1]), jnp.broadcast_to(row.astype(F32).astype(BF16), (8, row.shape[1])))[:, :1]


def remote(src, dst, send_sem, recv_sem, target):
    return pltpu.make_async_remote_copy(
        src_ref=src, dst_ref=dst, send_sem=send_sem, recv_sem=recv_sem, device_id=target, device_id_type=MESH
    )


def greet(targets):
    barrier = pltpu.get_barrier_semaphore()
    for target in targets:
        pl.semaphore_signal(barrier, inc=1, device_id=target, device_id_type=MESH)
    pl.semaphore_wait(barrier, len(targets))


def greet_line(me, runs, others=()):
    barrier = pltpu.get_barrier_semaphore()
    for target in others:
        pl.semaphore_signal(barrier, inc=1, device_id=target, device_id_type=MESH)

    @pl.when(me > 0)
    def _():
        pl.semaphore_signal(barrier, inc=1, device_id={"seq": me - 1}, device_id_type=MESH)

    @pl.when(me < runs - 1)
    def _():
        pl.semaphore_signal(barrier, inc=1, device_id={"seq": me + 1}, device_id_type=MESH)

    neighbours = lax.div(me + runs - 1, runs) + lax.div(2 * runs - 2 - me, runs)
    pl.semaphore_wait(barrier, neighbours + len(others))


def swap_along_line(me, runs, ups, downs, start):
    up = [remote(src, dst, ss, rs, {"seq": me + 1}) for src, dst, ss, rs in ups]
    down = [remote(src, dst, ss, rs, {"seq": me - 1}) for src, dst, ss, rs in downs]

    @pl.when(me < runs - 1)
    def _():
        for copy in up:
            if start:
                copy.start()
            else:
                copy.wait_send()
        if not start:
            for copy in down:
                copy.wait_recv()

    @pl.when(me > 0)
    def _():
        for copy in down:
            if start:
                copy.start()
            else:
                copy.wait_send()
        if not start:
            for copy in up:
                copy.wait_recv()


def enter_kernel(
    runs, tok, cot, mask, counts, step, ada, ada_bias, win, wout,
    xe, dy, z_out, hid_out, mod_out, rim_out,
    mods, prev_tok, next_tok, prev_mask, next_mask, send_sem, recv_sem,
):
    slots, toks, dim = tok.shape
    inner = wout.shape[0]
    me = lax.axis_index("seq")
    i = pl.program_id(0)
    ups = [
        (tok.at[:, pl.ds(toks - HALO, HALO), :], prev_tok, send_sem.at[0], recv_sem.at[0]),
        (mask, prev_mask, send_sem.at[1], recv_sem.at[1]),
    ]
    downs = [
        (tok.at[:, pl.ds(0, HALO), :], next_tok, send_sem.at[2], recv_sem.at[2]),
        (mask, next_mask, send_sem.at[3], recv_sem.at[3]),
    ]

    @pl.when(i == 0)
    def _():
        greet_line(me, runs)
        swap_along_line(me, runs, ups, downs, True)

        @pl.when(me == 0)
        def _():
            prev_tok[...] = jnp.zeros(prev_tok.shape, BF16)
            prev_mask[...] = jnp.zeros(prev_mask.shape, jnp.int32)

        @pl.when(me == runs - 1)
        def _():
            next_tok[...] = jnp.zeros(next_tok.shape, BF16)
            next_mask[...] = jnp.zeros(next_mask.shape, jnp.int32)

    live = jnp.where(counts[0] > i, 1.0, 0.0)

    @pl.when(i == 0)
    def _():
        time_f = step[...].astype(F32)
        time_low = (time_f * jax.nn.sigmoid(time_f)).astype(BF16)
        mods[...] = dot(time_low, ada[...]) + ada_bias[...].reshape(1, 3 * dim)

    mod = mods[pl.ds(i, 1), :]
    mod_out[...] = mod
    shift, scale, gate = mod[:, :dim], mod[:, dim : 2 * dim], mod[:, 2 * dim :]

    def hidden_of(part, scale, shift):
        normed, _ = normalise(part.astype(F32))
        return (normed * (1.0 + scale) + shift).astype(BF16)

    hid = hidden_of(tok[i], scale, shift)
    hid_out[...] = hid
    xz = dot(hid, win[...]) * (as_column(mask[pl.ds(i, 1), :]) * live)
    x_low = xz[:, :inner].astype(BF16)
    z = xz[:, inner:]
    z_out[...] = z
    d_branch = (cot[...].astype(F32) * gate).astype(BF16)
    d_summed = dot_nt(d_branch, wout[...]) * z * jax.nn.sigmoid(z)
    dy[0] = d_summed
    dy[1] = flip_full(d_summed)
    xe[0] = x_low
    xe[1] = flip_low(x_low)

    @pl.when(i == slots - 1)
    def _():
        swap_along_line(me, runs, ups, downs, False)
        hidden, seen = [], []
        for item in range(slots):
            row = mods[item : item + 1, :]
            rims = jnp.concatenate([prev_tok[item], next_tok[item]], axis=0)
            hidden.append(hidden_of(rims, row[:, dim : 2 * dim], row[:, :dim]))
            prev_col = as_column(prev_mask[item : item + 1, :])[toks - HALO :]
            next_col = as_column(next_mask[item : item + 1, :])[:HALO]
            live = jnp.where(counts[0] > item, 1.0, 0.0)
            seen.append(jnp.concatenate([prev_col, next_col], axis=0) * live)
        rim_x = dot(jnp.concatenate(hidden, axis=0), win[:, :inner]) * jnp.concatenate(seen, axis=0)
        for item in range(slots):
            part = rim_x[2 * HALO * item : 2 * HALO * (item + 1)]
            rim_out[item, 0] = part[:HALO].astype(BF16)
            rim_out[item, 1] = flip_full(part[HALO:]).astype(BF16)


def columns(inner, width=128):
    return [slice(at, at + width) for at in range(0, inner, width)]


def twice(row8):
    return jnp.concatenate([row8, row8], axis=0)


def spread(ref, index):
    return twice(ref[pl.ds(index, 8, stride=0), :])


def lay_out(wide, rows, picks):
    count, toks = rows.shape
    high = rows.astype(BF16).astype(F32)
    halves = jnp.concatenate([high, rows - high], axis=0).T.astype(BF16)
    for n in range(0, count, 2):
        pair = dot(halves, picks[:, n * 128 : (n + 2) * 128])
        for t in range(0, toks, 8):
            for k in range(2):
                at = 8 * (count * (t // 8) + n + k)
                wide[at : at + 8, :] = pair[t : t + 8, k * 128 : (k + 1) * 128]


def wide_tile(wide, i, count):
    at = 8 * count * (i // 8) + i % 8
    return jnp.concatenate([wide[pl.ds(at + 64 * n, 8, stride=8), :] for n in range(count // 8)], axis=0)


def across_lanes(tile, inner):
    return jnp.concatenate([tile] * (inner // 128), axis=1)


def softplus_parts(pre):
    e = jnp.exp2(-LOG2E * jnp.abs(pre))
    more = jnp.where(e < 1e-3, e - 0.5 * e * e, jnp.log(1.0 + e))
    return jnp.maximum(pre, 0.0) + more, jax.nn.sigmoid(pre)


def bit_of(index, bit):
    return lax.rem(lax.div(index, 1 << bit), 2)


def across(axis, bit):
    me = lax.axis_index(axis)
    mine = bit_of(me, bit)
    return mine, {axis: me + (1 - 2 * mine) * (1 << bit)}


class Exchange:
    def __init__(self, runs, branch, ends, backs, totals, rate, results, group, span, pre, pre_span, sends, arrivals, sems):
        self.branch, self.rate = branch, rate
        self.sources, self.totals, self.results = (ends, backs), totals, results
        self.group, self.span, self.pre, self.pre_span = group, span, pre, pre_span
        self.sends, self.arrivals, self.sems = sends, arrivals, sems
        self.links = [across("seq", bit) for bit in range(int(math.log2(runs)))]
        self.slots = ends.shape[0]
        self.states, self.inner = rate.shape

    def flow(self, kind):
        return kind if self.branch == 0 else 1 - kind

    def targets(self):
        return [target for _, target in self.links]

    def copy(self, stage, kind):
        at = 2 * stage + kind
        return remote(
            self.sends.at[at], self.arrivals.at[at], self.sems.at[0, at], self.sems.at[1, at], self.links[stage][1]
        )

    def send(self, stage, kind):
        rows = self.slots * self.states
        at = 2 * stage + kind
        for i in range(self.slots):
            self.sends[at, i * self.states : (i + 1) * self.states, :] = self.group[kind, i].astype(BF16)
        high = self.span[kind].astype(BF16).astype(F32)
        self.sends[at, rows:, :] = jnp.concatenate([high, self.span[kind] - high], axis=0).astype(BF16)
        self.copy(stage, kind).start()

    def join(self, stage, kind, last):
        mine = self.links[stage][0]
        self.copy(stage, kind).wait()
        at = 2 * stage + kind
        earlier = (mine == 1) if self.flow(kind) == 0 else (mine == 0)
        both = self.arrivals[at, self.slots * self.states :, :].astype(F32)
        length = both[: both.shape[0] // 2] + both[both.shape[0] // 2 :]
        own_span, pre_span = self.span[kind], self.pre_span[kind]
        second_span = jnp.where(earlier, own_span, length)
        rate = self.rate[...] * -LOG2E
        for i in range(self.slots):
            state = self.arrivals[at, i * self.states : (i + 1) * self.states, :].astype(F32)
            before = self.pre[kind, i]
            self.pre[kind, i] = jnp.where(earlier, state * jnp.exp2(rate * pre_span[i : i + 1]) + before, before)
            if not last:
                own = self.group[kind, i]
                first, second = jnp.where(earlier, state, own), jnp.where(earlier, own, state)
                self.group[kind, i] = first * jnp.exp2(rate * second_span[i : i + 1]) + second
        self.pre_span[kind] = jnp.where(earlier, length + pre_span, pre_span)
        if not last:
            self.span[kind] = own_span + length

    def points(self):
        count = len(self.links)

        def begin():
            self.pre[...] = jnp.zeros(self.pre.shape, F32)
            self.pre_span[...] = jnp.zeros(self.pre_span.shape, F32)
            self.span[...] = jnp.zeros(self.span.shape, F32)
            for kind in range(2):
                for i in range(self.slots):
                    self.group[kind, i] = self.sources[kind][i]
                    self.span[kind, i : i + 1, :] = self.totals[i][:1]
                if count:
                    self.send(0, kind)

        def step(stage):
            last = stage == count - 1
            for kind in range(2):
                self.join(stage, kind, last)
                if not last:
                    self.send(stage + 1, kind)

        def end():
            for kind in range(2):
                for i in range(self.slots):
                    self.results[kind][i] = self.pre[kind, i]

        return [begin] + [functools.partial(step, stage) for stage in range(count)] + [end]


def exchange_shapes(runs, slots, states, inner):
    pairs = max(int(math.log2(runs)), 1)
    span_rows = -(-slots // 8) * 8
    return [
        pltpu.VMEM((2, slots, states, inner), F32), pltpu.VMEM((2, span_rows, inner), F32),
        pltpu.VMEM((2, slots, states, inner), F32), pltpu.VMEM((2, span_rows, inner), F32),
        pltpu.VMEM((2 * pairs, slots * states + 2 * span_rows, inner), BF16),
        pltpu.VMEM((2 * pairs, slots * states + 2 * span_rows, inner), BF16),
        pltpu.SemaphoreType.DMA((2, 2 * pairs)),
    ]


def beside(points, step, first, count):
    for at in range(min(len(points), count)):
        todo = points[at:] if at == count - 1 else points[at : at + 1]

        @pl.when(step == first + at)
        def _():
            for point in todo:
                point()


def first_kernel(
    runs, slots, ahead, xe, dy, taps, tap_bias, x_rows, dt_rows, dt_bias, rate,
    act_out, planes, proj_out, last_out, starts_out, tiles, weights, first_in,
    x_cols, dx, decay, through, rate2, wide, picks, ends, backs, totals, first_rate, *exchange_scratch,
):
    toks, inner = dy.shape
    states = rate.shape[0]
    blocks = toks // BLK
    rank = WIDE_RANK
    xwt, dtw = weights.at[: weights.shape[0] - rank], weights.at[weights.shape[0] - rank :]
    delta_out, sig_out, dsilu_out = (planes.at[at] for at in range(3))
    end_out, back_out = last_out.at[:states], last_out.at[states : 2 * states]
    tap_count = taps.shape[0]
    branch, item = pl.program_id(0), pl.program_id(1)
    results = (first_in.at[0], first_in.at[1])
    exchange = Exchange(runs, 0, ends, backs, totals, first_rate, results, *exchange_scratch)

    @pl.when((branch == 0) & (item == 0))
    def _():
        greet(exchange.targets())
        first_rate[...] = rate[...]

    beside(exchange.points(), branch * slots + item, slots, slots)

    @pl.when(item == 0)
    def _():
        rate2[...] = rate[...] * -LOG2E
        picks[...] = (
            lax.broadcasted_iota(jnp.int32, picks.shape, 0) % (2 * states)
            == lax.broadcasted_iota(jnp.int32, picks.shape, 1) // 128
        ).astype(BF16)
        held = dt_rows.shape[0]
        rows = x_rows[...].astype(F32)
        gap = jnp.zeros((rank - held, inner), F32)
        wide = [rows[:held], gap, rows[held:], dt_rows[...].astype(F32), gap]
        weights[...] = jnp.concatenate(wide, axis=0).astype(BF16)

    tap_row, dt_row = tap_bias[pl.ds(branch, 1), :], dt_bias[pl.ds(branch, 1), :]
    for cols in columns(inner):
        at_col = cols.start // 128
        x_cols[at_col] = jnp.concatenate([ahead[:, cols], xe[:, cols]], axis=0).astype(F32)
        parts = []
        for row in range(0, toks, 8):
            part = tap_row[:, cols]
            for k in range(tap_count):
                part = part + taps[k : k + 1, cols] * x_cols[at_col, pl.ds(HALO - tap_count + 1 + k + row, 8), :]
            parts.append(part)
        conv = jnp.concatenate(parts, axis=0)
        open_part = jax.nn.sigmoid(conv)
        act_f = conv * open_part
        act_out[:, cols] = act_f.astype(BF16)
        dsilu_out[:, cols] = open_part + act_f * (1.0 - open_part)
    proj = dot_nt(xwt[...], act_out[...])
    proj_out[...] = proj
    dt_low = proj[:rank, :].astype(BF16)
    for cols in columns(inner, 256):
        pre = dot_tn(dt_low, dtw[:, cols]) + dt_row[:, cols]
        delta, slope = softplus_parts(pre)
        delta_out[:, cols] = delta
        sig_out[:, cols] = slope
        dx[:, cols] = delta * act_out[:, cols].astype(F32)
    lay_out(wide, proj[rank:, :], picks)
    end_out[...] = jnp.zeros((states, inner), F32)
    back_out[...] = jnp.zeros((states, inner), F32)
    through[...] = jnp.zeros((8, inner), F32)

    def one_block(j, slot):
        t0 = pl.multiple_of(j * BLK, BLK)
        dr, xr, yr = (ref.at[pl.ds(t0, BLK), :] for ref in (delta_out, dx, dy))
        count = 2 * states
        wide_rows = wide.at[pl.ds(pl.multiple_of(j * (BLK * count), BLK * count), BLK * count), :]
        s = end_out[...]
        before = through[...]
        starts_out[j] = jnp.concatenate([s, before], axis=0)
        rates = rate2[...]
        for i in range(BLK):
            a = jnp.exp2(spread(dr, i) * rates)
            decay[slot, i] = a
            tile = wide_tile(wide_rows, i, count)
            tiles[t0 + i] = tile
            s = a * s + spread(xr, i) * across_lanes(tile[:states], inner)
        end_out[...] = s
        m = jnp.zeros((states, inner), F32)
        for i in reversed(range(BLK)):
            m = decay[slot, i] * (m + spread(yr, i) * across_lanes(tiles[t0 + i, states:], inner))
        back_out[...] = back_out[...] + m * jnp.exp2(twice(before) * rates)
        through[...] = before + jnp.sum(dr[...], axis=0, keepdims=True)

    def block_step(k, _):
        one_block(2 * k, 0)
        one_block(2 * k + 1, 1)
        return 0

    lax.fori_loop(0, blocks // 2, block_step, 0)
    last_out[2 * states :, :] = through[...]

    @pl.when(branch == 0)
    def _():
        ends[item] = end_out[...]
        backs[item] = back_out[...]
        totals[item] = through[:1, :]


def second_kernel(
    runs, first_in, lasts, last_rate, starts, tiles, rate, ahead, xe, act, planes, dy, proj, weights, taps, skip,
    y_out, dx_out, rims, grads,
    rate2, carry, dxs, bdiag, cdiag, decay, states_low, lam_low, rq_low, qd_low, dots, racc, gsum, hsum, db, dc,
    d_cols, d_pre_low, s_in, s_last, lam_last, *exchange_scratch,
):
    toks, inner = dy.shape
    states = rate.shape[0]
    blocks = toks // BLK
    rank = WIDE_RANK
    xwt, dtw = weights.at[: weights.shape[0] - rank], weights.at[weights.shape[0] - rank :]
    delta, sig, dsilu = (planes.at[at] for at in range(3))
    tap_count = taps.shape[0]
    held = (grads.shape[0] - 3 * states - 8) // 2
    xp_grad, dtp_grad = grads.at[: held + 2 * states], grads.at[held + 2 * states : 2 * held + 2 * states]
    at = 2 * held + 2 * states
    rate_grad, row_grads = grads.at[at : at + states], grads.at[at + states : at + states + 8]
    tapb_at, skip_at, dtb_at = (slice(tap_count + row, tap_count + row + 1) for row in range(3))
    item = pl.program_id(1)
    branch = pl.program_id(0)
    slots = lasts.shape[0]
    ends, backs = lasts.at[:, :states], lasts.at[:, states : 2 * states]
    totals = lasts.at[:, 2 * states :]
    exchange = Exchange(runs, 1, ends, backs, totals, last_rate, (s_last, lam_last), *exchange_scratch)

    @pl.when((item == 0) & (branch == 0))
    def _():
        greet(exchange.targets())

    beside(exchange.points(), branch * slots + item, 0, slots)

    @pl.when(branch == 0)
    def _():
        s_in[...] = first_in[0, item]
        carry[...] = first_in[1, item]

    @pl.when(branch == 1)
    def _():
        s_in[...] = s_last[item]
        carry[...] = lam_last[item]

    gain = skip[pl.ds(pl.program_id(0), 1), :]
    rate2[...] = rate[...] * -LOG2E
    width = BLK * states

    @pl.when(item == 0)
    def _():
        grads[...] = jnp.zeros(grads.shape, F32)

    for cols in columns(inner):
        dxs[:toks, cols] = delta[:, cols] * act[:, cols].astype(F32)
    fold = (
        lax.broadcasted_iota(jnp.int32, (states, width), 1) % states == lax.broadcasted_iota(jnp.int32, (states, width), 0)
    ).astype(BF16)
    own = lax.broadcasted_iota(jnp.int32, (toks, width), 0) % BLK == lax.broadcasted_iota(jnp.int32, (toks, width), 1) // states
    bdiag[:toks, :] = jnp.where(own, dot_tn(proj[rank : rank + states, :].astype(BF16), fold), 0.0).astype(BF16)
    cdiag[...] = jnp.where(own, dot_tn(proj[rank + states :, :].astype(BF16), fold), 0.0).astype(BF16)
    mine = own[:BLK]
    picks = mine.astype(BF16)
    ones = jnp.ones((BLK, 128), BF16)
    racc[...] = jnp.zeros((states, inner), F32)

    def lane_sum(wide):
        part = [wide[:, at : at + 128] for at in range(0, inner, 128)]
        while len(part) > 1:
            pairs = [part[at] + part[at + 1] for at in range(0, len(part) - 1, 2)]
            part = pairs + part[2 * len(pairs) :]
        return part[0]

    def products(slot, j):
        t0 = pl.multiple_of(j * BLK, BLK)
        y_out[pl.ds(t0, BLK), :] = dot(cdiag[pl.ds(t0, BLK), :], states_low[slot, states:, :])
        half = width // 2
        rows = bdiag[pl.ds(t0, BLK), :]
        gsum[pl.ds(t0, BLK), :] = dot(rows[:, half:], lam_low[slot, half:]) + dot(rows[:, :half], lam_low[slot, :half])
        hsum[pl.ds(t0, BLK), :] = dot(picks[:, half:], rq_low[slot, half:]) + dot(picks[:, :half], rq_low[slot, :half])
        racc[...] += dot(fold[:, : BLK // 4 * states], qd_low[slot])
        dc[pl.ds(t0, BLK), :] = jnp.where(mine, dot_nt(ones, dots[slot, :, :128]), 0.0).astype(BF16)
        db[pl.ds(t0, BLK), :] = jnp.where(mine, dot_nt(ones, dots[slot, :, 128:]), 0.0).astype(BF16)

    def one_block(slot, j):
        t0 = pl.multiple_of(j * BLK, BLK)
        dr, xr, yr = (ref.at[pl.ds(t0, BLK), :] for ref in (delta, dxs, dy))
        tile = tiles.at[pl.ds(t0, BLK)]
        r2 = rate2[...]
        r_low = rate[...].astype(BF16)
        begin = starts[j]
        s = begin[:states] + s_in[...] * jnp.exp2(twice(begin[states:]) * r2)
        states_low[slot, :states, :] = s.astype(BF16)
        for i in range(BLK):
            a = jnp.exp2(spread(dr, i) * r2)
            decay[slot, i] = a
            s = a * s + spread(xr, i) * across_lanes(tile[i, :states], inner)
            s_low = s.astype(BF16)
            states_low[slot, (i + 1) * states : (i + 2) * states, :] = s_low
            dots[slot, i * states : (i + 1) * states, :128] = lane_sum(s_low * spread(yr, i).astype(BF16))
        cr = carry[...]
        qds = []
        for i in reversed(range(BLK)):
            lam = cr + spread(yr, i) * across_lanes(tile[i, states:], inner)
            l_low = lam.astype(BF16)
            lam_low[slot, i * states : (i + 1) * states, :] = l_low
            dots[slot, i * states : (i + 1) * states, 128:] = lane_sum(l_low * spread(xr, i).astype(BF16))
            cr = decay[slot, i] * lam
            q = cr.astype(BF16) * states_low[slot, i * states : (i + 1) * states, :]
            rq_low[slot, i * states : (i + 1) * states, :] = q * r_low
            qds.append(q * spread(dr, i).astype(BF16))
            if i % 4 == 0:
                qd_low[slot, i // 4 * states : (i // 4 + 1) * states, :] = (qds[0] + qds[1]) + (qds[2] + qds[3])
                qds = []
        carry[...] = cr

    def block_step(k, _):
        j = blocks - 1 - 2 * k
        for slot in range(2):
            one_block(slot, j - slot)
            products(slot, j - slot)
        return 0

    lax.fori_loop(0, blocks // 2, block_step, 0)
    rate_grad[...] += -racc[...]
    for cols in columns(inner):
        act_f = act[:, cols].astype(F32)
        row_grads[skip_at, cols] += jnp.sum(dy[:, cols] * act_f, axis=0, keepdims=True)
        y_out[:, cols] += gain[:, cols] * act_f
        d_pre = (act_f * gsum[:toks, cols] - hsum[:toks, cols]) * sig[:, cols]
        row_grads[dtb_at, cols] += jnp.sum(d_pre, axis=0, keepdims=True)
        d_pre_low[:, cols] = d_pre.astype(BF16)
    dtp_grad[...] += dot(proj[:rank, :].astype(BF16), d_pre_low[...])[:held]
    d_proj = jnp.concatenate(
        [dot_nt(dtw[...], d_pre_low[...]), dot_nt(fold, db[:toks, :]), dot_nt(fold, dc[:toks, :])], axis=0
    ).astype(BF16)
    xp_new = dot(d_proj, act[...])
    xp_grad[:held, :] += xp_new[:held]
    xp_grad[held:, :] += xp_new[rank:]
    d_cols[:, :HALO, :] = jnp.zeros((inner // 128, HALO, 128), F32)
    d_cols[:, HALO + toks :, :] = jnp.zeros((inner // 128, HALO, 128), F32)
    for wide_cols in columns(inner, 256):
        through = dot_tn(d_proj, xwt[:, wide_cols])
        for at in columns(256):
            cols = slice(wide_cols.start + at.start, wide_cols.start + at.stop)
            d_act = delta[:, cols] * gsum[:toks, cols] + gain[:, cols] * dy[:, cols] + through[:, at]
            d_conv = d_act * dsilu[:, cols]
            row_grads[tapb_at, cols] += jnp.sum(d_conv, axis=0, keepdims=True)
            x_f = jnp.concatenate([ahead[:, cols], xe[:, cols]], axis=0).astype(F32)
            at_col = cols.start // 128
            d_cols[at_col, HALO : HALO + toks, :] = d_conv
            sums = [jnp.zeros((8, 128), F32) for _ in range(tap_count)]
            for row in range(HALO - 8, HALO + toks, 8):
                part = jnp.zeros((8, 128), F32)
                for k in range(tap_count):
                    moved = d_cols[at_col, pl.ds(row + tap_count - 1 - k, 8), :]
                    part = part + taps[k : k + 1, cols] * moved
                    sums[k] = sums[k] + moved * x_f[row : row + 8]
                if row < HALO:
                    rims[branch, item, :, cols] = part
                else:
                    dx_out[row - HALO : row - HALO + 8, cols] = part
            for k in range(tap_count):
                row_grads[k : k + 1, cols] += jnp.sum(sums[k], axis=0, keepdims=True)


LAST_ROWS = 16
PART_ROWS = 512


class Ring:
    def __init__(self, bits):
        self.bits = bits
        self.size = 1 << len(bits)
        self.digits = [bit_of(lax.axis_index(axis), bit) for axis, bit in bits]
        self.place = sum(digit * (1 << at) for at, digit in enumerate(self.digits))

    def target(self, ahead):
        place = lax.rem(self.place + ahead, self.size)
        where = {}
        for at, (axis, bit) in enumerate(self.bits):
            base = where.get(axis, lax.axis_index(axis))
            where[axis] = base + (bit_of(place, at) - self.digits[at]) * (1 << bit)
        return where, place

    def targets(self):
        return [self.target(ahead)[0] for ahead in range(1, self.size)]


def stage_rings(runs, groups):
    bits = [("seq", bit) for bit in range(int(math.log2(runs)))] + [("dp", bit) for bit in range(int(math.log2(groups)))]
    return [Ring(bits[:1])] + [Ring(bits[at : at + 2]) for at in range(1, len(bits), 2)]


def part_count(rows):
    return -(-rows // PART_ROWS)


def buffer_rows(runs, groups):
    bits = int(math.log2(runs)) + int(math.log2(groups))
    size, total = PART_ROWS, 0
    for members in [2] + [1 << min(2, bits - at) for at in range(1, bits, 2)]:
        moved = size // members if size >= members * LAST_ROWS else size
        total += moved * (members - 1)
        size = moved
    return total


def reduce_shapes(parts, dim, runs, groups):
    bits = int(math.log2(runs)) + int(math.log2(groups))
    stages = 1 + bits // 2
    room = parts * buffer_rows(runs, groups)
    sems = pltpu.SemaphoreType.DMA((parts, 2 * stages, 3))
    return [
        pltpu.VMEM((parts * PART_ROWS, dim), F32), pltpu.VMEM((room, dim), BF16), pltpu.VMEM((room, dim), BF16),
        pltpu.VMEM((parts * PART_ROWS, dim), BF16), sems, sems,
    ]


class Reduction:
    def __init__(self, rings, turns, segments, acc, sends, arrivals, gathered, send_sem, recv_sem):
        self.rings = rings
        self.count = len(rings)
        self.parts = len(turns)
        self.segments = segments
        self.acc, self.sends, self.arrivals, self.gathered = acc, sends, arrivals, gathered
        self.send_sem, self.recv_sem = send_sem, recv_sem
        room = sends.shape[0] // self.parts
        self.steps = []
        for part, turn in enumerate(turns):
            later = rings[1:]
            turn = turn % max(len(later), 1)
            order = rings[:1] + later[turn:] + later[:turn]
            start, size, at = part * PART_ROWS, PART_ROWS, part * room
            steps = []
            for ring in order:
                split = size >= ring.size * LAST_ROWS
                moved = size // ring.size if split else size
                keep = pl.multiple_of(start + ring.place * moved, LAST_ROWS) if split else start
                steps.append((ring, start, split, moved, keep, at))
                at += moved * (ring.size - 1)
                start, size = keep, moved
            self.steps.append(steps)

    def assemble(self, part):
        low, high = part * PART_ROWS, (part + 1) * PART_ROWS
        at = 0
        for get, size in self.segments:
            first, last = max(at, low), min(at + size, high)
            if first < last:
                self.acc[first:last, :] = get(first - at, last - first)
            at += size
        if at < high:
            first = max(at, low)
            self.acc[first:high, :] = jnp.zeros((high - first, self.acc.shape[1]), F32)

    def scatter_copy(self, part, stage, ahead):
        ring, _, _, moved, _, at = self.steps[part][stage]
        at += (ahead - 1) * moved
        return remote(
            self.sends.at[pl.ds(at, moved), :], self.arrivals.at[pl.ds(at, moved), :],
            self.send_sem.at[part, stage, ahead - 1], self.recv_sem.at[part, stage, ahead - 1], ring.target(ahead)[0],
        )

    def scatter(self, part, stage):
        ring, start, split, moved, _, at = self.steps[part][stage]
        for ahead in range(1, ring.size):
            place = ring.target(ahead)[1]
            away = pl.multiple_of(start + place * moved, LAST_ROWS) if split else start
            here = at + (ahead - 1) * moved
            self.sends[here : here + moved, :] = self.acc[pl.ds(away, moved), :].astype(BF16)
            self.scatter_copy(part, stage, ahead).start()

    def settle(self, part, stage):
        ring, _, split, moved, keep, at = self.steps[part][stage]
        for ahead in range(1, ring.size):
            self.scatter_copy(part, stage, ahead).wait()
        held = self.acc[pl.ds(keep, moved), :]
        came = [
            self.arrivals[at + (ahead - 1) * moved : at + ahead * moved, :].astype(F32) for ahead in range(1, ring.size)
        ]
        if split:
            for part in came:
                held = held + part
        else:
            values = [held.astype(BF16).astype(F32)] + came
            total = jnp.zeros_like(held)
            for place in range(ring.size):
                behind = lax.rem(ring.place - place + ring.size, ring.size)
                chosen = values[0]
                for ahead in range(1, ring.size):
                    chosen = jnp.where(behind == ahead, values[ahead], chosen)
                total = total + chosen
            held = total
        self.acc[pl.ds(keep, moved), :] = held

    def gather_copies(self, part, stage):
        ring, _, split, moved, keep, _ = self.steps[part][stage]
        here = self.gathered.at[pl.ds(keep, moved), :]
        return [
            remote(
                here, here, self.send_sem.at[part, self.count + stage, ahead - 1],
                self.recv_sem.at[part, self.count + stage, ahead - 1], ring.target(ahead)[0],
            )
            for ahead in range(1, ring.size)
            if split
        ]

    def points(self):
        def begin():
            for part in range(self.parts):
                self.assemble(part)
                self.scatter(part, 0)

        def split(stage):
            for part in range(self.parts):
                self.settle(part, stage - 1)
                self.scatter(part, stage)

        def turn():
            for part in range(self.parts):
                self.settle(part, self.count - 1)
                _, _, _, moved, keep, _ = self.steps[part][-1]
                self.gathered[pl.ds(keep, moved), :] = self.acc[pl.ds(keep, moved), :].astype(BF16)
                for copy in self.gather_copies(part, self.count - 1):
                    copy.start()

        def join(stage):
            for part in range(self.parts):
                for copy in self.gather_copies(part, stage + 1):
                    copy.wait()
                if stage >= 0:
                    for copy in self.gather_copies(part, stage):
                        copy.start()

        points = [begin]
        points += [functools.partial(split, stage) for stage in range(1, self.count)]
        points += [turn]
        return points + [functools.partial(join, stage) for stage in reversed(range(-1, self.count - 1))]


def big_segments(ref, dim):
    return [
        (lambda at, size, lane=lane: ref[at : at + size, lane : lane + dim], ref.shape[0])
        for lane in range(0, ref.shape[1], dim)
    ]


def small_segments(ref, dim):
    return [
        (lambda at, size, branch=branch, lane=lane: ref[branch, at : at + size, lane : lane + dim], ref.shape[1])
        for lane in range(0, ref.shape[2], dim)
        for branch in range(2)
    ]


def tail_kernel(
    plan, tok, cot, mod, mask, counts, hid, z_in, y, dx, rims, win, wout, step,
    grads,
    mixed, d_tokens, result, x_result, factors, own_rows,
    late, rim_send, rim_recv, dz, d_xs, hids, out_grad, z_grad, x_grad, mod_sum, mod_in, table, small_send, small_recv, *reduce_scratch,
):
    runs, groups, slots = plan
    me = lax.axis_index("seq")
    downs = [(rims.at[0], late.at[0], rim_send.at[0], rim_recv.at[0])]
    ups = [(rims.at[1], late.at[1], rim_send.at[1], rim_recv.at[1])]
    dim = tok.shape[-1]
    toks, inner = z_in.shape
    now = pl.program_id(0)
    i = lax.rem(now, slots)
    rings = stage_rings(runs, groups)
    seq_ring = Ring([("seq", bit) for bit in range(int(math.log2(runs)))])
    dp_ring = Ring([("dp", bit) for bit in range(int(math.log2(groups)))])
    half = len(reduce_scratch) // 2
    smalls = small_segments(grads, dim)
    segments = big_segments(out_grad, dim) + big_segments(z_grad, dim) + smalls
    main = Reduction(rings, [part % 3 // 2 for part in range(result.shape[0] // PART_ROWS)], segments, *reduce_scratch[:half])
    rest = Reduction(rings, [part % 2 for part in range(x_result.shape[0] // PART_ROWS)], big_segments(x_grad, dim), *reduce_scratch[half:])
    main_points, rest_points = main.points(), rest.points()

    @pl.when(now == 0)
    def _():
        greet_line(me, runs, [target for ring in rings + [seq_ring, dp_ring] for target in ring.targets()])
        swap_along_line(me, runs, ups, downs, True)

        @pl.when(me == 0)
        def _():
            late[1] = jnp.zeros(late.shape[1:], F32)

        @pl.when(me == runs - 1)
        def _():
            late[0] = jnp.zeros(late.shape[1:], F32)

        out_grad[...] = jnp.zeros(out_grad.shape, F32)
        z_grad[...] = jnp.zeros(z_grad.shape, F32)
        x_grad[...] = jnp.zeros(x_grad.shape, F32)
        mod_sum[...] = jnp.zeros(mod_sum.shape, F32)

    scale, gate = mod[:, dim : 2 * dim], mod[:, 2 * dim :]
    valid = as_column(mask[pl.ds(i, 1), :]) * jnp.where(counts[0] > i, 1.0, 0.0)
    mod_rows = pl.ds(pl.multiple_of(8 * i, 8), 8)

    @pl.when(now < slots)
    def _():
        cot_f = cot[...].astype(F32)
        z = z_in[...]
        z_sig = jax.nn.sigmoid(z)
        z_silu = z * z_sig
        summed = y[0] + flip_full(y[1])
        gated = (summed * z_silu).astype(BF16)
        branch_out = dot(gated, wout[...])
        mixed[...] = (tok[...].astype(F32) + gate * branch_out).astype(BF16)
        d_branch = (cot_f * gate).astype(BF16)
        out_grad[...] += dot_tn(gated, d_branch)
        d_zgate = dot_nt(d_branch, wout[...]) * summed * (z_sig + z_silu * (1.0 - z_sig))
        d_low = (d_zgate * valid).astype(BF16)
        dz[i] = d_low
        z_grad[...] += dot_tn(hid[...], d_low)
        hids[i] = hid[...]
        d_gate = jnp.sum(cot_f * branch_out, axis=0, keepdims=True)
        mod_sum[mod_rows, :] = jnp.concatenate([jnp.zeros((2, dim), F32), d_gate, jnp.zeros((5, dim), F32)], axis=0)

    @pl.when(now == slots)
    def _():
        main_points[0]()
        swap_along_line(me, runs, ups, downs, False)
        edge = late.shape[2]

        def with_late(part, extra):
            return jnp.concatenate([part[: toks - edge], part[toks - edge :] + extra], axis=0)

        for item in range(slots):
            seen = as_column(mask[item : item + 1, :]) * jnp.where(counts[0] > item, 1.0, 0.0)
            d_x = with_late(dx[item, 0], late[0, item]) + flip_full(with_late(dx[item, 1], late[1, item]))
            d_low = (d_x * seen).astype(BF16)
            d_xs[item] = d_low
            x_grad[...] += dot_tn(hids[item], d_low)
        rest_points[0]()
        main_points[1]()

    @pl.when(now >= slots)
    def _():
        d_hidden = dot_nt(d_xs[i], win[:, :inner]) + dot_nt(dz[i], win[:, inner:])
        normed, inv_std = normalise(tok[...].astype(F32))
        d_shift = jnp.sum(d_hidden, axis=0, keepdims=True)
        d_scale = jnp.sum(d_hidden * normed, axis=0, keepdims=True)
        mod_sum[mod_rows, :] += jnp.concatenate([d_shift, d_scale, jnp.zeros((6, dim), F32)], axis=0)
        d_normed = d_hidden * (1.0 + scale)
        d_tokens[...] = cot[...].astype(F32) + inv_std * (
            d_normed
            - jnp.mean(d_normed, axis=-1, keepdims=True)
            - normed * jnp.mean(d_normed * normed, axis=-1, keepdims=True)
        )

    @pl.when(now == slots)
    def _():
        rest_points[1]()

    def sum_copies():
        return [
            remote(mod_sum, mod_in.at[ahead - 1], small_send.at[ahead - 1], small_recv.at[ahead - 1], seq_ring.target(ahead)[0])
            for ahead in range(1, seq_ring.size)
        ]

    def table_copies():
        at = pl.multiple_of(dp_ring.place * 16, 16)
        here = table.at[pl.ds(at, 16), :]
        base = seq_ring.size - 1
        return [
            remote(here, here, small_send.at[base + ahead - 1], small_recv.at[base + ahead - 1], dp_ring.target(ahead)[0])
            for ahead in range(1, dp_ring.size)
        ]

    def start_small():
        for copy in sum_copies():
            copy.start()

    def turn_small():
        for copy in sum_copies():
            copy.wait()
        values = [mod_sum[...]] + [mod_in[ahead - 1] for ahead in range(1, seq_ring.size)]
        total = jnp.zeros(mod_sum.shape, F32)
        for place in range(seq_ring.size):
            behind = lax.rem(seq_ring.place - place + seq_ring.size, seq_ring.size)
            chosen = values[0]
            for ahead in range(1, seq_ring.size):
                chosen = jnp.where(behind == ahead, values[ahead], chosen)
            total = total + chosen
        time_f = step[...].astype(F32)
        time_low = time_f * jax.nn.sigmoid(time_f)
        lines = [total[8 * item : 8 * item + 3] for item in range(slots)] + [time_low]
        lines.append(jnp.zeros((16 - 4 * slots, dim), F32))
        own = jnp.concatenate(lines, axis=0).astype(BF16)
        own_rows[...] = own
        table[pl.ds(pl.multiple_of(dp_ring.place * 16, 16), 16), :] = own
        for copy in table_copies():
            copy.start()

    def end_small():
        for copy in table_copies():
            copy.wait()
        factors[...] = table[...]

    @pl.when(now == 2 * slots - 1)
    def _():
        start_small()
        for at in range(2, len(main_points)):
            main_points[at]()
            if at == 2:
                turn_small()
            rest_points[at]()
        end_small()
        result[...] = main.gathered[...]
        x_result[...] = rest.gathered[...]


def finish_kernel(
    mixed_in, tokens_in, outs, zs, xs, smalls, factors, own, step, ada,
    mixed, d_tokens, grad_time, grad_ada, grad_ada_bias, in_grad, tap_grad, tapb_grad, xp_grad, dtp_grad, dtb_grad, rate_grad, skip_grad, out_grad,
):
    dim, inner = in_grad.shape[0], rate_grad.shape[2]
    slots = step.shape[0]
    now = pl.program_id(0)
    mixed[...] = mixed_in[...]
    d_tokens[...] = tokens_in[...]
    out_grad[...] = outs[...].astype(F32)
    in_grad[...] = jnp.where(now < inner // dim, xs[...], zs[...]).astype(F32)
    table = factors[...]
    length = table.shape[0]

    for part in range(3):

        @pl.when(now == part)
        def _():
            row = lax.broadcasted_iota(jnp.int32, (length, length), 0)
            col = lax.broadcasted_iota(jnp.int32, (length, length), 1)
            item = row % 16 - 3 * slots
            wanted = row // 16 * 16 + 3 * item + part
            mods = dot(((col == wanted) & (item >= 0) & (item < slots)).astype(BF16), table)
            lanes = slice(part * dim, (part + 1) * dim)
            grad_ada[...] = dot_tn(table, mods.astype(BF16))
            grad_ada_bias[lanes] = jnp.sum(mods, axis=0)
            mine = own[...].astype(F32)
            picked = jnp.concatenate([mine[3 * i + part : 3 * i + part + 1] for i in range(slots)], axis=0)
            d_time = dot_nt(picked.astype(BF16), ada[...])
            grad_time[...] = d_time if part == 0 else grad_time[...] + d_time

    @pl.when(now == 3)
    def _():
        time_f = step[...].astype(F32)
        time_sig = jax.nn.sigmoid(time_f)
        grad_time[...] = grad_time[...] * time_sig * (1.0 + time_f * (1.0 - time_sig))
        at = 0
        for first in range(0, inner, dim):
            lanes = slice(first, first + dim)
            for branch in range(2):
                for ref in (xp_grad, dtp_grad, rate_grad, tap_grad):
                    size = ref.shape[1]
                    ref[branch, :, lanes] = smalls[at : at + size, :].astype(F32)
                    at += size
                for ref in (tapb_grad, skip_grad, dtb_grad):
                    ref[branch : branch + 1, lanes] = smalls[at : at + 1, :].astype(F32)
                    at += 1
                at += 1


def params(**more):
    return pltpu.CompilerParams(vmem_limit_bytes=VMEM_LIMIT, **more)


def spec(block, index):
    return pl.BlockSpec(block, index)


def per_device(
    tokens, timestep, counts, token_mask, ada_weight, ada_bias, input_weight, conv_weight, conv_bias, x_weight, dt_weight,
    dt_bias, decay_rate, skip_gain, output_weight, cotangent,
):
    slots, toks, dim = tokens.shape
    inner = output_weight.shape[0]
    rank = dt_weight.shape[1]
    states = decay_rate.shape[1]
    tap_count = conv_weight.shape[1]
    wide_rank = WIDE_RANK
    proj_rows = wide_rank + 2 * states
    blocks = toks // BLK
    runs = lax.axis_size("seq")
    groups = lax.axis_size("dp")
    x_rows = jnp.swapaxes(x_weight, 1, 2)

    def item(*block):
        return spec((None,) + block, lambda i: (i,) + (0,) * len(block))

    def whole(*block):
        return spec(block, lambda *_: (0,) * len(block))

    xe, dy, z_gate, hid, modulate, ahead = pl.pallas_call(
        functools.partial(enter_kernel, runs),
        grid=(slots,),
        in_specs=[
            whole(slots, toks, dim), item(toks, dim), whole(slots, toks), pl.BlockSpec(memory_space=pltpu.SMEM), whole(slots, dim), whole(dim, 3 * dim),
            whole(3 * dim), whole(dim, 2 * inner), whole(inner, dim),
        ],
        out_specs=[
            item(2, toks, inner), item(2, toks, inner), item(toks, inner), item(toks, dim), item(1, 3 * dim),
            whole(slots, 2, HALO, inner),
        ],
        out_shape=[
            jax.ShapeDtypeStruct((slots, 2, toks, inner), BF16),
            jax.ShapeDtypeStruct((slots, 2, toks, inner), F32),
            jax.ShapeDtypeStruct((slots, toks, inner), F32),
            jax.ShapeDtypeStruct((slots, toks, dim), BF16),
            jax.ShapeDtypeStruct((slots, 1, 3 * dim), F32),
            jax.ShapeDtypeStruct((slots, 2, HALO, inner), BF16),
        ],
        scratch_shapes=[
            pltpu.VMEM((slots, 3 * dim), F32),
            pltpu.VMEM((slots, HALO, dim), BF16), pltpu.VMEM((slots, HALO, dim), BF16), pltpu.VMEM((slots, toks), jnp.int32),
            pltpu.VMEM((slots, toks), jnp.int32), pltpu.SemaphoreType.DMA((4,)), pltpu.SemaphoreType.DMA((4,)),
        ],
        compiler_params=params(collective_id=1, has_side_effects=True),
        name="enter",
    )(
        tokens, cotangent, token_mask, counts, timestep, ada_weight, ada_bias, input_weight, output_weight,
    )

    def unit(*block):
        return spec((None, None) + block, lambda b, i: (i, b) + (0,) * len(block))

    def branch(*block):
        return spec((None,) + block, lambda b, i: (b,) + (0,) * len(block))

    def unit_shape(*block, kind=F32):
        return jax.ShapeDtypeStruct((slots, 2) + block, kind)

    act, planes, proj, lasts, starts, tiles, weights, first_in = pl.pallas_call(
        functools.partial(first_kernel, runs, slots),
        grid=(2, slots),
        in_specs=[
            unit(HALO, inner), unit(toks, inner), unit(toks, inner), branch(tap_count, inner), whole(2, inner),
            branch(rank + 2 * states, inner), branch(rank, inner), whole(2, inner), branch(states, inner),
        ],
        out_specs=[
            unit(toks, inner), unit(3, toks, inner), unit(proj_rows, toks), unit(2 * states + 8, inner),
            unit(blocks, states + 8, inner), unit(toks, 2 * states, 128), branch(proj_rows + wide_rank, inner),
            whole(2, slots, states, inner),
        ],
        out_shape=[
            unit_shape(toks, inner, kind=BF16), unit_shape(3, toks, inner), unit_shape(proj_rows, toks),
            unit_shape(2 * states + 8, inner), unit_shape(blocks, states + 8, inner), unit_shape(toks, 2 * states, 128),
            jax.ShapeDtypeStruct((2, proj_rows + wide_rank, inner), BF16),
            jax.ShapeDtypeStruct((2, slots, states, inner), F32),
        ],
        scratch_shapes=[
            pltpu.VMEM((inner // 128, HALO + toks, 128), F32), pltpu.VMEM((toks, inner), F32),
            pltpu.VMEM((2, BLK, states, inner), F32), pltpu.VMEM((8, inner), F32),
            pltpu.VMEM((states, inner), F32), pltpu.VMEM((2 * states * toks, 128), F32),
            pltpu.VMEM((4 * states, 2 * states * 128), BF16), pltpu.VMEM((slots, states, inner), F32),
            pltpu.VMEM((slots, states, inner), F32), pltpu.VMEM((slots, 1, inner), F32), pltpu.VMEM((states, inner), F32),
            *exchange_shapes(runs, slots, states, inner),
        ],
        compiler_params=params(collective_id=2, has_side_effects=True),
        name="first",
    )(ahead, xe, dy, conv_weight, conv_bias, x_rows, dt_weight, dt_bias, decay_rate)

    vmem = pl.BlockSpec(memory_space=pltpu.VMEM)
    last = spec((slots, None, 2 * states + 8, inner), lambda b, i: (0, 1, 0, 0))
    last_branch = spec((None, states, inner), lambda b, i: (1, 0, 0))

    grad_rows = 2 * rank + 3 * states + 8
    y, dx, rims, grads = pl.pallas_call(
        functools.partial(second_kernel, runs),
        grid=(2, slots),
        in_specs=[
            whole(2, slots, states, inner), last, last_branch, unit(blocks, states + 8, inner), unit(toks, 2 * states, 128),
            branch(states, inner), unit(HALO, inner), unit(toks, inner), unit(toks, inner), unit(3, toks, inner), unit(toks, inner),
            unit(proj_rows, toks), branch(proj_rows + wide_rank, inner), branch(tap_count, inner), whole(2, inner),
        ],
        out_specs=[unit(toks, inner), unit(toks, inner), whole(2, slots, 8, inner), branch(grad_rows, inner)],
        out_shape=[
            unit_shape(toks, inner), unit_shape(toks, inner), jax.ShapeDtypeStruct((2, slots, 8, inner), F32),
            jax.ShapeDtypeStruct((2, grad_rows, inner), F32),
        ],
        scratch_shapes=[
            pltpu.VMEM((states, inner), F32), pltpu.VMEM((states, inner), F32), pltpu.VMEM((toks + BLK, inner), F32), pltpu.VMEM((toks + BLK, BLK * states), BF16),
            pltpu.VMEM((toks, BLK * states), BF16),
            pltpu.VMEM((2, BLK, states, inner), F32),
            pltpu.VMEM((2, (BLK + 1) * states, inner), BF16), pltpu.VMEM((2, BLK * states, inner), BF16),
            pltpu.VMEM((2, BLK * states, inner), BF16), pltpu.VMEM((2, BLK // 4 * states, inner), BF16),
            pltpu.VMEM((2, BLK * states, 256), BF16), pltpu.VMEM((states, inner), F32),
            pltpu.VMEM((toks + BLK, inner), F32), pltpu.VMEM((toks + BLK, inner), F32),
            pltpu.VMEM((toks + BLK, BLK * states), BF16), pltpu.VMEM((toks + BLK, BLK * states), BF16),
            pltpu.VMEM((inner // 128, toks + 2 * HALO, 128), F32), pltpu.VMEM((toks, inner), BF16),
            pltpu.VMEM((states, inner), F32), pltpu.VMEM((slots, states, inner), F32), pltpu.VMEM((slots, states, inner), F32),
            *exchange_shapes(runs, slots, states, inner),
        ],
        compiler_params=params(collective_id=3, has_side_effects=True),
        name="second",
    )(
        first_in, lasts, decay_rate, starts, tiles, decay_rate, ahead, xe, act, planes, dy, proj, weights, conv_weight, skip_gain,
    )

    def now(*block):
        return spec((None,) + block, lambda s: (s % slots,) + (0,) * len(block))

    def early(*block):
        return spec((None,) + block, lambda s: (jnp.minimum(s, slots - 1),) + (0,) * len(block))

    def after(*block):
        return spec((None,) + block, lambda s: (jnp.maximum(s - slots, 0),) + (0,) * len(block))

    small_rows = 2 * grad_rows * (inner // dim)
    main_parts = part_count(inner + dim * (inner // dim) + small_rows)
    rest_parts = part_count(dim * (inner // dim))
    mixed, d_tokens, result, x_result, factors, own = pl.pallas_call(
        functools.partial(tail_kernel, (runs, groups, slots)),
        grid=(2 * slots,),
        in_specs=[
            now(toks, dim), now(toks, dim), now(1, 3 * dim), whole(slots, toks), pl.BlockSpec(memory_space=pltpu.SMEM), now(toks, dim),
            early(toks, inner), early(2, toks, inner), whole(slots, 2, toks, inner), whole(2, slots, 8, inner),
            whole(dim, 2 * inner), whole(inner, dim), whole(slots, dim), whole(2, grad_rows, inner),
        ],
        out_specs=[
            early(toks, dim), after(toks, dim), whole(main_parts * PART_ROWS, dim), whole(rest_parts * PART_ROWS, dim),
            whole(16 * groups, dim), whole(16, dim),
        ],
        out_shape=[
            jax.ShapeDtypeStruct((slots, toks, dim), BF16), jax.ShapeDtypeStruct((slots, toks, dim), F32),
            jax.ShapeDtypeStruct((main_parts * PART_ROWS, dim), BF16), jax.ShapeDtypeStruct((rest_parts * PART_ROWS, dim), BF16),
            jax.ShapeDtypeStruct((16 * groups, dim), BF16), jax.ShapeDtypeStruct((16, dim), BF16),
        ],
        scratch_shapes=[
            pltpu.VMEM((2, slots, 8, inner), F32), pltpu.SemaphoreType.DMA((2,)), pltpu.SemaphoreType.DMA((2,)),
            pltpu.VMEM((slots, toks, inner), BF16), pltpu.VMEM((slots, toks, inner), BF16), pltpu.VMEM((slots, toks, dim), BF16),
            pltpu.VMEM((inner, dim), F32), pltpu.VMEM((dim, inner), F32),
            pltpu.VMEM((dim, inner), F32), pltpu.VMEM((8 * slots, dim), F32), pltpu.VMEM((max(runs - 1, 1), 8 * slots, dim), F32),
            pltpu.VMEM((16 * groups, dim), BF16), pltpu.SemaphoreType.DMA((runs + groups,)),
            pltpu.SemaphoreType.DMA((runs + groups,)), *reduce_shapes(main_parts, dim, runs, groups),
            *reduce_shapes(rest_parts, dim, runs, groups),
        ],
        compiler_params=params(collective_id=4, has_side_effects=True),
        name="tail",
    )(
        tokens, cotangent, modulate, token_mask, counts, hid, z_gate, y, dx, rims, input_weight, output_weight, timestep, grads,
    )

    def part(*block):
        return spec((None,) + block, lambda s: (jnp.minimum(s, slots - 1),) + (0,) * len(block))

    (
        mixed, d_tokens, d_time, grad_ada, grad_ada_bias, in_grad, tap_grad, tapb_grad, xp_grad, dtp_grad, dtb_grad, rate_grad, skip_grad,
        out_grad,
    ) = pl.pallas_call(
        finish_kernel,
        grid=(4,),
        in_specs=[
            part(toks, dim), part(toks, dim), spec((inner // 4, dim), lambda s: (s, 0)),
            spec((dim, dim), lambda s: (inner // dim + jnp.maximum(s - inner // dim, 0), 0)),
            spec((dim, dim), lambda s: (jnp.minimum(s, inner // dim - 1), 0)),
            spec((PART_ROWS, dim), lambda s: (2 * inner // PART_ROWS, 0)),
            whole(16 * groups, dim), whole(16, dim), whole(slots, dim), spec((dim, dim), lambda s: (0, jnp.minimum(s, 2))),
        ],
        out_specs=[
            part(toks, dim), part(toks, dim), whole(slots, dim), spec((dim, dim), lambda s: (0, jnp.minimum(s, 2))), whole(3 * dim),
            spec((dim, 2 * inner // 4), lambda s: (0, s)), whole(2, tap_count, inner), whole(2, inner),
            whole(2, rank + 2 * states, inner), whole(2, rank, inner), whole(2, inner), whole(2, states, inner), whole(2, inner),
            spec((inner // 4, dim), lambda s: (s, 0)),
        ],
        out_shape=[jax.ShapeDtypeStruct((slots, toks, dim), BF16)]
        + [
            jax.ShapeDtypeStruct(shape, F32)
            for shape in (
                (slots, toks, dim), (slots, dim), (dim, 3 * dim), (3 * dim,), (dim, 2 * inner), (2, tap_count, inner), (2, inner),
                (2, rank + 2 * states, inner), (2, rank, inner), (2, inner), (2, states, inner), (2, inner), (inner, dim),
            )
        ],
        compiler_params=params(),
        name="finish",
    )(mixed, d_tokens, result, result, x_result, result, factors, own, timestep, ada_weight)
    return (
        mixed, d_tokens, d_time, grad_ada, grad_ada_bias, in_grad, tap_grad, tapb_grad, jnp.swapaxes(xp_grad, 1, 2), dtp_grad, dtb_grad,
        rate_grad, skip_grad, out_grad,
    )


def solution(mesh):
    runs = P("dp", "seq", None)
    return jax.shard_map(
        per_device,
        mesh=mesh,
        in_specs=(runs, P("dp", None), P("dp"), P("dp", "seq")) + (P(),) * 11 + (runs,),
        out_specs=(runs, runs, P("dp", None)) + (P(),) * 11,
        check_vma=False,
    )
```

```python
import functools
import math

import jax
import jax.numpy as jnp
from jax import lax
from jax.experimental import pallas as pl
from jax.experimental.pallas import tpu as pltpu
from jax.sharding import PartitionSpec as P

EPSILON = 1e-06
BLK = 16
WIDE_RANK = 32
HALO = 16
SPARE = 8
LOG2E = math.log2(math.e)
F32, BF16 = jnp.float32, jnp.bfloat16
NT = (((1,), (1,)), ((), ()))
TN = (((0,), (0,)), ((), ()))
VMEM_LIMIT = 60 << 20
MESH = pl.DeviceIdType.MESH


def dot(a, b):
    return jnp.dot(a, b, preferred_element_type=F32)


def dot_nt(a, b):
    return lax.dot_general(a, b, NT, preferred_element_type=F32)


def dot_tn(a, b):
    return lax.dot_general(a, b, TN, preferred_element_type=F32)


def flip_full(value):
    turned = lax.broadcasted_iota(jnp.int32, (8, value.shape[1]), 0)
    groups = [value[at : at + 8] for at in range(0, value.shape[0], 8)]
    return jnp.concatenate([jnp.take_along_axis(group, 7 - turned, axis=0) for group in reversed(groups)], axis=0)


def flip_low(value):
    return flip_full(value.astype(F32)).astype(BF16)


def normalise(tokens_f):
    centered = tokens_f - jnp.mean(tokens_f, axis=-1, keepdims=True)
    inv_std = lax.rsqrt(jnp.mean(centered * centered, axis=-1, keepdims=True) + EPSILON)
    return centered * inv_std, inv_std


def eye(size):
    rows = lax.broadcasted_iota(jnp.int32, (size, size), 0)
    cols = lax.broadcasted_iota(jnp.int32, (size, size), 1)
    return (rows == cols).astype(BF16)


def as_column(row):
    return dot_nt(eye(row.shape[1]), jnp.broadcast_to(row.astype(F32).astype(BF16), (8, row.shape[1])))[:, :1]


def remote(src, dst, send_sem, recv_sem, target):
    return pltpu.make_async_remote_copy(
        src_ref=src, dst_ref=dst, send_sem=send_sem, recv_sem=recv_sem, device_id=target, device_id_type=MESH
    )


def greet(targets):
    barrier = pltpu.get_barrier_semaphore()
    for target in targets:
        pl.semaphore_signal(barrier, inc=1, device_id=target, device_id_type=MESH)
    pl.semaphore_wait(barrier, len(targets))


def greet_line(me, runs, others=()):
    barrier = pltpu.get_barrier_semaphore()
    for target in others:
        pl.semaphore_signal(barrier, inc=1, device_id=target, device_id_type=MESH)

    @pl.when(me > 0)
    def _():
        pl.semaphore_signal(barrier, inc=1, device_id={"seq": me - 1}, device_id_type=MESH)

    @pl.when(me < runs - 1)
    def _():
        pl.semaphore_signal(barrier, inc=1, device_id={"seq": me + 1}, device_id_type=MESH)

    neighbours = lax.div(me + runs - 1, runs) + lax.div(2 * runs - 2 - me, runs)
    pl.semaphore_wait(barrier, neighbours + len(others))


def swap_along_line(me, runs, ups, downs, start):
    up = [remote(src, dst, ss, rs, {"seq": me + 1}) for src, dst, ss, rs in ups]
    down = [remote(src, dst, ss, rs, {"seq": me - 1}) for src, dst, ss, rs in downs]

    @pl.when(me < runs - 1)
    def _():
        for copy in up:
            if start:
                copy.start()
            else:
                copy.wait_send()
        if not start:
            for copy in down:
                copy.wait_recv()

    @pl.when(me > 0)
    def _():
        for copy in down:
            if start:
                copy.start()
            else:
                copy.wait_send()
        if not start:
            for copy in up:
                copy.wait_recv()


def enter_kernel(
    runs, tok, cot, mask, counts, step, ada, ada_bias, win, wout,
    xe, dy, z_out, hid_out, mod_out, rim_out,
    mods, prev_tok, next_tok, prev_mask, next_mask, send_sem, recv_sem,
):
    slots, toks, dim = tok.shape
    inner = wout.shape[0]
    me = lax.axis_index("seq")
    i = pl.program_id(0)
    ups = [
        (tok.at[:, pl.ds(toks - HALO, HALO), :], prev_tok, send_sem.at[0], recv_sem.at[0]),
        (mask, prev_mask, send_sem.at[1], recv_sem.at[1]),
    ]
    downs = [
        (tok.at[:, pl.ds(0, HALO), :], next_tok, send_sem.at[2], recv_sem.at[2]),
        (mask, next_mask, send_sem.at[3], recv_sem.at[3]),
    ]

    @pl.when(i == 0)
    def _():
        greet_line(me, runs)
        swap_along_line(me, runs, ups, downs, True)

        @pl.when(me == 0)
        def _():
            prev_tok[...] = jnp.zeros(prev_tok.shape, BF16)
            prev_mask[...] = jnp.zeros(prev_mask.shape, jnp.int32)

        @pl.when(me == runs - 1)
        def _():
            next_tok[...] = jnp.zeros(next_tok.shape, BF16)
            next_mask[...] = jnp.zeros(next_mask.shape, jnp.int32)

    live = jnp.where(counts[0] > i, 1.0, 0.0)

    @pl.when(i == 0)
    def _():
        time_f = step[...].astype(F32)
        time_low = (time_f * jax.nn.sigmoid(time_f)).astype(BF16)
        mods[...] = dot(time_low, ada[...]) + ada_bias[...].reshape(1, 3 * dim)

    mod = mods[pl.ds(i, 1), :]
    mod_out[...] = mod
    shift, scale, gate = mod[:, :dim], mod[:, dim : 2 * dim], mod[:, 2 * dim :]

    def hidden_of(part, scale, shift):
        normed, _ = normalise(part.astype(F32))
        return (normed * (1.0 + scale) + shift).astype(BF16)

    hid = hidden_of(tok[i], scale, shift)
    hid_out[...] = hid
    xz = dot(hid, win[...]) * (as_column(mask[pl.ds(i, 1), :]) * live)
    x_low = xz[:, :inner].astype(BF16)
    z = xz[:, inner:]
    z_out[...] = z
    d_branch = (cot[...].astype(F32) * gate).astype(BF16)
    d_summed = dot_nt(d_branch, wout[...]) * z * jax.nn.sigmoid(z)
    dy[0, :toks] = d_summed
    dy[1, :toks] = flip_full(d_summed)
    dy[:, toks:] = jnp.zeros((2, SPARE, inner), F32)
    xe[0] = x_low
    xe[1] = flip_low(x_low)

    @pl.when(i == slots - 1)
    def _():
        swap_along_line(me, runs, ups, downs, False)
        hidden, seen = [], []
        for item in range(slots):
            row = mods[item : item + 1, :]
            rims = jnp.concatenate([prev_tok[item], next_tok[item]], axis=0)
            hidden.append(hidden_of(rims, row[:, dim : 2 * dim], row[:, :dim]))
            prev_col = as_column(prev_mask[item : item + 1, :])[toks - HALO :]
            next_col = as_column(next_mask[item : item + 1, :])[:HALO]
            live = jnp.where(counts[0] > item, 1.0, 0.0)
            seen.append(jnp.concatenate([prev_col, next_col], axis=0) * live)
        rim_x = dot(jnp.concatenate(hidden, axis=0), win[:, :inner]) * jnp.concatenate(seen, axis=0)
        for item in range(slots):
            part = rim_x[2 * HALO * item : 2 * HALO * (item + 1)]
            rim_out[item, 0] = part[:HALO].astype(BF16)
            rim_out[item, 1] = flip_full(part[HALO:]).astype(BF16)


def columns(inner, width=128):
    return [slice(at, at + width) for at in range(0, inner, width)]


def twice(row8):
    return jnp.concatenate([row8, row8], axis=0)


def spread(ref, index):
    return twice(ref[pl.ds(index, 8, stride=0), :])


def lay_out(wide, rows, picks):
    count, toks = rows.shape
    high = rows.astype(BF16).astype(F32)
    halves = jnp.concatenate([high, rows - high], axis=0).T.astype(BF16)
    for n in range(0, count, 2):
        pair = dot(halves, picks[:, n * 128 : (n + 2) * 128])
        for t in range(0, toks, 8):
            for k in range(2):
                at = 8 * (count * (t // 8) + n + k)
                wide[at : at + 8, :] = pair[t : t + 8, k * 128 : (k + 1) * 128]


def wide_tile(wide, i, count):
    at = 8 * count * (i // 8) + i % 8
    return jnp.concatenate([wide[pl.ds(at + 64 * n, 8, stride=8), :] for n in range(count // 8)], axis=0)


def across_lanes(tile, inner):
    return jnp.concatenate([tile] * (inner // 128), axis=1)


def softplus_parts(pre):
    e = jnp.exp2(-LOG2E * jnp.abs(pre))
    more = jnp.where(e < 1e-3, e - 0.5 * e * e, jnp.log(1.0 + e))
    return jnp.maximum(pre, 0.0) + more, jax.nn.sigmoid(pre)


def bit_of(index, bit):
    return lax.rem(lax.div(index, 1 << bit), 2)


def across(axis, bit):
    me = lax.axis_index(axis)
    mine = bit_of(me, bit)
    return mine, {axis: me + (1 - 2 * mine) * (1 << bit)}


class Exchange:
    def __init__(self, runs, branch, ends, backs, totals, rate, results, group, span, pre, pre_span, sends, arrivals, sems):
        self.branch, self.rate = branch, rate
        self.sources, self.totals, self.results = (ends, backs), totals, results
        self.group, self.span, self.pre, self.pre_span = group, span, pre, pre_span
        self.sends, self.arrivals, self.sems = sends, arrivals, sems
        self.links = [across("seq", bit) for bit in range(int(math.log2(runs)))]
        self.slots = ends.shape[0]
        self.states, self.inner = rate.shape

    def flow(self, kind):
        return kind if self.branch == 0 else 1 - kind

    def targets(self):
        return [target for _, target in self.links]

    def copy(self, stage, kind):
        at = 2 * stage + kind
        return remote(
            self.sends.at[at], self.arrivals.at[at], self.sems.at[0, at], self.sems.at[1, at], self.links[stage][1]
        )

    def send(self, stage, kind):
        rows = self.slots * self.states
        at = 2 * stage + kind
        for i in range(self.slots):
            self.sends[at, i * self.states : (i + 1) * self.states, :] = self.group[kind, i].astype(BF16)
        high = self.span[kind].astype(BF16).astype(F32)
        self.sends[at, rows:, :] = jnp.concatenate([high, self.span[kind] - high], axis=0).astype(BF16)
        self.copy(stage, kind).start()

    def join(self, stage, kind, last):
        mine = self.links[stage][0]
        self.copy(stage, kind).wait()
        at = 2 * stage + kind
        earlier = (mine == 1) if self.flow(kind) == 0 else (mine == 0)
        both = self.arrivals[at, self.slots * self.states :, :].astype(F32)
        length = both[: both.shape[0] // 2] + both[both.shape[0] // 2 :]
        own_span, pre_span = self.span[kind], self.pre_span[kind]
        second_span = jnp.where(earlier, own_span, length)
        rate = self.rate[...] * -LOG2E
        for i in range(self.slots):
            state = self.arrivals[at, i * self.states : (i + 1) * self.states, :].astype(F32)
            before = self.pre[kind, i]
            self.pre[kind, i] = jnp.where(earlier, state * jnp.exp2(rate * pre_span[i : i + 1]) + before, before)
            if not last:
                own = self.group[kind, i]
                first, second = jnp.where(earlier, state, own), jnp.where(earlier, own, state)
                self.group[kind, i] = first * jnp.exp2(rate * second_span[i : i + 1]) + second
        self.pre_span[kind] = jnp.where(earlier, length + pre_span, pre_span)
        if not last:
            self.span[kind] = own_span + length

    def points(self):
        count = len(self.links)

        def begin():
            self.pre[...] = jnp.zeros(self.pre.shape, F32)
            self.pre_span[...] = jnp.zeros(self.pre_span.shape, F32)
            self.span[...] = jnp.zeros(self.span.shape, F32)
            for kind in range(2):
                for i in range(self.slots):
                    self.group[kind, i] = self.sources[kind][i]
                    self.span[kind, i : i + 1, :] = self.totals[i][:1]
                if count:
                    self.send(0, kind)

        def step(stage):
            last = stage == count - 1
            for kind in range(2):
                self.join(stage, kind, last)
                if not last:
                    self.send(stage + 1, kind)

        def end():
            for kind in range(2):
                for i in range(self.slots):
                    self.results[kind][i] = self.pre[kind, i]

        return [begin] + [functools.partial(step, stage) for stage in range(count)] + [end]


def exchange_shapes(runs, slots, states, inner):
    pairs = max(int(math.log2(runs)), 1)
    span_rows = -(-slots // 8) * 8
    return [
        pltpu.VMEM((2, slots, states, inner), F32), pltpu.VMEM((2, span_rows, inner), F32),
        pltpu.VMEM((2, slots, states, inner), F32), pltpu.VMEM((2, span_rows, inner), F32),
        pltpu.VMEM((2 * pairs, slots * states + 2 * span_rows, inner), BF16),
        pltpu.VMEM((2 * pairs, slots * states + 2 * span_rows, inner), BF16),
        pltpu.SemaphoreType.DMA((2, 2 * pairs)),
    ]


def beside(points, step, first, count):
    for at in range(min(len(points), count)):
        todo = points[at:] if at == count - 1 else points[at : at + 1]

        @pl.when(step == first + at)
        def _():
            for point in todo:
                point()


def first_kernel(
    runs, slots, ahead, xe, dy, taps, tap_bias, x_rows, dt_rows, dt_bias, rate,
    act_out, planes, proj_out, last_out, starts_out, tiles, weights, first_in,
    x_cols, dx, decay, through, rate2, wide, picks, ends, backs, totals, first_rate, *exchange_scratch,
):
    toks, inner = xe.shape
    states = rate.shape[0]
    blocks = toks // BLK
    rank = WIDE_RANK
    xwt, dtw = weights.at[: weights.shape[0] - rank], weights.at[weights.shape[0] - rank :]
    delta_out, sig_out, dsilu_out = (planes.at[at] for at in range(3))
    end_out, back_out = last_out.at[:states], last_out.at[states : 2 * states]
    tap_count = taps.shape[0]
    branch, item = pl.program_id(0), pl.program_id(1)
    results = (first_in.at[0], first_in.at[1])
    exchange = Exchange(runs, 0, ends, backs, totals, first_rate, results, *exchange_scratch)

    @pl.when((branch == 0) & (item == 0))
    def _():
        greet(exchange.targets())
        first_rate[...] = rate[...]

    beside(exchange.points(), branch * slots + item, slots, slots)

    @pl.when(item == 0)
    def _():
        rate2[...] = rate[...] * -LOG2E
        picks[...] = (
            lax.broadcasted_iota(jnp.int32, picks.shape, 0) % (2 * states)
            == lax.broadcasted_iota(jnp.int32, picks.shape, 1) // 128
        ).astype(BF16)
        held = dt_rows.shape[0]
        rows = x_rows[...].astype(F32)
        gap = jnp.zeros((rank - held, inner), F32)
        wide = [rows[:held], gap, rows[held:], dt_rows[...].astype(F32), gap]
        weights[...] = jnp.concatenate(wide, axis=0).astype(BF16)

    tap_row, dt_row = tap_bias[pl.ds(branch, 1), :], dt_bias[pl.ds(branch, 1), :]
    for cols in columns(inner):
        at_col = cols.start // 128
        x_cols[at_col] = jnp.concatenate([ahead[:, cols], xe[:, cols]], axis=0).astype(F32)
        parts = []
        for row in range(0, toks, 8):
            part = tap_row[:, cols]
            for k in range(tap_count):
                part = part + taps[k : k + 1, cols] * x_cols[at_col, pl.ds(HALO - tap_count + 1 + k + row, 8), :]
            parts.append(part)
        conv = jnp.concatenate(parts, axis=0)
        open_part = jax.nn.sigmoid(conv)
        act_f = conv * open_part
        act_out[:, cols] = act_f.astype(BF16)
        dsilu_out[:, cols] = open_part + act_f * (1.0 - open_part)
    proj = dot_nt(xwt[...], act_out[...])
    proj_out[...] = proj
    dt_low = proj[:rank, :].astype(BF16)
    for cols in columns(inner, 256):
        pre = dot_tn(dt_low, dtw[:, cols]) + dt_row[:, cols]
        delta, slope = softplus_parts(pre)
        delta_out[:, cols] = delta
        sig_out[:, cols] = slope
        dx[:toks, cols] = delta * act_out[:, cols].astype(F32)
    lay_out(wide, proj[rank:, :], picks)
    end_out[...] = jnp.zeros((states, inner), F32)
    back_out[...] = jnp.zeros((states, inner), F32)
    through[...] = jnp.zeros((8, inner), F32)

    def one_block(j, slot):
        t0 = pl.multiple_of(j * BLK, BLK)
        dr, xr, yr = (ref.at[pl.ds(t0, BLK), :] for ref in (delta_out, dx, dy))
        count = 2 * states
        wide_rows = wide.at[pl.ds(pl.multiple_of(j * (BLK * count), BLK * count), BLK * count), :]
        s = end_out[...]
        before = through[...]
        starts_out[j] = jnp.concatenate([s, before], axis=0)
        rates = rate2[...]
        for i in range(BLK):
            a = jnp.exp2(spread(dr, i) * rates)
            decay[slot, i] = a
            tile = wide_tile(wide_rows, i, count)
            tiles[t0 + i] = tile
            s = a * s + spread(xr, i) * across_lanes(tile[:states], inner)
        end_out[...] = s
        m = jnp.zeros((states, inner), F32)
        for i in reversed(range(BLK)):
            m = decay[slot, i] * (m + spread(yr, i) * across_lanes(tiles[t0 + i, states:], inner))
        back_out[...] = back_out[...] + m * jnp.exp2(twice(before) * rates)
        through[...] = before + jnp.sum(dr[...], axis=0, keepdims=True)

    def block_step(k, _):
        one_block(2 * k, 0)
        one_block(2 * k + 1, 1)
        return 0

    lax.fori_loop(0, blocks // 2, block_step, 0)
    last_out[2 * states :, :] = through[...]

    @pl.when(branch == 0)
    def _():
        ends[item] = end_out[...]
        backs[item] = back_out[...]
        totals[item] = through[:1, :]


def second_kernel(
    runs, first_in, lasts, last_rate, starts, tiles, rate, ahead, xe, act, planes, dy, proj, weights, taps, skip,
    y_out, dx_out, rims, grads,
    rate2, carry, dxs, bdiag, cdiag, decay, states_low, kept_low, lam_low, rq_low, qd_low, dots, racc, gsum, hsum, db, dc,
    d_cols, d_pre_low, s_in, s_last, lam_last, *exchange_scratch,
):
    toks, inner = xe.shape
    states = rate.shape[0]
    blocks = toks // BLK
    rank = WIDE_RANK
    xwt, dtw = weights.at[: weights.shape[0] - rank], weights.at[weights.shape[0] - rank :]
    delta, sig, dsilu = (planes.at[at] for at in range(3))
    tap_count = taps.shape[0]
    held = (grads.shape[0] - 3 * states - 8) // 2
    xp_grad, dtp_grad = grads.at[: held + 2 * states], grads.at[held + 2 * states : 2 * held + 2 * states]
    at = 2 * held + 2 * states
    rate_grad, row_grads = grads.at[at : at + states], grads.at[at + states : at + states + 8]
    tapb_at, skip_at, dtb_at = (slice(tap_count + row, tap_count + row + 1) for row in range(3))
    item = pl.program_id(1)
    branch = pl.program_id(0)
    slots = lasts.shape[0]
    ends, backs = lasts.at[:, :states], lasts.at[:, states : 2 * states]
    totals = lasts.at[:, 2 * states :]
    exchange = Exchange(runs, 1, ends, backs, totals, last_rate, (s_last, lam_last), *exchange_scratch)

    @pl.when((item == 0) & (branch == 0))
    def _():
        greet(exchange.targets())

    beside(exchange.points(), branch * slots + item, 0, slots)

    @pl.when(branch == 0)
    def _():
        s_in[...] = first_in[0, item]
        carry[...] = first_in[1, item]

    @pl.when(branch == 1)
    def _():
        s_in[...] = s_last[item]
        carry[...] = lam_last[item]

    gain = skip[pl.ds(pl.program_id(0), 1), :]
    rate2[...] = rate[...] * -LOG2E
    width = BLK * states

    @pl.when(item == 0)
    def _():
        grads[...] = jnp.zeros(grads.shape, F32)

    for cols in columns(inner):
        dxs[:toks, cols] = delta[:, cols] * act[:, cols].astype(F32)
    pair_rows = 2 * states

    def inner_index(rows):
        at = lax.broadcasted_iota(jnp.int32, (rows, width), 1)
        token = lax.div(at, pair_rows) * 2 + lax.div(lax.rem(at, 16), 8)
        return token, lax.div(lax.rem(at, pair_rows), 16) * 8 + lax.rem(at, 8)

    fold = (inner_index(states)[1] == lax.broadcasted_iota(jnp.int32, (states, width), 0)).astype(BF16)
    own = lax.rem(lax.broadcasted_iota(jnp.int32, (toks, width), 0), BLK) == inner_index(toks)[0]
    bdiag[:toks, :] = jnp.where(own, dot_tn(proj[rank : rank + states, :].astype(BF16), fold), 0.0).astype(BF16)
    cdiag[...] = jnp.where(own, dot_tn(proj[rank + states :, :].astype(BF16), fold), 0.0).astype(BF16)
    mine = own[:BLK]
    picks = mine.astype(BF16)
    ones = jnp.ones((BLK, 128), BF16)
    racc[...] = jnp.zeros((states, inner), F32)

    def lane_sum(wide):
        part = [wide[:, at : at + 128] for at in range(0, inner, 128)]
        while len(part) > 1:
            pairs = [part[at] + part[at + 1] for at in range(0, len(part) - 1, 2)]
            part = pairs + part[2 * len(pairs) :]
        return part[0]

    def products(slot, j):
        t0 = pl.multiple_of(j * BLK, BLK)
        y_out[pl.ds(t0, BLK), :] = dot(cdiag[pl.ds(t0, BLK), :], states_low[slot])
        half = width // 2
        rows = bdiag[pl.ds(t0, BLK), :]
        gsum[pl.ds(t0, BLK), :] = dot(rows[:, half:], lam_low[slot, half:]) + dot(rows[:, :half], lam_low[slot, :half])
        hsum[pl.ds(t0, BLK), :] = dot(picks[:, half:], rq_low[slot, half:]) + dot(picks[:, :half], rq_low[slot, :half])
        racc[...] += dot(fold[:, : BLK // 4 * states], qd_low[slot])
        dc[pl.ds(t0, BLK), :] = jnp.where(mine, dot_nt(ones, dots[slot, :, :128]), 0.0).astype(BF16)
        db[pl.ds(t0, BLK), :] = jnp.where(mine, dot_nt(ones, dots[slot, :, 128:]), 0.0).astype(BF16)

    def one_block(slot, j):
        t0 = pl.multiple_of(j * BLK, BLK)
        dr, xr, yr = (ref.at[pl.ds(t0, BLK), :] for ref in (delta, dxs, dy))
        tile = tiles.at[pl.ds(t0, BLK)]
        r2 = rate2[...]
        groups = [slice(at, at + 8) for at in range(0, states, 8)]
        begin = starts[j]
        s = begin[:states] + s_in[...] * jnp.exp2(twice(begin[states:]) * r2)

        def both(first, second):
            return jnp.concatenate([first, second], axis=0).astype(BF16)

        def pair(ref, i):
            return both(ref[pl.ds(i, 8, stride=0), :], ref[pl.ds(i + 1, 8, stride=0), :])

        for i in range(0, BLK, 2):
            kept, after = [], []
            for t in (i, i + 1):
                a = jnp.exp2(spread(dr, t) * r2)
                decay[slot, t] = a
                kept.append(a * s)
                s = kept[-1] + spread(xr, t) * across_lanes(tile[t, :states], inner)
                after.append(s)
            y_pair = pair(yr, i)
            for number, group in enumerate(groups):
                rows = slice(i * states + 16 * number, i * states + 16 * (number + 1))
                s_low = both(after[0][group], after[1][group])
                states_low[slot, rows, :] = s_low
                kept_low[slot, rows, :] = both(kept[0][group], kept[1][group])
                dots[slot, rows, :128] = lane_sum(s_low * y_pair)
        cr = carry[...]
        r_low = [both(rate[group, :], rate[group, :]) for group in groups]
        qds = [[] for _ in groups]
        for i in reversed(range(0, BLK, 2)):
            lams = []
            for t in (i + 1, i):
                lam = cr + spread(yr, t) * across_lanes(tile[t, states:], inner)
                cr = decay[slot, t] * lam
                lams.append(lam)
            x_pair, d_pair = pair(xr, i), pair(dr, i)
            for number, group in enumerate(groups):
                rows = slice(i * states + 16 * number, i * states + 16 * (number + 1))
                l_low = both(lams[1][group], lams[0][group])
                lam_low[slot, rows, :] = l_low
                dots[slot, rows, 128:] = lane_sum(l_low * x_pair)
                q = l_low * kept_low[slot, rows, :]
                rq_low[slot, rows, :] = q * r_low[number]
                qds[number].append(q * d_pair)
                if i % 8 == 0:
                    at = i // 8 * pair_rows + 16 * number
                    part = qds[number]
                    qd_low[slot, at : at + 16, :] = (part[0] + part[1]) + (part[2] + part[3])
                    qds[number] = []
        carry[...] = cr

    def block_step(k, _):
        j = blocks - 1 - 2 * k
        for slot in range(2):
            one_block(slot, j - slot)
            products(slot, j - slot)
        return 0

    lax.fori_loop(0, blocks // 2, block_step, 0)
    rate_grad[...] += -racc[...]
    for cols in columns(inner):
        act_f = act[:, cols].astype(F32)
        row_grads[skip_at, cols] += jnp.sum(dy[:toks, cols] * act_f, axis=0, keepdims=True)
        y_out[:, cols] += gain[:, cols] * act_f
        d_pre = (act_f * gsum[:toks, cols] - hsum[:toks, cols]) * sig[:, cols]
        row_grads[dtb_at, cols] += jnp.sum(d_pre, axis=0, keepdims=True)
        d_pre_low[:, cols] = d_pre.astype(BF16)
    dtp_grad[...] += dot(proj[:rank, :].astype(BF16), d_pre_low[...])[:held]
    d_proj = jnp.concatenate(
        [dot_nt(dtw[...], d_pre_low[...]), dot_nt(fold, db[:toks, :]), dot_nt(fold, dc[:toks, :])], axis=0
    ).astype(BF16)
    xp_new = dot(d_proj, act[...])
    xp_grad[:held, :] += xp_new[:held]
    xp_grad[held:, :] += xp_new[rank:]
    d_cols[:, :HALO, :] = jnp.zeros((inner // 128, HALO, 128), F32)
    d_cols[:, HALO + toks :, :] = jnp.zeros((inner // 128, HALO, 128), F32)
    for wide_cols in columns(inner, 256):
        through = dot_tn(d_proj, xwt[:, wide_cols])
        for at in columns(256):
            cols = slice(wide_cols.start + at.start, wide_cols.start + at.stop)
            d_act = delta[:, cols] * gsum[:toks, cols] + gain[:, cols] * dy[:toks, cols] + through[:, at]
            d_conv = d_act * dsilu[:, cols]
            row_grads[tapb_at, cols] += jnp.sum(d_conv, axis=0, keepdims=True)
            x_f = jnp.concatenate([ahead[:, cols], xe[:, cols]], axis=0).astype(F32)
            at_col = cols.start // 128
            d_cols[at_col, HALO : HALO + toks, :] = d_conv
            sums = [jnp.zeros((8, 128), F32) for _ in range(tap_count)]
            for row in range(HALO - 8, HALO + toks, 8):
                part = jnp.zeros((8, 128), F32)
                for k in range(tap_count):
                    moved = d_cols[at_col, pl.ds(row + tap_count - 1 - k, 8), :]
                    part = part + taps[k : k + 1, cols] * moved
                    sums[k] = sums[k] + moved * x_f[row : row + 8]
                if row < HALO:
                    rims[branch, item, :, cols] = part
                else:
                    dx_out[row - HALO : row - HALO + 8, cols] = part
            for k in range(tap_count):
                row_grads[k : k + 1, cols] += jnp.sum(sums[k], axis=0, keepdims=True)


LAST_ROWS = 16
PART_ROWS = 512


class Ring:
    def __init__(self, bits):
        self.bits = bits
        self.size = 1 << len(bits)
        self.digits = [bit_of(lax.axis_index(axis), bit) for axis, bit in bits]
        self.place = sum(digit * (1 << at) for at, digit in enumerate(self.digits))

    def target(self, ahead):
        place = lax.rem(self.place + ahead, self.size)
        where = {}
        for at, (axis, bit) in enumerate(self.bits):
            base = where.get(axis, lax.axis_index(axis))
            where[axis] = base + (bit_of(place, at) - self.digits[at]) * (1 << bit)
        return where, place

    def targets(self):
        return [self.target(ahead)[0] for ahead in range(1, self.size)]


def stage_rings(runs, groups):
    bits = [("seq", bit) for bit in range(int(math.log2(runs)))] + [("dp", bit) for bit in range(int(math.log2(groups)))]
    return [Ring(bits[:1])] + [Ring(bits[at : at + 2]) for at in range(1, len(bits), 2)]


def part_count(rows):
    return -(-rows // PART_ROWS)


def buffer_rows(runs, groups):
    bits = int(math.log2(runs)) + int(math.log2(groups))
    size, total = PART_ROWS, 0
    for members in [2] + [1 << min(2, bits - at) for at in range(1, bits, 2)]:
        moved = size // members if size >= members * LAST_ROWS else size
        total += moved * (members - 1)
        size = moved
    return total


def reduce_shapes(parts, dim, runs, groups):
    bits = int(math.log2(runs)) + int(math.log2(groups))
    stages = 1 + bits // 2
    room = parts * buffer_rows(runs, groups)
    sems = pltpu.SemaphoreType.DMA((parts, 2 * stages, 3))
    return [
        pltpu.VMEM((parts * PART_ROWS, dim), F32), pltpu.VMEM((room, dim), BF16), pltpu.VMEM((room, dim), BF16),
        pltpu.VMEM((parts * PART_ROWS, dim), BF16), sems, sems,
    ]


class Reduction:
    def __init__(self, rings, turns, segments, acc, sends, arrivals, gathered, send_sem, recv_sem):
        self.rings = rings
        self.count = len(rings)
        self.parts = len(turns)
        self.segments = segments
        self.acc, self.sends, self.arrivals, self.gathered = acc, sends, arrivals, gathered
        self.send_sem, self.recv_sem = send_sem, recv_sem
        room = sends.shape[0] // self.parts
        self.steps = []
        for part, turn in enumerate(turns):
            later = rings[1:]
            turn = turn % max(len(later), 1)
            order = rings[:1] + later[turn:] + later[:turn]
            start, size, at = part * PART_ROWS, PART_ROWS, part * room
            steps = []
            for ring in order:
                split = size >= ring.size * LAST_ROWS
                moved = size // ring.size if split else size
                keep = pl.multiple_of(start + ring.place * moved, LAST_ROWS) if split else start
                steps.append((ring, start, split, moved, keep, at))
                at += moved * (ring.size - 1)
                start, size = keep, moved
            self.steps.append(steps)

    def assemble(self, part):
        low, high = part * PART_ROWS, (part + 1) * PART_ROWS
        at = 0
        for get, size in self.segments:
            first, last = max(at, low), min(at + size, high)
            if first < last:
                self.acc[first:last, :] = get(first - at, last - first)
            at += size
        if at < high:
            first = max(at, low)
            self.acc[first:high, :] = jnp.zeros((high - first, self.acc.shape[1]), F32)

    def scatter_copy(self, part, stage, ahead):
        ring, _, _, moved, _, at = self.steps[part][stage]
        at += (ahead - 1) * moved
        return remote(
            self.sends.at[pl.ds(at, moved), :], self.arrivals.at[pl.ds(at, moved), :],
            self.send_sem.at[part, stage, ahead - 1], self.recv_sem.at[part, stage, ahead - 1], ring.target(ahead)[0],
        )

    def scatter(self, part, stage):
        ring, start, split, moved, _, at = self.steps[part][stage]
        for ahead in range(1, ring.size):
            place = ring.target(ahead)[1]
            away = pl.multiple_of(start + place * moved, LAST_ROWS) if split else start
            here = at + (ahead - 1) * moved
            self.sends[here : here + moved, :] = self.acc[pl.ds(away, moved), :].astype(BF16)
            self.scatter_copy(part, stage, ahead).start()

    def settle(self, part, stage):
        ring, _, split, moved, keep, at = self.steps[part][stage]
        for ahead in range(1, ring.size):
            self.scatter_copy(part, stage, ahead).wait()
        held = self.acc[pl.ds(keep, moved), :]
        came = [
            self.arrivals[at + (ahead - 1) * moved : at + ahead * moved, :].astype(F32) for ahead in range(1, ring.size)
        ]
        if split:
            for part in came:
                held = held + part
        else:
            values = [held.astype(BF16).astype(F32)] + came
            total = jnp.zeros_like(held)
            for place in range(ring.size):
                behind = lax.rem(ring.place - place + ring.size, ring.size)
                chosen = values[0]
                for ahead in range(1, ring.size):
                    chosen = jnp.where(behind == ahead, values[ahead], chosen)
                total = total + chosen
            held = total
        self.acc[pl.ds(keep, moved), :] = held

    def gather_copies(self, part, stage):
        ring, _, split, moved, keep, _ = self.steps[part][stage]
        here = self.gathered.at[pl.ds(keep, moved), :]
        return [
            remote(
                here, here, self.send_sem.at[part, self.count + stage, ahead - 1],
                self.recv_sem.at[part, self.count + stage, ahead - 1], ring.target(ahead)[0],
            )
            for ahead in range(1, ring.size)
            if split
        ]

    def points(self):
        def begin():
            for part in range(self.parts):
                self.assemble(part)
                self.scatter(part, 0)

        def split(stage):
            for part in range(self.parts):
                self.settle(part, stage - 1)
                self.scatter(part, stage)

        def turn():
            for part in range(self.parts):
                self.settle(part, self.count - 1)
                _, _, _, moved, keep, _ = self.steps[part][-1]
                self.gathered[pl.ds(keep, moved), :] = self.acc[pl.ds(keep, moved), :].astype(BF16)
                for copy in self.gather_copies(part, self.count - 1):
                    copy.start()

        def join(stage):
            for part in range(self.parts):
                for copy in self.gather_copies(part, stage + 1):
                    copy.wait()
                if stage >= 0:
                    for copy in self.gather_copies(part, stage):
                        copy.start()

        points = [begin]
        points += [functools.partial(split, stage) for stage in range(1, self.count)]
        points += [turn]
        return points + [functools.partial(join, stage) for stage in reversed(range(-1, self.count - 1))]


def big_segments(ref, dim):
    return [
        (lambda at, size, lane=lane: ref[at : at + size, lane : lane + dim], ref.shape[0])
        for lane in range(0, ref.shape[1], dim)
    ]


def small_segments(ref, dim):
    return [
        (lambda at, size, branch=branch, lane=lane: ref[branch, at : at + size, lane : lane + dim], ref.shape[1])
        for lane in range(0, ref.shape[2], dim)
        for branch in range(2)
    ]


def tail_kernel(
    plan, tok, cot, mod, mask, counts, hid, z_in, y, dx, rims, win, wout, step,
    grads,
    mixed, d_tokens, result, x_result, factors, own_rows,
    late, rim_send, rim_recv, dz, d_xs, hids, out_grad, z_grad, x_grad, mod_sum, mod_in, table, small_send, small_recv, *reduce_scratch,
):
    runs, groups, slots = plan
    me = lax.axis_index("seq")
    downs = [(rims.at[0], late.at[0], rim_send.at[0], rim_recv.at[0])]
    ups = [(rims.at[1], late.at[1], rim_send.at[1], rim_recv.at[1])]
    dim = tok.shape[-1]
    toks, inner = z_in.shape
    now = pl.program_id(0)
    i = lax.rem(now, slots)
    rings = stage_rings(runs, groups)
    seq_ring = Ring([("seq", bit) for bit in range(int(math.log2(runs)))])
    dp_ring = Ring([("dp", bit) for bit in range(int(math.log2(groups)))])
    half = len(reduce_scratch) // 2
    smalls = small_segments(grads, dim)
    segments = big_segments(out_grad, dim) + big_segments(z_grad, dim) + smalls
    main = Reduction(rings, [part % 3 // 2 for part in range(result.shape[0] // PART_ROWS)], segments, *reduce_scratch[:half])
    rest = Reduction(rings, [part % 2 for part in range(x_result.shape[0] // PART_ROWS)], big_segments(x_grad, dim), *reduce_scratch[half:])
    main_points, rest_points = main.points(), rest.points()

    @pl.when(now == 0)
    def _():
        greet_line(me, runs, [target for ring in rings + [seq_ring, dp_ring] for target in ring.targets()])
        swap_along_line(me, runs, ups, downs, True)

        @pl.when(me == 0)
        def _():
            late[1] = jnp.zeros(late.shape[1:], F32)

        @pl.when(me == runs - 1)
        def _():
            late[0] = jnp.zeros(late.shape[1:], F32)

        out_grad[...] = jnp.zeros(out_grad.shape, F32)
        z_grad[...] = jnp.zeros(z_grad.shape, F32)
        x_grad[...] = jnp.zeros(x_grad.shape, F32)
        mod_sum[...] = jnp.zeros(mod_sum.shape, F32)

    scale, gate = mod[:, dim : 2 * dim], mod[:, 2 * dim :]
    valid = as_column(mask[pl.ds(i, 1), :]) * jnp.where(counts[0] > i, 1.0, 0.0)
    mod_rows = pl.ds(pl.multiple_of(8 * i, 8), 8)

    @pl.when(now < slots)
    def _():
        cot_f = cot[...].astype(F32)
        z = z_in[...]
        z_sig = jax.nn.sigmoid(z)
        z_silu = z * z_sig
        summed = y[0] + flip_full(y[1])
        gated = (summed * z_silu).astype(BF16)
        branch_out = dot(gated, wout[...])
        mixed[...] = (tok[...].astype(F32) + gate * branch_out).astype(BF16)
        d_branch = (cot_f * gate).astype(BF16)
        out_grad[...] += dot_tn(gated, d_branch)
        d_zgate = dot_nt(d_branch, wout[...]) * summed * (z_sig + z_silu * (1.0 - z_sig))
        d_low = (d_zgate * valid).astype(BF16)
        dz[i] = d_low
        z_grad[...] += dot_tn(hid[...], d_low)
        hids[i] = hid[...]
        d_gate = jnp.sum(cot_f * branch_out, axis=0, keepdims=True)
        mod_sum[mod_rows, :] = jnp.concatenate([jnp.zeros((2, dim), F32), d_gate, jnp.zeros((5, dim), F32)], axis=0)

    @pl.when(now == slots)
    def _():
        main_points[0]()
        swap_along_line(me, runs, ups, downs, False)
        edge = late.shape[2]

        def with_late(part, extra):
            return jnp.concatenate([part[: toks - edge], part[toks - edge :] + extra], axis=0)

        for item in range(slots):
            seen = as_column(mask[item : item + 1, :]) * jnp.where(counts[0] > item, 1.0, 0.0)
            d_x = with_late(dx[item, 0], late[0, item]) + flip_full(with_late(dx[item, 1], late[1, item]))
            d_low = (d_x * seen).astype(BF16)
            d_xs[item] = d_low
            x_grad[...] += dot_tn(hids[item], d_low)
        rest_points[0]()
        main_points[1]()

    @pl.when(now >= slots)
    def _():
        d_hidden = dot_nt(d_xs[i], win[:, :inner]) + dot_nt(dz[i], win[:, inner:])
        normed, inv_std = normalise(tok[...].astype(F32))
        d_shift = jnp.sum(d_hidden, axis=0, keepdims=True)
        d_scale = jnp.sum(d_hidden * normed, axis=0, keepdims=True)
        mod_sum[mod_rows, :] += jnp.concatenate([d_shift, d_scale, jnp.zeros((6, dim), F32)], axis=0)
        d_normed = d_hidden * (1.0 + scale)
        d_tokens[...] = cot[...].astype(F32) + inv_std * (
            d_normed
            - jnp.mean(d_normed, axis=-1, keepdims=True)
            - normed * jnp.mean(d_normed * normed, axis=-1, keepdims=True)
        )

    @pl.when(now == slots)
    def _():
        rest_points[1]()

    def sum_copies():
        return [
            remote(mod_sum, mod_in.at[ahead - 1], small_send.at[ahead - 1], small_recv.at[ahead - 1], seq_ring.target(ahead)[0])
            for ahead in range(1, seq_ring.size)
        ]

    def table_copies():
        at = pl.multiple_of(dp_ring.place * 16, 16)
        here = table.at[pl.ds(at, 16), :]
        base = seq_ring.size - 1
        return [
            remote(here, here, small_send.at[base + ahead - 1], small_recv.at[base + ahead - 1], dp_ring.target(ahead)[0])
            for ahead in range(1, dp_ring.size)
        ]

    def start_small():
        for copy in sum_copies():
            copy.start()

    def turn_small():
        for copy in sum_copies():
            copy.wait()
        values = [mod_sum[...]] + [mod_in[ahead - 1] for ahead in range(1, seq_ring.size)]
        total = jnp.zeros(mod_sum.shape, F32)
        for place in range(seq_ring.size):
            behind = lax.rem(seq_ring.place - place + seq_ring.size, seq_ring.size)
            chosen = values[0]
            for ahead in range(1, seq_ring.size):
                chosen = jnp.where(behind == ahead, values[ahead], chosen)
            total = total + chosen
        time_f = step[...].astype(F32)
        time_low = time_f * jax.nn.sigmoid(time_f)
        lines = [total[8 * item : 8 * item + 3] for item in range(slots)] + [time_low]
        lines.append(jnp.zeros((16 - 4 * slots, dim), F32))
        own = jnp.concatenate(lines, axis=0).astype(BF16)
        own_rows[...] = own
        table[pl.ds(pl.multiple_of(dp_ring.place * 16, 16), 16), :] = own
        for copy in table_copies():
            copy.start()

    def end_small():
        for copy in table_copies():
            copy.wait()
        factors[...] = table[...]

    @pl.when(now == 2 * slots - 1)
    def _():
        start_small()
        for at in range(2, len(main_points)):
            main_points[at]()
            if at == 2:
                turn_small()
            rest_points[at]()
        end_small()
        result[...] = main.gathered[...]
        x_result[...] = rest.gathered[...]


def finish_kernel(
    mixed_in, tokens_in, outs, zs, xs, smalls, factors, own, step, ada,
    mixed, d_tokens, grad_time, grad_ada, grad_ada_bias, in_grad, tap_grad, tapb_grad, xp_grad, dtp_grad, dtb_grad, rate_grad, skip_grad, out_grad,
):
    dim, inner = in_grad.shape[0], rate_grad.shape[2]
    slots = step.shape[0]
    now = pl.program_id(0)
    mixed[...] = mixed_in[...]
    d_tokens[...] = tokens_in[...]
    out_grad[...] = outs[...].astype(F32)
    in_grad[...] = jnp.where(now < inner // dim, xs[...], zs[...]).astype(F32)
    table = factors[...]
    length = table.shape[0]

    for part in range(3):

        @pl.when(now == part)
        def _():
            row = lax.broadcasted_iota(jnp.int32, (length, length), 0)
            col = lax.broadcasted_iota(jnp.int32, (length, length), 1)
            item = row % 16 - 3 * slots
            wanted = row // 16 * 16 + 3 * item + part
            mods = dot(((col == wanted) & (item >= 0) & (item < slots)).astype(BF16), table)
            lanes = slice(part * dim, (part + 1) * dim)
            grad_ada[...] = dot_tn(table, mods.astype(BF16))
            grad_ada_bias[lanes] = jnp.sum(mods, axis=0)
            mine = own[...].astype(F32)
            picked = jnp.concatenate([mine[3 * i + part : 3 * i + part + 1] for i in range(slots)], axis=0)
            d_time = dot_nt(picked.astype(BF16), ada[...])
            grad_time[...] = d_time if part == 0 else grad_time[...] + d_time

    @pl.when(now == 3)
    def _():
        time_f = step[...].astype(F32)
        time_sig = jax.nn.sigmoid(time_f)
        grad_time[...] = grad_time[...] * time_sig * (1.0 + time_f * (1.0 - time_sig))
        at = 0
        for first in range(0, inner, dim):
            lanes = slice(first, first + dim)
            for branch in range(2):
                for ref in (xp_grad, dtp_grad, rate_grad, tap_grad):
                    size = ref.shape[1]
                    ref[branch, :, lanes] = smalls[at : at + size, :].astype(F32)
                    at += size
                for ref in (tapb_grad, skip_grad, dtb_grad):
                    ref[branch : branch + 1, lanes] = smalls[at : at + 1, :].astype(F32)
                    at += 1
                at += 1


def params(**more):
    return pltpu.CompilerParams(vmem_limit_bytes=VMEM_LIMIT, **more)


def spec(block, index):
    return pl.BlockSpec(block, index)


def per_device(
    tokens, timestep, counts, token_mask, ada_weight, ada_bias, input_weight, conv_weight, conv_bias, x_weight, dt_weight,
    dt_bias, decay_rate, skip_gain, output_weight, cotangent,
):
    slots, toks, dim = tokens.shape
    inner = output_weight.shape[0]
    rank = dt_weight.shape[1]
    states = decay_rate.shape[1]
    tap_count = conv_weight.shape[1]
    wide_rank = WIDE_RANK
    proj_rows = wide_rank + 2 * states
    blocks = toks // BLK
    runs = lax.axis_size("seq")
    groups = lax.axis_size("dp")
    x_rows = jnp.swapaxes(x_weight, 1, 2)

    def item(*block):
        return spec((None,) + block, lambda i: (i,) + (0,) * len(block))

    def whole(*block):
        return spec(block, lambda *_: (0,) * len(block))

    xe, dy, z_gate, hid, modulate, ahead = pl.pallas_call(
        functools.partial(enter_kernel, runs),
        grid=(slots,),
        in_specs=[
            whole(slots, toks, dim), item(toks, dim), whole(slots, toks), pl.BlockSpec(memory_space=pltpu.SMEM), whole(slots, dim), whole(dim, 3 * dim),
            whole(3 * dim), whole(dim, 2 * inner), whole(inner, dim),
        ],
        out_specs=[
            item(2, toks, inner), item(2, toks + SPARE, inner), item(toks, inner), item(toks, dim), item(1, 3 * dim),
            whole(slots, 2, HALO, inner),
        ],
        out_shape=[
            jax.ShapeDtypeStruct((slots, 2, toks, inner), BF16),
            jax.ShapeDtypeStruct((slots, 2, toks + SPARE, inner), F32),
            jax.ShapeDtypeStruct((slots, toks, inner), F32),
            jax.ShapeDtypeStruct((slots, toks, dim), BF16),
            jax.ShapeDtypeStruct((slots, 1, 3 * dim), F32),
            jax.ShapeDtypeStruct((slots, 2, HALO, inner), BF16),
        ],
        scratch_shapes=[
            pltpu.VMEM((slots, 3 * dim), F32),
            pltpu.VMEM((slots, HALO, dim), BF16), pltpu.VMEM((slots, HALO, dim), BF16), pltpu.VMEM((slots, toks), jnp.int32),
            pltpu.VMEM((slots, toks), jnp.int32), pltpu.SemaphoreType.DMA((4,)), pltpu.SemaphoreType.DMA((4,)),
        ],
        compiler_params=params(collective_id=1, has_side_effects=True),
        name="enter",
    )(
        tokens, cotangent, token_mask, counts, timestep, ada_weight, ada_bias, input_weight, output_weight,
    )

    def unit(*block):
        return spec((None, None) + block, lambda b, i: (i, b) + (0,) * len(block))

    def branch(*block):
        return spec((None,) + block, lambda b, i: (b,) + (0,) * len(block))

    def unit_shape(*block, kind=F32):
        return jax.ShapeDtypeStruct((slots, 2) + block, kind)

    act, planes, proj, lasts, starts, tiles, weights, first_in = pl.pallas_call(
        functools.partial(first_kernel, runs, slots),
        grid=(2, slots),
        in_specs=[
            unit(HALO, inner), unit(toks, inner), unit(toks + SPARE, inner), branch(tap_count, inner), whole(2, inner),
            branch(rank + 2 * states, inner), branch(rank, inner), whole(2, inner), branch(states, inner),
        ],
        out_specs=[
            unit(toks, inner), unit(3, toks, inner), unit(proj_rows, toks), unit(2 * states + 8, inner),
            unit(blocks, states + 8, inner), unit(toks, 2 * states, 128), branch(proj_rows + wide_rank, inner),
            whole(2, slots, states, inner),
        ],
        out_shape=[
            unit_shape(toks, inner, kind=BF16), unit_shape(3, toks, inner), unit_shape(proj_rows, toks),
            unit_shape(2 * states + 8, inner), unit_shape(blocks, states + 8, inner), unit_shape(toks, 2 * states, 128),
            jax.ShapeDtypeStruct((2, proj_rows + wide_rank, inner), BF16),
            jax.ShapeDtypeStruct((2, slots, states, inner), F32),
        ],
        scratch_shapes=[
            pltpu.VMEM((inner // 128, HALO + toks, 128), F32), pltpu.VMEM((toks + SPARE, inner), F32),
            pltpu.VMEM((2, BLK, states, inner), F32), pltpu.VMEM((8, inner), F32),
            pltpu.VMEM((states, inner), F32), pltpu.VMEM((2 * states * toks, 128), F32),
            pltpu.VMEM((4 * states, 2 * states * 128), BF16), pltpu.VMEM((slots, states, inner), F32),
            pltpu.VMEM((slots, states, inner), F32), pltpu.VMEM((slots, 1, inner), F32), pltpu.VMEM((states, inner), F32),
            *exchange_shapes(runs, slots, states, inner),
        ],
        compiler_params=params(collective_id=2, has_side_effects=True),
        name="first",
    )(ahead, xe, dy, conv_weight, conv_bias, x_rows, dt_weight, dt_bias, decay_rate)

    vmem = pl.BlockSpec(memory_space=pltpu.VMEM)
    last = spec((slots, None, 2 * states + 8, inner), lambda b, i: (0, 1, 0, 0))
    last_branch = spec((None, states, inner), lambda b, i: (1, 0, 0))

    grad_rows = 2 * rank + 3 * states + 8
    y, dx, rims, grads = pl.pallas_call(
        functools.partial(second_kernel, runs),
        grid=(2, slots),
        in_specs=[
            whole(2, slots, states, inner), last, last_branch, unit(blocks, states + 8, inner), unit(toks, 2 * states, 128),
            branch(states, inner), unit(HALO, inner), unit(toks, inner), unit(toks, inner), unit(3, toks, inner), unit(toks + SPARE, inner),
            unit(proj_rows, toks), branch(proj_rows + wide_rank, inner), branch(tap_count, inner), whole(2, inner),
        ],
        out_specs=[unit(toks, inner), unit(toks, inner), whole(2, slots, 8, inner), branch(grad_rows, inner)],
        out_shape=[
            unit_shape(toks, inner), unit_shape(toks, inner), jax.ShapeDtypeStruct((2, slots, 8, inner), F32),
            jax.ShapeDtypeStruct((2, grad_rows, inner), F32),
        ],
        scratch_shapes=[
            pltpu.VMEM((states, inner), F32), pltpu.VMEM((states, inner), F32), pltpu.VMEM((toks + BLK, inner), F32), pltpu.VMEM((toks + BLK, BLK * states), BF16),
            pltpu.VMEM((toks, BLK * states), BF16),
            pltpu.VMEM((2, BLK, states, inner), F32),
            pltpu.VMEM((2, BLK * states, inner), BF16), pltpu.VMEM((2, BLK * states, inner), BF16),
            pltpu.VMEM((2, BLK * states, inner), BF16),
            pltpu.VMEM((2, BLK * states, inner), BF16), pltpu.VMEM((2, BLK // 4 * states, inner), BF16),
            pltpu.VMEM((2, BLK * states, 256), BF16), pltpu.VMEM((states, inner), F32),
            pltpu.VMEM((toks + BLK, inner), F32), pltpu.VMEM((toks + BLK, inner), F32),
            pltpu.VMEM((toks + BLK, BLK * states), BF16), pltpu.VMEM((toks + BLK, BLK * states), BF16),
            pltpu.VMEM((inner // 128, toks + 2 * HALO, 128), F32), pltpu.VMEM((toks, inner), BF16),
            pltpu.VMEM((states, inner), F32), pltpu.VMEM((slots, states, inner), F32), pltpu.VMEM((slots, states, inner), F32),
            *exchange_shapes(runs, slots, states, inner),
        ],
        compiler_params=params(collective_id=3, has_side_effects=True),
        name="second",
    )(
        first_in, lasts, decay_rate, starts, tiles, decay_rate, ahead, xe, act, planes, dy, proj, weights, conv_weight, skip_gain,
    )

    def now(*block):
        return spec((None,) + block, lambda s: (s % slots,) + (0,) * len(block))

    def early(*block):
        return spec((None,) + block, lambda s: (jnp.minimum(s, slots - 1),) + (0,) * len(block))

    def after(*block):
        return spec((None,) + block, lambda s: (jnp.maximum(s - slots, 0),) + (0,) * len(block))

    small_rows = 2 * grad_rows * (inner // dim)
    main_parts = part_count(inner + dim * (inner // dim) + small_rows)
    rest_parts = part_count(dim * (inner // dim))
    mixed, d_tokens, result, x_result, factors, own = pl.pallas_call(
        functools.partial(tail_kernel, (runs, groups, slots)),
        grid=(2 * slots,),
        in_specs=[
            now(toks, dim), now(toks, dim), now(1, 3 * dim), whole(slots, toks), pl.BlockSpec(memory_space=pltpu.SMEM), now(toks, dim),
            early(toks, inner), early(2, toks, inner), whole(slots, 2, toks, inner), whole(2, slots, 8, inner),
            whole(dim, 2 * inner), whole(inner, dim), whole(slots, dim), whole(2, grad_rows, inner),
        ],
        out_specs=[
            early(toks, dim), after(toks, dim), whole(main_parts * PART_ROWS, dim), whole(rest_parts * PART_ROWS, dim),
            whole(16 * groups, dim), whole(16, dim),
        ],
        out_shape=[
            jax.ShapeDtypeStruct((slots, toks, dim), BF16), jax.ShapeDtypeStruct((slots, toks, dim), F32),
            jax.ShapeDtypeStruct((main_parts * PART_ROWS, dim), BF16), jax.ShapeDtypeStruct((rest_parts * PART_ROWS, dim), BF16),
            jax.ShapeDtypeStruct((16 * groups, dim), BF16), jax.ShapeDtypeStruct((16, dim), BF16),
        ],
        scratch_shapes=[
            pltpu.VMEM((2, slots, 8, inner), F32), pltpu.SemaphoreType.DMA((2,)), pltpu.SemaphoreType.DMA((2,)),
            pltpu.VMEM((slots, toks, inner), BF16), pltpu.VMEM((slots, toks, inner), BF16), pltpu.VMEM((slots, toks, dim), BF16),
            pltpu.VMEM((inner, dim), F32), pltpu.VMEM((dim, inner), F32),
            pltpu.VMEM((dim, inner), F32), pltpu.VMEM((8 * slots, dim), F32), pltpu.VMEM((max(runs - 1, 1), 8 * slots, dim), F32),
            pltpu.VMEM((16 * groups, dim), BF16), pltpu.SemaphoreType.DMA((runs + groups,)),
            pltpu.SemaphoreType.DMA((runs + groups,)), *reduce_shapes(main_parts, dim, runs, groups),
            *reduce_shapes(rest_parts, dim, runs, groups),
        ],
        compiler_params=params(collective_id=4, has_side_effects=True),
        name="tail",
    )(
        tokens, cotangent, modulate, token_mask, counts, hid, z_gate, y, dx, rims, input_weight, output_weight, timestep, grads,
    )

    def part(*block):
        return spec((None,) + block, lambda s: (jnp.minimum(s, slots - 1),) + (0,) * len(block))

    (
        mixed, d_tokens, d_time, grad_ada, grad_ada_bias, in_grad, tap_grad, tapb_grad, xp_grad, dtp_grad, dtb_grad, rate_grad, skip_grad,
        out_grad,
    ) = pl.pallas_call(
        finish_kernel,
        grid=(4,),
        in_specs=[
            part(toks, dim), part(toks, dim), spec((inner // 4, dim), lambda s: (s, 0)),
            spec((dim, dim), lambda s: (inner // dim + jnp.maximum(s - inner // dim, 0), 0)),
            spec((dim, dim), lambda s: (jnp.minimum(s, inner // dim - 1), 0)),
            spec((PART_ROWS, dim), lambda s: (2 * inner // PART_ROWS, 0)),
            whole(16 * groups, dim), whole(16, dim), whole(slots, dim), spec((dim, dim), lambda s: (0, jnp.minimum(s, 2))),
        ],
        out_specs=[
            part(toks, dim), part(toks, dim), whole(slots, dim), spec((dim, dim), lambda s: (0, jnp.minimum(s, 2))), whole(3 * dim),
            spec((dim, 2 * inner // 4), lambda s: (0, s)), whole(2, tap_count, inner), whole(2, inner),
            whole(2, rank + 2 * states, inner), whole(2, rank, inner), whole(2, inner), whole(2, states, inner), whole(2, inner),
            spec((inner // 4, dim), lambda s: (s, 0)),
        ],
        out_shape=[jax.ShapeDtypeStruct((slots, toks, dim), BF16)]
        + [
            jax.ShapeDtypeStruct(shape, F32)
            for shape in (
                (slots, toks, dim), (slots, dim), (dim, 3 * dim), (3 * dim,), (dim, 2 * inner), (2, tap_count, inner), (2, inner),
                (2, rank + 2 * states, inner), (2, rank, inner), (2, inner), (2, states, inner), (2, inner), (inner, dim),
            )
        ],
        compiler_params=params(),
        name="finish",
    )(mixed, d_tokens, result, result, x_result, result, factors, own, timestep, ada_weight)
    return (
        mixed, d_tokens, d_time, grad_ada, grad_ada_bias, in_grad, tap_grad, tapb_grad, jnp.swapaxes(xp_grad, 1, 2), dtp_grad, dtb_grad,
        rate_grad, skip_grad, out_grad,
    )


def solution(mesh):
    runs = P("dp", "seq", None)
    return jax.shard_map(
        per_device,
        mesh=mesh,
        in_specs=(runs, P("dp", None), P("dp"), P("dp", "seq")) + (P(),) * 11 + (runs,),
        out_specs=(runs, runs, P("dp", None)) + (P(),) * 11,
        check_vma=False,
    )
```

```python
import functools
import math

import jax
import jax.numpy as jnp
from jax import lax
from jax.experimental import pallas as pl
from jax.experimental.pallas import tpu as pltpu
from jax.sharding import PartitionSpec as P

EPSILON = 1e-06
BLK = 16
WIDE_RANK = 32
HALO = 16
SPARE = 8
LOG2E = math.log2(math.e)
F32, BF16 = jnp.float32, jnp.bfloat16
NT = (((1,), (1,)), ((), ()))
TN = (((0,), (0,)), ((), ()))
VMEM_LIMIT = 60 << 20
MESH = pl.DeviceIdType.MESH


def dot(a, b):
    return jnp.dot(a, b, preferred_element_type=F32)


def dot_nt(a, b):
    return lax.dot_general(a, b, NT, preferred_element_type=F32)


def dot_tn(a, b):
    return lax.dot_general(a, b, TN, preferred_element_type=F32)


def flip_full(value):
    turned = lax.broadcasted_iota(jnp.int32, (8, value.shape[1]), 0)
    groups = [value[at : at + 8] for at in range(0, value.shape[0], 8)]
    return jnp.concatenate([jnp.take_along_axis(group, 7 - turned, axis=0) for group in reversed(groups)], axis=0)


def flip_low(value):
    return flip_full(value.astype(F32)).astype(BF16)


def normalise(tokens_f):
    centered = tokens_f - jnp.mean(tokens_f, axis=-1, keepdims=True)
    inv_std = lax.rsqrt(jnp.mean(centered * centered, axis=-1, keepdims=True) + EPSILON)
    return centered * inv_std, inv_std


def eye(size):
    rows = lax.broadcasted_iota(jnp.int32, (size, size), 0)
    cols = lax.broadcasted_iota(jnp.int32, (size, size), 1)
    return (rows == cols).astype(BF16)


def as_column(row):
    return dot_nt(eye(row.shape[1]), jnp.broadcast_to(row.astype(F32).astype(BF16), (8, row.shape[1])))[:, :1]


def remote(src, dst, send_sem, recv_sem, target):
    return pltpu.make_async_remote_copy(
        src_ref=src, dst_ref=dst, send_sem=send_sem, recv_sem=recv_sem, device_id=target, device_id_type=MESH
    )


def greet(targets):
    barrier = pltpu.get_barrier_semaphore()
    for target in targets:
        pl.semaphore_signal(barrier, inc=1, device_id=target, device_id_type=MESH)
    pl.semaphore_wait(barrier, len(targets))


def greet_line(me, runs, others=(), tell=True, wait=True):
    barrier = pltpu.get_barrier_semaphore()
    if tell:
        for target in others:
            pl.semaphore_signal(barrier, inc=1, device_id=target, device_id_type=MESH)

        @pl.when(me > 0)
        def _():
            pl.semaphore_signal(barrier, inc=1, device_id={"seq": me - 1}, device_id_type=MESH)

        @pl.when(me < runs - 1)
        def _():
            pl.semaphore_signal(barrier, inc=1, device_id={"seq": me + 1}, device_id_type=MESH)

    if wait:
        neighbours = lax.div(me + runs - 1, runs) + lax.div(2 * runs - 2 - me, runs)
        pl.semaphore_wait(barrier, neighbours + len(others))


def swap_along_line(me, runs, ups, downs, start):
    up = [remote(src, dst, ss, rs, {"seq": me + 1}) for src, dst, ss, rs in ups]
    down = [remote(src, dst, ss, rs, {"seq": me - 1}) for src, dst, ss, rs in downs]

    @pl.when(me < runs - 1)
    def _():
        for copy in up:
            if start:
                copy.start()
            else:
                copy.wait_send()
        if not start:
            for copy in down:
                copy.wait_recv()

    @pl.when(me > 0)
    def _():
        for copy in down:
            if start:
                copy.start()
            else:
                copy.wait_send()
        if not start:
            for copy in up:
                copy.wait_recv()


def enter_kernel(
    runs, tok, cot, mask, counts, step, ada, ada_bias, win, wout,
    xe, dy, z_out, hid_out, mod_out, rim_out,
    mods, prev_tok, next_tok, prev_mask, next_mask, send_sem, recv_sem,
):
    slots, toks, dim = tok.shape
    inner = wout.shape[0]
    me = lax.axis_index("seq")
    i = pl.program_id(0)
    ups = [
        (tok.at[:, pl.ds(toks - HALO, HALO), :], prev_tok, send_sem.at[0], recv_sem.at[0]),
        (mask, prev_mask, send_sem.at[1], recv_sem.at[1]),
    ]
    downs = [
        (tok.at[:, pl.ds(0, HALO), :], next_tok, send_sem.at[2], recv_sem.at[2]),
        (mask, next_mask, send_sem.at[3], recv_sem.at[3]),
    ]

    @pl.when(i == 0)
    def _():
        greet_line(me, runs, wait=False)

        @pl.when(me == 0)
        def _():
            prev_tok[...] = jnp.zeros(prev_tok.shape, BF16)
            prev_mask[...] = jnp.zeros(prev_mask.shape, jnp.int32)

        @pl.when(me == runs - 1)
        def _():
            next_tok[...] = jnp.zeros(next_tok.shape, BF16)
            next_mask[...] = jnp.zeros(next_mask.shape, jnp.int32)

    live = jnp.where(counts[0] > i, 1.0, 0.0)

    @pl.when(i == 0)
    def _():
        time_f = step[...].astype(F32)
        time_low = (time_f * jax.nn.sigmoid(time_f)).astype(BF16)
        mods[...] = dot(time_low, ada[...]) + ada_bias[...].reshape(1, 3 * dim)

    mod = mods[pl.ds(i, 1), :]
    mod_out[...] = mod
    shift, scale, gate = mod[:, :dim], mod[:, dim : 2 * dim], mod[:, 2 * dim :]

    def hidden_of(part, scale, shift):
        normed, _ = normalise(part.astype(F32))
        return (normed * (1.0 + scale) + shift).astype(BF16)

    hid = hidden_of(tok[i], scale, shift)
    hid_out[...] = hid
    xz = dot(hid, win[...]) * (as_column(mask[pl.ds(i, 1), :]) * live)
    x_low = xz[:, :inner].astype(BF16)
    z = xz[:, inner:]
    z_out[...] = z
    d_branch = (cot[...].astype(F32) * gate).astype(BF16)
    d_summed = dot_nt(d_branch, wout[...]) * z * jax.nn.sigmoid(z)
    dy[0, :toks] = d_summed
    dy[1, :toks] = flip_full(d_summed)
    dy[:, toks:] = jnp.zeros((2, SPARE, inner), F32)
    xe[0] = x_low
    xe[1] = flip_low(x_low)

    @pl.when(i == 0)
    def _():
        greet_line(me, runs, tell=False)
        swap_along_line(me, runs, ups, downs, True)

    @pl.when(i == slots - 1)
    def _():
        swap_along_line(me, runs, ups, downs, False)
        hidden, seen = [], []
        for item in range(slots):
            row = mods[item : item + 1, :]
            rims = jnp.concatenate([prev_tok[item], next_tok[item]], axis=0)
            hidden.append(hidden_of(rims, row[:, dim : 2 * dim], row[:, :dim]))
            prev_col = as_column(prev_mask[item : item + 1, :])[toks - HALO :]
            next_col = as_column(next_mask[item : item + 1, :])[:HALO]
            live = jnp.where(counts[0] > item, 1.0, 0.0)
            seen.append(jnp.concatenate([prev_col, next_col], axis=0) * live)
        rim_x = dot(jnp.concatenate(hidden, axis=0), win[:, :inner]) * jnp.concatenate(seen, axis=0)
        for item in range(slots):
            part = rim_x[2 * HALO * item : 2 * HALO * (item + 1)]
            rim_out[item, 0] = part[:HALO].astype(BF16)
            rim_out[item, 1] = flip_full(part[HALO:]).astype(BF16)


def columns(inner, width=128):
    return [slice(at, at + width) for at in range(0, inner, width)]


def twice(row8):
    return jnp.concatenate([row8, row8], axis=0)


def spread(ref, index):
    return twice(ref[pl.ds(index, 8, stride=0), :])


def lay_out(wide, rows, picks):
    count, toks = rows.shape
    high = rows.astype(BF16).astype(F32)
    halves = jnp.concatenate([high, rows - high], axis=0).T.astype(BF16)
    for n in range(0, count, 2):
        pair = dot(halves, picks[:, n * 128 : (n + 2) * 128])
        for t in range(0, toks, 8):
            for k in range(2):
                at = 8 * (count * (t // 8) + n + k)
                wide[at : at + 8, :] = pair[t : t + 8, k * 128 : (k + 1) * 128]


def wide_tile(wide, i, count):
    at = 8 * count * (i // 8) + i % 8
    return jnp.concatenate([wide[pl.ds(at + 64 * n, 8, stride=8), :] for n in range(count // 8)], axis=0)


def across_lanes(tile, inner):
    return jnp.concatenate([tile] * (inner // 128), axis=1)


def softplus_parts(pre):
    e = jnp.exp2(-LOG2E * jnp.abs(pre))
    more = jnp.where(e < 1e-3, e - 0.5 * e * e, jnp.log(1.0 + e))
    return jnp.maximum(pre, 0.0) + more, jax.nn.sigmoid(pre)


def bit_of(index, bit):
    return lax.rem(lax.div(index, 1 << bit), 2)


def across(axis, bit):
    me = lax.axis_index(axis)
    mine = bit_of(me, bit)
    return mine, {axis: me + (1 - 2 * mine) * (1 << bit)}


class Exchange:
    def __init__(self, runs, branch, ends, backs, totals, rate, results, group, span, pre, pre_span, sends, arrivals, sems):
        self.branch, self.rate = branch, rate
        self.sources, self.totals, self.results = (ends, backs), totals, results
        self.group, self.span, self.pre, self.pre_span = group, span, pre, pre_span
        self.sends, self.arrivals, self.sems = sends, arrivals, sems
        self.links = [across("seq", bit) for bit in range(int(math.log2(runs)))]
        self.slots = ends.shape[0]
        self.states, self.inner = rate.shape

    def flow(self, kind):
        return kind if self.branch == 0 else 1 - kind

    def targets(self):
        return [target for _, target in self.links]

    def copy(self, stage, kind):
        at = 2 * stage + kind
        return remote(
            self.sends.at[at], self.arrivals.at[at], self.sems.at[0, at], self.sems.at[1, at], self.links[stage][1]
        )

    def send(self, stage, kind):
        rows = self.slots * self.states
        at = 2 * stage + kind
        for i in range(self.slots):
            self.sends[at, i * self.states : (i + 1) * self.states, :] = self.group[kind, i].astype(BF16)
        high = self.span[kind].astype(BF16).astype(F32)
        self.sends[at, rows:, :] = jnp.concatenate([high, self.span[kind] - high], axis=0).astype(BF16)
        self.copy(stage, kind).start()

    def join(self, stage, kind, last):
        mine = self.links[stage][0]
        self.copy(stage, kind).wait()
        at = 2 * stage + kind
        earlier = (mine == 1) if self.flow(kind) == 0 else (mine == 0)
        both = self.arrivals[at, self.slots * self.states :, :].astype(F32)
        length = both[: both.shape[0] // 2] + both[both.shape[0] // 2 :]
        own_span, pre_span = self.span[kind], self.pre_span[kind]
        second_span = jnp.where(earlier, own_span, length)
        rate = self.rate[...] * -LOG2E
        for i in range(self.slots):
            state = self.arrivals[at, i * self.states : (i + 1) * self.states, :].astype(F32)
            before = self.pre[kind, i]
            self.pre[kind, i] = jnp.where(earlier, state * jnp.exp2(rate * pre_span[i : i + 1]) + before, before)
            if not last:
                own = self.group[kind, i]
                first, second = jnp.where(earlier, state, own), jnp.where(earlier, own, state)
                self.group[kind, i] = first * jnp.exp2(rate * second_span[i : i + 1]) + second
        self.pre_span[kind] = jnp.where(earlier, length + pre_span, pre_span)
        if not last:
            self.span[kind] = own_span + length

    def points(self):
        count = len(self.links)

        def begin():
            self.pre[...] = jnp.zeros(self.pre.shape, F32)
            self.pre_span[...] = jnp.zeros(self.pre_span.shape, F32)
            self.span[...] = jnp.zeros(self.span.shape, F32)
            for kind in range(2):
                for i in range(self.slots):
                    self.group[kind, i] = self.sources[kind][i]
                    self.span[kind, i : i + 1, :] = self.totals[i][:1]
                if count:
                    self.send(0, kind)

        def step(stage):
            last = stage == count - 1
            for kind in range(2):
                self.join(stage, kind, last)
                if not last:
                    self.send(stage + 1, kind)

        def end():
            for kind in range(2):
                for i in range(self.slots):
                    self.results[kind][i] = self.pre[kind, i]

        return [begin] + [functools.partial(step, stage) for stage in range(count)] + [end]


def exchange_shapes(runs, slots, states, inner):
    pairs = max(int(math.log2(runs)), 1)
    span_rows = -(-slots // 8) * 8
    return [
        pltpu.VMEM((2, slots, states, inner), F32), pltpu.VMEM((2, span_rows, inner), F32),
        pltpu.VMEM((2, slots, states, inner), F32), pltpu.VMEM((2, span_rows, inner), F32),
        pltpu.VMEM((2 * pairs, slots * states + 2 * span_rows, inner), BF16),
        pltpu.VMEM((2 * pairs, slots * states + 2 * span_rows, inner), BF16),
        pltpu.SemaphoreType.DMA((2, 2 * pairs)),
    ]


def beside(points, step, first, count):
    for at in range(min(len(points), count)):
        todo = points[at:] if at == count - 1 else points[at : at + 1]

        @pl.when(step == first + at)
        def _():
            for point in todo:
                point()


def first_kernel(
    runs, slots, ahead, xe, dy, taps, tap_bias, x_rows, dt_rows, dt_bias, rate,
    act_out, planes, proj_out, last_out, starts_out, tiles, weights, first_in,
    x_cols, dx, decay, through, rate2, wide, picks, ends, backs, totals, first_rate, *exchange_scratch,
):
    toks, inner = xe.shape
    states = rate.shape[0]
    blocks = toks // BLK
    rank = WIDE_RANK
    xwt, dtw = weights.at[: weights.shape[0] - rank], weights.at[weights.shape[0] - rank :]
    delta_out, sig_out, dsilu_out = (planes.at[at] for at in range(3))
    end_out, back_out = last_out.at[:states], last_out.at[states : 2 * states]
    tap_count = taps.shape[0]
    branch, item = pl.program_id(0), pl.program_id(1)
    results = (first_in.at[0], first_in.at[1])
    exchange = Exchange(runs, 0, ends, backs, totals, first_rate, results, *exchange_scratch)

    @pl.when((branch == 0) & (item == 0))
    def _():
        greet(exchange.targets())
        first_rate[...] = rate[...]

    beside(exchange.points(), branch * slots + item, slots, slots)

    @pl.when(item == 0)
    def _():
        rate2[...] = rate[...] * -LOG2E
        picks[...] = (
            lax.broadcasted_iota(jnp.int32, picks.shape, 0) % (2 * states)
            == lax.broadcasted_iota(jnp.int32, picks.shape, 1) // 128
        ).astype(BF16)
        held = dt_rows.shape[0]
        rows = x_rows[...].astype(F32)
        gap = jnp.zeros((rank - held, inner), F32)
        wide = [rows[:held], gap, rows[held:], dt_rows[...].astype(F32), gap]
        weights[...] = jnp.concatenate(wide, axis=0).astype(BF16)

    tap_row, dt_row = tap_bias[pl.ds(branch, 1), :], dt_bias[pl.ds(branch, 1), :]
    for cols in columns(inner):
        at_col = cols.start // 128
        x_cols[at_col] = jnp.concatenate([ahead[:, cols], xe[:, cols]], axis=0).astype(F32)
        parts = []
        for row in range(0, toks, 8):
            part = tap_row[:, cols]
            for k in range(tap_count):
                part = part + taps[k : k + 1, cols] * x_cols[at_col, pl.ds(HALO - tap_count + 1 + k + row, 8), :]
            parts.append(part)
        conv = jnp.concatenate(parts, axis=0)
        open_part = jax.nn.sigmoid(conv)
        act_f = conv * open_part
        act_out[:, cols] = act_f.astype(BF16)
        dsilu_out[:, cols] = open_part + act_f * (1.0 - open_part)
    proj = dot_nt(xwt[...], act_out[...])
    proj_out[...] = proj
    dt_low = proj[:rank, :].astype(BF16)
    for cols in columns(inner, 256):
        pre = dot_tn(dt_low, dtw[:, cols]) + dt_row[:, cols]
        delta, slope = softplus_parts(pre)
        delta_out[:, cols] = delta
        sig_out[:, cols] = slope
        dx[:toks, cols] = delta * act_out[:, cols].astype(F32)
    lay_out(wide, proj[rank:, :], picks)
    end_out[...] = jnp.zeros((states, inner), F32)
    back_out[...] = jnp.zeros((states, inner), F32)
    through[...] = jnp.zeros((8, inner), F32)

    def one_block(j, slot):
        t0 = pl.multiple_of(j * BLK, BLK)
        dr, xr, yr = (ref.at[pl.ds(t0, BLK), :] for ref in (delta_out, dx, dy))
        count = 2 * states
        wide_rows = wide.at[pl.ds(pl.multiple_of(j * (BLK * count), BLK * count), BLK * count), :]
        s = end_out[...]
        before = through[...]
        starts_out[j] = jnp.concatenate([s, before], axis=0)
        rates = rate2[...]
        for i in range(BLK):
            a = jnp.exp2(spread(dr, i) * rates)
            decay[slot, i] = a
            tile = wide_tile(wide_rows, i, count)
            tiles[t0 + i] = tile
            s = a * s + spread(xr, i) * across_lanes(tile[:states], inner)
        end_out[...] = s
        m = jnp.zeros((states, inner), F32)
        for i in reversed(range(BLK)):
            m = decay[slot, i] * (m + spread(yr, i) * across_lanes(tiles[t0 + i, states:], inner))
        back_out[...] = back_out[...] + m * jnp.exp2(twice(before) * rates)
        through[...] = before + jnp.sum(dr[...], axis=0, keepdims=True)

    def block_step(k, _):
        one_block(2 * k, 0)
        one_block(2 * k + 1, 1)
        return 0

    lax.fori_loop(0, blocks // 2, block_step, 0)
    last_out[2 * states :, :] = through[...]

    @pl.when(branch == 0)
    def _():
        ends[item] = end_out[...]
        backs[item] = back_out[...]
        totals[item] = through[:1, :]


def second_kernel(
    runs, first_in, lasts, last_rate, starts, tiles, rate, ahead, xe, act, planes, dy, proj, weights, taps, skip,
    y_out, dx_out, rims, grads,
    rate2, carry, dxs, bdiag, cdiag, decay, states_low, kept_low, lam_low, rq_low, qd_low, dots, racc, gsum, hsum, db, dc,
    d_cols, d_pre_low, s_in, s_last, lam_last, *exchange_scratch,
):
    toks, inner = xe.shape
    states = rate.shape[0]
    blocks = toks // BLK
    rank = WIDE_RANK
    xwt, dtw = weights.at[: weights.shape[0] - rank], weights.at[weights.shape[0] - rank :]
    delta, sig, dsilu = (planes.at[at] for at in range(3))
    tap_count = taps.shape[0]
    held = (grads.shape[0] - 3 * states - 8) // 2
    xp_grad, dtp_grad = grads.at[: held + 2 * states], grads.at[held + 2 * states : 2 * held + 2 * states]
    at = 2 * held + 2 * states
    rate_grad, row_grads = grads.at[at : at + states], grads.at[at + states : at + states + 8]
    tapb_at, skip_at, dtb_at = (slice(tap_count + row, tap_count + row + 1) for row in range(3))
    item = pl.program_id(1)
    branch = pl.program_id(0)
    slots = lasts.shape[0]
    ends, backs = lasts.at[:, :states], lasts.at[:, states : 2 * states]
    totals = lasts.at[:, 2 * states :]
    exchange = Exchange(runs, 1, ends, backs, totals, last_rate, (s_last, lam_last), *exchange_scratch)

    @pl.when((item == 0) & (branch == 0))
    def _():
        greet(exchange.targets())

    beside(exchange.points(), branch * slots + item, 0, slots)

    @pl.when(branch == 0)
    def _():
        s_in[...] = first_in[0, item]
        carry[...] = first_in[1, item]

    @pl.when(branch == 1)
    def _():
        s_in[...] = s_last[item]
        carry[...] = lam_last[item]

    gain = skip[pl.ds(pl.program_id(0), 1), :]
    rate2[...] = rate[...] * -LOG2E
    width = BLK * states

    @pl.when(item == 0)
    def _():
        grads[...] = jnp.zeros(grads.shape, F32)

    for cols in columns(inner):
        dxs[:toks, cols] = delta[:, cols] * act[:, cols].astype(F32)
    pair_rows = 2 * states

    def inner_index(rows):
        at = lax.broadcasted_iota(jnp.int32, (rows, width), 1)
        token = lax.div(at, pair_rows) * 2 + lax.div(lax.rem(at, 16), 8)
        return token, lax.div(lax.rem(at, pair_rows), 16) * 8 + lax.rem(at, 8)

    fold = (inner_index(states)[1] == lax.broadcasted_iota(jnp.int32, (states, width), 0)).astype(BF16)
    own = lax.rem(lax.broadcasted_iota(jnp.int32, (toks, width), 0), BLK) == inner_index(toks)[0]
    bdiag[:toks, :] = jnp.where(own, dot_tn(proj[rank : rank + states, :].astype(BF16), fold), 0.0).astype(BF16)
    cdiag[...] = jnp.where(own, dot_tn(proj[rank + states :, :].astype(BF16), fold), 0.0).astype(BF16)
    mine = own[:BLK]
    picks = mine.astype(BF16)
    ones = jnp.ones((BLK, 128), BF16)
    racc[...] = jnp.zeros((states, inner), F32)

    def lane_sum(wide):
        part = [wide[:, at : at + 128] for at in range(0, inner, 128)]
        while len(part) > 1:
            pairs = [part[at] + part[at + 1] for at in range(0, len(part) - 1, 2)]
            part = pairs + part[2 * len(pairs) :]
        return part[0]

    def products(slot, j):
        t0 = pl.multiple_of(j * BLK, BLK)
        y_out[pl.ds(t0, BLK), :] = dot(cdiag[pl.ds(t0, BLK), :], states_low[slot])
        half = width // 2
        rows = bdiag[pl.ds(t0, BLK), :]
        gsum[pl.ds(t0, BLK), :] = dot(rows[:, half:], lam_low[slot, half:]) + dot(rows[:, :half], lam_low[slot, :half])
        hsum[pl.ds(t0, BLK), :] = dot(picks[:, half:], rq_low[slot, half:]) + dot(picks[:, :half], rq_low[slot, :half])
        racc[...] += dot(fold[:, : BLK // 4 * states], qd_low[slot])
        dc[pl.ds(t0, BLK), :] = jnp.where(mine, dot_nt(ones, dots[slot, :, :128]), 0.0).astype(BF16)
        db[pl.ds(t0, BLK), :] = jnp.where(mine, dot_nt(ones, dots[slot, :, 128:]), 0.0).astype(BF16)

    def one_block(slot, j):
        t0 = pl.multiple_of(j * BLK, BLK)
        dr, xr, yr = (ref.at[pl.ds(t0, BLK), :] for ref in (delta, dxs, dy))
        tile = tiles.at[pl.ds(t0, BLK)]
        r2 = rate2[...]
        groups = [slice(at, at + 8) for at in range(0, states, 8)]
        begin = starts[j]
        s = begin[:states] + s_in[...] * jnp.exp2(twice(begin[states:]) * r2)

        def both(first, second):
            return jnp.concatenate([first, second], axis=0).astype(BF16)

        def pair(ref, i):
            return both(ref[pl.ds(i, 8, stride=0), :], ref[pl.ds(i + 1, 8, stride=0), :])

        for i in range(0, BLK, 2):
            kept, after = [], []
            for t in (i, i + 1):
                a = jnp.exp2(spread(dr, t) * r2)
                decay[slot, t] = a
                kept.append(a * s)
                s = kept[-1] + spread(xr, t) * across_lanes(tile[t, :states], inner)
                after.append(s)
            y_pair = pair(yr, i)
            for number, group in enumerate(groups):
                rows = slice(i * states + 16 * number, i * states + 16 * (number + 1))
                s_low = both(after[0][group], after[1][group])
                states_low[slot, rows, :] = s_low
                kept_low[slot, rows, :] = both(kept[0][group], kept[1][group])
                dots[slot, rows, :128] = lane_sum(s_low * y_pair)
        cr = carry[...]
        r_low = [both(rate[group, :], rate[group, :]) for group in groups]
        qds = [[] for _ in groups]
        for i in reversed(range(0, BLK, 2)):
            lams = []
            for t in (i + 1, i):
                lam = cr + spread(yr, t) * across_lanes(tile[t, states:], inner)
                cr = decay[slot, t] * lam
                lams.append(lam)
            x_pair, d_pair = pair(xr, i), pair(dr, i)
            for number, group in enumerate(groups):
                rows = slice(i * states + 16 * number, i * states + 16 * (number + 1))
                l_low = both(lams[1][group], lams[0][group])
                lam_low[slot, rows, :] = l_low
                dots[slot, rows, 128:] = lane_sum(l_low * x_pair)
                q = l_low * kept_low[slot, rows, :]
                rq_low[slot, rows, :] = q * r_low[number]
                qds[number].append(q * d_pair)
                if i % 8 == 0:
                    at = i // 8 * pair_rows + 16 * number
                    part = qds[number]
                    qd_low[slot, at : at + 16, :] = (part[0] + part[1]) + (part[2] + part[3])
                    qds[number] = []
        carry[...] = cr

    def block_step(k, _):
        j = blocks - 1 - 2 * k
        for slot in range(2):
            one_block(slot, j - slot)
            products(slot, j - slot)
        return 0

    lax.fori_loop(0, blocks // 2, block_step, 0)
    rate_grad[...] += -racc[...]
    for cols in columns(inner):
        act_f = act[:, cols].astype(F32)
        row_grads[skip_at, cols] += jnp.sum(dy[:toks, cols] * act_f, axis=0, keepdims=True)
        y_out[:, cols] += gain[:, cols] * act_f
        d_pre = (act_f * gsum[:toks, cols] - hsum[:toks, cols]) * sig[:, cols]
        row_grads[dtb_at, cols] += jnp.sum(d_pre, axis=0, keepdims=True)
        d_pre_low[:, cols] = d_pre.astype(BF16)
    dtp_grad[...] += dot(proj[:rank, :].astype(BF16), d_pre_low[...])[:held]
    d_proj = jnp.concatenate(
        [dot_nt(dtw[...], d_pre_low[...]), dot_nt(fold, db[:toks, :]), dot_nt(fold, dc[:toks, :])], axis=0
    ).astype(BF16)
    xp_new = dot(d_proj, act[...])
    xp_grad[:held, :] += xp_new[:held]
    xp_grad[held:, :] += xp_new[rank:]
    d_cols[:, :HALO, :] = jnp.zeros((inner // 128, HALO, 128), F32)
    d_cols[:, HALO + toks :, :] = jnp.zeros((inner // 128, HALO, 128), F32)
    for wide_cols in columns(inner, 256):
        through = dot_tn(d_proj, xwt[:, wide_cols])
        for at in columns(256):
            cols = slice(wide_cols.start + at.start, wide_cols.start + at.stop)
            d_act = delta[:, cols] * gsum[:toks, cols] + gain[:, cols] * dy[:toks, cols] + through[:, at]
            d_conv = d_act * dsilu[:, cols]
            row_grads[tapb_at, cols] += jnp.sum(d_conv, axis=0, keepdims=True)
            x_f = jnp.concatenate([ahead[:, cols], xe[:, cols]], axis=0).astype(F32)
            at_col = cols.start // 128
            d_cols[at_col, HALO : HALO + toks, :] = d_conv
            sums = [jnp.zeros((8, 128), F32) for _ in range(tap_count)]
            for row in range(HALO - 8, HALO + toks, 8):
                part = jnp.zeros((8, 128), F32)
                for k in range(tap_count):
                    moved = d_cols[at_col, pl.ds(row + tap_count - 1 - k, 8), :]
                    part = part + taps[k : k + 1, cols] * moved
                    sums[k] = sums[k] + moved * x_f[row : row + 8]
                if row < HALO:
                    rims[branch, item, :, cols] = part
                else:
                    dx_out[row - HALO : row - HALO + 8, cols] = part
            for k in range(tap_count):
                row_grads[k : k + 1, cols] += jnp.sum(sums[k], axis=0, keepdims=True)


LAST_ROWS = 16
PART_ROWS = 512


class Ring:
    def __init__(self, bits):
        self.bits = bits
        self.size = 1 << len(bits)
        self.digits = [bit_of(lax.axis_index(axis), bit) for axis, bit in bits]
        self.place = sum(digit * (1 << at) for at, digit in enumerate(self.digits))

    def target(self, ahead):
        place = lax.rem(self.place + ahead, self.size)
        where = {}
        for at, (axis, bit) in enumerate(self.bits):
            base = where.get(axis, lax.axis_index(axis))
            where[axis] = base + (bit_of(place, at) - self.digits[at]) * (1 << bit)
        return where, place

    def targets(self):
        return [self.target(ahead)[0] for ahead in range(1, self.size)]


def stage_rings(runs, groups):
    bits = [("seq", bit) for bit in range(int(math.log2(runs)))] + [("dp", bit) for bit in range(int(math.log2(groups)))]
    return [Ring(bits[:1])] + [Ring(bits[at : at + 2]) for at in range(1, len(bits), 2)]


def part_count(rows):
    return -(-rows // PART_ROWS)


def buffer_rows(runs, groups):
    bits = int(math.log2(runs)) + int(math.log2(groups))
    size, total = PART_ROWS, 0
    for members in [2] + [1 << min(2, bits - at) for at in range(1, bits, 2)]:
        moved = size // members if size >= members * LAST_ROWS else size
        total += moved * (members - 1)
        size = moved
    return total


def reduce_shapes(parts, dim, runs, groups):
    bits = int(math.log2(runs)) + int(math.log2(groups))
    stages = 1 + bits // 2
    room = parts * buffer_rows(runs, groups)
    sems = pltpu.SemaphoreType.DMA((parts, 2 * stages, 3))
    return [
        pltpu.VMEM((parts * PART_ROWS, dim), F32), pltpu.VMEM((room, dim), BF16), pltpu.VMEM((room, dim), BF16),
        pltpu.VMEM((parts * PART_ROWS, dim), BF16), sems, sems,
    ]


class Reduction:
    def __init__(self, rings, turns, segments, acc, sends, arrivals, gathered, send_sem, recv_sem):
        self.rings = rings
        self.count = len(rings)
        self.parts = len(turns)
        self.segments = segments
        self.acc, self.sends, self.arrivals, self.gathered = acc, sends, arrivals, gathered
        self.send_sem, self.recv_sem = send_sem, recv_sem
        room = sends.shape[0] // self.parts
        self.steps = []
        for part, turn in enumerate(turns):
            later = rings[1:]
            turn = turn % max(len(later), 1)
            order = rings[:1] + later[turn:] + later[:turn]
            start, size, at = part * PART_ROWS, PART_ROWS, part * room
            steps = []
            for ring in order:
                split = size >= ring.size * LAST_ROWS
                moved = size // ring.size if split else size
                keep = pl.multiple_of(start + ring.place * moved, LAST_ROWS) if split else start
                steps.append((ring, start, split, moved, keep, at))
                at += moved * (ring.size - 1)
                start, size = keep, moved
            self.steps.append(steps)

    def assemble(self, part):
        low, high = part * PART_ROWS, (part + 1) * PART_ROWS
        at = 0
        for get, size in self.segments:
            first, last = max(at, low), min(at + size, high)
            if first < last:
                self.acc[first:last, :] = get(first - at, last - first)
            at += size
        if at < high:
            first = max(at, low)
            self.acc[first:high, :] = jnp.zeros((high - first, self.acc.shape[1]), F32)

    def scatter_copy(self, part, stage, ahead):
        ring, _, _, moved, _, at = self.steps[part][stage]
        at += (ahead - 1) * moved
        return remote(
            self.sends.at[pl.ds(at, moved), :], self.arrivals.at[pl.ds(at, moved), :],
            self.send_sem.at[part, stage, ahead - 1], self.recv_sem.at[part, stage, ahead - 1], ring.target(ahead)[0],
        )

    def scatter(self, part, stage):
        ring, start, split, moved, _, at = self.steps[part][stage]
        for ahead in range(1, ring.size):
            place = ring.target(ahead)[1]
            away = pl.multiple_of(start + place * moved, LAST_ROWS) if split else start
            here = at + (ahead - 1) * moved
            self.sends[here : here + moved, :] = self.acc[pl.ds(away, moved), :].astype(BF16)
            self.scatter_copy(part, stage, ahead).start()

    def settle(self, part, stage):
        ring, _, split, moved, keep, at = self.steps[part][stage]
        for ahead in range(1, ring.size):
            self.scatter_copy(part, stage, ahead).wait()
        held = self.acc[pl.ds(keep, moved), :]
        came = [
            self.arrivals[at + (ahead - 1) * moved : at + ahead * moved, :].astype(F32) for ahead in range(1, ring.size)
        ]
        if split:
            for part in came:
                held = held + part
        else:
            values = [held.astype(BF16).astype(F32)] + came
            total = jnp.zeros_like(held)
            for place in range(ring.size):
                behind = lax.rem(ring.place - place + ring.size, ring.size)
                chosen = values[0]
                for ahead in range(1, ring.size):
                    chosen = jnp.where(behind == ahead, values[ahead], chosen)
                total = total + chosen
            held = total
        self.acc[pl.ds(keep, moved), :] = held

    def gather_copies(self, part, stage):
        ring, _, split, moved, keep, _ = self.steps[part][stage]
        here = self.gathered.at[pl.ds(keep, moved), :]
        return [
            remote(
                here, here, self.send_sem.at[part, self.count + stage, ahead - 1],
                self.recv_sem.at[part, self.count + stage, ahead - 1], ring.target(ahead)[0],
            )
            for ahead in range(1, ring.size)
            if split
        ]

    def points(self):
        def begin():
            for part in range(self.parts):
                self.assemble(part)
                self.scatter(part, 0)

        def split(stage):
            for part in range(self.parts):
                self.settle(part, stage - 1)
                self.scatter(part, stage)

        def turn():
            for part in range(self.parts):
                self.settle(part, self.count - 1)
                _, _, _, moved, keep, _ = self.steps[part][-1]
                self.gathered[pl.ds(keep, moved), :] = self.acc[pl.ds(keep, moved), :].astype(BF16)
                for copy in self.gather_copies(part, self.count - 1):
                    copy.start()

        def join(stage):
            for part in range(self.parts):
                for copy in self.gather_copies(part, stage + 1):
                    copy.wait()
                if stage >= 0:
                    for copy in self.gather_copies(part, stage):
                        copy.start()

        points = [begin]
        points += [functools.partial(split, stage) for stage in range(1, self.count)]
        points += [turn]
        return points + [functools.partial(join, stage) for stage in reversed(range(-1, self.count - 1))]


def big_segments(ref, dim):
    return [
        (lambda at, size, lane=lane: ref[at : at + size, lane : lane + dim], ref.shape[0])
        for lane in range(0, ref.shape[1], dim)
    ]


def small_segments(ref, dim):
    return [
        (lambda at, size, branch=branch, lane=lane: ref[branch, at : at + size, lane : lane + dim], ref.shape[1])
        for lane in range(0, ref.shape[2], dim)
        for branch in range(2)
    ]


def tail_kernel(
    plan, tok, cot, mod, mask, counts, hid, z_in, y, dx, rims, win, wout, step,
    grads,
    mixed, d_tokens, result, x_result, factors, own_rows,
    late, rim_send, rim_recv, dz, d_xs, hids, out_grad, z_grad, x_grad, mod_sum, mod_in, table, small_send, small_recv, *reduce_scratch,
):
    runs, groups, slots = plan
    me = lax.axis_index("seq")
    downs = [(rims.at[0], late.at[0], rim_send.at[0], rim_recv.at[0])]
    ups = [(rims.at[1], late.at[1], rim_send.at[1], rim_recv.at[1])]
    dim = tok.shape[-1]
    toks, inner = z_in.shape
    now = pl.program_id(0)
    i = lax.rem(now, slots)
    rings = stage_rings(runs, groups)
    seq_ring = Ring([("seq", bit) for bit in range(int(math.log2(runs)))])
    dp_ring = Ring([("dp", bit) for bit in range(int(math.log2(groups)))])
    half = len(reduce_scratch) // 2
    smalls = small_segments(grads, dim)
    segments = big_segments(out_grad, dim) + big_segments(z_grad, dim) + smalls
    main = Reduction(rings, [part % 3 // 2 for part in range(result.shape[0] // PART_ROWS)], segments, *reduce_scratch[:half])
    rest = Reduction(rings, [part % 2 for part in range(x_result.shape[0] // PART_ROWS)], big_segments(x_grad, dim), *reduce_scratch[half:])
    main_points, rest_points = main.points(), rest.points()

    @pl.when(now == 0)
    def _():
        greet_line(me, runs, [target for ring in rings + [seq_ring, dp_ring] for target in ring.targets()], wait=False)

        @pl.when(me == 0)
        def _():
            late[1] = jnp.zeros(late.shape[1:], F32)

        @pl.when(me == runs - 1)
        def _():
            late[0] = jnp.zeros(late.shape[1:], F32)

        out_grad[...] = jnp.zeros(out_grad.shape, F32)
        z_grad[...] = jnp.zeros(z_grad.shape, F32)
        x_grad[...] = jnp.zeros(x_grad.shape, F32)
        mod_sum[...] = jnp.zeros(mod_sum.shape, F32)

    scale, gate = mod[:, dim : 2 * dim], mod[:, 2 * dim :]
    valid = as_column(mask[pl.ds(i, 1), :]) * jnp.where(counts[0] > i, 1.0, 0.0)
    mod_rows = pl.ds(pl.multiple_of(8 * i, 8), 8)

    @pl.when(now < slots)
    def _():
        cot_f = cot[...].astype(F32)
        z = z_in[...]
        z_sig = jax.nn.sigmoid(z)
        z_silu = z * z_sig
        summed = y[0] + flip_full(y[1])
        gated = (summed * z_silu).astype(BF16)
        branch_out = dot(gated, wout[...])
        mixed[...] = (tok[...].astype(F32) + gate * branch_out).astype(BF16)
        d_branch = (cot_f * gate).astype(BF16)
        out_grad[...] += dot_tn(gated, d_branch)
        d_zgate = dot_nt(d_branch, wout[...]) * summed * (z_sig + z_silu * (1.0 - z_sig))
        d_low = (d_zgate * valid).astype(BF16)
        dz[i] = d_low
        z_grad[...] += dot_tn(hid[...], d_low)
        hids[i] = hid[...]
        d_gate = jnp.sum(cot_f * branch_out, axis=0, keepdims=True)
        mod_sum[mod_rows, :] = jnp.concatenate([jnp.zeros((2, dim), F32), d_gate, jnp.zeros((5, dim), F32)], axis=0)

    @pl.when(now == 0)
    def _():
        peers = [target for ring in rings + [seq_ring, dp_ring] for target in ring.targets()]
        greet_line(me, runs, peers, tell=False)
        swap_along_line(me, runs, ups, downs, True)

    @pl.when(now == slots)
    def _():
        main_points[0]()
        swap_along_line(me, runs, ups, downs, False)
        edge = late.shape[2]

        def with_late(part, extra):
            return jnp.concatenate([part[: toks - edge], part[toks - edge :] + extra], axis=0)

        for item in range(slots):
            seen = as_column(mask[item : item + 1, :]) * jnp.where(counts[0] > item, 1.0, 0.0)
            d_x = with_late(dx[item, 0], late[0, item]) + flip_full(with_late(dx[item, 1], late[1, item]))
            d_low = (d_x * seen).astype(BF16)
            d_xs[item] = d_low
            x_grad[...] += dot_tn(hids[item], d_low)
        rest_points[0]()
        main_points[1]()

    @pl.when(now >= slots)
    def _():
        d_hidden = dot_nt(d_xs[i], win[:, :inner]) + dot_nt(dz[i], win[:, inner:])
        normed, inv_std = normalise(tok[...].astype(F32))
        d_shift = jnp.sum(d_hidden, axis=0, keepdims=True)
        d_scale = jnp.sum(d_hidden * normed, axis=0, keepdims=True)
        mod_sum[mod_rows, :] += jnp.concatenate([d_shift, d_scale, jnp.zeros((6, dim), F32)], axis=0)
        d_normed = d_hidden * (1.0 + scale)
        d_tokens[...] = cot[...].astype(F32) + inv_std * (
            d_normed
            - jnp.mean(d_normed, axis=-1, keepdims=True)
            - normed * jnp.mean(d_normed * normed, axis=-1, keepdims=True)
        )

    @pl.when(now == slots)
    def _():
        rest_points[1]()

    def sum_copies():
        return [
            remote(mod_sum, mod_in.at[ahead - 1], small_send.at[ahead - 1], small_recv.at[ahead - 1], seq_ring.target(ahead)[0])
            for ahead in range(1, seq_ring.size)
        ]

    def table_copies():
        at = pl.multiple_of(dp_ring.place * 16, 16)
        here = table.at[pl.ds(at, 16), :]
        base = seq_ring.size - 1
        return [
            remote(here, here, small_send.at[base + ahead - 1], small_recv.at[base + ahead - 1], dp_ring.target(ahead)[0])
            for ahead in range(1, dp_ring.size)
        ]

    def start_small():
        for copy in sum_copies():
            copy.start()

    def turn_small():
        for copy in sum_copies():
            copy.wait()
        values = [mod_sum[...]] + [mod_in[ahead - 1] for ahead in range(1, seq_ring.size)]
        total = jnp.zeros(mod_sum.shape, F32)
        for place in range(seq_ring.size):
            behind = lax.rem(seq_ring.place - place + seq_ring.size, seq_ring.size)
            chosen = values[0]
            for ahead in range(1, seq_ring.size):
                chosen = jnp.where(behind == ahead, values[ahead], chosen)
            total = total + chosen
        time_f = step[...].astype(F32)
        time_low = time_f * jax.nn.sigmoid(time_f)
        lines = [total[8 * item : 8 * item + 3] for item in range(slots)] + [time_low]
        lines.append(jnp.zeros((16 - 4 * slots, dim), F32))
        own = jnp.concatenate(lines, axis=0).astype(BF16)
        own_rows[...] = own
        table[pl.ds(pl.multiple_of(dp_ring.place * 16, 16), 16), :] = own
        for copy in table_copies():
            copy.start()

    def end_small():
        for copy in table_copies():
            copy.wait()
        factors[...] = table[...]

    @pl.when(now == 2 * slots - 1)
    def _():
        start_small()
        for at in range(2, len(main_points)):
            main_points[at]()
            if at == 2:
                turn_small()
            rest_points[at]()
        end_small()
        result[...] = main.gathered[...]
        x_result[...] = rest.gathered[...]


def finish_kernel(
    mixed_in, tokens_in, outs, zs, xs, smalls, factors, own, step, ada,
    mixed, d_tokens, grad_time, grad_ada, grad_ada_bias, in_grad, tap_grad, tapb_grad, xp_grad, dtp_grad, dtb_grad, rate_grad, skip_grad, out_grad,
):
    dim, inner = in_grad.shape[0], rate_grad.shape[2]
    slots = step.shape[0]
    now = pl.program_id(0)
    mixed[...] = mixed_in[...]
    d_tokens[...] = tokens_in[...]
    out_grad[...] = outs[...].astype(F32)
    in_grad[...] = jnp.where(now < inner // dim, xs[...], zs[...]).astype(F32)
    table = factors[...]
    length = table.shape[0]

    for part in range(3):

        @pl.when(now == part)
        def _():
            row = lax.broadcasted_iota(jnp.int32, (length, length), 0)
            col = lax.broadcasted_iota(jnp.int32, (length, length), 1)
            item = row % 16 - 3 * slots
            wanted = row // 16 * 16 + 3 * item + part
            mods = dot(((col == wanted) & (item >= 0) & (item < slots)).astype(BF16), table)
            lanes = slice(part * dim, (part + 1) * dim)
            grad_ada[...] = dot_tn(table, mods.astype(BF16))
            grad_ada_bias[lanes] = jnp.sum(mods, axis=0)
            mine = own[...].astype(F32)
            picked = jnp.concatenate([mine[3 * i + part : 3 * i + part + 1] for i in range(slots)], axis=0)
            d_time = dot_nt(picked.astype(BF16), ada[...])
            grad_time[...] = d_time if part == 0 else grad_time[...] + d_time

    @pl.when(now == 3)
    def _():
        time_f = step[...].astype(F32)
        time_sig = jax.nn.sigmoid(time_f)
        grad_time[...] = grad_time[...] * time_sig * (1.0 + time_f * (1.0 - time_sig))
        at = 0
        for first in range(0, inner, dim):
            lanes = slice(first, first + dim)
            for branch in range(2):
                for ref in (xp_grad, dtp_grad, rate_grad, tap_grad):
                    size = ref.shape[1]
                    ref[branch, :, lanes] = smalls[at : at + size, :].astype(F32)
                    at += size
                for ref in (tapb_grad, skip_grad, dtb_grad):
                    ref[branch : branch + 1, lanes] = smalls[at : at + 1, :].astype(F32)
                    at += 1
                at += 1


def params(**more):
    return pltpu.CompilerParams(vmem_limit_bytes=VMEM_LIMIT, **more)


def spec(block, index):
    return pl.BlockSpec(block, index)


def per_device(
    tokens, timestep, counts, token_mask, ada_weight, ada_bias, input_weight, conv_weight, conv_bias, x_weight, dt_weight,
    dt_bias, decay_rate, skip_gain, output_weight, cotangent,
):
    slots, toks, dim = tokens.shape
    inner = output_weight.shape[0]
    rank = dt_weight.shape[1]
    states = decay_rate.shape[1]
    tap_count = conv_weight.shape[1]
    wide_rank = WIDE_RANK
    proj_rows = wide_rank + 2 * states
    blocks = toks // BLK
    runs = lax.axis_size("seq")
    groups = lax.axis_size("dp")
    x_rows = jnp.swapaxes(x_weight, 1, 2)

    def item(*block):
        return spec((None,) + block, lambda i: (i,) + (0,) * len(block))

    def whole(*block):
        return spec(block, lambda *_: (0,) * len(block))

    xe, dy, z_gate, hid, modulate, ahead = pl.pallas_call(
        functools.partial(enter_kernel, runs),
        grid=(slots,),
        in_specs=[
            whole(slots, toks, dim), item(toks, dim), whole(slots, toks), pl.BlockSpec(memory_space=pltpu.SMEM), whole(slots, dim), whole(dim, 3 * dim),
            whole(3 * dim), whole(dim, 2 * inner), whole(inner, dim),
        ],
        out_specs=[
            item(2, toks, inner), item(2, toks + SPARE, inner), item(toks, inner), item(toks, dim), item(1, 3 * dim),
            whole(slots, 2, HALO, inner),
        ],
        out_shape=[
            jax.ShapeDtypeStruct((slots, 2, toks, inner), BF16),
            jax.ShapeDtypeStruct((slots, 2, toks + SPARE, inner), F32),
            jax.ShapeDtypeStruct((slots, toks, inner), F32),
            jax.ShapeDtypeStruct((slots, toks, dim), BF16),
            jax.ShapeDtypeStruct((slots, 1, 3 * dim), F32),
            jax.ShapeDtypeStruct((slots, 2, HALO, inner), BF16),
        ],
        scratch_shapes=[
            pltpu.VMEM((slots, 3 * dim), F32),
            pltpu.VMEM((slots, HALO, dim), BF16), pltpu.VMEM((slots, HALO, dim), BF16), pltpu.VMEM((slots, toks), jnp.int32),
            pltpu.VMEM((slots, toks), jnp.int32), pltpu.SemaphoreType.DMA((4,)), pltpu.SemaphoreType.DMA((4,)),
        ],
        compiler_params=params(collective_id=1, has_side_effects=True),
        name="enter",
    )(
        tokens, cotangent, token_mask, counts, timestep, ada_weight, ada_bias, input_weight, output_weight,
    )

    def unit(*block):
        return spec((None, None) + block, lambda b, i: (i, b) + (0,) * len(block))

    def branch(*block):
        return spec((None,) + block, lambda b, i: (b,) + (0,) * len(block))

    def unit_shape(*block, kind=F32):
        return jax.ShapeDtypeStruct((slots, 2) + block, kind)

    act, planes, proj, lasts, starts, tiles, weights, first_in = pl.pallas_call(
        functools.partial(first_kernel, runs, slots),
        grid=(2, slots),
        in_specs=[
            unit(HALO, inner), unit(toks, inner), unit(toks + SPARE, inner), branch(tap_count, inner), whole(2, inner),
            branch(rank + 2 * states, inner), branch(rank, inner), whole(2, inner), branch(states, inner),
        ],
        out_specs=[
            unit(toks, inner), unit(3, toks, inner), unit(proj_rows, toks), unit(2 * states + 8, inner),
            unit(blocks, states + 8, inner), unit(toks, 2 * states, 128), branch(proj_rows + wide_rank, inner),
            whole(2, slots, states, inner),
        ],
        out_shape=[
            unit_shape(toks, inner, kind=BF16), unit_shape(3, toks, inner), unit_shape(proj_rows, toks),
            unit_shape(2 * states + 8, inner), unit_shape(blocks, states + 8, inner), unit_shape(toks, 2 * states, 128),
            jax.ShapeDtypeStruct((2, proj_rows + wide_rank, inner), BF16),
            jax.ShapeDtypeStruct((2, slots, states, inner), F32),
        ],
        scratch_shapes=[
            pltpu.VMEM((inner // 128, HALO + toks, 128), F32), pltpu.VMEM((toks + SPARE, inner), F32),
            pltpu.VMEM((2, BLK, states, inner), F32), pltpu.VMEM((8, inner), F32),
            pltpu.VMEM((states, inner), F32), pltpu.VMEM((2 * states * toks, 128), F32),
            pltpu.VMEM((4 * states, 2 * states * 128), BF16), pltpu.VMEM((slots, states, inner), F32),
            pltpu.VMEM((slots, states, inner), F32), pltpu.VMEM((slots, 1, inner), F32), pltpu.VMEM((states, inner), F32),
            *exchange_shapes(runs, slots, states, inner),
        ],
        compiler_params=params(collective_id=2, has_side_effects=True),
        name="first",
    )(ahead, xe, dy, conv_weight, conv_bias, x_rows, dt_weight, dt_bias, decay_rate)

    vmem = pl.BlockSpec(memory_space=pltpu.VMEM)
    last = spec((slots, None, 2 * states + 8, inner), lambda b, i: (0, 1, 0, 0))
    last_branch = spec((None, states, inner), lambda b, i: (1, 0, 0))

    grad_rows = 2 * rank + 3 * states + 8
    y, dx, rims, grads = pl.pallas_call(
        functools.partial(second_kernel, runs),
        grid=(2, slots),
        in_specs=[
            whole(2, slots, states, inner), last, last_branch, unit(blocks, states + 8, inner), unit(toks, 2 * states, 128),
            branch(states, inner), unit(HALO, inner), unit(toks, inner), unit(toks, inner), unit(3, toks, inner), unit(toks + SPARE, inner),
            unit(proj_rows, toks), branch(proj_rows + wide_rank, inner), branch(tap_count, inner), whole(2, inner),
        ],
        out_specs=[unit(toks, inner), unit(toks, inner), whole(2, slots, 8, inner), branch(grad_rows, inner)],
        out_shape=[
            unit_shape(toks, inner), unit_shape(toks, inner), jax.ShapeDtypeStruct((2, slots, 8, inner), F32),
            jax.ShapeDtypeStruct((2, grad_rows, inner), F32),
        ],
        scratch_shapes=[
            pltpu.VMEM((states, inner), F32), pltpu.VMEM((states, inner), F32), pltpu.VMEM((toks + BLK, inner), F32), pltpu.VMEM((toks + BLK, BLK * states), BF16),
            pltpu.VMEM((toks, BLK * states), BF16),
            pltpu.VMEM((2, BLK, states, inner), F32),
            pltpu.VMEM((2, BLK * states, inner), BF16), pltpu.VMEM((2, BLK * states, inner), BF16),
            pltpu.VMEM((2, BLK * states, inner), BF16),
            pltpu.VMEM((2, BLK * states, inner), BF16), pltpu.VMEM((2, BLK // 4 * states, inner), BF16),
            pltpu.VMEM((2, BLK * states, 256), BF16), pltpu.VMEM((states, inner), F32),
            pltpu.VMEM((toks + BLK, inner), F32), pltpu.VMEM((toks + BLK, inner), F32),
            pltpu.VMEM((toks + BLK, BLK * states), BF16), pltpu.VMEM((toks + BLK, BLK * states), BF16),
            pltpu.VMEM((inner // 128, toks + 2 * HALO, 128), F32), pltpu.VMEM((toks, inner), BF16),
            pltpu.VMEM((states, inner), F32), pltpu.VMEM((slots, states, inner), F32), pltpu.VMEM((slots, states, inner), F32),
            *exchange_shapes(runs, slots, states, inner),
        ],
        compiler_params=params(collective_id=3, has_side_effects=True),
        name="second",
    )(
        first_in, lasts, decay_rate, starts, tiles, decay_rate, ahead, xe, act, planes, dy, proj, weights, conv_weight, skip_gain,
    )

    def now(*block):
        return spec((None,) + block, lambda s: (s % slots,) + (0,) * len(block))

    def early(*block):
        return spec((None,) + block, lambda s: (jnp.minimum(s, slots - 1),) + (0,) * len(block))

    def after(*block):
        return spec((None,) + block, lambda s: (jnp.maximum(s - slots, 0),) + (0,) * len(block))

    small_rows = 2 * grad_rows * (inner // dim)
    main_parts = part_count(inner + dim * (inner // dim) + small_rows)
    rest_parts = part_count(dim * (inner // dim))
    mixed, d_tokens, result, x_result, factors, own = pl.pallas_call(
        functools.partial(tail_kernel, (runs, groups, slots)),
        grid=(2 * slots,),
        in_specs=[
            now(toks, dim), now(toks, dim), now(1, 3 * dim), whole(slots, toks), pl.BlockSpec(memory_space=pltpu.SMEM), now(toks, dim),
            early(toks, inner), early(2, toks, inner), whole(slots, 2, toks, inner), whole(2, slots, 8, inner),
            whole(dim, 2 * inner), whole(inner, dim), whole(slots, dim), whole(2, grad_rows, inner),
        ],
        out_specs=[
            early(toks, dim), after(toks, dim), whole(main_parts * PART_ROWS, dim), whole(rest_parts * PART_ROWS, dim),
            whole(16 * groups, dim), whole(16, dim),
        ],
        out_shape=[
            jax.ShapeDtypeStruct((slots, toks, dim), BF16), jax.ShapeDtypeStruct((slots, toks, dim), F32),
            jax.ShapeDtypeStruct((main_parts * PART_ROWS, dim), BF16), jax.ShapeDtypeStruct((rest_parts * PART_ROWS, dim), BF16),
            jax.ShapeDtypeStruct((16 * groups, dim), BF16), jax.ShapeDtypeStruct((16, dim), BF16),
        ],
        scratch_shapes=[
            pltpu.VMEM((2, slots, 8, inner), F32), pltpu.SemaphoreType.DMA((2,)), pltpu.SemaphoreType.DMA((2,)),
            pltpu.VMEM((slots, toks, inner), BF16), pltpu.VMEM((slots, toks, inner), BF16), pltpu.VMEM((slots, toks, dim), BF16),
            pltpu.VMEM((inner, dim), F32), pltpu.VMEM((dim, inner), F32),
            pltpu.VMEM((dim, inner), F32), pltpu.VMEM((8 * slots, dim), F32), pltpu.VMEM((max(runs - 1, 1), 8 * slots, dim), F32),
            pltpu.VMEM((16 * groups, dim), BF16), pltpu.SemaphoreType.DMA((runs + groups,)),
            pltpu.SemaphoreType.DMA((runs + groups,)), *reduce_shapes(main_parts, dim, runs, groups),
            *reduce_shapes(rest_parts, dim, runs, groups),
        ],
        compiler_params=params(collective_id=4, has_side_effects=True),
        name="tail",
    )(
        tokens, cotangent, modulate, token_mask, counts, hid, z_gate, y, dx, rims, input_weight, output_weight, timestep, grads,
    )

    def part(*block):
        return spec((None,) + block, lambda s: (jnp.minimum(s, slots - 1),) + (0,) * len(block))

    (
        mixed, d_tokens, d_time, grad_ada, grad_ada_bias, in_grad, tap_grad, tapb_grad, xp_grad, dtp_grad, dtb_grad, rate_grad, skip_grad,
        out_grad,
    ) = pl.pallas_call(
        finish_kernel,
        grid=(4,),
        in_specs=[
            part(toks, dim), part(toks, dim), spec((inner // 4, dim), lambda s: (s, 0)),
            spec((dim, dim), lambda s: (inner // dim + jnp.maximum(s - inner // dim, 0), 0)),
            spec((dim, dim), lambda s: (jnp.minimum(s, inner // dim - 1), 0)),
            spec((PART_ROWS, dim), lambda s: (2 * inner // PART_ROWS, 0)),
            whole(16 * groups, dim), whole(16, dim), whole(slots, dim), spec((dim, dim), lambda s: (0, jnp.minimum(s, 2))),
        ],
        out_specs=[
            part(toks, dim), part(toks, dim), whole(slots, dim), spec((dim, dim), lambda s: (0, jnp.minimum(s, 2))), whole(3 * dim),
            spec((dim, 2 * inner // 4), lambda s: (0, s)), whole(2, tap_count, inner), whole(2, inner),
            whole(2, rank + 2 * states, inner), whole(2, rank, inner), whole(2, inner), whole(2, states, inner), whole(2, inner),
            spec((inner // 4, dim), lambda s: (s, 0)),
        ],
        out_shape=[jax.ShapeDtypeStruct((slots, toks, dim), BF16)]
        + [
            jax.ShapeDtypeStruct(shape, F32)
            for shape in (
                (slots, toks, dim), (slots, dim), (dim, 3 * dim), (3 * dim,), (dim, 2 * inner), (2, tap_count, inner), (2, inner),
                (2, rank + 2 * states, inner), (2, rank, inner), (2, inner), (2, states, inner), (2, inner), (inner, dim),
            )
        ],
        compiler_params=params(),
        name="finish",
    )(mixed, d_tokens, result, result, x_result, result, factors, own, timestep, ada_weight)
    return (
        mixed, d_tokens, d_time, grad_ada, grad_ada_bias, in_grad, tap_grad, tapb_grad, jnp.swapaxes(xp_grad, 1, 2), dtp_grad, dtb_grad,
        rate_grad, skip_grad, out_grad,
    )


def solution(mesh):
    runs = P("dp", "seq", None)
    return jax.shard_map(
        per_device,
        mesh=mesh,
        in_specs=(runs, P("dp", None), P("dp"), P("dp", "seq")) + (P(),) * 11 + (runs,),
        out_specs=(runs, runs, P("dp", None)) + (P(),) * 11,
        check_vma=False,
    )
```
